32 devices in a mesh: section: 4 (over y, x), dp: 8 (over z, core).
Axes of the slice: x: 2, y: 2, z: 4, core: 2. Of those that a mesh axis runs over, the one named last changes fastest.
Arguments:
- images: bfloat16 [4, 16, 18, 18, 256], P('section', 'dp'), may hold values from -6 to 6
- res_ids: int32 [4, 16], P(None, 'dp'), may hold values from 0 to 2, as said below
- weights: bfloat16 [4, 4608, 512], P('section'), may hold values from -0.09375 to 0.09375
- bn_gain: float32 [4, 2, 512], P('section'), may hold values from 0.5 to 1.5
- bn_bias: float32 [4, 2, 512], P('section'), may hold values from -3 to 3
- cotangent: bfloat16 [4, 16, 9, 9, 512], P('section', 'dp'), may hold values from -6 to 6
Outputs:
- block_output: bfloat16 [4, 16, 9, 9, 512], P('section', 'dp')
- image_grad: bfloat16 [4, 16, 18, 18, 256], P('section', 'dp')
- weight_grad: float32 [4, 4608, 512], P('section')
- gain_grad: float32 [4, 2, 512], P('section')
- bias_grad: float32 [4, 2, 512], P('section')
The draws below stay inside these ranges and needn't reach their ends.
Inputs may be any that keep to these rules, and one draw needn't show every extreme that they name: In every micro-batch m, res_ids[m, 0] is 2 and res_ids[m, 1] is 0; the other entries are drawn evenly from the three levels.
All inputs are finite; a program needn't handle non-finite values.
Results may differ from the reference program's by a relative error of at most 0.014.
Values may be sent and summed in bfloat16 or wider, within the bound.
No kernel may reach another device: no remote copies, remote signals or barrier semaphores. Data moves between devices by JAX's collectives and lax.ppermute only.
A program may use at most 256 MiB of HBM per device.

```python
import jax
import jax.numpy as jnp
from jax import lax

C_IN = 256
C = 512
HALF = 9
SIDE = 18
MICRO = 4
IMAGES = 16


def draw_res_ids(key, part):
    key = jax.random.fold_in(key, 7)
    levels = jax.random.randint(key, (MICRO, IMAGES), 0, 3)
    levels = levels.at[:, 0].set(2)
    levels = levels.at[:, 1].set(0)
    return levels.astype(jnp.int32)


def shard_levels(key, extent, cuts, smallest, high):
    level, own = 1.0, jax.random.fold_in(key, 6)
    for axis_at, shards_of in cuts:
        heights = jnp.exp(jax.random.uniform(jax.random.fold_in(own, axis_at), (shards_of,), jnp.float32, smallest / len(cuts), high / len(cuts)))
        level = level * jnp.repeat(heights, extent[axis_at] // shards_of).reshape([-1 if axis == axis_at else 1 for axis in range(len(extent))])
    return level


def normal_values(rng, dims, width, most, cuts=(), kind=jnp.bfloat16):
    drawn = width * jax.random.normal(rng, dims, jnp.float32)
    if cuts:
        drawn = drawn * shard_levels(rng, dims, cuts, -0.22, 0.18)
    return jnp.clip(drawn, -most, most).astype(kind)


def setup_inputs(seed: int = 0) -> dict:
    arg_keys = jax.random.split(jax.random.key(seed), 7)
    images = normal_values(arg_keys[0], (MICRO, IMAGES, SIDE, SIDE, C_IN), 1.0, 6.0, ((0, 4), (1, 8)))
    res_ids = draw_res_ids(jax.random.fold_in(arg_keys[6], 71), 0)
    weights = normal_values(arg_keys[2], (4, 9 * C, C), (9 * C) ** -0.5, 0.09375, ((0, 4),))
    bn_gain = jnp.clip(1.0 + 0.1 * jax.random.normal(arg_keys[3], (4, 2, C), jnp.float32), 0.5, 1.5)
    bn_bias = normal_values(arg_keys[4], (4, 2, C), 0.5, 3.0, ((0, 4),), jnp.float32)
    cotangent = normal_values(arg_keys[5], (MICRO, IMAGES, HALF, HALF, C), 1.0, 6.0, ((0, 4), (1, 8)))
    return {"images": images, "res_ids": res_ids, "weights": weights, "bn_gain": bn_gain, "bn_bias": bn_bias, "cotangent": cotangent}


@jax.custom_vjp
def low(v):
    return lax.optimization_barrier(v.astype(jnp.bfloat16)).astype(jnp.float32)

@jax.custom_vjp
def low_back(v):
    return v

def low_keep(v):
    return (low(v), None)

def low_pass(kept, grad):
    return (grad,)

def back_keep(v):
    return (v, None)

def back_low(kept, grad):
    return (low(grad),)
low.defvjp(low_keep, low_pass)
low_back.defvjp(back_keep, back_low)
epsilon = 1e-05
highest = lax.Precision.HIGHEST

def regions(levels):
    inner_side = HALF - 2 * (2 - levels)
    small_rows = jnp.arange(HALF, dtype=jnp.int32)
    large_rows = jnp.arange(2 * HALF, dtype=jnp.int32)
    inner_mask = (small_rows[None, :] < inner_side[:, None]).astype(jnp.float32)
    outer_mask = (large_rows[None, :] < 2 * inner_side[:, None]).astype(jnp.float32)
    return (outer_mask[:, :, None] * outer_mask[:, None, :], inner_mask[:, :, None] * inner_mask[:, None, :])

def patches(field_in, stride):
    padded = jnp.pad(field_in, ((0, 0), (1, 1), (1, 1), (0, 0)))
    pieces = [padded[:, row_at:row_at + stride * HALF:stride, col_at:col_at + stride * HALF:stride, :] for row_at in range(3) for col_at in range(3)]
    joined = jnp.concatenate(pieces, axis=-1)
    return joined.reshape(-1, joined.shape[-1])

def batch_norm(values, flat_mask, gain_row, bias_row):
    valid_total = jnp.sum(flat_mask)
    mean_row = lax.optimization_barrier(jnp.sum(values * flat_mask[:, None], axis=0)) / valid_total
    centred = values - mean_row
    variance = lax.optimization_barrier(jnp.sum(centred * centred * flat_mask[:, None], axis=0)) / valid_total
    return centred * lax.rsqrt(variance + epsilon) * gain_row + bias_row

def product(left_side, right_side):
    return jnp.dot(left_side, right_side, precision=highest, preferred_element_type=jnp.float32)

def micro_block(image_block, level_row, weight_all, gain_all, bias_all):
    mask_in, mask_out = regions(level_row)
    flat_mask = mask_out.reshape(-1)
    image_count = image_block.shape[0]
    in_channels = image_block.shape[-1]
    taps_in = 9 * in_channels
    grid_shape = (image_count, HALF, HALF, C)
    entered = low_back(image_block) * mask_in[..., None]
    columns = patches(entered, 2)
    centre = columns[:, 4 * in_channels:5 * in_channels]
    conv_first = low_back(product(columns, weight_all[0, :taps_in]))
    conv_proj = low_back(product(centre, weight_all[0, taps_in:taps_in + in_channels]))
    hidden_one = low_back(low(jax.nn.silu(batch_norm(conv_first, flat_mask, gain_all[0, 0], bias_all[0, 0])) * flat_mask[:, None]))
    short_one = low_back(low(batch_norm(conv_proj, flat_mask, gain_all[0, 1], bias_all[0, 1]) * flat_mask[:, None]))
    conv_second = low_back(product(patches(hidden_one.reshape(grid_shape), 1), weight_all[1]))
    block_one = low_back(low(jax.nn.silu(batch_norm(conv_second, flat_mask, gain_all[1, 0], bias_all[1, 0]) + short_one) * flat_mask[:, None]))
    short_two = low_back(block_one)
    conv_third = low_back(product(patches(block_one.reshape(grid_shape), 1), weight_all[2]))
    hidden_two = low_back(low(jax.nn.silu(batch_norm(conv_third, flat_mask, gain_all[2, 0], bias_all[2, 0])) * flat_mask[:, None]))
    conv_fourth = low_back(product(patches(hidden_two.reshape(grid_shape), 1), weight_all[3]))
    block_two = jax.nn.silu(batch_norm(conv_fourth, flat_mask, gain_all[3, 0], bias_all[3, 0]) + short_two) * flat_mask[:, None]
    return block_two.reshape(grid_shape)

def reference(images, res_ids, weights, bn_gain, bn_bias, cotangent):

    def forward(image_values, weight_values, gain_values, bias_values):

        def advance(running, pair_in):
            return (running, jax.checkpoint(micro_block)(pair_in[0], pair_in[1], weight_values, gain_values, bias_values))
        _, outputs = lax.scan(advance, jnp.zeros((), jnp.float32), (image_values, res_ids))
        return outputs
    outputs, pull_back = jax.vjp(forward, images.astype(jnp.float32), weights.astype(jnp.float32), bn_gain, bn_bias)
    image_grad, weight_grad, gain_grad, bias_grad = pull_back(cotangent.astype(jnp.float32))
    return (outputs.astype(jnp.bfloat16), image_grad.astype(jnp.bfloat16), weight_grad, gain_grad, bias_grad)
```

```python
import jax
import jax.numpy as jnp
from jax import lax
from jax.experimental import pallas as pl
from jax.experimental.pallas import tpu as pltpu
from jax.sharding import PartitionSpec as P

epsilon = 1e-05


def passed_along(value, axis, steps):
    count = lax.axis_size(axis)
    leading, last = (max(0, -steps), min(count, count - steps))
    return lax.ppermute(value, axis, [(source, source + steps) for source in range(leading, last)])


def regions(levels, half_side):
    inner_side = half_side - 2 * (2 - levels)
    small_rows = jnp.arange(half_side, dtype=jnp.int32)
    large_rows = jnp.arange(2 * half_side, dtype=jnp.int32)
    inner_mask = (small_rows < inner_side[..., None]).astype(jnp.float32)
    outer_mask = (large_rows < 2 * inner_side[..., None]).astype(jnp.float32)
    return (
        outer_mask[..., :, None] * outer_mask[..., None, :],
        inner_mask[..., :, None] * inner_mask[..., None, :],
    )


def patches(field_in, stride, half_side):
    padded = jnp.pad(field_in, ((0, 0), (1, 1), (1, 1), (0, 0)))
    pieces = [
        padded[
            :,
            row_at : row_at + stride * half_side : stride,
            col_at : col_at + stride * half_side : stride,
            :,
        ]
        for row_at in range(3)
        for col_at in range(3)
    ]
    joined = jnp.concatenate(pieces, axis=-1)
    return joined.reshape(-1, joined.shape[-1])


def contract_rows(left_side, right_side):
    return lax.dot_general(
        left_side, right_side, (((0,), (0,)), ((), ())), preferred_element_type=jnp.float32
    )


def contract_cols(left_side, right_side):
    return lax.dot_general(
        left_side, right_side, (((1,), (1,)), ((), ())), preferred_element_type=jnp.float32
    )


def silu_slope(values):
    sigmoid = jax.nn.sigmoid(values)
    return sigmoid * (1.0 + values * (1.0 - sigmoid))


def spread_taps(tap_grads, image_count, half_side, channels):
    tap_grid = tap_grads.reshape(image_count, half_side, half_side, 9, channels)
    empty_phase = jnp.zeros((image_count, half_side + 1, half_side + 1, channels), jnp.float32)
    phases = [[empty_phase, empty_phase], [empty_phase, empty_phase]]
    for row_at in range(3):
        for col_at in range(3):
            tap_piece = tap_grid[:, :, :, 3 * row_at + col_at, :]
            top_pad = 1 if row_at == 2 else 0
            left_pad = 1 if col_at == 2 else 0
            placed = jnp.pad(
                tap_piece, ((0, 0), (top_pad, 1 - top_pad), (left_pad, 1 - left_pad), (0, 0))
            )
            phases[row_at % 2][col_at % 2] = phases[row_at % 2][col_at % 2] + placed
    row_phases = [jnp.stack([phases[parity][0], phases[parity][1]], axis=3) for parity in range(2)]
    alternated = jnp.stack(row_phases, axis=2).reshape(
        image_count, 2 * half_side + 2, 2 * half_side + 2, channels
    )
    return alternated[:, 1 : 2 * half_side + 1, 1 : 2 * half_side + 1, :]


def keep_slot(buffer_all, new_value, slot_at, keep_flag):
    current = lax.dynamic_index_in_dim(buffer_all, slot_at, 0, keepdims=False)
    return lax.dynamic_update_index_in_dim(
        buffer_all, jnp.where(keep_flag, new_value, current), slot_at, 0
    )


def pipeline_body(images, res_ids, weights, bn_gain, bn_bias, cotangent):
    sections = lax.axis_size("section")
    last_section = sections - 1
    position = lax.axis_index("section")
    micro_count = res_ids.shape[0]
    image_count = images.shape[1]
    half_side = cotangent.shape[2]
    channels = weights.shape[2]
    in_channels = images.shape[4]
    pixel_rows = image_count * half_side * half_side
    taps_in = 9 * in_channels
    matrix = weights[0]
    gain_rows = bn_gain[0]
    bias_rows = bn_bias[0]
    is_first = position == 0
    adds_short = (position == 1) | (position == 3)
    passes_short = position == 2
    makes_short = position == 1
    back_matrix = jnp.transpose(matrix.reshape(9, channels, channels)[::-1], (0, 2, 1)).reshape(
        9 * channels, channels
    )
    mask_in_all, mask_out_all = regions(res_ids, half_side)
    act_shape = (image_count, half_side, half_side, channels)
    zero_pixels = jnp.zeros((pixel_rows, channels), jnp.float32)
    zero_input = jnp.zeros((image_count, 2 * half_side, 2 * half_side, in_channels), jnp.float32)
    zero_weight = jnp.zeros((9 * channels, channels), jnp.float32)
    own_images = images[0]
    gathered = [own_images]
    for source in range(1, micro_count):
        gathered.append(passed_along(own_images, "section", -source))
    section_inputs = jnp.stack(gathered)
    own_cot = cotangent[0]
    arrived = []
    for source in range(micro_count):
        if source == last_section:
            arrived.append(own_cot)
        else:
            arrived.append(passed_along(own_cot, "section", last_section - source))
    cot_all = jnp.stack(arrived)

    def conv_first(prev_act, first_in):
        columns = patches(first_in, 2, half_side)
        main_out = jnp.dot(columns, matrix[:taps_in], preferred_element_type=jnp.float32)
        proj_out = jnp.dot(
            columns[:, 4 * in_channels : 5 * in_channels],
            matrix[taps_in : taps_in + in_channels],
            preferred_element_type=jnp.float32,
        )
        return jnp.stack([main_out, proj_out])

    def conv_rest(prev_act, first_in):
        columns = patches(prev_act, 1, half_side)
        return jnp.stack(
            [jnp.dot(columns, matrix, preferred_element_type=jnp.float32), zero_pixels]
        )

    def conv_spare(prev_act, first_in):
        return jnp.stack([zero_pixels, zero_pixels])

    def back_first(grad_conv, prev_act, first_in):
        columns = patches(first_in, 2, half_side)
        centre = columns[:, 4 * in_channels : 5 * in_channels]
        main_grad = contract_rows(columns, grad_conv[0])
        proj_grad = contract_rows(centre, grad_conv[1])
        filler = jnp.zeros((9 * channels - taps_in - in_channels, channels), jnp.float32)
        weight_now = jnp.concatenate([main_grad, proj_grad, filler], axis=0)
        tap_grads = contract_cols(grad_conv[0], matrix[:taps_in])
        centre_grad = contract_cols(grad_conv[1], matrix[taps_in : taps_in + in_channels])
        tap_grads = tap_grads + jnp.pad(centre_grad, ((0, 0), (4 * in_channels, 4 * in_channels)))
        return (
            weight_now,
            zero_pixels,
            spread_taps(tap_grads, image_count, half_side, in_channels),
        )

    def back_rest(grad_conv, prev_act, first_in):
        columns = patches(prev_act, 1, half_side)
        weight_now = contract_rows(columns, grad_conv[0])
        grad_image = grad_conv[0].reshape(act_shape)
        prev_grad = jnp.dot(
            patches(grad_image, 1, half_side), back_matrix, preferred_element_type=jnp.float32
        )
        return (weight_now, prev_grad, zero_input)

    def back_spare(grad_conv, prev_act, first_in):
        return (zero_weight, zero_pixels, zero_input)

    def finish(conv_out, mean_rows, scale_rows, flat_mask, short_in):
        normed = (conv_out - mean_rows[:, None, :]) * scale_rows[:, None, :] * gain_rows[
            :, None, :
        ] + bias_rows[:, None, :]
        pre_act = normed[0] + jnp.where(adds_short, short_in, 0.0)
        activated = jax.nn.silu(pre_act) * flat_mask[:, None]
        proj_short = normed[1] * flat_mask[:, None]
        short_out = jnp.where(is_first, proj_short, jnp.where(makes_short, activated, short_in))
        return (pre_act, activated, short_out)

    empty_act = jnp.zeros(act_shape, jnp.bfloat16)
    recv_act = empty_act
    recv_short = empty_act
    saved_act = jnp.zeros((micro_count,) + act_shape, jnp.bfloat16)
    saved_short = saved_act
    saved_final = saved_act
    saved_mean = jnp.zeros((micro_count, 2, channels), jnp.float32)
    saved_scale = saved_mean
    saved_total = jnp.zeros((micro_count,), jnp.float32)
    sweep_len = micro_count + last_section
    for tick_at in range(sweep_len):
        slot_raw = tick_at - position
        is_valid = (slot_raw >= 0) & (slot_raw < micro_count)
        slot_at = jnp.clip(slot_raw, 0, micro_count - 1)
        flat_mask = mask_out_all[slot_at].reshape(-1) * is_valid.astype(jnp.float32)
        first_in = section_inputs[slot_at] * mask_in_all[slot_at][..., None].astype(jnp.bfloat16)
        branch = jnp.where(is_valid, jnp.where(is_first, 0, 1), 2).astype(jnp.int32)
        conv_out = lax.switch(branch, [conv_first, conv_rest, conv_spare], recv_act, first_in)
        local_total = jnp.sum(flat_mask)
        weighted = conv_out * flat_mask[None, :, None]
        grand_total, sum_rows = lax.psum((local_total, jnp.sum(weighted, axis=1)), "dp")
        grand_total = jnp.maximum(grand_total, 1.0)
        statistics_mean_rows = sum_rows / grand_total
        centred = conv_out - statistics_mean_rows[:, None, :]
        variance = (
            lax.psum(jnp.sum(centred * centred * flat_mask[None, :, None], axis=1), "dp")
            / grand_total
        )
        grand_total, mean_rows, scale_rows = (
            grand_total,
            statistics_mean_rows,
            lax.rsqrt(variance + epsilon),
        )
        short_in = recv_short.reshape(pixel_rows, channels).astype(jnp.float32)
        pre_act, activated, short_out = finish(conv_out, mean_rows, scale_rows, flat_mask, short_in)
        act_low = activated.astype(jnp.bfloat16).reshape(act_shape)
        short_low = short_out.astype(jnp.bfloat16).reshape(act_shape)
        saved_act = keep_slot(saved_act, recv_act, slot_at, is_valid)
        saved_short = keep_slot(saved_short, recv_short, slot_at, is_valid)
        saved_mean = keep_slot(saved_mean, mean_rows, slot_at, is_valid)
        saved_scale = keep_slot(saved_scale, scale_rows, slot_at, is_valid)
        saved_total = keep_slot(saved_total, grand_total, slot_at, is_valid)
        saved_final = keep_slot(
            saved_final, act_low, slot_at, is_valid & (position == last_section)
        )
        if tick_at + 1 < sweep_len:
            recv_act, recv_short = passed_along((act_low, short_low), "section", 1)
    grad_act = empty_act
    grad_short = empty_act
    weight_acc = zero_weight
    gain_acc = jnp.zeros((2, channels), jnp.float32)
    bias_acc = gain_acc
    saved_dx = jnp.zeros(
        (micro_count, image_count, 2 * half_side, 2 * half_side, in_channels), jnp.bfloat16
    )
    for tick_at in range(sweep_len):
        slot_raw = tick_at - (last_section - position)
        is_valid = (slot_raw >= 0) & (slot_raw < micro_count)
        slot_at = jnp.clip(slot_raw, 0, micro_count - 1)
        flat_mask = mask_out_all[slot_at].reshape(-1) * is_valid.astype(jnp.float32)
        first_in = section_inputs[slot_at] * mask_in_all[slot_at][..., None].astype(jnp.bfloat16)
        branch = jnp.where(is_valid, jnp.where(is_first, 0, 1), 2).astype(jnp.int32)
        prev_act = saved_act[slot_at]
        conv_out = lax.switch(branch, [conv_first, conv_rest, conv_spare], prev_act, first_in)
        mean_rows = saved_mean[slot_at]
        scale_rows = saved_scale[slot_at]
        valid_total = saved_total[slot_at]
        short_in = saved_short[slot_at].reshape(pixel_rows, channels).astype(jnp.float32)
        pre_act, activated, short_out = finish(conv_out, mean_rows, scale_rows, flat_mask, short_in)
        from_act = (
            jnp.where(position == last_section, cot_all[slot_at], grad_act)
            .reshape(pixel_rows, channels)
            .astype(jnp.float32)
        )
        from_short = grad_short.reshape(pixel_rows, channels).astype(jnp.float32)
        slope = silu_slope(pre_act) * flat_mask[:, None]
        grad_pre = (from_act + jnp.where(adds_short, from_short, 0.0)) * slope
        grad_proj = jnp.where(is_first, from_short * flat_mask[:, None], 0.0)
        grad_normed = jnp.stack([grad_pre, grad_proj])
        normalized = (conv_out - mean_rows[:, None, :]) * scale_rows[:, None, :]
        bias_now, gain_now = lax.psum(
            (jnp.sum(grad_normed, axis=1), jnp.sum(grad_normed * normalized, axis=1)), "dp"
        )
        bias_acc = bias_acc + bias_now
        gain_acc = gain_acc + gain_now
        grad_conv = (
            flat_mask[None, :, None]
            * gain_rows[:, None, :]
            * scale_rows[:, None, :]
            * (
                grad_normed
                - (bias_now[:, None, :] + normalized * gain_now[:, None, :]) / valid_total
            )
        )
        grad_conv = grad_conv.astype(jnp.bfloat16)
        weight_now, prev_grad, input_grad = lax.switch(
            branch, [back_first, back_rest, back_spare], grad_conv, prev_act, first_in
        )
        weight_acc = weight_acc + weight_now
        masked_input = (input_grad * mask_in_all[slot_at][..., None]).astype(jnp.bfloat16)
        saved_dx = keep_slot(saved_dx, masked_input, slot_at, is_valid & is_first)
        send_act = (
            (prev_grad + jnp.where(passes_short, from_short, 0.0))
            .astype(jnp.bfloat16)
            .reshape(act_shape)
        )
        send_short = jnp.where(adds_short, grad_pre, 0.0).astype(jnp.bfloat16).reshape(act_shape)
        if tick_at + 1 < sweep_len:
            grad_act, grad_short = passed_along((send_act, send_short), "section", -1)
    weight_total = lax.psum(weight_acc, "dp")
    result = saved_final[last_section]
    for source in range(last_section):
        arrived_piece = passed_along(saved_final[source], "section", source - last_section)
        result = jnp.where(position == source, arrived_piece, result)
    grad_result = saved_dx[0]
    for source in range(1, micro_count):
        arrived_piece = passed_along(saved_dx[source], "section", source)
        grad_result = jnp.where(position == source, arrived_piece, grad_result)
    return (result[None], grad_result[None], weight_total[None], gain_acc[None], bias_acc[None])


f32, bf16 = jnp.float32, jnp.bfloat16
HALF_C = 256


def flip(value, axis, mask, pairs_kept=None):
    count = lax.axis_size(axis)
    pairs = [(i, i ^ mask) for i in range(count) if pairs_kept is None or pairs_kept(i)]
    return lax.ppermute(value, axis, pairs)


def in_vmem(count):
    return [pl.BlockSpec(memory_space=pltpu.VMEM)] * count


def anywhere(count):
    return [pl.BlockSpec(memory_space=pl.ANY)] * count


def scalars():
    return [pl.BlockSpec(memory_space=pltpu.SMEM)]


def struct(shape, kind):
    return jax.ShapeDtypeStruct(shape, kind)


def call(kernel, name, ins, outs, scratch, flops=0, moved=0, limit=40):
    return pl.pallas_call(
        kernel,
        out_shape=outs,
        in_specs=ins,
        out_specs=in_vmem(len(outs)),
        scratch_shapes=scratch,
        name=name,
        compiler_params=pltpu.CompilerParams(vmem_limit_bytes=limit * 2**20),
        cost_estimate=pl.CostEstimate(flops=flops, bytes_accessed=moved, transcendentals=0),
    )


def dot(left, right):
    return jnp.dot(left, right, preferred_element_type=f32)


def dot_t(left, right):
    return lax.dot_general(left, right, (((1,), (1,)), ((), ())), preferred_element_type=f32)


def row_mask(row, side):
    cols = lax.broadcasted_iota(jnp.int32, (9, 16, HALF_C), 0)
    return jnp.maximum(cols, row).astype(f32) < side[None]


def pad_into(dst, src):
    blank = jnp.zeros((11, 16, HALF_C), bf16)
    dst[0] = blank
    dst[10] = blank
    dst[:, 0] = blank
    dst[:, 10] = blank
    dst[1:10, 1:10] = src[...].reshape(9, 9, 16, HALF_C)


def norm_stats(acc, side, count):
    total = jnp.zeros((16, HALF_C), f32)
    for row in range(9):
        total += jnp.sum(jnp.where(row_mask(row, side), acc[row], 0.0), axis=0)
    mean = jnp.sum(total, axis=0, keepdims=True) / count
    spread = jnp.zeros((16, HALF_C), f32)
    for row in range(9):
        centred = jnp.where(row_mask(row, side), acc[row] - mean, 0.0)
        spread += jnp.sum(centred * centred, axis=0)
    variance = jnp.sum(spread, axis=0, keepdims=True) / count
    return mean, lax.rsqrt(variance + epsilon)


def col_sum(values):
    return jnp.sum(values, axis=0, keepdims=True)


def pack_rows(ref, rows):
    for at, row in enumerate(rows):
        ref[at : at + 1] = row
    ref[len(rows) :] = jnp.zeros((8 - len(rows), HALF_C), f32)


def turn_matrix(image_of_row):
    out_row = lax.broadcasted_iota(jnp.int32, (256, 256), 0)
    in_row = lax.broadcasted_iota(jnp.int32, (256, 256), 1)
    pixel_same = (out_row >> 4) == (in_row & 15)
    return jnp.where(pixel_same & ((out_row & 15) == image_of_row(in_row)), 1.0, 0.0).astype(bf16)


def prepare_images(sc, pieces):
    def kernel(sc_ref, *refs):
        piece_refs, out, side_out = refs[:8], refs[8], refs[9]
        core = sc_ref[2]
        turn = turn_matrix(lambda r: ((r >> 4) + 8 * core) & 15)
        out[:, :, 0] = jnp.zeros((2, 2, 10, 16, HALF_C), bf16)
        out[:, :, :, 0] = jnp.zeros((2, 2, 10, 16, HALF_C), bf16)

        def block(at):
            source = jnp.concatenate([ref[:, 16 * at : 16 * at + 16] for ref in piece_refs], axis=0)
            return dot(turn, source.reshape(256, HALF_C)).reshape(16, 16, HALF_C)

        last = block(20)
        side = last[4]
        side_out[...] = side
        for at in range(21):
            turned = last if at == 20 else block(at)
            for step in range(16 if at < 20 else 4):
                row, col = divmod(16 * at + step, 18)
                kept = jnp.where(2.0 * side > max(row, col), turned[step], 0.0)
                out[row % 2, col % 2, 1 + row // 2, 1 + col // 2] = kept.astype(bf16)

    return call(
        kernel,
        "prepare_images",
        scalars() + in_vmem(8),
        [struct((2, 2, 10, 10, 16, HALF_C), bf16), struct((16, HALF_C), f32)],
        [],
        flops=21 * 2 * 256**3,
        moved=8_000_000,
    )(sc, *pieces)


def prepare_cotangent(sc, pieces):
    def kernel(sc_ref, *refs):
        piece_refs, out = refs[:4], refs[4]
        core = sc_ref[2]
        turn = turn_matrix(
            lambda r: (((r >> 5) & 1) ^ core) * 8 + 2 * (r >> 6) + ((r >> 4) & 1)
        )
        for at in range(6):
            source = jnp.concatenate(
                [ref[:, :, 16 * at : 16 * at + 16].reshape(64, HALF_C) for ref in piece_refs],
                axis=0,
            )
            turned = dot(turn, source).astype(bf16).reshape(16, 16, HALF_C)
            kept = 16 if at < 5 else 1
            out[16 * at : 16 * at + kept] = turned[:kept]

    return call(
        kernel,
        "prepare_cotangent",
        scalars() + in_vmem(4),
        [struct((81, 16, HALF_C), bf16)],
        [],
        flops=6 * 2 * 256**3,
        moved=2_000_000,
    )(sc, *pieces)[0]


def load_first(section, refs, dst, sems):
    own_a, own_b, x_a, y_a, x_b, y_b = refs
    cut = own_a.shape[0]
    end = cut + own_b.shape[0]

    def start(when, ref, lo, hi, sem):
        @pl.when(when)
        def _():
            pltpu.make_async_copy(ref, dst.at[lo:hi], sems.at[sem]).start()

    start(section == 0, own_a, 0, cut, 0)
    start(section == 1, x_a, 0, cut, 0)
    start(section >= 2, y_a, 0, cut, 0)
    start(section == 0, own_b, cut, end, 1)
    start(section == 2, y_b, cut, end, 1)
    start((section == 1) | (section == 3), x_b, cut, end, 1)

    def wait():
        pltpu.make_async_copy(own_a, dst.at[0:cut], sems.at[0]).wait()
        pltpu.make_async_copy(own_b, dst.at[cut:end], sems.at[1]).wait()

    return wait


def load_part(section, part, refs, dst, sems):
    which = section ^ part
    for at in range(4):

        @pl.when(which == at)
        def _():
            for half in range(2):
                pltpu.make_async_copy(
                    refs[2 * at + half], dst.at[9 * half : 9 * half + 9], sems.at[half]
                ).start()

    def wait():
        for half in range(2):
            pltpu.make_async_copy(
                refs[half], dst.at[9 * half : 9 * half + 9], sems.at[half]
            ).wait()

    return wait


def stage_first(sc, side, vectors, fields, weight_refs):
    def kernel(sc_ref, side_ref, vec, field, *refs):
        weights = refs[:6]
        hidden, short, zhat, zhat_p, stats, w_out = refs[6:12]
        w, acc, acc_p, sems, out_sem = refs[12:]
        wait = load_first(sc_ref[0], weights, w, sems)
        wait()
        keep = pltpu.make_async_copy(w, w_out, out_sem)
        keep.start()
        for chunk in range(3):
            total = jnp.zeros((432, HALF_C), f32)
            for a in range(3):
                for b in range(3):
                    row_at = 3 * chunk + (0 if a == 0 else 1)
                    col_at = 0 if b == 0 else 1
                    left = field[
                        (a + 1) % 2, (b + 1) % 2, row_at : row_at + 3, col_at : col_at + 9
                    ].reshape(432, HALF_C)
                    total = total + dot(left, w[3 * a + b])
            acc[3 * chunk : 3 * chunk + 3] = total.reshape(3, 9, 16, HALF_C)
            centre = field[0, 0, 3 * chunk + 1 : 3 * chunk + 4, 1:10].reshape(432, HALF_C)
            acc_p[3 * chunk : 3 * chunk + 3] = dot(centre, w[9]).reshape(3, 9, 16, HALF_C)
        side_now = side_ref[...]
        count = col_sum(side_now * side_now)
        mean, scale = norm_stats(acc, side_now, count)
        mean_p, scale_p = norm_stats(acc_p, side_now, count)
        gain, gain_p, bias, bias_p = [vec[at : at + 1] for at in range(4)]
        for row in range(9):
            inside = row_mask(row, side_now)
            normed = jnp.where(inside, (acc[row] - mean) * scale, 0.0)
            zhat[row] = normed
            pre = normed * gain + bias
            hidden[9 * row : 9 * row + 9] = jnp.where(
                inside, pre * jax.nn.sigmoid(pre), 0.0
            ).astype(bf16)
            normed = jnp.where(inside, (acc_p[row] - mean_p) * scale_p, 0.0)
            zhat_p[row] = normed
            short[9 * row : 9 * row + 9] = jnp.where(
                inside, normed * gain_p + bias_p, 0.0
            ).astype(bf16)
        pack_rows(stats, [scale, scale_p])
        keep.wait()

    grid = (9, 9, 16, HALF_C)
    outs = [
        struct((81, 16, HALF_C), bf16),
        struct((81, 16, HALF_C), bf16),
        struct(grid, f32),
        struct(grid, f32),
        struct((8, HALF_C), f32),
        struct((10, HALF_C, HALF_C), bf16),
    ]
    return pl.pallas_call(
        kernel,
        out_shape=outs,
        in_specs=scalars() + in_vmem(3) + anywhere(6),
        out_specs=in_vmem(5) + anywhere(1),
        scratch_shapes=[
            pltpu.VMEM((10, HALF_C, HALF_C), bf16),
            pltpu.VMEM(grid, f32),
            pltpu.VMEM(grid, f32),
            pltpu.SemaphoreType.DMA((2,)),
            pltpu.SemaphoreType.DMA,
        ],
        name="stage_first",
        compiler_params=pltpu.CompilerParams(vmem_limit_bytes=40 * 2**20),
        cost_estimate=pl.CostEstimate(
            flops=2 * 1296 * 2560 * HALF_C, bytes_accessed=8_000_000, transcendentals=0
        ),
    )(sc, side, vectors, fields, *weight_refs)


def convolve(padded, w, core, acc):
    for chunk in range(3):
        total = jnp.zeros((432, HALF_C), f32)
        for a in range(3):
            for b in range(3):
                for other in range(2):
                    left = padded[other, 3 * chunk + a : 3 * chunk + a + 3, b : b + 9]
                    which = core if other == 0 else 1 - core
                    right = w[2 * (3 * a + b) + which]
                    total = total + dot(left.reshape(432, HALF_C), right)
        acc[3 * chunk : 3 * chunk + 3] = total.reshape(3, 9, 16, HALF_C)


def start_weight_outs(w, core, keep_ref, send_ref, sems):
    copies = []
    for tap in range(9):
        copies.append(pltpu.make_async_copy(w.at[2 * tap + core], keep_ref.at[tap], sems.at[0, tap]))
        copies.append(
            pltpu.make_async_copy(w.at[2 * tap + 1 - core], send_ref.at[tap], sems.at[1, tap])
        )
    for copy in copies:
        copy.start()
    return copies


def stage_rest(part, sc, side, vectors, own, other, weight_refs, short=None):
    shorted = short is not None

    def kernel(sc_ref, side_ref, vec, own_ref, oth_ref, *refs):
        short_ref = refs[0] if shorted else None
        refs = refs[1:] if shorted else refs
        weights = refs[:8]
        hidden, zhat, stats, w_keep, w_send = refs[8:13]
        w, padded, acc, sems, out_sems = refs[13:]
        core = sc_ref[2]
        wait = load_part(sc_ref[0], part, weights, w, sems)
        pad_into(padded.at[0], own_ref)
        pad_into(padded.at[1], oth_ref)
        wait()
        copies = start_weight_outs(w, core, w_keep, w_send, out_sems)
        convolve(padded, w, core, acc)
        side_now = side_ref[...]
        mean, scale = norm_stats(acc, side_now, col_sum(side_now * side_now))
        gain, bias = vec[4 * part : 4 * part + 1], vec[4 * part + 2 : 4 * part + 3]
        for row in range(9):
            inside = row_mask(row, side_now)
            normed = jnp.where(inside, (acc[row] - mean) * scale, 0.0)
            zhat[row] = normed
            pre = normed * gain + bias
            if shorted:
                pre = pre + short_ref[9 * row : 9 * row + 9].astype(f32)
            hidden[9 * row : 9 * row + 9] = jnp.where(
                inside, pre * jax.nn.sigmoid(pre), 0.0
            ).astype(bf16)
        pack_rows(stats, [scale])
        for copy in copies:
            copy.wait()

    grid = (9, 9, 16, HALF_C)
    return pl.pallas_call(
        kernel,
        out_shape=[
            struct((81, 16, HALF_C), bf16),
            struct(grid, f32),
            struct((8, HALF_C), f32),
            struct((9, HALF_C, HALF_C), bf16),
            struct((9, HALF_C, HALF_C), bf16),
        ],
        in_specs=scalars() + in_vmem(5 if shorted else 4) + anywhere(8),
        out_specs=in_vmem(3) + anywhere(2),
        scratch_shapes=[
            pltpu.VMEM((18, HALF_C, HALF_C), bf16),
            pltpu.VMEM((2, 11, 11, 16, HALF_C), bf16),
            pltpu.VMEM(grid, f32),
            pltpu.SemaphoreType.DMA((2,)),
            pltpu.SemaphoreType.DMA((2, 9)),
        ],
        name=f"stage_{part}",
        compiler_params=pltpu.CompilerParams(vmem_limit_bytes=40 * 2**20),
        cost_estimate=pl.CostEstimate(
            flops=2 * 1296 * 4608 * HALF_C, bytes_accessed=8_000_000, transcendentals=0
        ),
    )(sc, side, vectors, own, other, *([short] if shorted else []), *weight_refs)


def pick_matrix(core):
    out_row = lax.broadcasted_iota(jnp.int32, (4, 96, 1296), 1)
    slot = lax.broadcasted_iota(jnp.int32, (4, 96, 1296), 0)
    in_row = lax.broadcasted_iota(jnp.int32, (4, 96, 1296), 2)
    image = 8 * ((slot >> 1) ^ core) + (slot & 1)
    return jnp.where(in_row == 16 * out_row + image, 1.0, 0.0).astype(bf16).reshape(384, 1296)


def slope_of(pre):
    sigmoid = jax.nn.sigmoid(pre)
    return sigmoid * (1.0 + pre * (1.0 - sigmoid))


def norm_back(dy, zhat, side, count, gain, scale, bias_now, gain_now, dz):
    bias_part, gain_part = bias_now / count, gain_now / count
    for row in range(9):
        inside = row_mask(row, side)
        dz[9 * row : 9 * row + 9] = jnp.where(
            inside, gain * scale * (dy[row] - (bias_part + zhat[row] * gain_part)), 0.0
        ).astype(bf16)


def stage_last(part, sc, side, vectors, own, other, short, cot, weight_refs):
    def kernel(sc_ref, side_ref, vec, own_ref, oth_ref, short_ref, cot_ref, *refs):
        weights = refs[:8]
        dz, passed, picked, sums, w_keep, w_send = refs[8:14]
        w, padded, acc, dy, out, sems, out_sems = refs[14:]
        core = sc_ref[2]
        wait = load_part(sc_ref[0], part, weights, w, sems)
        pad_into(padded.at[0], own_ref)
        pad_into(padded.at[1], oth_ref)
        wait()
        copies = start_weight_outs(w, core, w_keep, w_send, out_sems)
        convolve(padded, w, core, acc)
        side_now = side_ref[...]
        count = col_sum(side_now * side_now)
        mean, scale = norm_stats(acc, side_now, count)
        gain, bias = vec[4 * part : 4 * part + 1], vec[4 * part + 2 : 4 * part + 3]
        bias_acc = jnp.zeros((16, HALF_C), f32)
        gain_acc = jnp.zeros((16, HALF_C), f32)
        for row in range(9):
            inside = row_mask(row, side_now)
            at = slice(9 * row, 9 * row + 9)
            normed = jnp.where(inside, (acc[row] - mean) * scale, 0.0)
            acc[row] = normed
            pre = normed * gain + bias + short_ref[at].astype(f32)
            sigmoid = jax.nn.sigmoid(pre)
            out[at] = jnp.where(inside, pre * sigmoid, 0.0).astype(bf16)
            grad = cot_ref[at].astype(f32) * (sigmoid * (1.0 + pre * (1.0 - sigmoid)))
            grad = jnp.where(inside, grad, 0.0)
            dy[row] = grad
            passed[at] = grad.astype(bf16)
            bias_acc += jnp.sum(grad, axis=0)
            gain_acc += jnp.sum(grad * normed, axis=0)
        bias_now, gain_now = col_sum(bias_acc), col_sum(gain_acc)
        norm_back(dy, acc, side_now, count, gain, scale, bias_now, gain_now, dz)
        pack_rows(sums, [gain_now, bias_now])
        picked[...] = (
            dot(pick_matrix(core), out[...].reshape(1296, HALF_C))
            .astype(bf16)
            .reshape(4, 96, HALF_C)
        )
        for copy in copies:
            copy.wait()

    grid = (9, 9, 16, HALF_C)
    return pl.pallas_call(
        kernel,
        out_shape=[
            struct((81, 16, HALF_C), bf16),
            struct((81, 16, HALF_C), bf16),
            struct((4, 96, HALF_C), bf16),
            struct((8, HALF_C), f32),
            struct((9, HALF_C, HALF_C), bf16),
            struct((9, HALF_C, HALF_C), bf16),
        ],
        in_specs=scalars() + in_vmem(6) + anywhere(8),
        out_specs=in_vmem(4) + anywhere(2),
        scratch_shapes=[
            pltpu.VMEM((18, HALF_C, HALF_C), bf16),
            pltpu.VMEM((2, 11, 11, 16, HALF_C), bf16),
            pltpu.VMEM(grid, f32),
            pltpu.VMEM(grid, f32),
            pltpu.VMEM((81, 16, HALF_C), bf16),
            pltpu.SemaphoreType.DMA((2,)),
            pltpu.SemaphoreType.DMA((2, 9)),
        ],
        name="stage_last",
        compiler_params=pltpu.CompilerParams(vmem_limit_bytes=40 * 2**20),
        cost_estimate=pl.CostEstimate(
            flops=2 * 1296 * 4608 * HALF_C, bytes_accessed=8_000_000, transcendentals=0
        ),
    )(sc, side, vectors, own, other, short, cot, *weight_refs)


def stage_back(
    part, sc, side, vectors, dz_own, dz_other, w_own, w_other, zhat, stats, short=None, extra=None,
    proj=None,
):
    first = proj is not None

    def kernel(sc_ref, side_ref, vec, dz_own_ref, dz_oth_ref, w_own_ref, w_oth_ref, *refs):
        refs = list(refs)
        zhat_ref, stats_ref = refs.pop(0), refs.pop(0)
        short_ref = refs.pop(0) if short is not None else None
        extra_ref = refs.pop(0) if extra is not None else None
        if first:
            dyp_ref, zhat_p_ref = refs.pop(0), refs.pop(0)
        dz, sums = refs.pop(0), refs.pop(0)
        passed = refs.pop(0) if short is not None else None
        if first:
            dz_p, picked, picked_p = refs.pop(0), refs.pop(0), refs.pop(0)
        padded, acc = refs
        pad_into(padded.at[0], dz_own_ref)
        pad_into(padded.at[1], dz_oth_ref)
        for chunk in range(3):
            total = jnp.zeros((432, HALF_C), f32)
            for a in range(3):
                for b in range(3):
                    for other, weight in ((0, w_own_ref), (1, w_oth_ref)):
                        row_at = 3 * chunk + 2 - a
                        left = padded[other, row_at : row_at + 3, 2 - b : 11 - b]
                        total = total + dot_t(left.reshape(432, HALF_C), weight[3 * a + b])
            acc[3 * chunk : 3 * chunk + 3] = total.reshape(3, 9, 16, HALF_C)
        side_now = side_ref[...]
        count = col_sum(side_now * side_now)
        gain, bias = vec[4 * part : 4 * part + 1], vec[4 * part + 2 : 4 * part + 3]
        bias_acc = jnp.zeros((16, HALF_C), f32)
        gain_acc = jnp.zeros((16, HALF_C), f32)
        bias_acc_p = jnp.zeros((16, HALF_C), f32)
        gain_acc_p = jnp.zeros((16, HALF_C), f32)
        for row in range(9):
            inside = row_mask(row, side_now)
            at = slice(9 * row, 9 * row + 9)
            normed = zhat_ref[row]
            pre = normed * gain + bias
            grad = acc[row]
            if extra is not None:
                grad = grad + extra_ref[at].astype(f32)
            if short is not None:
                pre = pre + short_ref[at].astype(f32)
            grad = grad.astype(bf16).astype(f32) * slope_of(pre)
            grad = jnp.where(inside, grad, 0.0)
            acc[row] = grad
            if short is not None:
                passed[at] = grad.astype(bf16)
            bias_acc += jnp.sum(grad, axis=0)
            gain_acc += jnp.sum(grad * normed, axis=0)
            if first:
                grad = jnp.where(inside, dyp_ref[at].astype(f32), 0.0)
                bias_acc_p += jnp.sum(grad, axis=0)
                gain_acc_p += jnp.sum(grad * zhat_p_ref[row], axis=0)
        bias_now, gain_now = col_sum(bias_acc), col_sum(gain_acc)
        scale = stats_ref[0:1]
        norm_back(acc, zhat_ref, side_now, count, gain, scale, bias_now, gain_now, dz)
        rows = [gain_now, bias_now]
        if first:
            bias_p, gain_p = col_sum(bias_acc_p), col_sum(gain_acc_p)
            rows += [gain_p, bias_p]
            for row in range(9):
                at = slice(9 * row, 9 * row + 9)
                acc[row] = dyp_ref[at].astype(f32)
            norm_back(
                acc, zhat_p_ref, side_now, count, vec[1:2], stats_ref[1:2], bias_p, gain_p, dz_p
            )
            pick = pick_matrix(sc_ref[2])
            for source, target in ((dz, picked), (dz_p, picked_p)):
                target[...] = (
                    dot(pick, source[...].reshape(1296, HALF_C))
                    .astype(bf16)
                    .reshape(4, 96, HALF_C)
                )
        pack_rows(sums, rows)

    grid = (9, 9, 16, HALF_C)
    ins = [sc, side, vectors, dz_own, dz_other, w_own, w_other, zhat, stats]
    outs = [struct((81, 16, HALF_C), bf16), struct((8, HALF_C), f32)]
    if short is not None:
        ins.append(short)
        outs.append(struct((81, 16, HALF_C), bf16))
    if extra is not None:
        ins.append(extra)
    if first:
        ins += list(proj)
        outs += [struct((81, 16, HALF_C), bf16)] + [struct((4, 96, HALF_C), bf16)] * 2
    return call(
        kernel,
        f"back_{part}",
        scalars() + in_vmem(len(ins) - 1),
        outs,
        [pltpu.VMEM((2, 11, 11, 16, HALF_C), bf16), pltpu.VMEM(grid, f32)],
        flops=2 * 1296 * 4608 * HALF_C,
        moved=10_000_000,
    )(*ins)


def weight_rest(part, sc, own, other, dz):
    def kernel(sc_ref, own_ref, oth_ref, dz_ref, out, turned, padded):
        zone, core = sc_ref[1], sc_ref[2]
        lane = pl.multiple_of(128 * (zone & 1), 128)
        is_own = (zone >> 1) == core

        @pl.when(is_own)
        def _():
            turned[...] = own_ref[:, :, pl.ds(lane, 128)].reshape(1296, 128).T

        @pl.when(jnp.logical_not(is_own))
        def _():
            turned[...] = oth_ref[:, :, pl.ds(lane, 128)].reshape(1296, 128).T

        pad_into(padded, dz_ref)
        left = turned[...]
        for a in range(3):
            for b in range(3):
                right = padded[2 - a : 11 - a, 2 - b : 11 - b].reshape(1296, HALF_C)
                out[3 * a + b] = dot(left, right).astype(bf16)

    return call(
        kernel,
        f"weight_{part}",
        scalars() + in_vmem(3),
        [struct((9, 128, HALF_C), bf16)],
        [pltpu.VMEM((128, 1296), bf16), pltpu.VMEM((11, 11, 16, HALF_C), bf16)],
        flops=2 * 1296 * 1152 * HALF_C,
        moved=3_000_000,
    )(sc, own, other, dz)[0].reshape(18, 64, HALF_C)


def weight_first(sc, fields, dz, dz_p):
    def kernel(sc_ref, field, dz_ref, dz_p_ref, out, turned, padded):
        zone = sc_ref[1]
        lane = pl.multiple_of(128 * (zone >> 1), 128)
        at = pl.multiple_of(64 * (zone & 1), 64)
        for phase in range(4):
            chosen = field[phase // 2, phase % 2, 1:10, 1:10, :, pl.ds(lane, 128)]
            turned[phase] = chosen.reshape(1296, 128).T
        pad_into(padded, dz_ref)
        for a in range(3):
            for b in range(3):
                left = turned[2 * ((a + 1) % 2) + (b + 1) % 2, pl.ds(at, 64)]
                row_at, col_at = 2 if a == 0 else 1, 2 if b == 0 else 1
                right = padded[row_at : row_at + 9, col_at : col_at + 9].reshape(1296, HALF_C)
                out[3 * a + b] = dot(left, right).astype(bf16)
        out[9] = dot(turned[0, pl.ds(at, 64)], dz_p_ref[...].reshape(1296, HALF_C)).astype(bf16)

    return call(
        kernel,
        "weight_first",
        scalars() + in_vmem(3),
        [struct((10, 64, HALF_C), bf16)],
        [pltpu.VMEM((4, 128, 1296), bf16), pltpu.VMEM((11, 11, 16, HALF_C), bf16)],
        flops=2 * 1296 * 640 * HALF_C,
        moved=3_000_000,
    )(sc, fields, dz, dz_p)[0]


def image_back(own, other, own_p, other_p, w_own, w_other):
    def kernel(own_ref, oth_ref, own_p_ref, oth_p_ref, w_own_ref, w_oth_ref, out):
        row = lax.broadcasted_iota(jnp.int32, (192, 192), 0)
        col = lax.broadcasted_iota(jnp.int32, (192, 192), 1)
        pixel = jnp.where(row >= 96, row - 96, row)
        line = (pixel * 57) >> 9
        across = pixel - 9 * line
        shifted = {}
        for down in range(2):
            for right in range(2):
                if down + right == 0:
                    shifted[0, 0] = (
                        own_ref[...].reshape(192, HALF_C),
                        oth_ref[...].reshape(192, HALF_C),
                    )
                    continue
                fits = (pixel < 81) & (line + down < 9) & (across + right < 9)
                move = jnp.where(fits & (col == row + 9 * down + right), 1.0, 0.0).astype(bf16)
                shifted[down, right] = tuple(
                    dot(move, ref[...].reshape(192, HALF_C)).astype(bf16)
                    for ref in (own_ref, oth_ref)
                )
        phases = [jnp.zeros((192, HALF_C), f32) for _ in range(4)]
        for a in range(3):
            for b in range(3):
                at = 2 * ((a + 1) % 2) + (b + 1) % 2
                left = shifted[1 if a == 0 else 0, 1 if b == 0 else 0]
                phases[at] = phases[at] + dot_t(left[0], w_own_ref[3 * a + b])
                phases[at] = phases[at] + dot_t(left[1], w_oth_ref[3 * a + b])
        phases[0] = phases[0] + dot_t(own_p_ref[...].reshape(192, HALF_C), w_own_ref[9])
        phases[0] = phases[0] + dot_t(oth_p_ref[...].reshape(192, HALF_C), w_oth_ref[9])
        joined = jnp.concatenate([phase.astype(bf16) for phase in phases], axis=0)
        out_row = lax.broadcasted_iota(jnp.int32, (336, 768), 0)
        in_row = lax.broadcasted_iota(jnp.int32, (336, 768), 1)
        line = (out_row * 3641) >> 16
        across = out_row - 18 * line
        source = (2 * (line & 1) + (across & 1)) * 192 + 9 * (line >> 1) + (across >> 1)
        for image in range(2):
            spread = jnp.where(
                (in_row == source + 96 * image) & (out_row < 324), 1.0, 0.0
            ).astype(bf16)
            out[image] = dot(spread, joined).astype(bf16)

    return call(
        kernel,
        "image_back",
        in_vmem(6),
        [struct((2, 336, HALF_C), bf16)],
        [],
        flops=2 * 192 * 2560 * 512 + 4 * 336 * 768 * 256,
        moved=4_000_000,
    )(own, other, own_p, other_p, w_own, w_other)[0]


def sum_parts(sc, groups):
    sizes = [group[0].shape[0] for group in groups]

    def kernel(sc_ref, *refs):
        sources, out, held, sems = refs[:16], refs[16], refs[17], refs[18]
        section = sc_ref[0]
        for part in range(4):
            size = sizes[part]

            @pl.when(section == part)
            def _():
                copies = [
                    pltpu.make_async_copy(
                        sources[4 * part + at], held.at[at, 0:size], sems.at[at]
                    )
                    for at in range(4)
                ]
                for copy in copies:
                    copy.start()
                for copy in copies:
                    copy.wait()
                total = held[0, 0:size].astype(f32)
                for at in range(1, 4):
                    total = total + held[at, 0:size].astype(f32)
                out[0:size] = total.astype(bf16)
                if size < 18:
                    out[size:18] = jnp.zeros((18 - size, 64, HALF_C), bf16)

    return call(
        kernel,
        "sum_parts",
        scalars() + anywhere(16),
        [struct((18, 64, HALF_C), bf16)],
        [pltpu.VMEM((4, 18, 64, HALF_C), bf16), pltpu.SemaphoreType.DMA((4,))],
        flops=1_000_000,
        moved=3_000_000,
    )(sc, *[one for group in groups for one in group])[0]


def lay_out(sc, own, other):
    def kernel(sc_ref, *refs):
        pieces, out = refs[:8], refs[8]
        section, zone, core = sc_ref[0], sc_ref[1], sc_ref[2]
        for at in range(8):
            where_from = zone ^ (at % 4)
            half = core if at < 4 else 1 - core
            lane = pl.multiple_of(HALF_C * half, HALF_C)
            for step in range(2):
                row = jnp.where(section == 0, 4 * step + where_from, 2 * where_from + step)
                out[row, :, pl.ds(lane, HALF_C)] = pieces[at][step].astype(f32)

    piece = pl.BlockSpec((2, 64, HALF_C), lambda at: (at, 0, 0))
    return pl.pallas_call(
        kernel,
        out_shape=struct((72, 64, 512), f32),
        grid=(9,),
        in_specs=scalars() + [piece] * 8,
        out_specs=pl.BlockSpec((8, 64, 512), lambda at: (at, 0, 0)),
        name="lay_out",
        compiler_params=pltpu.CompilerParams(vmem_limit_bytes=24 * 2**20),
        cost_estimate=pl.CostEstimate(flops=0, bytes_accessed=15_000_000, transcendentals=0),
    )(sc, *own, *other)


def half_of(value, half):
    return lax.dynamic_slice_in_dim(value, HALF_C * half, HALF_C, axis=value.ndim - 1)


def join_halves(own, other, core):
    first = jnp.where(core == 0, own, other)
    second = jnp.where(core == 0, other, own)
    return jnp.concatenate([first, second], axis=-1)


def chip_body(images, res_ids, weights, bn_gain, bn_bias, cotangent):
    section = lax.axis_index("section")
    position = lax.axis_index("dp")
    zone, core = position // 2, position % 2
    sc = jnp.stack([section, zone, core, core]).astype(jnp.int32)

    own_matrix = weights[0].reshape(18, 256, 512)
    w_first_a = half_of(own_matrix[0:5], core)
    w_first_b = half_of(own_matrix[5:10], core)
    first_x_a = flip(w_first_a, "section", 1, lambda i: i == 0)
    first_y_b = flip(w_first_b, "section", 2, lambda i: i == 0)
    first_x_b = flip(
        jnp.where(section == 0, w_first_b, first_y_b), "section", 1, lambda i: i in (0, 2)
    )
    first_y_a = flip(
        jnp.where(section == 0, w_first_a, first_x_a), "section", 2, lambda i: i in (0, 1)
    )
    first_refs = [w_first_a, w_first_b, first_x_a, first_y_a, first_x_b, first_y_b]

    level = lax.dynamic_index_in_dim(res_ids, section, 0, keepdims=False)
    side_own = (9 - 2 * (2 - level)).astype(f32)
    tail = jnp.broadcast_to(side_own[:, None, None], (2, 12, 256)).astype(bf16)
    image_own = jnp.concatenate([images[0].reshape(2, 324, 256), tail], axis=1)
    pieces = [image_own] + [flip(image_own, "dp", 2 * at) for at in range(1, 4)]
    pieces = pieces + [flip(piece, "dp", 1) for piece in pieces]

    w_a = half_of(own_matrix[0:9], core)
    w_b = half_of(own_matrix[9:18], core)
    x_a = flip(w_a, "section", 1, lambda i: i != 0)
    y_b = flip(w_b, "section", 2, lambda i: i != 0)
    x_b = flip(w_b, "section", 1, lambda i: i != 0)
    y_a = flip(w_a, "section", 2, lambda i: i != 0)
    d_b = flip(y_b, "section", 1, lambda i: i != 2)
    d_a = flip(x_a, "section", 2, lambda i: i != 1)
    part_refs = [w_a, w_b, x_a, x_b, y_a, y_b, d_a, d_b]

    vector_own = half_of(jnp.concatenate([bn_gain[0], bn_bias[0]], axis=0), core)
    vector_all = jnp.stack([vector_own] + [flip(vector_own, "section", at) for at in range(1, 4)])
    vectors = vector_all[section ^ jnp.arange(4)].reshape(16, HALF_C)

    cot_own = cotangent[0].reshape(2, 81, 512)
    cot_mine = half_of(cot_own, core)
    cot_got = flip(half_of(cot_own, 1 - core), "dp", 1)
    cot_pair = jnp.pad(jnp.stack([cot_mine, cot_got]), ((0, 0), (0, 0), (0, 15), (0, 0)))
    cot_pieces = [cot_pair] + [flip(cot_pair, "dp", 2 * at) for at in range(1, 4)]

    fields, side = prepare_images(sc, pieces)
    cot = prepare_cotangent(sc, cot_pieces)

    hidden_one, short_one, zhat_0, zhat_p, stats_0, w_first = stage_first(
        sc, side, vectors, fields, first_refs
    )
    w_first_other = flip(w_first, "dp", 1)
    hidden_one_other = flip(hidden_one, "dp", 1)
    block_one, zhat_1, stats_1, keep_1, send_1 = stage_rest(
        1, sc, side, vectors, hidden_one, hidden_one_other, part_refs, short_one
    )
    other_1 = flip(send_1, "dp", 1)
    block_one_other = flip(block_one, "dp", 1)
    hidden_two, zhat_2, stats_2, keep_2, send_2 = stage_rest(
        2, sc, side, vectors, block_one, block_one_other, part_refs
    )
    other_2 = flip(send_2, "dp", 1)
    hidden_two_other = flip(hidden_two, "dp", 1)
    dz_3, passed, picked, sums_3, keep_3, send_3 = stage_last(
        3, sc, side, vectors, hidden_two, hidden_two_other, block_one, cot, part_refs
    )
    other_3 = flip(send_3, "dp", 1)
    dz_3_other = flip(dz_3, "dp", 1)
    picked_other = flip(picked[2:4], "dp", 1)
    block_output = join_halves(picked[0:2, 0:81], picked_other[:, 0:81], core)

    def to_owner(part, piece):
        return [piece] + [
            flip(piece, "section", at, lambda i, at=at: i ^ at == part) for at in range(1, 4)
        ]

    grads_3 = to_owner(3, weight_rest(3, sc, hidden_two, hidden_two_other, dz_3))
    dz_2, sums_2 = stage_back(
        2, sc, side, vectors, dz_3, dz_3_other, keep_3, other_3, zhat_2, stats_2
    )
    dz_2_other = flip(dz_2, "dp", 1)
    grads_2 = to_owner(2, weight_rest(2, sc, block_one, block_one_other, dz_2))
    dz_1, sums_1, short_grad = stage_back(
        1, sc, side, vectors, dz_2, dz_2_other, keep_2, other_2, zhat_1, stats_1,
        short=short_one, extra=passed,
    )
    dz_1_other = flip(dz_1, "dp", 1)
    grads_1 = to_owner(1, weight_rest(1, sc, hidden_one, hidden_one_other, dz_1))
    dz_0, sums_0, dz_p, pick_0, pick_p = stage_back(
        0, sc, side, vectors, dz_1, dz_1_other, keep_1, other_1, zhat_0, stats_0,
        proj=(short_grad, zhat_p),
    )
    grads_0 = to_owner(0, weight_first(sc, fields, dz_0, dz_p))
    total = sum_parts(sc, [grads_0, grads_1, grads_2, grads_3])
    gathered = [total] + [flip(total, "dp", 2 * at) for at in range(1, 4)]
    gathered_other = [flip(piece, "dp", 1) for piece in gathered]
    weight_grad = lay_out(sc, gathered, gathered_other).reshape(1, 4608, 512)

    pick_0_other = flip(pick_0[2:4], "dp", 1)
    pick_p_other = flip(pick_p[2:4], "dp", 1)
    image_grad = image_back(
        pick_0[0:2], pick_0_other, pick_p[0:2], pick_p_other, w_first, w_first_other
    )
    rows = jnp.arange(18, dtype=jnp.int32)
    inner = (rows < 2 * (9 - 2 * (2 - level))[:, None]).astype(bf16)
    mask_in = inner[:, :, None] * inner[:, None, :]
    image_grad = image_grad[:, 0:324].reshape(2, 18, 18, 256) * mask_in[..., None]

    blank = jnp.zeros((1, HALF_C), f32)
    sums = jnp.stack(
        [
            jnp.concatenate([sums_0[0:1], sums_0[2:3], sums_0[1:2], sums_0[3:4]]),
            jnp.concatenate([sums_1[0:1], blank, sums_1[1:2], blank]),
            jnp.concatenate([sums_2[0:1], blank, sums_2[1:2], blank]),
            jnp.concatenate([sums_3[0:1], blank, sums_3[1:2], blank]),
        ]
    )
    sums = sums + flip(sums, "section", 1) + flip(sums, "section", 2) + flip(sums, "section", 3)
    sums = lax.dynamic_index_in_dim(sums, section, 0, keepdims=False)
    sums = join_halves(sums, flip(sums, "dp", 1), core)
    return (
        block_output.reshape(1, 2, 9, 9, 512),
        image_grad[None],
        weight_grad,
        sums[None, 0:2],
        sums[None, 2:4],
    )


def solution(mesh):
    placed = (
        P("section", "dp", None, None, None),
        P(None, "dp"),
        P("section", None, None),
        P("section", None, None),
        P("section", None, None),
        P("section", "dp", None, None, None),
    )
    on_chip = mesh.shape["section"] == 4 and mesh.shape["dp"] == 8
    return jax.shard_map(
        chip_body if on_chip else pipeline_body,
        mesh=mesh,
        in_specs=placed,
        out_specs=(
            P("section", "dp", None, None, None),
            P("section", "dp", None, None, None),
            P("section", None, None),
            P("section", None, None),
            P("section", None, None),
        ),
        check_vma=False,
    )
```

```python
import jax
import jax.numpy as jnp
from jax import lax
from jax.experimental import pallas as pl
from jax.experimental.pallas import tpu as pltpu
from jax.sharding import PartitionSpec as P

epsilon = 1e-05


def passed_along(value, axis, steps):
    count = lax.axis_size(axis)
    leading, last = (max(0, -steps), min(count, count - steps))
    return lax.ppermute(value, axis, [(source, source + steps) for source in range(leading, last)])


def regions(levels, half_side):
    inner_side = half_side - 2 * (2 - levels)
    small_rows = jnp.arange(half_side, dtype=jnp.int32)
    large_rows = jnp.arange(2 * half_side, dtype=jnp.int32)
    inner_mask = (small_rows < inner_side[..., None]).astype(jnp.float32)
    outer_mask = (large_rows < 2 * inner_side[..., None]).astype(jnp.float32)
    return (
        outer_mask[..., :, None] * outer_mask[..., None, :],
        inner_mask[..., :, None] * inner_mask[..., None, :],
    )


def patches(field_in, stride, half_side):
    padded = jnp.pad(field_in, ((0, 0), (1, 1), (1, 1), (0, 0)))
    pieces = [
        padded[
            :,
            row_at : row_at + stride * half_side : stride,
            col_at : col_at + stride * half_side : stride,
            :,
        ]
        for row_at in range(3)
        for col_at in range(3)
    ]
    joined = jnp.concatenate(pieces, axis=-1)
    return joined.reshape(-1, joined.shape[-1])


def contract_rows(left_side, right_side):
    return lax.dot_general(
        left_side, right_side, (((0,), (0,)), ((), ())), preferred_element_type=jnp.float32
    )


def contract_cols(left_side, right_side):
    return lax.dot_general(
        left_side, right_side, (((1,), (1,)), ((), ())), preferred_element_type=jnp.float32
    )


def silu_slope(values):
    sigmoid = jax.nn.sigmoid(values)
    return sigmoid * (1.0 + values * (1.0 - sigmoid))


def spread_taps(tap_grads, image_count, half_side, channels):
    tap_grid = tap_grads.reshape(image_count, half_side, half_side, 9, channels)
    empty_phase = jnp.zeros((image_count, half_side + 1, half_side + 1, channels), jnp.float32)
    phases = [[empty_phase, empty_phase], [empty_phase, empty_phase]]
    for row_at in range(3):
        for col_at in range(3):
            tap_piece = tap_grid[:, :, :, 3 * row_at + col_at, :]
            top_pad = 1 if row_at == 2 else 0
            left_pad = 1 if col_at == 2 else 0
            placed = jnp.pad(
                tap_piece, ((0, 0), (top_pad, 1 - top_pad), (left_pad, 1 - left_pad), (0, 0))
            )
            phases[row_at % 2][col_at % 2] = phases[row_at % 2][col_at % 2] + placed
    row_phases = [jnp.stack([phases[parity][0], phases[parity][1]], axis=3) for parity in range(2)]
    alternated = jnp.stack(row_phases, axis=2).reshape(
        image_count, 2 * half_side + 2, 2 * half_side + 2, channels
    )
    return alternated[:, 1 : 2 * half_side + 1, 1 : 2 * half_side + 1, :]


def keep_slot(buffer_all, new_value, slot_at, keep_flag):
    current = lax.dynamic_index_in_dim(buffer_all, slot_at, 0, keepdims=False)
    return lax.dynamic_update_index_in_dim(
        buffer_all, jnp.where(keep_flag, new_value, current), slot_at, 0
    )


def pipeline_body(images, res_ids, weights, bn_gain, bn_bias, cotangent):
    sections = lax.axis_size("section")
    last_section = sections - 1
    position = lax.axis_index("section")
    micro_count = res_ids.shape[0]
    image_count = images.shape[1]
    half_side = cotangent.shape[2]
    channels = weights.shape[2]
    in_channels = images.shape[4]
    pixel_rows = image_count * half_side * half_side
    taps_in = 9 * in_channels
    matrix = weights[0]
    gain_rows = bn_gain[0]
    bias_rows = bn_bias[0]
    is_first = position == 0
    adds_short = (position == 1) | (position == 3)
    passes_short = position == 2
    makes_short = position == 1
    back_matrix = jnp.transpose(matrix.reshape(9, channels, channels)[::-1], (0, 2, 1)).reshape(
        9 * channels, channels
    )
    mask_in_all, mask_out_all = regions(res_ids, half_side)
    act_shape = (image_count, half_side, half_side, channels)
    zero_pixels = jnp.zeros((pixel_rows, channels), jnp.float32)
    zero_input = jnp.zeros((image_count, 2 * half_side, 2 * half_side, in_channels), jnp.float32)
    zero_weight = jnp.zeros((9 * channels, channels), jnp.float32)
    own_images = images[0]
    gathered = [own_images]
    for source in range(1, micro_count):
        gathered.append(passed_along(own_images, "section", -source))
    section_inputs = jnp.stack(gathered)
    own_cot = cotangent[0]
    arrived = []
    for source in range(micro_count):
        if source == last_section:
            arrived.append(own_cot)
        else:
            arrived.append(passed_along(own_cot, "section", last_section - source))
    cot_all = jnp.stack(arrived)

    def conv_first(prev_act, first_in):
        columns = patches(first_in, 2, half_side)
        main_out = jnp.dot(columns, matrix[:taps_in], preferred_element_type=jnp.float32)
        proj_out = jnp.dot(
            columns[:, 4 * in_channels : 5 * in_channels],
            matrix[taps_in : taps_in + in_channels],
            preferred_element_type=jnp.float32,
        )
        return jnp.stack([main_out, proj_out])

    def conv_rest(prev_act, first_in):
        columns = patches(prev_act, 1, half_side)
        return jnp.stack(
            [jnp.dot(columns, matrix, preferred_element_type=jnp.float32), zero_pixels]
        )

    def conv_spare(prev_act, first_in):
        return jnp.stack([zero_pixels, zero_pixels])

    def back_first(grad_conv, prev_act, first_in):
        columns = patches(first_in, 2, half_side)
        centre = columns[:, 4 * in_channels : 5 * in_channels]
        main_grad = contract_rows(columns, grad_conv[0])
        proj_grad = contract_rows(centre, grad_conv[1])
        filler = jnp.zeros((9 * channels - taps_in - in_channels, channels), jnp.float32)
        weight_now = jnp.concatenate([main_grad, proj_grad, filler], axis=0)
        tap_grads = contract_cols(grad_conv[0], matrix[:taps_in])
        centre_grad = contract_cols(grad_conv[1], matrix[taps_in : taps_in + in_channels])
        tap_grads = tap_grads + jnp.pad(centre_grad, ((0, 0), (4 * in_channels, 4 * in_channels)))
        return (
            weight_now,
            zero_pixels,
            spread_taps(tap_grads, image_count, half_side, in_channels),
        )

    def back_rest(grad_conv, prev_act, first_in):
        columns = patches(prev_act, 1, half_side)
        weight_now = contract_rows(columns, grad_conv[0])
        grad_image = grad_conv[0].reshape(act_shape)
        prev_grad = jnp.dot(
            patches(grad_image, 1, half_side), back_matrix, preferred_element_type=jnp.float32
        )
        return (weight_now, prev_grad, zero_input)

    def back_spare(grad_conv, prev_act, first_in):
        return (zero_weight, zero_pixels, zero_input)

    def finish(conv_out, mean_rows, scale_rows, flat_mask, short_in):
        normed = (conv_out - mean_rows[:, None, :]) * scale_rows[:, None, :] * gain_rows[
            :, None, :
        ] + bias_rows[:, None, :]
        pre_act = normed[0] + jnp.where(adds_short, short_in, 0.0)
        activated = jax.nn.silu(pre_act) * flat_mask[:, None]
        proj_short = normed[1] * flat_mask[:, None]
        short_out = jnp.where(is_first, proj_short, jnp.where(makes_short, activated, short_in))
        return (pre_act, activated, short_out)

    empty_act = jnp.zeros(act_shape, jnp.bfloat16)
    recv_act = empty_act
    recv_short = empty_act
    saved_act = jnp.zeros((micro_count,) + act_shape, jnp.bfloat16)
    saved_short = saved_act
    saved_final = saved_act
    saved_mean = jnp.zeros((micro_count, 2, channels), jnp.float32)
    saved_scale = saved_mean
    saved_total = jnp.zeros((micro_count,), jnp.float32)
    sweep_len = micro_count + last_section
    for tick_at in range(sweep_len):
        slot_raw = tick_at - position
        is_valid = (slot_raw >= 0) & (slot_raw < micro_count)
        slot_at = jnp.clip(slot_raw, 0, micro_count - 1)
        flat_mask = mask_out_all[slot_at].reshape(-1) * is_valid.astype(jnp.float32)
        first_in = section_inputs[slot_at] * mask_in_all[slot_at][..., None].astype(jnp.bfloat16)
        branch = jnp.where(is_valid, jnp.where(is_first, 0, 1), 2).astype(jnp.int32)
        conv_out = lax.switch(branch, [conv_first, conv_rest, conv_spare], recv_act, first_in)
        local_total = jnp.sum(flat_mask)
        weighted = conv_out * flat_mask[None, :, None]
        grand_total, sum_rows = lax.psum((local_total, jnp.sum(weighted, axis=1)), "dp")
        grand_total = jnp.maximum(grand_total, 1.0)
        statistics_mean_rows = sum_rows / grand_total
        centred = conv_out - statistics_mean_rows[:, None, :]
        variance = (
            lax.psum(jnp.sum(centred * centred * flat_mask[None, :, None], axis=1), "dp")
            / grand_total
        )
        grand_total, mean_rows, scale_rows = (
            grand_total,
            statistics_mean_rows,
            lax.rsqrt(variance + epsilon),
        )
        short_in = recv_short.reshape(pixel_rows, channels).astype(jnp.float32)
        pre_act, activated, short_out = finish(conv_out, mean_rows, scale_rows, flat_mask, short_in)
        act_low = activated.astype(jnp.bfloat16).reshape(act_shape)
        short_low = short_out.astype(jnp.bfloat16).reshape(act_shape)
        saved_act = keep_slot(saved_act, recv_act, slot_at, is_valid)
        saved_short = keep_slot(saved_short, recv_short, slot_at, is_valid)
        saved_mean = keep_slot(saved_mean, mean_rows, slot_at, is_valid)
        saved_scale = keep_slot(saved_scale, scale_rows, slot_at, is_valid)
        saved_total = keep_slot(saved_total, grand_total, slot_at, is_valid)
        saved_final = keep_slot(
            saved_final, act_low, slot_at, is_valid & (position == last_section)
        )
        if tick_at + 1 < sweep_len:
            recv_act, recv_short = passed_along((act_low, short_low), "section", 1)
    grad_act = empty_act
    grad_short = empty_act
    weight_acc = zero_weight
    gain_acc = jnp.zeros((2, channels), jnp.float32)
    bias_acc = gain_acc
    saved_dx = jnp.zeros(
        (micro_count, image_count, 2 * half_side, 2 * half_side, in_channels), jnp.bfloat16
    )
    for tick_at in range(sweep_len):
        slot_raw = tick_at - (last_section - position)
        is_valid = (slot_raw >= 0) & (slot_raw < micro_count)
        slot_at = jnp.clip(slot_raw, 0, micro_count - 1)
        flat_mask = mask_out_all[slot_at].reshape(-1) * is_valid.astype(jnp.float32)
        first_in = section_inputs[slot_at] * mask_in_all[slot_at][..., None].astype(jnp.bfloat16)
        branch = jnp.where(is_valid, jnp.where(is_first, 0, 1), 2).astype(jnp.int32)
        prev_act = saved_act[slot_at]
        conv_out = lax.switch(branch, [conv_first, conv_rest, conv_spare], prev_act, first_in)
        mean_rows = saved_mean[slot_at]
        scale_rows = saved_scale[slot_at]
        valid_total = saved_total[slot_at]
        short_in = saved_short[slot_at].reshape(pixel_rows, channels).astype(jnp.float32)
        pre_act, activated, short_out = finish(conv_out, mean_rows, scale_rows, flat_mask, short_in)
        from_act = (
            jnp.where(position == last_section, cot_all[slot_at], grad_act)
            .reshape(pixel_rows, channels)
            .astype(jnp.float32)
        )
        from_short = grad_short.reshape(pixel_rows, channels).astype(jnp.float32)
        slope = silu_slope(pre_act) * flat_mask[:, None]
        grad_pre = (from_act + jnp.where(adds_short, from_short, 0.0)) * slope
        grad_proj = jnp.where(is_first, from_short * flat_mask[:, None], 0.0)
        grad_normed = jnp.stack([grad_pre, grad_proj])
        normalized = (conv_out - mean_rows[:, None, :]) * scale_rows[:, None, :]
        bias_now, gain_now = lax.psum(
            (jnp.sum(grad_normed, axis=1), jnp.sum(grad_normed * normalized, axis=1)), "dp"
        )
        bias_acc = bias_acc + bias_now
        gain_acc = gain_acc + gain_now
        grad_conv = (
            flat_mask[None, :, None]
            * gain_rows[:, None, :]
            * scale_rows[:, None, :]
            * (
                grad_normed
                - (bias_now[:, None, :] + normalized * gain_now[:, None, :]) / valid_total
            )
        )
        grad_conv = grad_conv.astype(jnp.bfloat16)
        weight_now, prev_grad, input_grad = lax.switch(
            branch, [back_first, back_rest, back_spare], grad_conv, prev_act, first_in
        )
        weight_acc = weight_acc + weight_now
        masked_input = (input_grad * mask_in_all[slot_at][..., None]).astype(jnp.bfloat16)
        saved_dx = keep_slot(saved_dx, masked_input, slot_at, is_valid & is_first)
        send_act = (
            (prev_grad + jnp.where(passes_short, from_short, 0.0))
            .astype(jnp.bfloat16)
            .reshape(act_shape)
        )
        send_short = jnp.where(adds_short, grad_pre, 0.0).astype(jnp.bfloat16).reshape(act_shape)
        if tick_at + 1 < sweep_len:
            grad_act, grad_short = passed_along((send_act, send_short), "section", -1)
    weight_total = lax.psum(weight_acc, "dp")
    result = saved_final[last_section]
    for source in range(last_section):
        arrived_piece = passed_along(saved_final[source], "section", source - last_section)
        result = jnp.where(position == source, arrived_piece, result)
    grad_result = saved_dx[0]
    for source in range(1, micro_count):
        arrived_piece = passed_along(saved_dx[source], "section", source)
        grad_result = jnp.where(position == source, arrived_piece, grad_result)
    return (result[None], grad_result[None], weight_total[None], gain_acc[None], bias_acc[None])


f32, bf16 = jnp.float32, jnp.bfloat16
LANES = 256
GRID = (9, 9, 16, LANES)


def flip(value, axis, mask, senders=None):
    count = lax.axis_size(axis)
    pairs = [(i, i ^ mask) for i in range(count) if senders is None or senders(i)]
    return lax.ppermute(value, axis, pairs)


def struct(shape, kind=bf16):
    return jax.ShapeDtypeStruct(shape, kind)


def call(kernel, name, operands, places, outs, out_places, scratch, flops, moved, limit):
    spaces = {"s": pltpu.SMEM, "v": pltpu.VMEM, "a": pl.ANY, "h": pltpu.HBM}
    return pl.pallas_call(
        kernel,
        out_shape=outs,
        in_specs=[pl.BlockSpec(memory_space=spaces[place]) for place in places],
        out_specs=[pl.BlockSpec(memory_space=spaces[place]) for place in out_places],
        scratch_shapes=scratch,
        name=name,
        compiler_params=pltpu.CompilerParams(vmem_limit_bytes=limit * 2**20),
        cost_estimate=pl.CostEstimate(flops=1, bytes_accessed=1, transcendentals=0),
    )(*operands)


def dot(left, right):
    return jnp.dot(left, right, preferred_element_type=f32)


def dot_t(left, right):
    return lax.dot_general(left, right, (((1,), (1,)), ((), ())), preferred_element_type=f32)


def col_sum(values):
    return jnp.sum(values, axis=0, keepdims=True)


def blank_edges(dst):
    blank = jnp.zeros((11, 16, LANES), bf16)
    dst[0] = blank
    dst[10] = blank
    dst[:, 0] = blank
    dst[:, 10] = blank


def inner(dst):
    return dst.at[1:10, 1:10]


class Inside:
    def __init__(self, side):
        self.count = col_sum(side * side)
        self.masks = (None, side > 6.0, side > 8.0)

    def keep(self, ring, values):
        mask = self.masks[self.level(ring)]
        return values if mask is None else jnp.where(mask, values, 0.0)

    @staticmethod
    def level(ring):
        return 0 if ring < 5 else 1 if ring < 7 else 2

    def total(self, values_at):
        sums = [None, None, None]
        for row in range(9):
            for col in range(9):
                at = self.level(max(row, col))
                value = values_at(row, col)
                sums[at] = value if sums[at] is None else sums[at] + value
        return col_sum(sums[0] + self.keep(5, sums[1]) + self.keep(7, sums[2]))


def norm_stats(acc, inside):
    mean = inside.total(lambda row, col: acc[row, col]) / inside.count

    def squared(row, col):
        centred = acc[row, col] - mean
        return centred * centred

    return mean, lax.rsqrt(inside.total(squared) / inside.count + epsilon)


def sigmoid_of(values):
    return 0.5 * jnp.tanh(0.5 * values) + 0.5


def split_three(row):
    high = row.astype(bf16)
    rest = row - high.astype(f32)
    middle = rest.astype(bf16)
    low = (rest - middle.astype(f32)).astype(bf16)
    return [high, middle, low]


def pack_vectors(rows):
    pieces = [one.astype(f32) for row in rows for one in split_three(row)]
    pieces.append(jnp.zeros((16 - len(pieces), LANES), f32))
    return jnp.concatenate(pieces, axis=0).astype(bf16)


def unpack_vectors(block):
    wide = block.astype(f32)
    return [wide[3 * at : 3 * at + 1] + wide[3 * at + 1 : 3 * at + 2] + wide[3 * at + 2 : 3 * at + 3] for at in range(4)]


def pack_rows(ref, rows):
    ref[...] = jnp.concatenate(rows + [jnp.zeros((8 - len(rows), LANES), f32)], axis=0)


def turn_matrix(image_of_row):
    out_row = lax.broadcasted_iota(jnp.int32, (256, 256), 0)
    in_row = lax.broadcasted_iota(jnp.int32, (256, 256), 1)
    pixel_same = (out_row >> 4) == (in_row & 15)
    return jnp.where(pixel_same & ((out_row & 15) == image_of_row(in_row)), 1.0, 0.0).astype(bf16)


def split_weights(sc, matrix, vectors):
    def kernel(sc_ref, matrix_ref, vec_ref, first_a, first_b, part_a, part_b, sems):
        lane = pl.multiple_of(LANES * sc_ref[2], LANES)
        chosen = matrix_ref.at[:, pl.ds(lane, LANES)]
        copies = []
        for target, start, rows in (
            (first_a, 0, 1280), (first_b, 1280, 1280), (part_a, 0, 2304), (part_b, 2304, 2304)
        ):
            for at in range(0, rows, rows // 2):
                copies.append(
                    pltpu.make_async_copy(
                        chosen.at[start + at : start + at + rows // 2],
                        target.at[at : at + rows // 2],
                        sems.at[len(copies)],
                    )
                )
                copies[-1].start()
        small = pack_vectors([vec_ref[at : at + 1, pl.ds(lane, LANES)] for at in range(4)])
        first_a[1280:1296] = small
        part_a[2304:2320] = small
        for copy in copies:
            copy.wait()

    outs = [struct((rows, LANES)) for rows in (1296, 1280, 2320, 2304)]
    return call(
        kernel, "split_weights", (sc, matrix, vectors), "shv", outs, "vvvv",
        [pltpu.SemaphoreType.DMA((8,))], 0, 14_000_000, 40,
    )


def prepare_images(pieces):
    def kernel(pieces_ref, out, side_out, held, sems):
        copies = [
            pltpu.make_async_copy(pieces_ref.at[at], held.at[2 * at : 2 * at + 2], sems.at[at])
            for at in range(8)
        ]
        for copy in copies:
            copy.start()
        turn = turn_matrix(lambda r: r >> 4)
        out[:, :, 0] = jnp.zeros((2, 2, 10, 16, LANES), bf16)
        out[:, :, :, 0] = jnp.zeros((2, 2, 10, 16, LANES), bf16)
        for copy in copies:
            copy.wait()

        def block(at):
            source = held[:, 16 * at : 16 * at + 16].reshape(256, LANES)
            return dot(turn, source).reshape(16, 16, LANES)

        last = block(20)
        side = last[4]
        side_out[...] = side
        masks = (None, 2.0 * side > 13.0, 2.0 * side > 17.0)
        for at in range(21):
            turned = last if at == 20 else block(at)
            for step in range(16 if at < 20 else 4):
                row, col = divmod(16 * at + step, 18)
                mask = masks[Inside.level(max(row, col) // 2)]
                kept = turned[step] if mask is None else jnp.where(mask, turned[step], 0.0)
                out[row % 2, col % 2, 1 + row // 2, 1 + col // 2] = kept.astype(bf16)

    outs = [struct((2, 2, 10, 10, 16, LANES)), struct((16, LANES), f32)]
    scratch = [pltpu.VMEM((16, 336, LANES), bf16), pltpu.SemaphoreType.DMA((8,))]
    return call(
        kernel, "prepare_images", (pieces,), "h", outs, "vv", scratch, 21 * 2 * 256**3, 8_000_000, 40
    )


def prepare_cotangent(sc, pieces):
    def kernel(sc_ref, pieces_ref, out, held, sems):
        lane = pl.multiple_of(LANES * sc_ref[2], LANES)
        load = pltpu.make_async_copy(
            pieces_ref.at[:, :, :, pl.ds(lane, LANES)], held, sems.at[0]
        )
        load.start()
        turn = turn_matrix(lambda r: r >> 4)
        load.wait()
        for at in range(6):
            source = held[:, :, 16 * at : 16 * at + 16].reshape(256, LANES)
            turned = dot(turn, source).astype(bf16).reshape(16, 16, LANES)
            for step in range(16 if at < 5 else 1):
                row, col = divmod(16 * at + step, 9)
                out[row, col] = turned[step]

    scratch = [pltpu.VMEM((8, 2, 96, LANES), bf16), pltpu.SemaphoreType.DMA((1,))]
    return call(
        kernel, "prepare_cotangent", (sc, pieces), "sh", [struct(GRID)], "v", scratch,
        6 * 2 * 256**3, 2_000_000, 40,
    )[0]


def load_chosen(section, table, dst, sem):
    copies = []
    for sections, ref in table:
        copy = pltpu.make_async_copy(ref.at[0 : dst.shape[0]], dst, sem)
        chosen = section == sections[0]
        for other in sections[1:]:
            chosen = chosen | (section == other)
        pl.when(chosen)(copy.start)
        copies.append(copy)
    return copies[0]


def load_vectors(section, table, dst, sem):
    copies = []
    for sections, ref in table:
        rows = ref.shape[0]
        copy = pltpu.make_async_copy(ref.at[rows - 16 : rows], dst, sem)
        chosen = section == sections[0]
        for other in sections[1:]:
            chosen = chosen | (section == other)
        pl.when(chosen)(copy.start)
        copies.append(copy)
    return copies[0]


def stage_first(sc, side, fields, messages):
    def kernel(sc_ref, side_ref, field, own_a, own_b, x_1, y_1, x_2, y_2, x_3, y_3, hidden, short, zhat, zhat_p, stats, w_out, w, vec, acc, acc_p, sems, out_sems):
        section = sc_ref[0]
        table_a = [((0,), own_a), ((1,), x_1), ((2,), y_2), ((3,), y_3)]
        table_b = [((0,), own_b), ((2,), y_1), ((1,), x_2), ((3,), x_3)]
        loads = [
            load_chosen(section, table_a, w.at[0:1280], sems.at[0]),
            load_chosen(section, table_b, w.at[1280:2560], sems.at[1]),
            load_vectors(section, table_a, vec, sems.at[2]),
        ]
        for copy in loads:
            copy.wait()
        outs = [pltpu.make_async_copy(w, w_out, out_sems.at[0])]
        outs[0].start()
        for chunk in range(3):
            total = jnp.zeros((432, LANES), f32)
            for a in range(3):
                for b in range(3):
                    row_at, col_at = 3 * chunk + (0 if a == 0 else 1), 0 if b == 0 else 1
                    left = field[(a + 1) % 2, (b + 1) % 2, row_at : row_at + 3, col_at : col_at + 9]
                    at = LANES * (3 * a + b)
                    total = total + dot(left.reshape(432, LANES), w[at : at + LANES])
            acc[3 * chunk : 3 * chunk + 3] = total.reshape(3, 9, 16, LANES)
            centre = field[0, 0, 3 * chunk + 1 : 3 * chunk + 4, 1:10].reshape(432, LANES)
            acc_p[3 * chunk : 3 * chunk + 3] = dot(centre, w[2304:2560]).reshape(3, 9, 16, LANES)
        inside = Inside(side_ref[...])
        mean, scale = norm_stats(acc, inside)
        mean_p, scale_p = norm_stats(acc_p, inside)
        gain, gain_p, bias, bias_p = unpack_vectors(vec[...])
        for row in range(9):
            for col in range(9):
                ring = max(row, col)
                normed = (acc[row, col] - mean) * scale
                acc[row, col] = normed
                pre = normed * gain + bias
                hidden[row, col] = inside.keep(ring, pre * sigmoid_of(pre)).astype(bf16)
                normed = (acc_p[row, col] - mean_p) * scale_p
                acc_p[row, col] = normed
                short[row, col] = inside.keep(ring, normed * gain_p + bias_p).astype(bf16)
            for at, (source, target) in enumerate(((acc, zhat), (acc_p, zhat_p))):
                copy = pltpu.make_async_copy(source.at[row], target.at[row], out_sems.at[1 + 9 * at + row])
                copy.start()
                outs.append(copy)
        pack_rows(stats, [scale, gain, bias, scale_p, gain_p])
        for copy in outs:
            copy.wait()

    outs = [
        struct(GRID), struct(GRID), struct(GRID, f32), struct(GRID, f32), struct((8, LANES), f32),
        struct((2560, LANES)),
    ]
    scratch = [
        pltpu.VMEM((2560, LANES), bf16), pltpu.VMEM((16, LANES), bf16), pltpu.VMEM(GRID, f32),
        pltpu.VMEM(GRID, f32), pltpu.SemaphoreType.DMA((3,)), pltpu.SemaphoreType.DMA((19,)),
    ]
    return call(
        kernel, "stage_first", (sc, side, fields, *messages), "svv" + 8 * "h", outs, "vvhhvh",
        scratch, 2 * 1296 * 2560 * LANES, 8_000_000, 44,
    )


def load_fields(padded, own_ref, oth_ref, sems):
    copies = [
        pltpu.make_async_copy(own_ref, inner(padded.at[0]), sems.at[0]),
        pltpu.make_async_copy(oth_ref, inner(padded.at[1]), sems.at[1]),
    ]
    for copy in copies:
        copy.start()
    blank_edges(padded.at[0])
    blank_edges(padded.at[1])
    return copies


def weight_tables(part, messages):
    own_a, own_b, x_1, y_1, x_2, y_2 = messages
    return {
        1: ([((0,), x_1), ((1,), own_a), ((2, 3), y_2)], [((0, 2), x_2), ((1,), own_b), ((3,), y_1)]),
        2: ([((0, 1), y_2), ((2,), own_a), ((3,), x_1)], [((0,), y_1), ((2,), own_b), ((1, 3), x_2)]),
        3: ([((0, 1), y_2), ((2,), x_1), ((3,), own_a)], [((0, 2), x_2), ((1,), y_1), ((3,), own_b)]),
    }[part]


def stage_rest(part, sc, side, own, other, messages, short, cot=None, after=()):
    last = cot is not None
    extra = [one for one in (short, cot) if one is not None]

    def kernel(sc_ref, side_ref, own_ref, oth_ref, *refs):
        refs = list(refs)
        short_ref = refs.pop(0) if short is not None else None
        cot_ref = refs.pop(0) if last else None
        tables = weight_tables(part, refs[:6])
        refs = refs[6 + len(after) :]
        if last:
            dz, passed, out, sums = refs[:4]
            refs = refs[4:]
        else:
            hidden, zhat, stats = refs[:3]
            refs = refs[3:]
        w_keep, w_send, w, vec, padded, acc = refs[:6]
        grads = refs[6] if last else None
        sems, out_sems = refs[-2:]
        section, core = sc_ref[0], sc_ref[2]
        loads = [
            load_chosen(section, tables[0], w.at[0:2304], sems.at[0]),
            load_chosen(section, tables[1], w.at[2304:4608], sems.at[1]),
            load_vectors(section, tables[0], vec, sems.at[2]),
        ] + load_fields(padded, own_ref, oth_ref, sems.at[3:5])
        for copy in loads:
            copy.wait()
        outs = []
        for tap in range(9):
            for at, target in ((core, w_keep), (1 - core, w_send)):
                from_row = pl.multiple_of(LANES * (2 * tap + at), LANES)
                outs.append(
                    pltpu.make_async_copy(
                        w.at[pl.ds(from_row, LANES)],
                        target.at[LANES * tap : LANES * tap + LANES],
                        out_sems.at[len(outs)],
                    )
                )
                outs[-1].start()
        for chunk in range(3):
            total = jnp.zeros((432, LANES), f32)
            for a in range(3):
                for b in range(3):
                    for at in range(2):
                        left = padded[at, 3 * chunk + a : 3 * chunk + a + 3, b : b + 9]
                        which = core if at == 0 else 1 - core
                        from_row = pl.multiple_of(LANES * (2 * (3 * a + b) + which), LANES)
                        total = total + dot(left.reshape(432, LANES), w[pl.ds(from_row, LANES)])
            acc[3 * chunk : 3 * chunk + 3] = total.reshape(3, 9, 16, LANES)
        inside = Inside(side_ref[...])
        mean, scale = norm_stats(acc, inside)
        gain, _, bias, _ = unpack_vectors(vec[...])
        if last:
            sums_now = [None, None]
            parts = [[], []]
        for row in range(9):
            for col in range(9):
                ring = max(row, col)
                normed = (acc[row, col] - mean) * scale
                acc[row, col] = normed
                pre = normed * gain + bias
                if short is not None:
                    pre = pre + short_ref[row, col].astype(f32)
                sigmoid = sigmoid_of(pre)
                target = out if last else hidden
                target[row, col] = inside.keep(ring, pre * sigmoid).astype(bf16)
                if last:
                    slope = sigmoid * (1.0 + pre * (1.0 - sigmoid))
                    grad = inside.keep(ring, cot_ref[row, col].astype(f32) * slope)
                    grads[row, col] = grad
                    passed[row, col] = grad.astype(bf16)
                    for at, value in enumerate((grad, grad * normed)):
                        sums_now[at] = value if sums_now[at] is None else sums_now[at] + value
            if not last:
                copy = pltpu.make_async_copy(acc.at[row], zhat.at[row], out_sems.at[18 + row])
                copy.start()
                outs.append(copy)
        if last:
            bias_now, gain_now = col_sum(sums_now[0]), col_sum(sums_now[1])
            norm_back(dz, grads, acc, inside, gain * scale, bias_now, gain_now)
            pack_rows(sums, [gain_now, bias_now])
        else:
            pack_rows(stats, [scale, gain, bias])
        for copy in outs:
            copy.wait()

    half = struct((2304, LANES))
    if last:
        outs, places = [struct(GRID), struct(GRID), struct(GRID), struct((8, LANES), f32)], "vvvv"
    else:
        outs, places = [struct(GRID), struct(GRID, f32), struct((8, LANES), f32)], "vhv"
    scratch = [
        pltpu.VMEM((4608, LANES), bf16), pltpu.VMEM((16, LANES), bf16),
        pltpu.VMEM((2, 11, 11, 16, LANES), bf16), pltpu.VMEM(GRID, f32),
    ] + ([pltpu.VMEM(GRID, f32)] if last else [])
    scratch += [pltpu.SemaphoreType.DMA((5,)), pltpu.SemaphoreType.DMA((27,))]
    return call(
        kernel, f"stage_{part}", (sc, side, own, other, *extra, *messages, *after),
        "svaa" + len(extra) * "v" + (6 + len(after)) * "h", outs + [half, half], places + "hh", scratch,
        2 * 1296 * 4608 * LANES, 8_000_000, 44,
    )


def norm_back(dz, grads, zhat, inside, weight, bias_now, gain_now):
    constant, slope = weight * bias_now / inside.count, weight * gain_now / inside.count
    for row in range(9):
        for col in range(9):
            value = weight * grads[row, col] - (constant + slope * zhat[row, col])
            dz[row, col] = inside.keep(max(row, col), value).astype(bf16)


def stage_back(part, sc, side, dz_own, dz_other, w_own, w_other, zhat, stats, short=None, extra=None, proj=None):
    first = proj is not None
    optional = [one for one in (short, extra) if one is not None] + (list(proj) if first else [])

    def kernel(sc_ref, side_ref, stats_ref, dz_own_ref, dz_oth_ref, w_own_ref, w_oth_ref, zhat_ref, *refs):
        refs = list(refs)
        short_ref = refs.pop(0) if short is not None else None
        extra_ref = refs.pop(0) if extra is not None else None
        if first:
            dyp_ref, zhat_p_ref = refs.pop(0), refs.pop(0)
        dz, sums = refs.pop(0), refs.pop(0)
        passed = refs.pop(0) if short is not None else None
        dz_p = refs.pop(0) if first else None
        padded, acc, held, w = refs[:4]
        held_p = refs[4] if first else None
        sems = refs[-1]
        fields = load_fields(padded, dz_own_ref, dz_oth_ref, sems.at[0:2])
        loads = [
            pltpu.make_async_copy(w_own_ref, w.at[0], sems.at[2]),
            pltpu.make_async_copy(w_oth_ref, w.at[1], sems.at[3]),
        ]
        later = [pltpu.make_async_copy(zhat_ref, held, sems.at[4])]
        if first:
            later.append(pltpu.make_async_copy(zhat_p_ref, held_p, sems.at[5]))
        for copy in loads + later:
            copy.start()
        for copy in fields + loads:
            copy.wait()
        for chunk in range(3):
            total = jnp.zeros((432, LANES), f32)
            for a in range(3):
                for b in range(3):
                    for at in range(2):
                        row_at = 3 * chunk + 2 - a
                        left = padded[at, row_at : row_at + 3, 2 - b : 11 - b]
                        from_row = LANES * (3 * a + b)
                        right = w[at, from_row : from_row + LANES]
                        total = total + dot_t(left.reshape(432, LANES), right)
            acc[3 * chunk : 3 * chunk + 3] = total.reshape(3, 9, 16, LANES)
        for copy in later:
            copy.wait()
        inside = Inside(side_ref[...])
        scale, gain, bias, scale_p, gain_p = [stats_ref[at : at + 1] for at in range(5)]
        sums_now = [None] * 4
        for row in range(9):
            for col in range(9):
                ring = max(row, col)
                normed = held[row, col]
                pre = normed * gain + bias
                grad = acc[row, col]
                if extra is not None:
                    grad = grad + extra_ref[row, col].astype(f32)
                if short is not None:
                    pre = pre + short_ref[row, col].astype(f32)
                sigmoid = sigmoid_of(pre)
                slope = sigmoid * (1.0 + pre * (1.0 - sigmoid))
                grad = inside.keep(ring, grad.astype(bf16).astype(f32) * slope)
                acc[row, col] = grad
                if short is not None:
                    passed[row, col] = grad.astype(bf16)
                terms = [grad, grad * normed]
                if first:
                    grad_p = dyp_ref[row, col].astype(f32)
                    terms += [grad_p, grad_p * held_p[row, col]]
                for at, value in enumerate(terms):
                    sums_now[at] = value if sums_now[at] is None else sums_now[at] + value
        totals = [col_sum(value) for value in sums_now if value is not None]
        norm_back(dz, acc, held, inside, gain * scale, totals[0], totals[1])
        rows = [totals[1], totals[0]]
        if first:
            for row in range(9):
                for col in range(9):
                    acc[row, col] = dyp_ref[row, col].astype(f32)
            norm_back(dz_p, acc, held_p, inside, gain_p * scale_p, totals[2], totals[3])
            rows += [totals[3], totals[2]]
        pack_rows(sums, rows)

    outs, places = [struct(GRID), struct((8, LANES), f32)], "vv"
    if short is not None:
        outs, places = outs + [struct(GRID)], places + "v"
    if first:
        outs, places = outs + [struct(GRID)], places + "v"
    scratch = [
        pltpu.VMEM((2, 11, 11, 16, LANES), bf16), pltpu.VMEM(GRID, f32), pltpu.VMEM(GRID, f32),
        pltpu.VMEM((2, 2304, LANES), bf16),
    ] + ([pltpu.VMEM(GRID, f32)] if first else [])
    scratch += [pltpu.SemaphoreType.DMA((6,))]
    kinds = "v" * ((short is not None) + (extra is not None)) + ("vh" if first else "")
    return call(
        kernel, f"back_{part}",
        (sc, side, stats, dz_own, dz_other, w_own, w_other, zhat, *optional),
        "svvaahhh" + kinds, outs, places, scratch, 2 * 1296 * 4608 * LANES, 10_000_000, 44,
    )


def pick_images(sc, *fields):
    def kernel(sc_ref, *refs):
        zone, core = sc_ref[1], sc_ref[2]
        out_row = lax.broadcasted_iota(jnp.int32, (4, 96, 1296), 1)
        slot = lax.broadcasted_iota(jnp.int32, (4, 96, 1296), 0)
        in_row = lax.broadcasted_iota(jnp.int32, (4, 96, 1296), 2)
        image = 4 * zone + 2 * ((slot >> 1) ^ core) + (slot & 1)
        pick = jnp.where(in_row == 16 * out_row + image, 1.0, 0.0).astype(bf16).reshape(384, 1296)
        for source, target in zip(refs[: len(fields)], refs[len(fields) :]):
            chosen = dot(pick, source[...].reshape(1296, LANES))
            target[...] = chosen.astype(bf16).reshape(4, 96, LANES)

    count = len(fields)
    return call(
        kernel, f"pick_images_{count}", (sc, *fields), "s" + count * "v", count * [struct((4, 96, LANES))],
        count * "v", [], count * 2 * 384 * 1296 * LANES, 3_000_000, 40,
    )


def weight_rest(part, sc, own, other, dz, sums):
    def kernel(sc_ref, own_ref, oth_ref, dz_ref, sums_ref, out, turned, padded, sems):
        zone, core = sc_ref[1], sc_ref[2]
        load = pltpu.make_async_copy(dz_ref, inner(padded), sems.at[0])
        load.start()
        blank_edges(padded)
        lane = pl.multiple_of(128 * (zone & 1), 128)
        is_own = (zone >> 1) == core

        @pl.when(is_own)
        def _():
            turned[...] = own_ref[:, :, :, pl.ds(lane, 128)].reshape(1296, 128).T

        @pl.when(jnp.logical_not(is_own))
        def _():
            turned[...] = oth_ref[:, :, :, pl.ds(lane, 128)].reshape(1296, 128).T

        load.wait()
        left = turned[...]
        for a in range(3):
            for b in range(3):
                right = padded[2 - a : 11 - a, 2 - b : 11 - b].reshape(1296, LANES)
                at = 128 * (3 * a + b)
                out[at : at + 128] = dot(left, right).astype(bf16)
        blank = jnp.zeros((1, LANES), f32)
        out[1152:1168] = pack_vectors([sums_ref[0:1], blank, sums_ref[1:2], blank])

    scratch = [
        pltpu.VMEM((128, 1296), bf16), pltpu.VMEM((11, 11, 16, LANES), bf16),
        pltpu.SemaphoreType.DMA((1,)),
    ]
    return call(
        kernel, f"weight_{part}", (sc, own, other, dz, sums), "svvav", [struct((1168, LANES))], "v",
        scratch, 2 * 1296 * 1152 * LANES, 3_000_000, 40,
    )[0]


def weight_first(sc, fields, dz, dz_p, sums):
    def kernel(sc_ref, field, dz_ref, dz_p_ref, sums_ref, out, turned, padded, sems):
        zone = sc_ref[1]
        load = pltpu.make_async_copy(dz_ref, inner(padded), sems.at[0])
        load.start()
        blank_edges(padded)
        lane = pl.multiple_of(128 * (zone >> 1), 128)
        at = pl.multiple_of(64 * (zone & 1), 64)
        for phase in range(4):
            chosen = field[phase // 2, phase % 2, 1:10, 1:10, :, pl.ds(lane, 128)]
            turned[phase] = chosen.reshape(1296, 128).T
        load.wait()
        for tap in range(10):
            if tap < 9:
                a, b = divmod(tap, 3)
                left = turned[2 * ((a + 1) % 2) + (b + 1) % 2, pl.ds(at, 64)]
                row_at, col_at = 2 if a == 0 else 1, 2 if b == 0 else 1
                right = padded[row_at : row_at + 9, col_at : col_at + 9].reshape(1296, LANES)
            else:
                left = turned[0, pl.ds(at, 64)]
                right = dz_p_ref[...].reshape(1296, LANES)
            out[64 * tap : 64 * tap + 64] = dot(left, right).astype(bf16)
        out[640:656] = pack_vectors([sums_ref[0:1], sums_ref[2:3], sums_ref[1:2], sums_ref[3:4]])

    scratch = [
        pltpu.VMEM((4, 128, 1296), bf16), pltpu.VMEM((11, 11, 16, LANES), bf16),
        pltpu.SemaphoreType.DMA((1,)),
    ]
    return call(
        kernel, "weight_first", (sc, fields, dz, dz_p, sums), "svavv", [struct((656, LANES))], "v",
        scratch, 2 * 1296 * 640 * LANES, 3_000_000, 40,
    )[0]


def image_back(own, other, own_p, other_p, w_own, w_other):
    def kernel(own_ref, oth_ref, own_p_ref, oth_p_ref, w_own_ref, w_oth_ref, out):
        row = lax.broadcasted_iota(jnp.int32, (192, 192), 0)
        col = lax.broadcasted_iota(jnp.int32, (192, 192), 1)
        pixel = jnp.where(row >= 96, row - 96, row)
        line = (pixel * 57) >> 9
        across = pixel - 9 * line
        shifted = {}
        for down in range(2):
            for right in range(2):
                if down + right == 0:
                    shifted[0, 0] = (
                        own_ref[...].reshape(192, LANES),
                        oth_ref[...].reshape(192, LANES),
                    )
                    continue
                fits = (pixel < 81) & (line + down < 9) & (across + right < 9)
                move = jnp.where(fits & (col == row + 9 * down + right), 1.0, 0.0).astype(bf16)
                shifted[down, right] = tuple(
                    dot(move, ref[...].reshape(192, LANES)).astype(bf16)
                    for ref in (own_ref, oth_ref)
                )
        phases = [jnp.zeros((192, LANES), f32) for _ in range(4)]
        for a in range(3):
            for b in range(3):
                at = 2 * ((a + 1) % 2) + (b + 1) % 2
                left = shifted[1 if a == 0 else 0, 1 if b == 0 else 0]
                rows = slice(LANES * (3 * a + b), LANES * (3 * a + b + 1))
                phases[at] = phases[at] + dot_t(left[0], w_own_ref[rows])
                phases[at] = phases[at] + dot_t(left[1], w_oth_ref[rows])
        phases[0] = phases[0] + dot_t(own_p_ref[...].reshape(192, LANES), w_own_ref[2304:2560])
        phases[0] = phases[0] + dot_t(oth_p_ref[...].reshape(192, LANES), w_oth_ref[2304:2560])
        joined = jnp.concatenate([phase.astype(bf16) for phase in phases], axis=0)
        out_row = lax.broadcasted_iota(jnp.int32, (336, 768), 0)
        in_row = lax.broadcasted_iota(jnp.int32, (336, 768), 1)
        line = (out_row * 3641) >> 16
        across = out_row - 18 * line
        source = (2 * (line & 1) + (across & 1)) * 192 + 9 * (line >> 1) + (across >> 1)
        for image in range(2):
            spread = jnp.where(
                (in_row == source + 96 * image) & (out_row < 324), 1.0, 0.0
            ).astype(bf16)
            out[image] = dot(spread, joined).astype(bf16)

    return call(
        kernel, "image_back", (own, other, own_p, other_p, w_own, w_other), "vvvvvv",
        [struct((2, 336, LANES))], "v", [], 2 * 192 * 2560 * 512 + 4 * 336 * 768 * 256, 4_000_000, 40,
    )[0]


def add_into(out, rows, one, two, vector_rows):
    for at in range(0, rows, 64):
        span = slice(at, at + 64)
        out[span] = (one[span].astype(f32) + two[span].astype(f32)).astype(bf16)
    pairs = zip(unpack_vectors(one[rows : rows + 16]), unpack_vectors(two[rows : rows + 16]))
    out[vector_rows : vector_rows + 16] = pack_vectors([left + right for left, right in pairs])


def add_pieces(part, one, two):
    rows = one.shape[0] - 16

    def kernel(one_ref, two_ref, out):
        add_into(out, rows, one_ref, two_ref, rows)

    return call(
        kernel, f"add_{part}", (one, two), "vv", [struct(one.shape)], "v", [], 1, 1_000_000, 40
    )[0]


def own_piece(sc, sums, received):
    def kernel(sc_ref, *refs):
        out, held, sems = refs[8:]
        for part in range(4):
            rows = sums[part].shape[0] - 16

            @pl.when(sc_ref[0] == part)
            def _():
                copies = [
                    pltpu.make_async_copy(ref, held.at[at, 0 : rows + 16], sems.at[at])
                    for at, ref in enumerate((refs[part], refs[4 + part]))
                ]
                for copy in copies:
                    copy.start()
                for copy in copies:
                    copy.wait()
                add_into(out, rows, held.at[0], held.at[1], 1152)

    return call(
        kernel, "own_piece", (sc, *sums, *received), "s" + 8 * "a", [struct((1168, LANES))], "v",
        [pltpu.VMEM((2, 1168, LANES), bf16), pltpu.SemaphoreType.DMA((2,))], 1, 1_000_000, 40,
    )[0]


def lay_out(sc, gathered):
    def kernel(sc_ref, ref, out, vectors, held, wide, sems, out_sems):
        section, zone = sc_ref[0], sc_ref[1]
        loads = [
            pltpu.make_async_copy(ref.at[at // 2, at % 2], held.at[at // 2, at % 2], sems.at[at])
            for at in range(8)
        ]
        for load in loads:
            load.start()
        for load in loads:
            load.wait()
        for core in range(2):
            rows = unpack_vectors(held[zone, core, 1152:1168])
            vectors[:, LANES * core : LANES * core + LANES] = jnp.concatenate(rows, axis=0)
        for tap in range(9):
            slot = tap % 2
            leaving = pltpu.make_async_copy(
                wide.at[slot], out.at[512 * tap : 512 * tap + 512], out_sems.at[slot]
            )
            if tap >= 2:
                leaving.wait()

            @pl.when(section != 0)
            def _():
                for origin in range(4):
                    for core in range(2):
                        value = held[origin, core, 128 * tap : 128 * tap + 128].astype(f32)
                        wide[slot, 128 * origin : 128 * origin + 128, LANES * core : LANES * core + LANES] = value

            @pl.when(section == 0)
            def _():
                for half in range(2):
                    start = 64 * (2 * tap + half)
                    for origin in range(4):
                        row = 256 * half + 64 * origin
                        for core in range(2):
                            value = jnp.zeros((64, LANES), f32)
                            if start < 640:
                                value = held[origin, core, start : start + 64].astype(f32)
                            wide[slot, row : row + 64, LANES * core : LANES * core + LANES] = value

            leaving.start()
        for slot in range(2):
            pltpu.make_async_copy(wide.at[slot], out.at[0:512], out_sems.at[slot]).wait()

    return call(
        kernel, "lay_out", (sc, gathered), "sh", [struct((4608, 512), f32), struct((4, 512), f32)], "hv",
        [
            pltpu.VMEM((4, 2, 1168, LANES), bf16), pltpu.VMEM((2, 512, 512), f32),
            pltpu.SemaphoreType.DMA((8,)), pltpu.SemaphoreType.DMA((2,)),
        ],
        0, 15_000_000, 60,
    )


def half_of(value, half):
    return lax.dynamic_slice_in_dim(value, LANES * half, LANES, axis=value.ndim - 1)


def join_halves(own, other, core):
    first = jnp.where(core == 0, own, other)
    second = jnp.where(core == 0, other, own)
    return jnp.concatenate([first, second], axis=-1)


def chip_body(images, res_ids, weights, bn_gain, bn_bias, cotangent):
    section = lax.axis_index("section")
    position = lax.axis_index("dp")
    zone, core = position // 2, position % 2
    sc = jnp.stack([section, zone, core, core]).astype(jnp.int32)

    level = lax.dynamic_index_in_dim(res_ids, section, 0, keepdims=False)
    side_own = (9 - 2 * (2 - level)).astype(f32)
    tail = jnp.broadcast_to(side_own[:, None, None], (2, 12, 256)).astype(bf16)
    image_own = jnp.concatenate([images[0].reshape(2, 324, 256), tail], axis=1)
    pieces = lax.all_gather(image_own, "dp")

    first_a, first_b, own_a, own_b = split_weights(
        sc, weights[0], jnp.concatenate([bn_gain[0], bn_bias[0]], axis=0)
    )
    first_x1 = flip(first_a, "section", 1, lambda i: i == 0)
    first_y1 = flip(first_b, "section", 2, lambda i: i == 0)
    first_x2 = flip(first_b, "section", 1, lambda i: i == 0)
    first_y2 = flip(first_a, "section", 2, lambda i: i == 0)
    x_1 = flip(own_a, "section", 1, lambda i: i != 0)
    y_1 = flip(own_b, "section", 2, lambda i: i != 0)
    first_x3 = flip(first_y1, "section", 1, lambda i: i == 2)
    first_y3 = flip(first_x1, "section", 2, lambda i: i == 1)
    first_messages = [first_a, first_b, first_x1, first_y1, first_x2, first_y2, first_x3, first_y3]

    cot_own = jnp.pad(cotangent[0].reshape(2, 81, 512), ((0, 0), (0, 15), (0, 0)))
    cot_pieces = lax.all_gather(cot_own, "dp")
    def after(value, *tokens):
        return lax.optimization_barrier((value, *tokens))[0]

    fields, side = prepare_images(after(pieces, x_1, y_1))
    sends_own = (section == 1) | (section == 2)
    for_x = jnp.where(sends_own, own_b, y_1)
    for_y = jnp.where(sends_own, own_a, x_1)
    x_2 = flip(for_x, "section", 1)
    y_2 = flip(for_y, "section", 2)
    hidden_one, short_one, zhat_0, zhat_p, stats_0, w_first = stage_first(
        sc, side, after(fields, for_x, for_y), first_messages
    )
    hidden_one_other = flip(hidden_one, "dp", 1)
    w_first_other = flip(w_first, "dp", 1)
    for_x, for_y = after((for_x, for_y), stats_0)
    x_3 = flip(jnp.where(section == 3, own_b, y_1), "section", 1, lambda i: i in (1, 3))
    y_3 = flip(jnp.where(section == 3, own_a, x_1), "section", 2, lambda i: i in (2, 3))
    messages = [own_a, own_b, x_1, y_1, x_2, y_2]
    block_one, zhat_1, stats_1, keep_1, send_1 = stage_rest(
        1, sc, side, hidden_one, hidden_one_other, messages, short_one, after=(cot_pieces,)
    )
    block_one_other = flip(block_one, "dp", 1)
    other_1 = flip(send_1, "dp", 1)
    cot = prepare_cotangent(sc, after(cot_pieces, stats_1))
    hidden_two, zhat_2, stats_2, keep_2, send_2 = stage_rest(
        2, sc, side, block_one, block_one_other, messages, None, after=(cot, x_3, y_3)
    )
    hidden_two_other = flip(hidden_two, "dp", 1)
    other_2 = flip(send_2, "dp", 1)
    messages = [own_a, own_b, x_1, y_1, x_3, y_3]
    dz_3, passed, out, sums_3, keep_3, send_3 = stage_rest(
        3, sc, side, hidden_two, hidden_two_other, messages, block_one, cot
    )
    other_3 = flip(send_3, "dp", 1)
    dz_3_other = flip(dz_3, "dp", 1)

    def to_pair(part, piece):
        return flip(piece, "section", 2, lambda i: i ^ 2 in (part, part ^ 1))

    def to_owner(part, piece):
        return flip(piece, "section", 1, lambda i: i ^ 1 == part)

    piece_3 = weight_rest(3, sc, hidden_two, hidden_two_other, dz_3, sums_3)
    came_3 = to_pair(3, piece_3)
    dz_2, sums_2 = stage_back(
        2, sc, side, after(dz_3, piece_3), dz_3_other, keep_3, other_3, zhat_2, stats_2
    )
    dz_2_other = flip(dz_2, "dp", 1)
    piece_2 = weight_rest(2, sc, block_one, block_one_other, dz_2, sums_2)
    came_2 = to_pair(2, piece_2)
    dz_1, sums_1, short_grad = stage_back(
        1, sc, side, after(dz_2, piece_2), dz_2_other, keep_2, other_2, zhat_1, stats_1, short_one,
        passed,
    )
    dz_1_other = flip(dz_1, "dp", 1)
    piece_1 = weight_rest(1, sc, hidden_one, hidden_one_other, dz_1, sums_1)
    came_1 = to_pair(1, piece_1)
    sum_3 = add_pieces(3, after(piece_3, piece_1), came_3)
    last_3 = to_owner(3, sum_3)
    dz_0, sums_0, dz_p = stage_back(
        0, sc, side, after(dz_1, sum_3), dz_1_other, keep_1, other_1, zhat_0, stats_0,
        proj=(short_grad, zhat_p),
    )
    piece_0 = weight_first(sc, fields, dz_0, dz_p, sums_0)
    came_0 = to_pair(0, piece_0)
    sum_2 = add_pieces(2, after(piece_2, piece_0), came_2)
    last_2 = to_owner(2, sum_2)
    sum_1 = add_pieces(1, after(piece_1, sum_2), came_1)
    last_1 = to_owner(1, sum_1)
    pick_0, pick_p, pick_out = pick_images(sc, *after((dz_0, dz_p, out), sum_1))
    sum_0 = add_pieces(0, after(piece_0, pick_out), came_0)
    last_0 = to_owner(0, sum_0)
    total = own_piece(sc, (sum_0, sum_1, sum_2, sum_3), (last_0, last_1, last_2, last_3))
    gathered = lax.all_gather(total, "dp").reshape(4, 2, 1168, LANES)
    weight_grad, vectors = lay_out(sc, gathered)

    pick_out_other = flip(pick_out[2:4], "dp", 1)
    block_output = join_halves(pick_out[0:2, 0:81], pick_out_other[:, 0:81], core)
    pick_0_other = flip(pick_0[2:4], "dp", 1)
    pick_p_other = flip(pick_p[2:4], "dp", 1)
    image_grad = image_back(
        pick_0[0:2], pick_0_other, pick_p[0:2], pick_p_other, w_first, w_first_other
    )
    rows = jnp.arange(18, dtype=jnp.int32)
    inner_rows = (rows < 2 * (9 - 2 * (2 - level))[:, None]).astype(bf16)
    mask_in = inner_rows[:, :, None] * inner_rows[:, None, :]
    image_grad = image_grad[:, 0:324].reshape(2, 18, 18, 256) * mask_in[..., None]
    return (
        block_output.reshape(1, 2, 9, 9, 512),
        image_grad[None],
        weight_grad[None],
        vectors[None, 0:2],
        vectors[None, 2:4],
    )


def solution(mesh):
    placed = (
        P("section", "dp", None, None, None),
        P(None, "dp"),
        P("section", None, None),
        P("section", None, None),
        P("section", None, None),
        P("section", "dp", None, None, None),
    )
    on_chip = mesh.shape["section"] == 4 and mesh.shape["dp"] == 8
    return jax.shard_map(
        chip_body if on_chip else pipeline_body,
        mesh=mesh,
        in_specs=placed,
        out_specs=(
            P("section", "dp", None, None, None),
            P("section", "dp", None, None, None),
            P("section", None, None),
            P("section", None, None),
            P("section", None, None),
        ),
        check_vma=False,
    )
```

```python
import jax
import jax.numpy as jnp
from jax import lax
from jax.experimental import pallas as pl
from jax.experimental.pallas import tpu as pltpu
from jax.sharding import PartitionSpec as P

epsilon = 1e-05


def passed_along(value, axis, steps):
    count = lax.axis_size(axis)
    leading, last = (max(0, -steps), min(count, count - steps))
    return lax.ppermute(value, axis, [(source, source + steps) for source in range(leading, last)])


def regions(levels, half_side):
    inner_side = half_side - 2 * (2 - levels)
    small_rows = jnp.arange(half_side, dtype=jnp.int32)
    large_rows = jnp.arange(2 * half_side, dtype=jnp.int32)
    inner_mask = (small_rows < inner_side[..., None]).astype(jnp.float32)
    outer_mask = (large_rows < 2 * inner_side[..., None]).astype(jnp.float32)
    return (
        outer_mask[..., :, None] * outer_mask[..., None, :],
        inner_mask[..., :, None] * inner_mask[..., None, :],
    )


def patches(field_in, stride, half_side):
    padded = jnp.pad(field_in, ((0, 0), (1, 1), (1, 1), (0, 0)))
    pieces = [
        padded[
            :,
            row_at : row_at + stride * half_side : stride,
            col_at : col_at + stride * half_side : stride,
            :,
        ]
        for row_at in range(3)
        for col_at in range(3)
    ]
    joined = jnp.concatenate(pieces, axis=-1)
    return joined.reshape(-1, joined.shape[-1])


def contract_rows(left_side, right_side):
    return lax.dot_general(
        left_side, right_side, (((0,), (0,)), ((), ())), preferred_element_type=jnp.float32
    )


def contract_cols(left_side, right_side):
    return lax.dot_general(
        left_side, right_side, (((1,), (1,)), ((), ())), preferred_element_type=jnp.float32
    )


def silu_slope(values):
    sigmoid = jax.nn.sigmoid(values)
    return sigmoid * (1.0 + values * (1.0 - sigmoid))


def spread_taps(tap_grads, image_count, half_side, channels):
    tap_grid = tap_grads.reshape(image_count, half_side, half_side, 9, channels)
    empty_phase = jnp.zeros((image_count, half_side + 1, half_side + 1, channels), jnp.float32)
    phases = [[empty_phase, empty_phase], [empty_phase, empty_phase]]
    for row_at in range(3):
        for col_at in range(3):
            tap_piece = tap_grid[:, :, :, 3 * row_at + col_at, :]
            top_pad = 1 if row_at == 2 else 0
            left_pad = 1 if col_at == 2 else 0
            placed = jnp.pad(
                tap_piece, ((0, 0), (top_pad, 1 - top_pad), (left_pad, 1 - left_pad), (0, 0))
            )
            phases[row_at % 2][col_at % 2] = phases[row_at % 2][col_at % 2] + placed
    row_phases = [jnp.stack([phases[parity][0], phases[parity][1]], axis=3) for parity in range(2)]
    alternated = jnp.stack(row_phases, axis=2).reshape(
        image_count, 2 * half_side + 2, 2 * half_side + 2, channels
    )
    return alternated[:, 1 : 2 * half_side + 1, 1 : 2 * half_side + 1, :]


def keep_slot(buffer_all, new_value, slot_at, keep_flag):
    current = lax.dynamic_index_in_dim(buffer_all, slot_at, 0, keepdims=False)
    return lax.dynamic_update_index_in_dim(
        buffer_all, jnp.where(keep_flag, new_value, current), slot_at, 0
    )


def pipeline_body(images, res_ids, weights, bn_gain, bn_bias, cotangent):
    sections = lax.axis_size("section")
    last_section = sections - 1
    position = lax.axis_index("section")
    micro_count = res_ids.shape[0]
    image_count = images.shape[1]
    half_side = cotangent.shape[2]
    channels = weights.shape[2]
    in_channels = images.shape[4]
    pixel_rows = image_count * half_side * half_side
    taps_in = 9 * in_channels
    matrix = weights[0]
    gain_rows = bn_gain[0]
    bias_rows = bn_bias[0]
    is_first = position == 0
    adds_short = (position == 1) | (position == 3)
    passes_short = position == 2
    makes_short = position == 1
    back_matrix = jnp.transpose(matrix.reshape(9, channels, channels)[::-1], (0, 2, 1)).reshape(
        9 * channels, channels
    )
    mask_in_all, mask_out_all = regions(res_ids, half_side)
    act_shape = (image_count, half_side, half_side, channels)
    zero_pixels = jnp.zeros((pixel_rows, channels), jnp.float32)
    zero_input = jnp.zeros((image_count, 2 * half_side, 2 * half_side, in_channels), jnp.float32)
    zero_weight = jnp.zeros((9 * channels, channels), jnp.float32)
    own_images = images[0]
    gathered = [own_images]
    for source in range(1, micro_count):
        gathered.append(passed_along(own_images, "section", -source))
    section_inputs = jnp.stack(gathered)
    own_cot = cotangent[0]
    arrived = []
    for source in range(micro_count):
        if source == last_section:
            arrived.append(own_cot)
        else:
            arrived.append(passed_along(own_cot, "section", last_section - source))
    cot_all = jnp.stack(arrived)

    def conv_first(prev_act, first_in):
        columns = patches(first_in, 2, half_side)
        main_out = jnp.dot(columns, matrix[:taps_in], preferred_element_type=jnp.float32)
        proj_out = jnp.dot(
            columns[:, 4 * in_channels : 5 * in_channels],
            matrix[taps_in : taps_in + in_channels],
            preferred_element_type=jnp.float32,
        )
        return jnp.stack([main_out, proj_out])

    def conv_rest(prev_act, first_in):
        columns = patches(prev_act, 1, half_side)
        return jnp.stack(
            [jnp.dot(columns, matrix, preferred_element_type=jnp.float32), zero_pixels]
        )

    def conv_spare(prev_act, first_in):
        return jnp.stack([zero_pixels, zero_pixels])

    def back_first(grad_conv, prev_act, first_in):
        columns = patches(first_in, 2, half_side)
        centre = columns[:, 4 * in_channels : 5 * in_channels]
        main_grad = contract_rows(columns, grad_conv[0])
        proj_grad = contract_rows(centre, grad_conv[1])
        filler = jnp.zeros((9 * channels - taps_in - in_channels, channels), jnp.float32)
        weight_now = jnp.concatenate([main_grad, proj_grad, filler], axis=0)
        tap_grads = contract_cols(grad_conv[0], matrix[:taps_in])
        centre_grad = contract_cols(grad_conv[1], matrix[taps_in : taps_in + in_channels])
        tap_grads = tap_grads + jnp.pad(centre_grad, ((0, 0), (4 * in_channels, 4 * in_channels)))
        return (
            weight_now,
            zero_pixels,
            spread_taps(tap_grads, image_count, half_side, in_channels),
        )

    def back_rest(grad_conv, prev_act, first_in):
        columns = patches(prev_act, 1, half_side)
        weight_now = contract_rows(columns, grad_conv[0])
        grad_image = grad_conv[0].reshape(act_shape)
        prev_grad = jnp.dot(
            patches(grad_image, 1, half_side), back_matrix, preferred_element_type=jnp.float32
        )
        return (weight_now, prev_grad, zero_input)

    def back_spare(grad_conv, prev_act, first_in):
        return (zero_weight, zero_pixels, zero_input)

    def finish(conv_out, mean_rows, scale_rows, flat_mask, short_in):
        normed = (conv_out - mean_rows[:, None, :]) * scale_rows[:, None, :] * gain_rows[
            :, None, :
        ] + bias_rows[:, None, :]
        pre_act = normed[0] + jnp.where(adds_short, short_in, 0.0)
        activated = jax.nn.silu(pre_act) * flat_mask[:, None]
        proj_short = normed[1] * flat_mask[:, None]
        short_out = jnp.where(is_first, proj_short, jnp.where(makes_short, activated, short_in))
        return (pre_act, activated, short_out)

    empty_act = jnp.zeros(act_shape, jnp.bfloat16)
    recv_act = empty_act
    recv_short = empty_act
    saved_act = jnp.zeros((micro_count,) + act_shape, jnp.bfloat16)
    saved_short = saved_act
    saved_final = saved_act
    saved_mean = jnp.zeros((micro_count, 2, channels), jnp.float32)
    saved_scale = saved_mean
    saved_total = jnp.zeros((micro_count,), jnp.float32)
    sweep_len = micro_count + last_section
    for tick_at in range(sweep_len):
        slot_raw = tick_at - position
        is_valid = (slot_raw >= 0) & (slot_raw < micro_count)
        slot_at = jnp.clip(slot_raw, 0, micro_count - 1)
        flat_mask = mask_out_all[slot_at].reshape(-1) * is_valid.astype(jnp.float32)
        first_in = section_inputs[slot_at] * mask_in_all[slot_at][..., None].astype(jnp.bfloat16)
        branch = jnp.where(is_valid, jnp.where(is_first, 0, 1), 2).astype(jnp.int32)
        conv_out = lax.switch(branch, [conv_first, conv_rest, conv_spare], recv_act, first_in)
        local_total = jnp.sum(flat_mask)
        weighted = conv_out * flat_mask[None, :, None]
        grand_total, sum_rows = lax.psum((local_total, jnp.sum(weighted, axis=1)), "dp")
        grand_total = jnp.maximum(grand_total, 1.0)
        statistics_mean_rows = sum_rows / grand_total
        centred = conv_out - statistics_mean_rows[:, None, :]
        variance = (
            lax.psum(jnp.sum(centred * centred * flat_mask[None, :, None], axis=1), "dp")
            / grand_total
        )
        grand_total, mean_rows, scale_rows = (
            grand_total,
            statistics_mean_rows,
            lax.rsqrt(variance + epsilon),
        )
        short_in = recv_short.reshape(pixel_rows, channels).astype(jnp.float32)
        pre_act, activated, short_out = finish(conv_out, mean_rows, scale_rows, flat_mask, short_in)
        act_low = activated.astype(jnp.bfloat16).reshape(act_shape)
        short_low = short_out.astype(jnp.bfloat16).reshape(act_shape)
        saved_act = keep_slot(saved_act, recv_act, slot_at, is_valid)
        saved_short = keep_slot(saved_short, recv_short, slot_at, is_valid)
        saved_mean = keep_slot(saved_mean, mean_rows, slot_at, is_valid)
        saved_scale = keep_slot(saved_scale, scale_rows, slot_at, is_valid)
        saved_total = keep_slot(saved_total, grand_total, slot_at, is_valid)
        saved_final = keep_slot(
            saved_final, act_low, slot_at, is_valid & (position == last_section)
        )
        if tick_at + 1 < sweep_len:
            recv_act, recv_short = passed_along((act_low, short_low), "section", 1)
    grad_act = empty_act
    grad_short = empty_act
    weight_acc = zero_weight
    gain_acc = jnp.zeros((2, channels), jnp.float32)
    bias_acc = gain_acc
    saved_dx = jnp.zeros(
        (micro_count, image_count, 2 * half_side, 2 * half_side, in_channels), jnp.bfloat16
    )
    for tick_at in range(sweep_len):
        slot_raw = tick_at - (last_section - position)
        is_valid = (slot_raw >= 0) & (slot_raw < micro_count)
        slot_at = jnp.clip(slot_raw, 0, micro_count - 1)
        flat_mask = mask_out_all[slot_at].reshape(-1) * is_valid.astype(jnp.float32)
        first_in = section_inputs[slot_at] * mask_in_all[slot_at][..., None].astype(jnp.bfloat16)
        branch = jnp.where(is_valid, jnp.where(is_first, 0, 1), 2).astype(jnp.int32)
        prev_act = saved_act[slot_at]
        conv_out = lax.switch(branch, [conv_first, conv_rest, conv_spare], prev_act, first_in)
        mean_rows = saved_mean[slot_at]
        scale_rows = saved_scale[slot_at]
        valid_total = saved_total[slot_at]
        short_in = saved_short[slot_at].reshape(pixel_rows, channels).astype(jnp.float32)
        pre_act, activated, short_out = finish(conv_out, mean_rows, scale_rows, flat_mask, short_in)
        from_act = (
            jnp.where(position == last_section, cot_all[slot_at], grad_act)
            .reshape(pixel_rows, channels)
            .astype(jnp.float32)
        )
        from_short = grad_short.reshape(pixel_rows, channels).astype(jnp.float32)
        slope = silu_slope(pre_act) * flat_mask[:, None]
        grad_pre = (from_act + jnp.where(adds_short, from_short, 0.0)) * slope
        grad_proj = jnp.where(is_first, from_short * flat_mask[:, None], 0.0)
        grad_normed = jnp.stack([grad_pre, grad_proj])
        normalized = (conv_out - mean_rows[:, None, :]) * scale_rows[:, None, :]
        bias_now, gain_now = lax.psum(
            (jnp.sum(grad_normed, axis=1), jnp.sum(grad_normed * normalized, axis=1)), "dp"
        )
        bias_acc = bias_acc + bias_now
        gain_acc = gain_acc + gain_now
        grad_conv = (
            flat_mask[None, :, None]
            * gain_rows[:, None, :]
            * scale_rows[:, None, :]
            * (
                grad_normed
                - (bias_now[:, None, :] + normalized * gain_now[:, None, :]) / valid_total
            )
        )
        grad_conv = grad_conv.astype(jnp.bfloat16)
        weight_now, prev_grad, input_grad = lax.switch(
            branch, [back_first, back_rest, back_spare], grad_conv, prev_act, first_in
        )
        weight_acc = weight_acc + weight_now
        masked_input = (input_grad * mask_in_all[slot_at][..., None]).astype(jnp.bfloat16)
        saved_dx = keep_slot(saved_dx, masked_input, slot_at, is_valid & is_first)
        send_act = (
            (prev_grad + jnp.where(passes_short, from_short, 0.0))
            .astype(jnp.bfloat16)
            .reshape(act_shape)
        )
        send_short = jnp.where(adds_short, grad_pre, 0.0).astype(jnp.bfloat16).reshape(act_shape)
        if tick_at + 1 < sweep_len:
            grad_act, grad_short = passed_along((send_act, send_short), "section", -1)
    weight_total = lax.psum(weight_acc, "dp")
    result = saved_final[last_section]
    for source in range(last_section):
        arrived_piece = passed_along(saved_final[source], "section", source - last_section)
        result = jnp.where(position == source, arrived_piece, result)
    grad_result = saved_dx[0]
    for source in range(1, micro_count):
        arrived_piece = passed_along(saved_dx[source], "section", source)
        grad_result = jnp.where(position == source, arrived_piece, grad_result)
    return (result[None], grad_result[None], weight_total[None], gain_acc[None], bias_acc[None])


f32, bf16 = jnp.float32, jnp.bfloat16
LANES = 256
GRID = (9, 9, 16, LANES)


def flip(value, axis, mask, senders=None):
    count = lax.axis_size(axis)
    pairs = [(i, i ^ mask) for i in range(count) if senders is None or senders(i)]
    return lax.ppermute(value, axis, pairs)


def struct(shape, kind=bf16):
    return jax.ShapeDtypeStruct(shape, kind)


def call(kernel, name, operands, places, outs, out_places, scratch, flops, moved, limit):
    spaces = {"s": pltpu.SMEM, "v": pltpu.VMEM, "a": pl.ANY, "h": pltpu.HBM}
    operands = [
        pltpu.with_memory_space_constraint(one, pltpu.HBM) if place == "h" else one
        for one, place in zip(operands, places)
    ]
    outs = [
        spaces[place](one.shape, one.dtype) if place in "hv" else one
        for one, place in zip(outs, out_places)
    ]
    return pl.pallas_call(
        kernel,
        out_shape=outs,
        in_specs=[pl.BlockSpec(memory_space=spaces[place]) for place in places],
        out_specs=[pl.BlockSpec(memory_space=spaces[place]) for place in out_places],
        scratch_shapes=scratch,
        name=name,
        compiler_params=pltpu.CompilerParams(vmem_limit_bytes=limit * 2**20),
        cost_estimate=pl.CostEstimate(flops=1, bytes_accessed=1, transcendentals=0),
    )(*operands)


def dot(left, right):
    return jnp.dot(left, right, preferred_element_type=f32)


def dot_t(left, right):
    return lax.dot_general(left, right, (((1,), (1,)), ((), ())), preferred_element_type=f32)


def col_sum(values):
    return jnp.sum(values, axis=0, keepdims=True)


def blank_edges(dst):
    blank = jnp.zeros((11, 16, LANES), bf16)
    dst[0] = blank
    dst[10] = blank
    dst[:, 0] = blank
    dst[:, 10] = blank


def inner(dst):
    return dst.at[1:10, 1:10]


class Inside:
    def __init__(self, side):
        self.count = col_sum(side * side)
        self.masks = (None, side > 6.0, side > 8.0)

    def keep(self, ring, values):
        mask = self.masks[self.level(ring)]
        return values if mask is None else jnp.where(mask, values, 0.0)

    @staticmethod
    def level(ring):
        return 0 if ring < 5 else 1 if ring < 7 else 2

    def total(self, values_at):
        sums = [None, None, None]
        for row in range(9):
            for col in range(9):
                at = self.level(max(row, col))
                value = values_at(row, col)
                sums[at] = value if sums[at] is None else sums[at] + value
        return col_sum(sums[0] + self.keep(5, sums[1]) + self.keep(7, sums[2]))


def norm_stats(acc, inside):
    mean = inside.total(lambda row, col: acc[row, col]) / inside.count

    def squared(row, col):
        centred = acc[row, col] - mean
        return centred * centred

    return mean, lax.rsqrt(inside.total(squared) / inside.count + epsilon)


def sigmoid_of(values):
    return 0.5 * jnp.tanh(0.5 * values) + 0.5


def split_three(row):
    high = row.astype(bf16)
    rest = row - high.astype(f32)
    middle = rest.astype(bf16)
    low = (rest - middle.astype(f32)).astype(bf16)
    return [high, middle, low]


def pack_vectors(rows):
    pieces = [one.astype(f32) for row in rows for one in split_three(row)]
    pieces.append(jnp.zeros((16 - len(pieces), LANES), f32))
    return jnp.concatenate(pieces, axis=0).astype(bf16)


def unpack_vectors(block):
    wide = block.astype(f32)
    return [wide[3 * at : 3 * at + 1] + wide[3 * at + 1 : 3 * at + 2] + wide[3 * at + 2 : 3 * at + 3] for at in range(4)]


def pack_rows(ref, rows):
    ref[...] = jnp.concatenate(rows + [jnp.zeros((8 - len(rows), LANES), f32)], axis=0)


def turn_matrix(image_of_row):
    out_row = lax.broadcasted_iota(jnp.int32, (256, 256), 0)
    in_row = lax.broadcasted_iota(jnp.int32, (256, 256), 1)
    pixel_same = (out_row >> 4) == (in_row & 15)
    return jnp.where(pixel_same & ((out_row & 15) == image_of_row(in_row)), 1.0, 0.0).astype(bf16)


def split_weights(sc, matrix, vectors):
    def kernel(sc_ref, matrix_ref, vec_ref, for_x, for_y, sems):
        lane = pl.multiple_of(LANES * sc_ref[2], LANES)
        chosen = matrix_ref.at[:, pl.ds(lane, LANES)]

        def copies(target, first, at):
            return [
                pltpu.make_async_copy(
                    chosen.at[first + 640 * cut : first + 640 * cut + 640],
                    target.at[16 + 640 * cut : 656 + 640 * cut],
                    sems.at[at + cut],
                )
                for cut in range(4)
            ]

        along_x = copies(for_x, 0, 0)
        for copy in along_x:
            copy.start()
        small = pack_vectors([vec_ref[at : at + 1, pl.ds(lane, LANES)] for at in range(4)])
        for_x[0:16] = small
        for_y[0:16] = small
        for first, here in ((0, sc_ref[0] == 0), (2048, sc_ref[0] != 0)):

            @pl.when(here)
            def _():
                along_y = copies(for_y, first, 4)
                for copy in along_y:
                    copy.start()
                for copy in along_y:
                    copy.wait()

        for copy in along_x:
            copy.wait()

    return call(
        kernel, "split_weights", (sc, matrix, vectors), "shv", [struct((2576, LANES))] * 2, "vv",
        [pltpu.SemaphoreType.DMA((8,))], 0, 14_000_000, 28,
    )


def relay_weights(name, is_own, operands, first=None):
    def kernel(sc_ref, own_x, own_y, x_1, y_1, for_x, for_y, *refs):
        sems = refs[-1]
        chosen = is_own(sc_ref[0])
        copies = []
        for x_from, y_from, here in ((own_x, own_y, chosen), (x_1, y_1, jnp.logical_not(chosen))):
            copies = [
                pltpu.make_async_copy(y_from.at[272:1424], for_x.at[0:1152], sems.at[0]),
                pltpu.make_async_copy(y_from.at[1424:2576], for_x.at[1152:2304], sems.at[1]),
                pltpu.make_async_copy(x_from.at[0:1168], for_y.at[0:1168], sems.at[2]),
                pltpu.make_async_copy(x_from.at[1168:2320], for_y.at[1168:2320], sems.at[3]),
            ]

            @pl.when(here)
            def _():
                for copy in copies:
                    copy.start()

        if len(refs) > 1:
            top, bottom = refs[:2]
            more = [
                pltpu.make_async_copy(y_1.at[0:1296], top, sems.at[4]),
                pltpu.make_async_copy(x_1.at[1296:2576], bottom, sems.at[5]),
            ]
            for copy in more:
                copy.start()
            copies = copies + more
        for copy in copies:
            copy.wait()

    outs = [struct((2304, LANES)), struct((2320, LANES))]
    if first:
        outs += [struct((1296, LANES)), struct((1280, LANES))]
    return call(
        kernel, name, operands, "saaaa", outs, len(outs) * "v", [pltpu.SemaphoreType.DMA((6,))],
        0, 14_000_000, 28,
    )


def prepare_images(sc, pieces):
    def kernel(sc_ref, *refs):
        piece_refs, (out, side_out, held, sems) = refs[:8], refs[8:]
        core = sc_ref[2]
        copies = [
            pltpu.make_async_copy(ref, held.at[2 * at : 2 * at + 2], sems.at[at])
            for at, ref in enumerate(piece_refs)
        ]
        for copy in copies:
            copy.start()
        turn = turn_matrix(lambda r: ((r >> 4) + 8 * core) & 15)
        out[:, :, 0] = jnp.zeros((2, 2, 10, 16, LANES), bf16)
        out[:, :, :, 0] = jnp.zeros((2, 2, 10, 16, LANES), bf16)
        for copy in copies:
            copy.wait()

        def block(at):
            source = held[:, 16 * at : 16 * at + 16].reshape(256, LANES)
            return dot(turn, source).reshape(16, 16, LANES)

        last = block(20)
        side = last[4]
        side_out[...] = side
        masks = (None, 2.0 * side > 13.0, 2.0 * side > 17.0)
        for at in range(21):
            turned = last if at == 20 else block(at)
            for step in range(16 if at < 20 else 4):
                row, col = divmod(16 * at + step, 18)
                mask = masks[Inside.level(max(row, col) // 2)]
                kept = turned[step] if mask is None else jnp.where(mask, turned[step], 0.0)
                out[row % 2, col % 2, 1 + row // 2, 1 + col // 2] = kept.astype(bf16)

    outs = [struct((2, 2, 10, 10, 16, LANES)), struct((16, LANES), f32)]
    scratch = [pltpu.VMEM((16, 336, LANES), bf16), pltpu.SemaphoreType.DMA((8,))]
    return call(
        kernel, "prepare_images", (sc, *pieces), "s" + 8 * "h", outs, "vv", scratch,
        21 * 2 * 256**3, 8_000_000, 28,
    )


def prepare_cotangent(sc, pieces):
    def kernel(sc_ref, *refs):
        piece_refs, (out, held, sems) = refs[:2], refs[2:]
        core = sc_ref[2]
        copies = [
            pltpu.make_async_copy(ref, held.at[2 * at : 2 * at + 2], sems.at[at])
            for at, ref in enumerate(piece_refs)
        ]
        for copy in copies:
            copy.start()
        turn = turn_matrix(
            lambda r: (((r >> 5) & 1) ^ core) * 8 + 2 * (r >> 6) + ((r >> 4) & 1)
        )
        for copy in copies:
            copy.wait()
        for at in range(6):
            source = held[:, :, :, 16 * at : 16 * at + 16].reshape(256, LANES)
            turned = dot(turn, source).astype(bf16).reshape(16, 16, LANES)
            for step in range(16 if at < 5 else 1):
                row, col = divmod(16 * at + step, 9)
                out[row, col] = turned[step]

    scratch = [pltpu.VMEM((4, 2, 2, 96, LANES), bf16), pltpu.SemaphoreType.DMA((4,))]
    return call(
        kernel, "prepare_cotangent", (sc, *pieces), "saa", [struct(GRID)], "v", scratch,
        6 * 2 * 256**3, 2_000_000, 28,
    )[0]


def load_chosen(section, table, dst, sem):
    for sections, ref, first in table:
        copy = pltpu.make_async_copy(ref.at[first : first + dst.shape[0]], dst, sem)
        chosen = section == sections[0]
        for other in sections[1:]:
            chosen = chosen | (section == other)
        pl.when(chosen)(copy.start)
    return copy


def stage_first(sc, side, fields, messages):
    def kernel(sc_ref, side_ref, field, own_x, x_1, y_1, top, bottom, hidden, short, zhat, zhat_p, stats, w_out, w, vec, acc, acc_p, short_now, sems, out_sems):
        section = sc_ref[0]
        whole = [((0,), own_x), ((1,), x_1), ((2,), y_1)]
        loads = []
        for at in range(10):
            entries = [(*entry, 16 + 256 * at) for entry in whole]
            entries.append(((3,), bottom, 256 * (at - 5)) if at >= 5 else ((3,), top, 16 + 256 * at))
            loads.append(load_chosen(section, entries, w.at[256 * at : 256 * at + 256], sems.at[at]))
        entries = [(*entry, 0) for entry in whole + [((3,), top)]]
        vec_load = load_chosen(section, entries, vec, sems.at[10])
        for chunk in range(3):
            total = jnp.zeros((432, LANES), f32)
            for a in range(3):
                for b in range(3):
                    row_at, col_at = 3 * chunk + (0 if a == 0 else 1), 0 if b == 0 else 1
                    left = field[(a + 1) % 2, (b + 1) % 2, row_at : row_at + 3, col_at : col_at + 9]
                    at = LANES * (3 * a + b)
                    if chunk == 0:
                        loads[3 * a + b].wait()
                    total = total + dot(left.reshape(432, LANES), w[at : at + LANES])
            if chunk == 0:
                loads[9].wait()
                outs = [pltpu.make_async_copy(w, w_out, out_sems.at[0])]
                outs[0].start()
            span = slice(3 * chunk, 3 * chunk + 3)
            acc[span] = total.reshape(3, 9, 16, LANES)
            centre = field[0, 0, 3 * chunk + 1 : 3 * chunk + 4, 1:10].reshape(432, LANES)
            acc_p[span] = dot(centre, w[2304:2560]).reshape(3, 9, 16, LANES)
            for at, (source, target) in enumerate(((acc, zhat), (acc_p, zhat_p))):
                outs.append(
                    pltpu.make_async_copy(
                        source.at[span], target.at[span], out_sems.at[1 + 3 * at + chunk]
                    )
                )
                outs[-1].start()
        inside = Inside(side_ref[...])
        mean, scale = norm_stats(acc, inside)
        mean_p, scale_p = norm_stats(acc_p, inside)
        vec_load.wait()
        gain, gain_p, bias, bias_p = unpack_vectors(vec[...])
        for row in range(9):
            for col in range(9):
                ring = max(row, col)
                pre = (acc[row, col] - mean) * scale * gain + bias
                hidden[row, col] = inside.keep(ring, pre * sigmoid_of(pre)).astype(bf16)
                normed = (acc_p[row, col] - mean_p) * scale_p
                short_now[row, col] = inside.keep(ring, normed * gain_p + bias_p).astype(bf16)
            outs.append(pltpu.make_async_copy(short_now.at[row], short.at[row], out_sems.at[7 + row]))
            outs[-1].start()
        pack_rows(stats, [scale, gain, bias, mean, scale_p, gain_p, mean_p])
        for copy in outs:
            copy.wait()

    outs = [
        struct(GRID), struct(GRID), struct(GRID, f32), struct(GRID, f32), struct((8, LANES), f32),
        struct((2560, LANES)),
    ]
    scratch = [
        pltpu.VMEM((2560, LANES), bf16), pltpu.VMEM((16, LANES), bf16), pltpu.VMEM(GRID, f32),
        pltpu.VMEM(GRID, f32), pltpu.VMEM(GRID, bf16), pltpu.SemaphoreType.DMA((11,)),
        pltpu.SemaphoreType.DMA((16,)),
    ]
    return call(
        kernel, "stage_first", (sc, side, fields, *messages), "svv" + 5 * "a", outs, "vhhhvh",
        scratch, 2 * 1296 * 2560 * LANES, 8_000_000, 28,
    )


def load_fields(padded, own_ref, oth_ref, sems):
    copies = [
        pltpu.make_async_copy(own_ref, inner(padded.at[0]), sems.at[0]),
        pltpu.make_async_copy(oth_ref, inner(padded.at[1]), sems.at[1]),
    ]
    for copy in copies:
        copy.start()
    blank_edges(padded.at[0])
    blank_edges(padded.at[1])
    return copies


def weight_tables(part, messages):
    own_x, own_y, x_1, y_1, x_2, y_2 = messages
    upper = {1: {0: x_1, 1: own_x}, 2: {2: own_x, 3: x_1}, 3: {2: x_1, 3: own_x}}[part]
    lower = {1: {1: own_y, 3: y_1}, 2: {0: y_1, 2: own_y}, 3: {1: y_1, 3: own_y}}[part]
    upper = [((section,), ref) for section, ref in upper.items()] + [
        ([section for section in range(4) if section not in upper], y_2)
    ]
    far = [section for section in range(4) if section not in lower]
    lower = list(lower.items())
    tables = [
        [(*entry, 16) for entry in upper],
        [(*entry, 1296) for entry in upper],
        [((section,), ref, 272) for section, ref in lower] + [(far, x_2, 0)],
        [((section,), ref, 1296) for section, ref in lower] + [(far, x_2, 1024)],
    ]
    return tables, [(*entry, 0) for entry in upper]


def stage_rest(part, sc, side, own, other, messages, short, cot=None, after=()):
    last = cot is not None
    extra = [one for one in (short, cot) if one is not None]

    def kernel(sc_ref, side_ref, own_ref, oth_ref, *refs):
        refs = list(refs)
        late_refs = [refs.pop(0) for _ in extra]
        tables, vectors = weight_tables(part, refs[0:6])
        refs = refs[6 + len(after) :]
        if last:
            dz, passed, out, sums = refs[:4]
            refs = refs[4:]
        else:
            hidden, zhat, stats = refs[:3]
            refs = refs[3:]
        w_keep, w_send, w, vec, padded, acc = refs[:6]
        grads, passed_now = refs[6:8] if last else (None, None)
        late, sems, out_sems = refs[-3:]
        short_ref = late.at[0] if short is not None else None
        cot_ref = late.at[1] if last else None
        section, core = sc_ref[0], sc_ref[2]
        fields = load_fields(padded, own_ref, oth_ref, sems.at[0:2])
        cuts = (0, 1280, 2304, 3328, 4608)
        loads = [
            load_chosen(section, table, w.at[cuts[at] : cuts[at + 1]], sems.at[2 + at])
            for at, table in enumerate(tables)
        ]
        vec_load = load_chosen(section, vectors, vec, sems.at[6])
        late_loads = [
            pltpu.make_async_copy(ref, late.at[at], sems.at[7 + at])
            for at, ref in enumerate(late_refs)
        ]
        for copy in late_loads:
            copy.start()
        for copy in fields:
            copy.wait()
        outs = []
        for chunk in range(3):
            total = jnp.zeros((432, LANES), f32)
            for a in range(3):
                for b in range(3):
                    for at in range(2):
                        if chunk == 0 and at == 0 and (3 * a + b) in (0, 2, 4, 6):
                            loads[(3 * a + b) // 2].wait()
                        left = padded[at, 3 * chunk + a : 3 * chunk + a + 3, b : b + 9]
                        which = core if at == 0 else 1 - core
                        from_row = pl.multiple_of(LANES * (2 * (3 * a + b) + which), LANES)
                        total = total + dot(left.reshape(432, LANES), w[pl.ds(from_row, LANES)])
            acc[3 * chunk : 3 * chunk + 3] = total.reshape(3, 9, 16, LANES)
            if not last:
                outs.append(
                    pltpu.make_async_copy(
                        acc.at[3 * chunk : 3 * chunk + 3],
                        zhat.at[3 * chunk : 3 * chunk + 3],
                        out_sems.at[18 + chunk],
                    )
                )
                outs[-1].start()
            if chunk == 0:
                for tap in range(9):
                    for at, target in ((core, w_keep), (1 - core, w_send)):
                        from_row = pl.multiple_of(LANES * (2 * tap + at), LANES)
                        outs.append(
                            pltpu.make_async_copy(
                                w.at[pl.ds(from_row, LANES)],
                                target.at[LANES * tap : LANES * tap + LANES],
                                out_sems.at[2 * tap + (0 if target is w_keep else 1)],
                            )
                        )
                        outs[-1].start()
        inside = Inside(side_ref[...])
        mean, scale = norm_stats(acc, inside)
        for copy in [vec_load] + late_loads:
            copy.wait()
        gain, _, bias, _ = unpack_vectors(vec[...])
        if last:
            sums_now = [None, None]
            parts = [[], []]
        for row in range(9):
            for col in range(9):
                ring = max(row, col)
                normed = (acc[row, col] - mean) * scale
                if last:
                    acc[row, col] = normed
                pre = normed * gain + bias
                if short is not None:
                    pre = pre + short_ref[row, col].astype(f32)
                sigmoid = sigmoid_of(pre)
                target = out if last else hidden
                target[row, col] = inside.keep(ring, pre * sigmoid).astype(bf16)
                if last:
                    slope = sigmoid * (1.0 + pre * (1.0 - sigmoid))
                    grad = inside.keep(ring, cot_ref[row, col].astype(f32) * slope)
                    grads[row, col] = grad
                    passed_now[row, col] = grad.astype(bf16)
                    for at, value in enumerate((grad, grad * normed)):
                        sums_now[at] = value if sums_now[at] is None else sums_now[at] + value
            if last:
                outs.append(
                    pltpu.make_async_copy(passed_now.at[row], passed.at[row], out_sems.at[18 + row])
                )
                outs[-1].start()
        if last:
            bias_now, gain_now = col_sum(sums_now[0]), col_sum(sums_now[1])
            norm_back(dz, grads, acc, inside, gain * scale, bias_now, gain_now)
            pack_rows(sums, [gain_now, bias_now])
        else:
            pack_rows(stats, [scale, gain, bias, mean])
        for copy in outs:
            copy.wait()

    half = struct((2304, LANES))
    if last:
        outs, places = [struct(GRID), struct(GRID), struct(GRID), struct((8, LANES), f32)], "vhvv"
    else:
        outs, places = [struct(GRID), struct(GRID, f32), struct((8, LANES), f32)], "vhv"
    scratch = [
        pltpu.VMEM((4608, LANES), bf16), pltpu.VMEM((16, LANES), bf16),
        pltpu.VMEM((2, 11, 11, 16, LANES), bf16), pltpu.VMEM(GRID, f32),
    ] + ([pltpu.VMEM(GRID, f32), pltpu.VMEM(GRID, bf16)] if last else [])
    scratch += [
        pltpu.VMEM((2, *GRID), bf16), pltpu.SemaphoreType.DMA((9,)), pltpu.SemaphoreType.DMA((27,)),
    ]
    return call(
        kernel, f"stage_{part}", (sc, side, own, other, *extra, *messages, *after),
        "svvv" + len(extra) * "h" + (6 + len(after)) * "h", outs + [half, half], places + "hh", scratch,
        2 * 1296 * 4608 * LANES, 8_000_000, 28,
    )


def norm_back(dz, grads, zhat, inside, weight, bias_now, gain_now):
    constant, slope = weight * bias_now / inside.count, weight * gain_now / inside.count
    for row in range(9):
        for col in range(9):
            value = weight * grads[row, col] - (constant + slope * zhat[row, col])
            dz[row, col] = inside.keep(max(row, col), value).astype(bf16)


def stage_back(part, sc, side, dz_own, dz_other, w_own, w_other, zhat, stats, short=None, extra=None, proj=None):
    first = proj is not None
    optional = [one for one in (short, extra) if one is not None] + (list(proj) if first else [])

    def kernel(sc_ref, side_ref, stats_ref, dz_own_ref, dz_oth_ref, w_own_ref, w_oth_ref, zhat_ref, *refs):
        refs = list(refs)
        late_refs = [refs.pop(0) for one in (short, extra) if one is not None]
        if first:
            dyp_ref, zhat_p_ref = refs.pop(0), refs.pop(0)
        dz, sums = refs.pop(0), refs.pop(0)
        passed = refs.pop(0) if short is not None else None
        dz_p = refs.pop(0) if first else None
        padded, acc, held, w = refs[:4]
        held_p = refs[4] if first else None
        late = None if first else refs[4]
        sems = refs[-1]
        short_ref = late.at[0] if short is not None else None
        extra_ref = late.at[1] if extra is not None else None
        fields = load_fields(padded, dz_own_ref, dz_oth_ref, sems.at[0:2])
        loads = [
            pltpu.make_async_copy(w_own_ref, w.at[0], sems.at[2]),
            pltpu.make_async_copy(w_oth_ref, w.at[1], sems.at[3]),
        ]
        later = [pltpu.make_async_copy(zhat_ref, held, sems.at[4])]
        if first:
            later.append(pltpu.make_async_copy(zhat_p_ref, held_p, sems.at[5]))
        for at, ref in enumerate(late_refs):
            later.append(pltpu.make_async_copy(ref, late.at[at], sems.at[6 + at]))
        for copy in loads + later:
            copy.start()
        for copy in fields + loads:
            copy.wait()
        for chunk in range(3):
            total = jnp.zeros((432, LANES), f32)
            for a in range(3):
                for b in range(3):
                    for at in range(2):
                        row_at = 3 * chunk + 2 - a
                        left = padded[at, row_at : row_at + 3, 2 - b : 11 - b]
                        from_row = LANES * (3 * a + b)
                        right = w[at, from_row : from_row + LANES]
                        total = total + dot_t(left.reshape(432, LANES), right)
            acc[3 * chunk : 3 * chunk + 3] = total.reshape(3, 9, 16, LANES)
        for copy in later:
            copy.wait()
        inside = Inside(side_ref[...])
        scale, gain, bias, mean, scale_p, gain_p, mean_p = [stats_ref[at : at + 1] for at in range(7)]
        sums_now = [None] * 4
        for row in range(9):
            for col in range(9):
                ring = max(row, col)
                normed = (held[row, col] - mean) * scale
                held[row, col] = normed
                pre = normed * gain + bias
                grad = acc[row, col]
                if extra is not None:
                    grad = grad + extra_ref[row, col].astype(f32)
                if short is not None:
                    pre = pre + short_ref[row, col].astype(f32)
                sigmoid = sigmoid_of(pre)
                slope = sigmoid * (1.0 + pre * (1.0 - sigmoid))
                grad = inside.keep(ring, grad.astype(bf16).astype(f32) * slope)
                acc[row, col] = grad
                if short is not None:
                    passed[row, col] = grad.astype(bf16)
                terms = [grad, grad * normed]
                if first:
                    grad_p = dyp_ref[row, col].astype(f32)
                    normed_p = (held_p[row, col] - mean_p) * scale_p
                    held_p[row, col] = normed_p
                    terms += [grad_p, grad_p * normed_p]
                for at, value in enumerate(terms):
                    sums_now[at] = value if sums_now[at] is None else sums_now[at] + value
        totals = [col_sum(value) for value in sums_now if value is not None]
        norm_back(dz, acc, held, inside, gain * scale, totals[0], totals[1])
        rows = [totals[1], totals[0]]
        if first:
            for row in range(9):
                for col in range(9):
                    acc[row, col] = dyp_ref[row, col].astype(f32)
            norm_back(dz_p, acc, held_p, inside, gain_p * scale_p, totals[2], totals[3])
            rows += [totals[3], totals[2]]
        pack_rows(sums, rows)

    outs, places = [struct(GRID), struct((8, LANES), f32)], "vv"
    if short is not None:
        outs, places = outs + [struct(GRID)], places + "v"
    if first:
        outs, places = outs + [struct(GRID)], places + "v"
    scratch = [
        pltpu.VMEM((2, 11, 11, 16, LANES), bf16), pltpu.VMEM(GRID, f32), pltpu.VMEM(GRID, f32),
        pltpu.VMEM((2, 2304, LANES), bf16),
    ] + [pltpu.VMEM(GRID, f32) if first else pltpu.VMEM((2, *GRID), bf16)]
    scratch += [pltpu.SemaphoreType.DMA((8,))]
    kinds = "h" * ((short is not None) + (extra is not None)) + ("vh" if first else "")
    return call(
        kernel, f"back_{part}",
        (sc, side, stats, dz_own, dz_other, w_own, w_other, zhat, *optional),
        "svvvvhah" + kinds, outs, places, scratch, 2 * 1296 * 4608 * LANES, 10_000_000, 28,
    )


def pick_images(sc, *fields):
    def kernel(sc_ref, *refs):
        core = sc_ref[2]
        out_row = lax.broadcasted_iota(jnp.int32, (4, 96, 1296), 1)
        slot = lax.broadcasted_iota(jnp.int32, (4, 96, 1296), 0)
        in_row = lax.broadcasted_iota(jnp.int32, (4, 96, 1296), 2)
        image = 8 * ((slot >> 1) ^ core) + (slot & 1)
        pick = jnp.where(in_row == 16 * out_row + image, 1.0, 0.0).astype(bf16).reshape(384, 1296)
        for source, target in zip(refs[: len(fields)], refs[len(fields) :]):
            chosen = dot(pick, source[...].reshape(1296, LANES))
            target[...] = chosen.astype(bf16).reshape(4, 96, LANES)

    count = len(fields)
    return call(
        kernel, f"pick_images_{count}", (sc, *fields), "s" + count * "v", count * [struct((4, 96, LANES))],
        count * "v", [], count * 2 * 384 * 1296 * LANES, 3_000_000, 28,
    )


def weight_rest(part, sc, own, other, dz, sums):
    def kernel(sc_ref, own_ref, oth_ref, dz_ref, sums_ref, out, turned, padded, sems):
        zone, core = sc_ref[1], sc_ref[2]
        load = pltpu.make_async_copy(dz_ref, inner(padded), sems.at[0])
        load.start()
        blank_edges(padded)
        lane = pl.multiple_of(128 * (zone & 1), 128)
        is_own = (zone >> 1) == core

        @pl.when(is_own)
        def _():
            turned[...] = own_ref[:, :, :, pl.ds(lane, 128)].reshape(1296, 128).T

        @pl.when(jnp.logical_not(is_own))
        def _():
            turned[...] = oth_ref[:, :, :, pl.ds(lane, 128)].reshape(1296, 128).T

        load.wait()
        left = turned[...]
        for a in range(3):
            for b in range(3):
                right = padded[2 - a : 11 - a, 2 - b : 11 - b].reshape(1296, LANES)
                at = 128 * (3 * a + b)
                out[at : at + 128] = dot(left, right).astype(bf16)
        blank = jnp.zeros((1, LANES), f32)
        out[1152:1168] = pack_vectors([sums_ref[0:1], blank, sums_ref[1:2], blank])

    scratch = [
        pltpu.VMEM((128, 1296), bf16), pltpu.VMEM((11, 11, 16, LANES), bf16),
        pltpu.SemaphoreType.DMA((1,)),
    ]
    return call(
        kernel, f"weight_{part}", (sc, own, other, dz, sums), "svvvv", [struct((1168, LANES))], "v",
        scratch, 2 * 1296 * 1152 * LANES, 3_000_000, 28,
    )[0]


def weight_first(sc, fields, dz, dz_p, sums):
    def kernel(sc_ref, field, dz_ref, dz_p_ref, sums_ref, out, turned, padded, sems):
        zone = sc_ref[1]
        load = pltpu.make_async_copy(dz_ref, inner(padded), sems.at[0])
        load.start()
        blank_edges(padded)
        lane = pl.multiple_of(128 * (zone >> 1), 128)
        at = pl.multiple_of(64 * (zone & 1), 64)
        for phase in range(4):
            chosen = field[phase // 2, phase % 2, 1:10, 1:10, :, pl.ds(lane, 128)]
            turned[phase] = chosen.reshape(1296, 128).T
        load.wait()
        for tap in range(10):
            if tap < 9:
                a, b = divmod(tap, 3)
                left = turned[2 * ((a + 1) % 2) + (b + 1) % 2, pl.ds(at, 64)]
                row_at, col_at = 2 if a == 0 else 1, 2 if b == 0 else 1
                right = padded[row_at : row_at + 9, col_at : col_at + 9].reshape(1296, LANES)
            else:
                left = turned[0, pl.ds(at, 64)]
                right = dz_p_ref[...].reshape(1296, LANES)
            out[64 * tap : 64 * tap + 64] = dot(left, right).astype(bf16)
        out[640:656] = pack_vectors([sums_ref[0:1], sums_ref[2:3], sums_ref[1:2], sums_ref[3:4]])

    scratch = [
        pltpu.VMEM((4, 128, 1296), bf16), pltpu.VMEM((11, 11, 16, LANES), bf16),
        pltpu.SemaphoreType.DMA((1,)),
    ]
    return call(
        kernel, "weight_first", (sc, fields, dz, dz_p, sums), "svvvv", [struct((656, LANES))], "v",
        scratch, 2 * 1296 * 640 * LANES, 3_000_000, 28,
    )[0]


def image_back(own, other, own_p, other_p, w_own, w_other):
    def kernel(own_ref, oth_ref, own_p_ref, oth_p_ref, w_own_ref, w_oth_ref, out):
        row = lax.broadcasted_iota(jnp.int32, (192, 192), 0)
        col = lax.broadcasted_iota(jnp.int32, (192, 192), 1)
        pixel = jnp.where(row >= 96, row - 96, row)
        line = (pixel * 57) >> 9
        across = pixel - 9 * line
        shifted = {}
        for down in range(2):
            for right in range(2):
                if down + right == 0:
                    shifted[0, 0] = (
                        own_ref[...].reshape(192, LANES),
                        oth_ref[...].reshape(192, LANES),
                    )
                    continue
                fits = (pixel < 81) & (line + down < 9) & (across + right < 9)
                move = jnp.where(fits & (col == row + 9 * down + right), 1.0, 0.0).astype(bf16)
                shifted[down, right] = tuple(
                    dot(move, ref[...].reshape(192, LANES)).astype(bf16)
                    for ref in (own_ref, oth_ref)
                )
        phases = [jnp.zeros((192, LANES), f32) for _ in range(4)]
        for a in range(3):
            for b in range(3):
                at = 2 * ((a + 1) % 2) + (b + 1) % 2
                left = shifted[1 if a == 0 else 0, 1 if b == 0 else 0]
                rows = slice(LANES * (3 * a + b), LANES * (3 * a + b + 1))
                phases[at] = phases[at] + dot_t(left[0], w_own_ref[rows])
                phases[at] = phases[at] + dot_t(left[1], w_oth_ref[rows])
        phases[0] = phases[0] + dot_t(own_p_ref[...].reshape(192, LANES), w_own_ref[2304:2560])
        phases[0] = phases[0] + dot_t(oth_p_ref[...].reshape(192, LANES), w_oth_ref[2304:2560])
        joined = jnp.concatenate([phase.astype(bf16) for phase in phases], axis=0)
        out_row = lax.broadcasted_iota(jnp.int32, (336, 768), 0)
        in_row = lax.broadcasted_iota(jnp.int32, (336, 768), 1)
        line = (out_row * 3641) >> 16
        across = out_row - 18 * line
        source = (2 * (line & 1) + (across & 1)) * 192 + 9 * (line >> 1) + (across >> 1)
        for image in range(2):
            spread = jnp.where(
                (in_row == source + 96 * image) & (out_row < 324), 1.0, 0.0
            ).astype(bf16)
            out[image] = dot(spread, joined).astype(bf16)

    return call(
        kernel, "image_back", (own, other, own_p, other_p, w_own, w_other), "vvvvvv",
        [struct((2, 336, LANES))], "v", [], 2 * 192 * 2560 * 512 + 4 * 336 * 768 * 256, 4_000_000, 28,
    )[0]


def add_into(out, rows, sources, vector_rows):
    for at in range(0, rows, 64):
        total = sources[0][at : at + 64].astype(f32)
        for source in sources[1:]:
            total = total + source[at : at + 64].astype(f32)
        out[at : at + 64] = total.astype(bf16)
    totals = [unpack_vectors(source[rows : rows + 16]) for source in sources]
    sums = [sum(one[1:], one[0]) for one in zip(*totals)]
    out[vector_rows : vector_rows + 16] = pack_vectors(sums)


def add_pieces(part, one, two):
    rows = one.shape[0] - 16

    def kernel(one_ref, two_ref, out):
        add_into(out, rows, (one_ref, two_ref), rows)

    return call(
        kernel, f"add_{part}", (one, two), "vv", [struct(one.shape)], "v", [], 1, 1_000_000, 28
    )[0]


def add_halves(one, top, bottom):
    def kernel(one_ref, top_ref, bottom_ref, out):
        for at in range(0, 768, 64):
            span = slice(at, at + 64)
            out[span] = (one_ref[span].astype(f32) + top_ref[span].astype(f32)).astype(bf16)
        add_into(out.at[768:1168], 384, (one_ref.at[768:1168], bottom_ref), 384)

    return call(
        kernel, "add_halves", (one, top, bottom), "vvv", [struct(one.shape)], "v", [], 1, 1_000_000, 28
    )[0]


def own_piece(sc, groups):
    pieces = [piece for group in groups for piece in group]

    def kernel(sc_ref, *refs):
        out, held, sems = refs[len(pieces) :]
        used = 0
        for part, group in enumerate(groups):
            sources = refs[used : used + len(group)]
            used += len(group)
            rows = group[0].shape[0] - 16

            @pl.when(sc_ref[0] == part)
            def _():
                copies = [
                    pltpu.make_async_copy(ref, held.at[at, 0 : rows + 16], sems.at[at])
                    for at, ref in enumerate(sources)
                ]
                for copy in copies:
                    copy.start()
                for copy in copies:
                    copy.wait()
                add_into(out, rows, [held.at[at] for at in range(len(sources))], 1152)

    return call(
        kernel, "own_piece", (sc, *pieces), "s" + len(pieces) * "a", [struct((1168, LANES))], "v",
        [pltpu.VMEM((4, 1168, LANES), bf16), pltpu.SemaphoreType.DMA((4,))], 1, 1_000_000, 28,
    )[0]


def lay_out(sc, own, other):
    def kernel(sc_ref, *refs):
        pieces, (out, vectors, held, wide, sems, out_sems) = refs[:8], refs[8:]
        section, zone, core = sc_ref[0], sc_ref[1], sc_ref[2]
        loads = []
        for tap in range(9):
            span = slice(128 * tap, 128 * tap + (144 if tap == 8 else 128))
            loads.append(
                [
                    pltpu.make_async_copy(
                        piece.at[span], held.at[zone ^ (at % 4), core ^ (at // 4), span], sems.at[tap, at]
                    )
                    for at, piece in enumerate(pieces)
                ]
            )
        for group in loads:
            for load in group:
                load.start()
        for tap in range(9):
            slot = tap % 2
            leaving = pltpu.make_async_copy(
                wide.at[slot], out.at[512 * tap : 512 * tap + 512], out_sems.at[slot]
            )
            for load in loads[tap]:
                load.wait()
            if tap >= 2:
                leaving.wait()

            @pl.when(section != 0)
            def _():
                for origin in range(4):
                    for core in range(2):
                        value = held[origin, core, 128 * tap : 128 * tap + 128].astype(f32)
                        wide[slot, 128 * origin : 128 * origin + 128, LANES * core : LANES * core + LANES] = value

            @pl.when(section == 0)
            def _():
                for half in range(2):
                    start = 64 * (2 * tap + half)
                    for origin in range(4):
                        row = 256 * half + 64 * origin
                        for core in range(2):
                            value = jnp.zeros((64, LANES), f32)
                            if start < 640:
                                value = held[origin, core, start : start + 64].astype(f32)
                            wide[slot, row : row + 64, LANES * core : LANES * core + LANES] = value

            leaving.start()
        for core in range(2):
            rows = unpack_vectors(held[zone, core, 1152:1168])
            vectors[:, LANES * core : LANES * core + LANES] = jnp.concatenate(rows, axis=0)
        for slot in range(2):
            pltpu.make_async_copy(wide.at[slot], out.at[0:512], out_sems.at[slot]).wait()

    return call(
        kernel, "lay_out", (sc, *own, *other), "s" + 8 * "a", [struct((4608, 512), f32), struct((4, 512), f32)], "hv",
        [
            pltpu.VMEM((4, 2, 1168, LANES), bf16), pltpu.VMEM((2, 512, 512), f32),
            pltpu.SemaphoreType.DMA((9, 8)), pltpu.SemaphoreType.DMA((2,)),
        ],
        0, 15_000_000, 60,
    )


def half_of(value, half):
    return lax.dynamic_slice_in_dim(value, LANES * half, LANES, axis=value.ndim - 1)


def join_halves(own, other, core):
    first = jnp.where(core == 0, own, other)
    second = jnp.where(core == 0, other, own)
    return jnp.concatenate([first, second], axis=-1)


def chip_body(images, res_ids, weights, bn_gain, bn_bias, cotangent):
    section = lax.axis_index("section")
    position = lax.axis_index("dp")
    zone, core = position // 2, position % 2
    sc = jnp.stack([section, zone, core, core]).astype(jnp.int32)

    def after(value, *tokens):
        return lax.optimization_barrier((value, *tokens))[0]

    own = split_weights(sc, weights[0], jnp.concatenate([bn_gain[0], bn_bias[0]], axis=0))
    x_1 = flip(own[0], "section", 1)
    y_1 = flip(own[1], "section", 2)

    level = lax.dynamic_index_in_dim(res_ids, section, 0, keepdims=False)
    side_own = (9 - 2 * (2 - level)).astype(f32)
    tail = jnp.broadcast_to(side_own[:, None, None], (2, 12, 256)).astype(bf16)
    image_own = jnp.concatenate([after(images, own[0])[0].reshape(2, 324, 256), tail], axis=1)
    pieces = [image_own] + [flip(image_own, "dp", 2 * at) for at in range(1, 4)]
    pieces += [flip(piece, "dp", 1) for piece in pieces]
    cot_own = after(cotangent, image_own)[0].reshape(2, 81, 512)
    cot_pair = jnp.stack([half_of(cot_own, core), flip(half_of(cot_own, 1 - core), "dp", 1)])
    cot_pair = jnp.pad(cot_pair, ((0, 0), (0, 0), (0, 15), (0, 0)))
    cot_near = jnp.stack([cot_pair, flip(cot_pair, "dp", 2)])
    cot_pieces = (cot_near, flip(cot_near, "dp", 4))

    for_x, for_y, top, bottom = relay_weights(
        "relay_2", lambda at: (at == 1) | (at == 2), (sc, *own, x_1, y_1), True
    )
    top = flip(top, "section", 1, lambda i: i == 2)
    bottom = flip(bottom, "section", 2, lambda i: i == 1)
    fields, side = prepare_images(sc, pieces)
    x_2 = flip(for_x, "section", 1)
    y_2 = flip(for_y, "section", 2)
    hidden_one, short_one, zhat_0, zhat_p, stats_0, w_first = stage_first(
        sc, side, after(fields, for_x), (own[0], x_1, y_1, top, bottom)
    )
    hidden_one_other = flip(hidden_one, "dp", 1)
    w_first_other = flip(w_first, "dp", 1)
    for_x, for_y = relay_weights("relay_3", lambda at: at == 3, (after(sc, stats_0), *own, x_1, y_1))
    x_3 = flip(for_x, "section", 1, lambda i: i in (1, 3))
    y_3 = flip(for_y, "section", 2, lambda i: i in (2, 3))
    messages = (*own, x_1, y_1, x_2, y_2)
    block_one, zhat_1, stats_1, keep_1, send_1 = stage_rest(
        1, sc, side, hidden_one, hidden_one_other, messages, short_one, after=cot_pieces
    )
    block_one_other = flip(block_one, "dp", 1)
    other_1 = flip(send_1, "dp", 1)
    cot = prepare_cotangent(sc, after(cot_pieces, stats_1))
    hidden_two, zhat_2, stats_2, keep_2, send_2 = stage_rest(
        2, sc, side, block_one, block_one_other, messages, None, after=(x_3, y_3, cot)
    )
    hidden_two_other = flip(hidden_two, "dp", 1)
    other_2 = flip(send_2, "dp", 1)
    messages = (*own, x_1, y_1, x_3, y_3)
    dz_3, passed, out, sums_3, keep_3, send_3 = stage_rest(
        3, sc, side, hidden_two, hidden_two_other, messages, block_one, cot
    )
    other_3 = flip(send_3, "dp", 1)
    dz_3_other = flip(dz_3, "dp", 1)

    def to_pair(part, piece):
        return flip(piece, "section", 2, lambda i: i ^ 2 in (part, part ^ 1))

    def to_owner(part, piece):
        return flip(piece, "section", 1, lambda i: i ^ 1 == part)

    piece_3 = weight_rest(3, sc, hidden_two, hidden_two_other, dz_3, sums_3)
    came_3 = [to_pair(3, piece_3[0:768])]
    came_3.append(to_pair(3, after(piece_3[768:1168], came_3[0])))
    dz_2, sums_2 = stage_back(
        2, sc, side, after(dz_3, piece_3), dz_3_other, keep_3, other_3, zhat_2, stats_2
    )
    dz_2_other = flip(dz_2, "dp", 1)
    piece_2 = weight_rest(2, sc, block_one, block_one_other, dz_2, sums_2)
    came_2 = to_pair(2, piece_2)
    dz_1, sums_1, short_grad = stage_back(
        1, sc, side, after(dz_2, piece_2), dz_2_other, keep_2, other_2, zhat_1, stats_1, short_one,
        passed,
    )
    dz_1_other = flip(dz_1, "dp", 1)
    piece_1 = weight_rest(
        1, sc, hidden_one, hidden_one_other, after(dz_1, came_3[0]), sums_1
    )
    came_1 = to_pair(1, piece_1)
    dz_0, sums_0, dz_p = stage_back(
        0, sc, side, after(dz_1, piece_1), dz_1_other, keep_1, other_1, zhat_0, stats_0,
        proj=(short_grad, zhat_p),
    )
    piece_0 = weight_first(sc, fields, dz_0, dz_p, sums_0)
    came_0 = to_pair(0, piece_0)
    sum_3 = add_halves(after(piece_3, piece_0), *came_3)
    last_3 = to_owner(3, sum_3)
    sum_2 = add_pieces(2, after(piece_2, sum_3), came_2)
    last_2 = to_owner(2, sum_2)
    sum_1 = add_pieces(1, after(piece_1, sum_2), came_1)
    last_1 = to_owner(1, sum_1)
    pick_0, pick_p, pick_out = pick_images(sc, *after((dz_0, dz_p, out), sum_1))
    sum_0 = add_pieces(0, after(piece_0, pick_out), came_0)
    last_0 = to_owner(0, sum_0)
    total = own_piece(
        sc, [(sum_0, last_0), (sum_1, last_1), (sum_2, last_2), (sum_3, last_3)]
    )
    gathered = [total] + [flip(total, "dp", 2 * at) for at in range(1, 4)]
    weight_grad, vectors = lay_out(sc, gathered, [flip(piece, "dp", 1) for piece in gathered])

    pick_out_other = flip(pick_out[2:4], "dp", 1)
    block_output = join_halves(pick_out[0:2, 0:81], pick_out_other[:, 0:81], core)
    pick_0_other = flip(pick_0[2:4], "dp", 1)
    pick_p_other = flip(pick_p[2:4], "dp", 1)
    image_grad = image_back(
        pick_0[0:2], pick_0_other, pick_p[0:2], pick_p_other, w_first, w_first_other
    )
    rows = jnp.arange(18, dtype=jnp.int32)
    inner_rows = (rows < 2 * (9 - 2 * (2 - level))[:, None]).astype(bf16)
    mask_in = inner_rows[:, :, None] * inner_rows[:, None, :]
    image_grad = image_grad[:, 0:324].reshape(2, 18, 18, 256) * mask_in[..., None]
    return (
        block_output.reshape(1, 2, 9, 9, 512),
        image_grad[None],
        weight_grad[None],
        vectors[None, 0:2],
        vectors[None, 2:4],
    )


def solution(mesh):
    placed = (
        P("section", "dp", None, None, None),
        P(None, "dp"),
        P("section", None, None),
        P("section", None, None),
        P("section", None, None),
        P("section", "dp", None, None, None),
    )
    on_chip = mesh.shape["section"] == 4 and mesh.shape["dp"] == 8
    return jax.shard_map(
        chip_body if on_chip else pipeline_body,
        mesh=mesh,
        in_specs=placed,
        out_specs=(
            P("section", "dp", None, None, None),
            P("section", "dp", None, None, None),
            P("section", None, None),
            P("section", None, None),
            P("section", None, None),
        ),
        check_vma=False,
    )
```

```python
import jax
import jax.numpy as jnp
from jax import lax
from jax.experimental import pallas as pl
from jax.experimental.pallas import tpu as pltpu
from jax.sharding import PartitionSpec as P

epsilon = 1e-05


def passed_along(value, axis, steps):
    count = lax.axis_size(axis)
    leading, last = (max(0, -steps), min(count, count - steps))
    return lax.ppermute(value, axis, [(source, source + steps) for source in range(leading, last)])


def regions(levels, half_side):
    inner_side = half_side - 2 * (2 - levels)
    small_rows = jnp.arange(half_side, dtype=jnp.int32)
    large_rows = jnp.arange(2 * half_side, dtype=jnp.int32)
    inner_mask = (small_rows < inner_side[..., None]).astype(jnp.float32)
    outer_mask = (large_rows < 2 * inner_side[..., None]).astype(jnp.float32)
    return (
        outer_mask[..., :, None] * outer_mask[..., None, :],
        inner_mask[..., :, None] * inner_mask[..., None, :],
    )


def patches(field_in, stride, half_side):
    padded = jnp.pad(field_in, ((0, 0), (1, 1), (1, 1), (0, 0)))
    pieces = [
        padded[
            :,
            row_at : row_at + stride * half_side : stride,
            col_at : col_at + stride * half_side : stride,
            :,
        ]
        for row_at in range(3)
        for col_at in range(3)
    ]
    joined = jnp.concatenate(pieces, axis=-1)
    return joined.reshape(-1, joined.shape[-1])


def contract_rows(left_side, right_side):
    return lax.dot_general(
        left_side, right_side, (((0,), (0,)), ((), ())), preferred_element_type=jnp.float32
    )


def contract_cols(left_side, right_side):
    return lax.dot_general(
        left_side, right_side, (((1,), (1,)), ((), ())), preferred_element_type=jnp.float32
    )


def silu_slope(values):
    sigmoid = jax.nn.sigmoid(values)
    return sigmoid * (1.0 + values * (1.0 - sigmoid))


def spread_taps(tap_grads, image_count, half_side, channels):
    tap_grid = tap_grads.reshape(image_count, half_side, half_side, 9, channels)
    empty_phase = jnp.zeros((image_count, half_side + 1, half_side + 1, channels), jnp.float32)
    phases = [[empty_phase, empty_phase], [empty_phase, empty_phase]]
    for row_at in range(3):
        for col_at in range(3):
            tap_piece = tap_grid[:, :, :, 3 * row_at + col_at, :]
            top_pad = 1 if row_at == 2 else 0
            left_pad = 1 if col_at == 2 else 0
            placed = jnp.pad(
                tap_piece, ((0, 0), (top_pad, 1 - top_pad), (left_pad, 1 - left_pad), (0, 0))
            )
            phases[row_at % 2][col_at % 2] = phases[row_at % 2][col_at % 2] + placed
    row_phases = [jnp.stack([phases[parity][0], phases[parity][1]], axis=3) for parity in range(2)]
    alternated = jnp.stack(row_phases, axis=2).reshape(
        image_count, 2 * half_side + 2, 2 * half_side + 2, channels
    )
    return alternated[:, 1 : 2 * half_side + 1, 1 : 2 * half_side + 1, :]


def keep_slot(buffer_all, new_value, slot_at, keep_flag):
    current = lax.dynamic_index_in_dim(buffer_all, slot_at, 0, keepdims=False)
    return lax.dynamic_update_index_in_dim(
        buffer_all, jnp.where(keep_flag, new_value, current), slot_at, 0
    )


def pipeline_body(images, res_ids, weights, bn_gain, bn_bias, cotangent):
    sections = lax.axis_size("section")
    last_section = sections - 1
    position = lax.axis_index("section")
    micro_count = res_ids.shape[0]
    image_count = images.shape[1]
    half_side = cotangent.shape[2]
    channels = weights.shape[2]
    in_channels = images.shape[4]
    pixel_rows = image_count * half_side * half_side
    taps_in = 9 * in_channels
    matrix = weights[0]
    gain_rows = bn_gain[0]
    bias_rows = bn_bias[0]
    is_first = position == 0
    adds_short = (position == 1) | (position == 3)
    passes_short = position == 2
    makes_short = position == 1
    back_matrix = jnp.transpose(matrix.reshape(9, channels, channels)[::-1], (0, 2, 1)).reshape(
        9 * channels, channels
    )
    mask_in_all, mask_out_all = regions(res_ids, half_side)
    act_shape = (image_count, half_side, half_side, channels)
    zero_pixels = jnp.zeros((pixel_rows, channels), jnp.float32)
    zero_input = jnp.zeros((image_count, 2 * half_side, 2 * half_side, in_channels), jnp.float32)
    zero_weight = jnp.zeros((9 * channels, channels), jnp.float32)
    own_images = images[0]
    gathered = [own_images]
    for source in range(1, micro_count):
        gathered.append(passed_along(own_images, "section", -source))
    section_inputs = jnp.stack(gathered)
    own_cot = cotangent[0]
    arrived = []
    for source in range(micro_count):
        if source == last_section:
            arrived.append(own_cot)
        else:
            arrived.append(passed_along(own_cot, "section", last_section - source))
    cot_all = jnp.stack(arrived)

    def conv_first(prev_act, first_in):
        columns = patches(first_in, 2, half_side)
        main_out = jnp.dot(columns, matrix[:taps_in], preferred_element_type=jnp.float32)
        proj_out = jnp.dot(
            columns[:, 4 * in_channels : 5 * in_channels],
            matrix[taps_in : taps_in + in_channels],
            preferred_element_type=jnp.float32,
        )
        return jnp.stack([main_out, proj_out])

    def conv_rest(prev_act, first_in):
        columns = patches(prev_act, 1, half_side)
        return jnp.stack(
            [jnp.dot(columns, matrix, preferred_element_type=jnp.float32), zero_pixels]
        )

    def conv_spare(prev_act, first_in):
        return jnp.stack([zero_pixels, zero_pixels])

    def back_first(grad_conv, prev_act, first_in):
        columns = patches(first_in, 2, half_side)
        centre = columns[:, 4 * in_channels : 5 * in_channels]
        main_grad = contract_rows(columns, grad_conv[0])
        proj_grad = contract_rows(centre, grad_conv[1])
        filler = jnp.zeros((9 * channels - taps_in - in_channels, channels), jnp.float32)
        weight_now = jnp.concatenate([main_grad, proj_grad, filler], axis=0)
        tap_grads = contract_cols(grad_conv[0], matrix[:taps_in])
        centre_grad = contract_cols(grad_conv[1], matrix[taps_in : taps_in + in_channels])
        tap_grads = tap_grads + jnp.pad(centre_grad, ((0, 0), (4 * in_channels, 4 * in_channels)))
        return (
            weight_now,
            zero_pixels,
            spread_taps(tap_grads, image_count, half_side, in_channels),
        )

    def back_rest(grad_conv, prev_act, first_in):
        columns = patches(prev_act, 1, half_side)
        weight_now = contract_rows(columns, grad_conv[0])
        grad_image = grad_conv[0].reshape(act_shape)
        prev_grad = jnp.dot(
            patches(grad_image, 1, half_side), back_matrix, preferred_element_type=jnp.float32
        )
        return (weight_now, prev_grad, zero_input)

    def back_spare(grad_conv, prev_act, first_in):
        return (zero_weight, zero_pixels, zero_input)

    def finish(conv_out, mean_rows, scale_rows, flat_mask, short_in):
        normed = (conv_out - mean_rows[:, None, :]) * scale_rows[:, None, :] * gain_rows[
            :, None, :
        ] + bias_rows[:, None, :]
        pre_act = normed[0] + jnp.where(adds_short, short_in, 0.0)
        activated = jax.nn.silu(pre_act) * flat_mask[:, None]
        proj_short = normed[1] * flat_mask[:, None]
        short_out = jnp.where(is_first, proj_short, jnp.where(makes_short, activated, short_in))
        return (pre_act, activated, short_out)

    empty_act = jnp.zeros(act_shape, jnp.bfloat16)
    recv_act = empty_act
    recv_short = empty_act
    saved_act = jnp.zeros((micro_count,) + act_shape, jnp.bfloat16)
    saved_short = saved_act
    saved_final = saved_act
    saved_mean = jnp.zeros((micro_count, 2, channels), jnp.float32)
    saved_scale = saved_mean
    saved_total = jnp.zeros((micro_count,), jnp.float32)
    sweep_len = micro_count + last_section
    for tick_at in range(sweep_len):
        slot_raw = tick_at - position
        is_valid = (slot_raw >= 0) & (slot_raw < micro_count)
        slot_at = jnp.clip(slot_raw, 0, micro_count - 1)
        flat_mask = mask_out_all[slot_at].reshape(-1) * is_valid.astype(jnp.float32)
        first_in = section_inputs[slot_at] * mask_in_all[slot_at][..., None].astype(jnp.bfloat16)
        branch = jnp.where(is_valid, jnp.where(is_first, 0, 1), 2).astype(jnp.int32)
        conv_out = lax.switch(branch, [conv_first, conv_rest, conv_spare], recv_act, first_in)
        local_total = jnp.sum(flat_mask)
        weighted = conv_out * flat_mask[None, :, None]
        grand_total, sum_rows = lax.psum((local_total, jnp.sum(weighted, axis=1)), "dp")
        grand_total = jnp.maximum(grand_total, 1.0)
        statistics_mean_rows = sum_rows / grand_total
        centred = conv_out - statistics_mean_rows[:, None, :]
        variance = (
            lax.psum(jnp.sum(centred * centred * flat_mask[None, :, None], axis=1), "dp")
            / grand_total
        )
        grand_total, mean_rows, scale_rows = (
            grand_total,
            statistics_mean_rows,
            lax.rsqrt(variance + epsilon),
        )
        short_in = recv_short.reshape(pixel_rows, channels).astype(jnp.float32)
        pre_act, activated, short_out = finish(conv_out, mean_rows, scale_rows, flat_mask, short_in)
        act_low = activated.astype(jnp.bfloat16).reshape(act_shape)
        short_low = short_out.astype(jnp.bfloat16).reshape(act_shape)
        saved_act = keep_slot(saved_act, recv_act, slot_at, is_valid)
        saved_short = keep_slot(saved_short, recv_short, slot_at, is_valid)
        saved_mean = keep_slot(saved_mean, mean_rows, slot_at, is_valid)
        saved_scale = keep_slot(saved_scale, scale_rows, slot_at, is_valid)
        saved_total = keep_slot(saved_total, grand_total, slot_at, is_valid)
        saved_final = keep_slot(
            saved_final, act_low, slot_at, is_valid & (position == last_section)
        )
        if tick_at + 1 < sweep_len:
            recv_act, recv_short = passed_along((act_low, short_low), "section", 1)
    grad_act = empty_act
    grad_short = empty_act
    weight_acc = zero_weight
    gain_acc = jnp.zeros((2, channels), jnp.float32)
    bias_acc = gain_acc
    saved_dx = jnp.zeros(
        (micro_count, image_count, 2 * half_side, 2 * half_side, in_channels), jnp.bfloat16
    )
    for tick_at in range(sweep_len):
        slot_raw = tick_at - (last_section - position)
        is_valid = (slot_raw >= 0) & (slot_raw < micro_count)
        slot_at = jnp.clip(slot_raw, 0, micro_count - 1)
        flat_mask = mask_out_all[slot_at].reshape(-1) * is_valid.astype(jnp.float32)
        first_in = section_inputs[slot_at] * mask_in_all[slot_at][..., None].astype(jnp.bfloat16)
        branch = jnp.where(is_valid, jnp.where(is_first, 0, 1), 2).astype(jnp.int32)
        prev_act = saved_act[slot_at]
        conv_out = lax.switch(branch, [conv_first, conv_rest, conv_spare], prev_act, first_in)
        mean_rows = saved_mean[slot_at]
        scale_rows = saved_scale[slot_at]
        valid_total = saved_total[slot_at]
        short_in = saved_short[slot_at].reshape(pixel_rows, channels).astype(jnp.float32)
        pre_act, activated, short_out = finish(conv_out, mean_rows, scale_rows, flat_mask, short_in)
        from_act = (
            jnp.where(position == last_section, cot_all[slot_at], grad_act)
            .reshape(pixel_rows, channels)
            .astype(jnp.float32)
        )
        from_short = grad_short.reshape(pixel_rows, channels).astype(jnp.float32)
        slope = silu_slope(pre_act) * flat_mask[:, None]
        grad_pre = (from_act + jnp.where(adds_short, from_short, 0.0)) * slope
        grad_proj = jnp.where(is_first, from_short * flat_mask[:, None], 0.0)
        grad_normed = jnp.stack([grad_pre, grad_proj])
        normalized = (conv_out - mean_rows[:, None, :]) * scale_rows[:, None, :]
        bias_now, gain_now = lax.psum(
            (jnp.sum(grad_normed, axis=1), jnp.sum(grad_normed * normalized, axis=1)), "dp"
        )
        bias_acc = bias_acc + bias_now
        gain_acc = gain_acc + gain_now
        grad_conv = (
            flat_mask[None, :, None]
            * gain_rows[:, None, :]
            * scale_rows[:, None, :]
            * (
                grad_normed
                - (bias_now[:, None, :] + normalized * gain_now[:, None, :]) / valid_total
            )
        )
        grad_conv = grad_conv.astype(jnp.bfloat16)
        weight_now, prev_grad, input_grad = lax.switch(
            branch, [back_first, back_rest, back_spare], grad_conv, prev_act, first_in
        )
        weight_acc = weight_acc + weight_now
        masked_input = (input_grad * mask_in_all[slot_at][..., None]).astype(jnp.bfloat16)
        saved_dx = keep_slot(saved_dx, masked_input, slot_at, is_valid & is_first)
        send_act = (
            (prev_grad + jnp.where(passes_short, from_short, 0.0))
            .astype(jnp.bfloat16)
            .reshape(act_shape)
        )
        send_short = jnp.where(adds_short, grad_pre, 0.0).astype(jnp.bfloat16).reshape(act_shape)
        if tick_at + 1 < sweep_len:
            grad_act, grad_short = passed_along((send_act, send_short), "section", -1)
    weight_total = lax.psum(weight_acc, "dp")
    result = saved_final[last_section]
    for source in range(last_section):
        arrived_piece = passed_along(saved_final[source], "section", source - last_section)
        result = jnp.where(position == source, arrived_piece, result)
    grad_result = saved_dx[0]
    for source in range(1, micro_count):
        arrived_piece = passed_along(saved_dx[source], "section", source)
        grad_result = jnp.where(position == source, arrived_piece, grad_result)
    return (result[None], grad_result[None], weight_total[None], gain_acc[None], bias_acc[None])


f32, bf16 = jnp.float32, jnp.bfloat16
LANES = 256
GRID = (9, 9, 16, LANES)


def flip(value, axis, mask, senders=None):
    count = lax.axis_size(axis)
    pairs = [(i, i ^ mask) for i in range(count) if senders is None or senders(i)]
    return lax.ppermute(value, axis, pairs)


def struct(shape, kind=bf16):
    return jax.ShapeDtypeStruct(shape, kind)


def call(kernel, name, operands, places, outs, out_places, scratch, flops, moved, limit):
    spaces = {"s": pltpu.SMEM, "v": pltpu.VMEM, "a": pl.ANY, "h": pltpu.HBM}
    operands = [
        pltpu.with_memory_space_constraint(one, pltpu.HBM) if place == "h" else one
        for one, place in zip(operands, places)
    ]
    outs = [
        spaces[place](one.shape, one.dtype) if place in "hv" else one
        for one, place in zip(outs, out_places)
    ]
    return pl.pallas_call(
        kernel,
        out_shape=outs,
        in_specs=[pl.BlockSpec(memory_space=spaces[place]) for place in places],
        out_specs=[pl.BlockSpec(memory_space=spaces[place]) for place in out_places],
        scratch_shapes=scratch,
        name=name,
        compiler_params=pltpu.CompilerParams(vmem_limit_bytes=limit * 2**20),
        cost_estimate=pl.CostEstimate(flops=1, bytes_accessed=1, transcendentals=0),
    )(*operands)


def dot(left, right):
    return jnp.dot(left, right, preferred_element_type=f32)


def dot_t(left, right):
    return lax.dot_general(left, right, (((1,), (1,)), ((), ())), preferred_element_type=f32)


def col_sum(values):
    return jnp.sum(values, axis=0, keepdims=True)


def blank_edges(dst):
    blank = jnp.zeros((11, 16, LANES), bf16)
    dst[0] = blank
    dst[10] = blank
    dst[:, 0] = blank
    dst[:, 10] = blank


class Inside:
    def __init__(self, side):
        self.count = col_sum(side * side)
        self.masks = (None, side > 6.0, side > 8.0)

    def keep(self, ring, values):
        mask = self.masks[self.level(ring)]
        return values if mask is None else jnp.where(mask, values, 0.0)

    @staticmethod
    def level(ring):
        return 0 if ring < 5 else 1 if ring < 7 else 2

    def total(self, values_at):
        sums = [None, None, None]
        for row in range(9):
            for col in range(9):
                at = self.level(max(row, col))
                value = values_at(row, col)
                sums[at] = value if sums[at] is None else sums[at] + value
        return col_sum(sums[0] + self.keep(5, sums[1]) + self.keep(7, sums[2]))


def norm_stats(acc, inside):
    mean = inside.total(lambda row, col: acc[row, col]) / inside.count

    def squared(row, col):
        centred = acc[row, col] - mean
        return centred * centred

    return mean, lax.rsqrt(inside.total(squared) / inside.count + epsilon)


def sigmoid_of(values):
    return 0.5 * jnp.tanh(0.5 * values) + 0.5


def split_three(row):
    high = row.astype(bf16)
    rest = row - high.astype(f32)
    middle = rest.astype(bf16)
    low = (rest - middle.astype(f32)).astype(bf16)
    return [high, middle, low]


def pack_vectors(rows):
    pieces = [one.astype(f32) for row in rows for one in split_three(row)]
    pieces.append(jnp.zeros((16 - len(pieces), LANES), f32))
    return jnp.concatenate(pieces, axis=0).astype(bf16)


def unpack_vectors(block):
    wide = block.astype(f32)
    return [wide[3 * at : 3 * at + 1] + wide[3 * at + 1 : 3 * at + 2] + wide[3 * at + 2 : 3 * at + 3] for at in range(4)]


def pack_rows(ref, rows):
    ref[...] = jnp.concatenate(rows + [jnp.zeros((8 - len(rows), LANES), f32)], axis=0)


def turn_matrix(image_of_row):
    out_row = lax.broadcasted_iota(jnp.int32, (256, 256), 0)
    in_row = lax.broadcasted_iota(jnp.int32, (256, 256), 1)
    pixel_same = (out_row >> 4) == (in_row & 15)
    return jnp.where(pixel_same & ((out_row & 15) == image_of_row(in_row)), 1.0, 0.0).astype(bf16)


def split_weights(sc, matrix, vectors):
    def kernel(sc_ref, matrix_ref, vec_ref, for_x, for_y, sems):
        lane = pl.multiple_of(LANES * sc_ref[2], LANES)
        chosen = matrix_ref.at[:, pl.ds(lane, LANES)]

        def copies(target, first, at):
            return [
                pltpu.make_async_copy(
                    chosen.at[first + 640 * cut : first + 640 * cut + 640],
                    target.at[16 + 640 * cut : 656 + 640 * cut],
                    sems.at[at + cut],
                )
                for cut in range(4)
            ]

        along_x = copies(for_x, 0, 0)
        for copy in along_x:
            copy.start()
        small = pack_vectors([vec_ref[at : at + 1, pl.ds(lane, LANES)] for at in range(4)])
        for_x[0:16] = small
        for_y[0:16] = small
        for first, here in ((0, sc_ref[0] == 0), (2048, sc_ref[0] != 0)):

            @pl.when(here)
            def _():
                along_y = copies(for_y, first, 4)
                for copy in along_y:
                    copy.start()
                for copy in along_y:
                    copy.wait()

        for copy in along_x:
            copy.wait()

    return call(
        kernel, "split_weights", (sc, matrix, vectors), "shv", [struct((2576, LANES))] * 2, "vv",
        [pltpu.SemaphoreType.DMA((8,))], 0, 14_000_000, 20,
    )


def relay_weights(name, is_own, operands, first=None):
    def kernel(sc_ref, own_x, own_y, x_1, y_1, for_x, for_y, *more):
        chosen = is_own(sc_ref[0])
        for x_from, y_from, here in ((own_x, own_y, chosen), (x_1, y_1, jnp.logical_not(chosen))):

            @pl.when(here)
            def _():
                for_x[...] = y_from[272:2576]
                for_y[...] = x_from[0:2320]

        if more:
            more[0][...] = y_1[0:1296]
            more[1][...] = x_1[1296:2576]

    outs = [struct((2304, LANES)), struct((2320, LANES))]
    if first:
        outs += [struct((1296, LANES)), struct((1280, LANES))]
    return call(kernel, name, operands, "svvvv", outs, len(outs) * "v", [], 0, 14_000_000, 20)


def prepare_images(sc, pieces):
    def kernel(sc_ref, *refs):
        piece_refs, (out, side_out, held, sems) = refs[:8], refs[8:]
        core = sc_ref[2]
        copies = [
            pltpu.make_async_copy(ref, held.at[2 * at : 2 * at + 2], sems.at[at])
            for at, ref in enumerate(piece_refs)
        ]
        for copy in copies:
            copy.start()
        turn = turn_matrix(lambda r: ((r >> 4) + 8 * core) & 15)
        out[:, :, 0] = jnp.zeros((2, 2, 10, 16, LANES), bf16)
        out[:, :, :, 0] = jnp.zeros((2, 2, 10, 16, LANES), bf16)
        for copy in copies:
            copy.wait()

        def block(at):
            source = held[:, 16 * at : 16 * at + 16].reshape(256, LANES)
            return dot(turn, source).reshape(16, 16, LANES)

        last = block(20)
        side = last[4]
        side_out[...] = side
        masks = (None, 2.0 * side > 13.0, 2.0 * side > 17.0)
        for at in range(21):
            turned = last if at == 20 else block(at)
            for step in range(16 if at < 20 else 4):
                row, col = divmod(16 * at + step, 18)
                mask = masks[Inside.level(max(row, col) // 2)]
                kept = turned[step] if mask is None else jnp.where(mask, turned[step], 0.0)
                out[row % 2, col % 2, 1 + row // 2, 1 + col // 2] = kept.astype(bf16)

    outs = [struct((2, 2, 10, 10, 16, LANES)), struct((16, LANES), f32)]
    scratch = [pltpu.VMEM((16, 336, LANES), bf16), pltpu.SemaphoreType.DMA((8,))]
    return call(
        kernel, "prepare_images", (sc, *pieces), "s" + 8 * "h", outs, "vv", scratch,
        21 * 2 * 256**3, 8_000_000, 20,
    )


def prepare_cotangent(sc, pieces):
    def kernel(sc_ref, *refs):
        piece_refs, (out, held, sems) = refs[:2], refs[2:]
        core = sc_ref[2]
        copies = [
            pltpu.make_async_copy(ref, held.at[2 * at : 2 * at + 2], sems.at[at])
            for at, ref in enumerate(piece_refs)
        ]
        for copy in copies:
            copy.start()
        turn = turn_matrix(
            lambda r: (((r >> 5) & 1) ^ core) * 8 + 2 * (r >> 6) + ((r >> 4) & 1)
        )
        for copy in copies:
            copy.wait()
        for at in range(6):
            source = held[:, :, :, 16 * at : 16 * at + 16].reshape(256, LANES)
            turned = dot(turn, source).astype(bf16).reshape(16, 16, LANES)
            for step in range(16 if at < 5 else 1):
                row, col = divmod(16 * at + step, 9)
                out[row, col] = turned[step]

    scratch = [pltpu.VMEM((4, 2, 2, 96, LANES), bf16), pltpu.SemaphoreType.DMA((4,))]
    return call(
        kernel, "prepare_cotangent", (sc, *pieces), "saa", [struct(GRID)], "v", scratch,
        6 * 2 * 256**3, 2_000_000, 20,
    )[0]


def any_of(section, sections):
    chosen = section == sections[0]
    for other in sections[1:]:
        chosen = chosen | (section == other)
    return chosen


def stage_first(sc, side, fields, messages):
    def kernel(sc_ref, side_ref, field, own_x, x_1, y_1, top, bottom, hidden, short, zhat, zhat_p, stats, w, vec, acc, acc_p, short_now, out_sems):
        section = sc_ref[0]
        for at, whole in enumerate((own_x, x_1, y_1)):

            @pl.when(section == at)
            def _():
                w[...] = whole[16:2576]
                vec[...] = whole[0:16]

        @pl.when(section == 3)
        def _():
            w[0:1280] = top[16:1296]
            w[1280:2560] = bottom[...]
            vec[...] = top[0:16]

        outs = []
        for chunk in range(3):
            total = jnp.zeros((432, LANES), f32)
            for a in range(3):
                for b in range(3):
                    row_at, col_at = 3 * chunk + (0 if a == 0 else 1), 0 if b == 0 else 1
                    left = field[(a + 1) % 2, (b + 1) % 2, row_at : row_at + 3, col_at : col_at + 9]
                    at = LANES * (3 * a + b)
                    total = total + dot(left.reshape(432, LANES), w[at : at + LANES])
            span = slice(3 * chunk, 3 * chunk + 3)
            acc[span] = total.reshape(3, 9, 16, LANES)
            centre = field[0, 0, 3 * chunk + 1 : 3 * chunk + 4, 1:10].reshape(432, LANES)
            acc_p[span] = dot(centre, w[2304:2560]).reshape(3, 9, 16, LANES)
            for at, (source, target) in enumerate(((acc, zhat), (acc_p, zhat_p))):
                outs.append(
                    pltpu.make_async_copy(
                        source.at[span], target.at[span], out_sems.at[1 + 3 * at + chunk]
                    )
                )
                outs[-1].start()
        inside = Inside(side_ref[...])
        mean, scale = norm_stats(acc, inside)
        mean_p, scale_p = norm_stats(acc_p, inside)
        gain, gain_p, bias, bias_p = unpack_vectors(vec[...])
        for row in range(9):
            for col in range(9):
                ring = max(row, col)
                pre = (acc[row, col] - mean) * scale * gain + bias
                hidden[row, col] = inside.keep(ring, pre * sigmoid_of(pre)).astype(bf16)
                normed = (acc_p[row, col] - mean_p) * scale_p
                short_now[row, col] = inside.keep(ring, normed * gain_p + bias_p).astype(bf16)
            outs.append(pltpu.make_async_copy(short_now.at[row], short.at[row], out_sems.at[7 + row]))
            outs[-1].start()
        pack_rows(stats, [scale, gain, bias, mean, scale_p, gain_p, mean_p])
        for copy in outs:
            copy.wait()

    outs = [
        struct(GRID), struct(GRID), struct(GRID, f32), struct(GRID, f32), struct((8, LANES), f32),
        struct((2560, LANES)),
    ]
    scratch = [
        pltpu.VMEM((16, LANES), bf16), pltpu.VMEM(GRID, f32), pltpu.VMEM(GRID, f32),
        pltpu.VMEM(GRID, bf16), pltpu.SemaphoreType.DMA((16,)),
    ]
    return call(
        kernel, "stage_first", (sc, side, fields, *messages), "svv" + 5 * "v", outs, "vhhhvv",
        scratch, 2 * 1296 * 2560 * LANES, 8_000_000, 20,
    )


def fill_field(padded, source):
    blank_edges(padded)
    padded[1:10, 1:10] = source[...]


def fill_weights(part, section, core, messages, keep, send, vec):
    own_x, own_y, x_1, y_1, x_2, y_2 = messages
    upper = {1: {0: x_1, 1: own_x}, 2: {2: own_x, 3: x_1}, 3: {2: x_1, 3: own_x}}[part]
    lower = {1: {1: own_y, 3: y_1}, 2: {0: y_1, 2: own_y}, 3: {1: y_1, 3: own_y}}[part]
    far_upper = [section for section in range(4) if section not in upper]
    far_lower = [section for section in range(4) if section not in lower]
    entries = [((at,), ref, 16, 0) for at, ref in upper.items()] + [(far_upper, y_2, 16, 0)]
    entries += [((at,), ref, 272, 9) for at, ref in lower.items()] + [(far_lower, x_2, 0, 9)]
    for half in range(2):
        for sections, ref, first, block in entries:

            @pl.when((core == half) & any_of(section, sections))
            def _():
                for at in range(9):
                    tap, which = divmod(block + at, 2)
                    target = keep if which == half else send
                    start = first + LANES * at
                    target[LANES * tap : LANES * tap + LANES] = ref[start : start + LANES]
                if block == 0:
                    vec[...] = ref[0:16]


def stage_rest(part, sc, side, own, other, messages, short, cot=None, after=()):
    last = cot is not None
    extra = [one for one in (short, cot) if one is not None]

    def kernel(sc_ref, side_ref, own_ref, oth_ref, *refs):
        refs = list(refs)
        late_refs = [refs.pop(0) for _ in extra]
        weights = refs[0:6]
        refs = refs[6 + len(after) :]
        if last:
            dz, passed, out, sums = refs[:4]
            refs = refs[4:]
        else:
            hidden, zhat, stats = refs[:3]
            refs = refs[3:]
        w_keep, w_send, vec, padded, acc = refs[:5]
        grads, passed_now = refs[5:7] if last else (None, None)
        late, sems, out_sems = refs[-3:]
        short_ref = late.at[0] if short is not None else None
        cot_ref = late.at[1] if last else None
        section, core = sc_ref[0], sc_ref[2]
        late_loads = [
            pltpu.make_async_copy(ref, late.at[at], sems.at[at]) for at, ref in enumerate(late_refs)
        ]
        for copy in late_loads:
            copy.start()
        fill_weights(part, section, core, weights, w_keep, w_send, vec)
        fill_field(padded.at[0], own_ref)
        fill_field(padded.at[1], oth_ref)
        outs = []
        for chunk in range(3):
            total = jnp.zeros((432, LANES), f32)
            for a in range(3):
                for b in range(3):
                    for at in range(2):
                        left = padded[at, 3 * chunk + a : 3 * chunk + a + 3, b : b + 9]
                        from_row = LANES * (3 * a + b)
                        right = (w_keep, w_send)[at][from_row : from_row + LANES]
                        total = total + dot(left.reshape(432, LANES), right)
            acc[3 * chunk : 3 * chunk + 3] = total.reshape(3, 9, 16, LANES)
            if not last:
                outs.append(
                    pltpu.make_async_copy(
                        acc.at[3 * chunk : 3 * chunk + 3],
                        zhat.at[3 * chunk : 3 * chunk + 3],
                        out_sems.at[18 + chunk],
                    )
                )
                outs[-1].start()
        inside = Inside(side_ref[...])
        mean, scale = norm_stats(acc, inside)
        for copy in late_loads:
            copy.wait()
        gain, _, bias, _ = unpack_vectors(vec[...])
        if last:
            sums_now = [None, None]
        for row in range(9):
            for col in range(9):
                ring = max(row, col)
                normed = (acc[row, col] - mean) * scale
                if last:
                    acc[row, col] = normed
                pre = normed * gain + bias
                if short is not None:
                    pre = pre + short_ref[row, col].astype(f32)
                sigmoid = sigmoid_of(pre)
                target = out if last else hidden
                target[row, col] = inside.keep(ring, pre * sigmoid).astype(bf16)
                if last:
                    slope = sigmoid * (1.0 + pre * (1.0 - sigmoid))
                    grad = inside.keep(ring, cot_ref[row, col].astype(f32) * slope)
                    grads[row, col] = grad
                    passed_now[row, col] = grad.astype(bf16)
                    for at, value in enumerate((grad, grad * normed)):
                        sums_now[at] = value if sums_now[at] is None else sums_now[at] + value
            if last:
                outs.append(
                    pltpu.make_async_copy(passed_now.at[row], passed.at[row], out_sems.at[18 + row])
                )
                outs[-1].start()
        if last:
            bias_now, gain_now = col_sum(sums_now[0]), col_sum(sums_now[1])
            norm_back(dz, grads, acc, inside, gain * scale, bias_now, gain_now)
            pack_rows(sums, [gain_now, bias_now])
        else:
            pack_rows(stats, [scale, gain, bias, mean])
        for copy in outs:
            copy.wait()

    half = struct((2304, LANES))
    if last:
        outs, places = [struct(GRID), struct(GRID), struct(GRID), struct((8, LANES), f32)], "vhvv"
    else:
        outs, places = [struct(GRID), struct(GRID, f32), struct((8, LANES), f32)], "vhv"
    scratch = [
        pltpu.VMEM((16, LANES), bf16), pltpu.VMEM((2, 11, 11, 16, LANES), bf16), pltpu.VMEM(GRID, f32)
    ] + ([pltpu.VMEM(GRID, f32), pltpu.VMEM(GRID, bf16)] if last else [])
    scratch += [
        pltpu.VMEM((2, *GRID), bf16), pltpu.SemaphoreType.DMA((2,)), pltpu.SemaphoreType.DMA((27,)),
    ]
    return call(
        kernel, f"stage_{part}", (sc, side, own, other, *extra, *messages, *after),
        "svvv" + len(extra) * "a" + 6 * "v" + len(after) * "a", outs + [half, half], places + "vv", scratch,
        2 * 1296 * 4608 * LANES, 8_000_000, 20,
    )


def norm_back(dz, grads, zhat, inside, weight, bias_now, gain_now):
    constant, slope = weight * bias_now / inside.count, weight * gain_now / inside.count
    for row in range(9):
        for col in range(9):
            value = weight * grads[row, col] - (constant + slope * zhat[row, col])
            dz[row, col] = inside.keep(max(row, col), value).astype(bf16)


def stage_back(part, sc, side, dz_own, dz_other, w_own, w_other, zhat, stats, short=None, extra=None, proj=None):
    first = proj is not None
    optional = [one for one in (short, extra) if one is not None] + (list(proj) if first else [])

    def kernel(sc_ref, side_ref, stats_ref, dz_own_ref, dz_oth_ref, w_own_ref, w_oth_ref, zhat_ref, *refs):
        refs = list(refs)
        late_refs = [refs.pop(0) for one in (short, extra) if one is not None]
        if first:
            dyp_ref, zhat_p_ref = refs.pop(0), refs.pop(0)
        dz, sums = refs.pop(0), refs.pop(0)
        passed = refs.pop(0) if short is not None else None
        dz_p = refs.pop(0) if first else None
        padded, acc, held = refs[:3]
        held_p = refs[3] if first else None
        late = None if first else refs[3]
        sems = refs[-1]
        short_ref = late.at[0] if short is not None else None
        extra_ref = late.at[1] if extra is not None else None
        later = [pltpu.make_async_copy(zhat_ref, held, sems.at[4])]
        if first:
            later.append(pltpu.make_async_copy(zhat_p_ref, held_p, sems.at[5]))
        for at, ref in enumerate(late_refs):
            later.append(pltpu.make_async_copy(ref, late.at[at], sems.at[6 + at]))
        for copy in later:
            copy.start()
        fill_field(padded.at[0], dz_own_ref)
        fill_field(padded.at[1], dz_oth_ref)
        for chunk in range(3):
            total = jnp.zeros((432, LANES), f32)
            for a in range(3):
                for b in range(3):
                    for at in range(2):
                        row_at = 3 * chunk + 2 - a
                        left = padded[at, row_at : row_at + 3, 2 - b : 11 - b]
                        from_row = LANES * (3 * a + b)
                        right = (w_own_ref, w_oth_ref)[at][from_row : from_row + LANES]
                        total = total + dot_t(left.reshape(432, LANES), right)
            acc[3 * chunk : 3 * chunk + 3] = total.reshape(3, 9, 16, LANES)
        for copy in later:
            copy.wait()
        inside = Inside(side_ref[...])
        scale, gain, bias, mean, scale_p, gain_p, mean_p = [stats_ref[at : at + 1] for at in range(7)]
        sums_now = [None] * 4
        for row in range(9):
            for col in range(9):
                ring = max(row, col)
                normed = (held[row, col] - mean) * scale
                held[row, col] = normed
                pre = normed * gain + bias
                grad = acc[row, col]
                if extra is not None:
                    grad = grad + extra_ref[row, col].astype(f32)
                if short is not None:
                    pre = pre + short_ref[row, col].astype(f32)
                sigmoid = sigmoid_of(pre)
                slope = sigmoid * (1.0 + pre * (1.0 - sigmoid))
                grad = inside.keep(ring, grad.astype(bf16).astype(f32) * slope)
                acc[row, col] = grad
                if short is not None:
                    passed[row, col] = grad.astype(bf16)
                terms = [grad, grad * normed]
                if first:
                    grad_p = dyp_ref[row, col].astype(f32)
                    normed_p = (held_p[row, col] - mean_p) * scale_p
                    held_p[row, col] = normed_p
                    terms += [grad_p, grad_p * normed_p]
                for at, value in enumerate(terms):
                    sums_now[at] = value if sums_now[at] is None else sums_now[at] + value
        totals = [col_sum(value) for value in sums_now if value is not None]
        norm_back(dz, acc, held, inside, gain * scale, totals[0], totals[1])
        rows = [totals[1], totals[0]]
        if first:
            for row in range(9):
                for col in range(9):
                    acc[row, col] = dyp_ref[row, col].astype(f32)
            norm_back(dz_p, acc, held_p, inside, gain_p * scale_p, totals[2], totals[3])
            rows += [totals[3], totals[2]]
        pack_rows(sums, rows)

    outs, places = [struct(GRID), struct((8, LANES), f32)], "vv"
    if short is not None:
        outs, places = outs + [struct(GRID)], places + "v"
    if first:
        outs, places = outs + [struct(GRID)], places + "v"
    scratch = [
        pltpu.VMEM((2, 11, 11, 16, LANES), bf16), pltpu.VMEM(GRID, f32), pltpu.VMEM(GRID, f32)
    ] + [pltpu.VMEM(GRID, f32) if first else pltpu.VMEM((2, *GRID), bf16)]
    scratch += [pltpu.SemaphoreType.DMA((8,))]
    kinds = "h" * ((short is not None) + (extra is not None)) + ("vh" if first else "")
    return call(
        kernel, f"back_{part}",
        (sc, side, stats, dz_own, dz_other, w_own, w_other, zhat, *optional),
        "svvvvvvh" + kinds, outs, places, scratch, 2 * 1296 * 4608 * LANES, 10_000_000, 20,
    )


def pick_images(sc, *fields):
    def kernel(sc_ref, *refs):
        core = sc_ref[2]
        keep, give = refs[-2:]
        out_row = lax.broadcasted_iota(jnp.int32, (4, 96, 1296), 1)
        slot = lax.broadcasted_iota(jnp.int32, (4, 96, 1296), 0)
        in_row = lax.broadcasted_iota(jnp.int32, (4, 96, 1296), 2)
        image = 8 * ((slot >> 1) ^ core) + (slot & 1)
        pick = jnp.where(in_row == 16 * out_row + image, 1.0, 0.0).astype(bf16).reshape(384, 1296)
        for at, source in enumerate(refs[:-2]):
            chosen = dot(pick, source[...].reshape(1296, LANES)).astype(bf16).reshape(4, 96, LANES)
            keep[at] = chosen[0:2]
            give[at] = chosen[2:4]

    count = len(fields)
    return call(
        kernel, "pick_images", (sc, *fields), "s" + count * "v", 2 * [struct((count, 2, 96, LANES))],
        "vv", [], count * 2 * 384 * 1296 * LANES, 3_000_000, 20,
    )


def weight_rest(part, sc, own, other, dz, sums, tail=None):
    def kernel(sc_ref, own_ref, oth_ref, dz_ref, sums_ref, *refs):
        out, turned, padded = refs[-3:]
        if tail is not None:
            out[1168:1568] = refs[0][768:1168]
        zone, core = sc_ref[1], sc_ref[2]
        fill_field(padded, dz_ref)
        lane = pl.multiple_of(128 * (zone & 1), 128)
        is_own = (zone >> 1) == core

        @pl.when(is_own)
        def _():
            turned[...] = own_ref[:, :, :, pl.ds(lane, 128)].reshape(1296, 128).T

        @pl.when(jnp.logical_not(is_own))
        def _():
            turned[...] = oth_ref[:, :, :, pl.ds(lane, 128)].reshape(1296, 128).T

        left = turned[...]
        for a in range(3):
            for b in range(3):
                right = padded[2 - a : 11 - a, 2 - b : 11 - b].reshape(1296, LANES)
                at = 128 * (3 * a + b)
                out[at : at + 128] = dot(left, right).astype(bf16)
        blank = jnp.zeros((1, LANES), f32)
        out[1152:1168] = pack_vectors([sums_ref[0:1], blank, sums_ref[1:2], blank])

    scratch = [
        pltpu.VMEM((128, 1296), bf16), pltpu.VMEM((11, 11, 16, LANES), bf16)
    ]
    return call(
        kernel, f"weight_{part}", (sc, own, other, dz, sums) + (() if tail is None else (tail,)),
        "svvvv" + ("" if tail is None else "v"), [struct((1168 if tail is None else 1568, LANES))], "v",
        scratch, 2 * 1296 * 1152 * LANES, 3_000_000, 20,
    )[0]


def weight_first(sc, fields, dz, dz_p, sums):
    def kernel(sc_ref, field, dz_ref, dz_p_ref, sums_ref, out, turned, padded):
        zone = sc_ref[1]
        fill_field(padded, dz_ref)
        lane = pl.multiple_of(128 * (zone >> 1), 128)
        at = pl.multiple_of(64 * (zone & 1), 64)
        for phase in range(4):
            chosen = field[phase // 2, phase % 2, 1:10, 1:10, :, pl.ds(lane, 128)]
            turned[phase] = chosen.reshape(1296, 128).T
        for tap in range(10):
            if tap < 9:
                a, b = divmod(tap, 3)
                left = turned[2 * ((a + 1) % 2) + (b + 1) % 2, pl.ds(at, 64)]
                row_at, col_at = 2 if a == 0 else 1, 2 if b == 0 else 1
                right = padded[row_at : row_at + 9, col_at : col_at + 9].reshape(1296, LANES)
            else:
                left = turned[0, pl.ds(at, 64)]
                right = dz_p_ref[...].reshape(1296, LANES)
            out[64 * tap : 64 * tap + 64] = dot(left, right).astype(bf16)
        out[640:656] = pack_vectors([sums_ref[0:1], sums_ref[2:3], sums_ref[1:2], sums_ref[3:4]])

    scratch = [
        pltpu.VMEM((4, 128, 1296), bf16), pltpu.VMEM((11, 11, 16, LANES), bf16)
    ]
    return call(
        kernel, "weight_first", (sc, fields, dz, dz_p, sums), "svvvv", [struct((656, LANES))], "v",
        scratch, 2 * 1296 * 640 * LANES, 3_000_000, 20,
    )[0]


def image_back(sc, own, other, w_own, w_other):
    def kernel(sc_ref, own_all, oth_all, w_own_ref, w_oth_ref, out, block):
        for source, half in ((own_all, sc_ref[2]), (oth_all, 1 - sc_ref[2])):
            block[:, :, pl.ds(pl.multiple_of(LANES * half, LANES), LANES)] = source[2]
        own_ref, own_p_ref = own_all.at[0], own_all.at[1]
        oth_ref, oth_p_ref = oth_all.at[0], oth_all.at[1]
        row = lax.broadcasted_iota(jnp.int32, (192, 192), 0)
        col = lax.broadcasted_iota(jnp.int32, (192, 192), 1)
        pixel = jnp.where(row >= 96, row - 96, row)
        line = (pixel * 57) >> 9
        across = pixel - 9 * line
        shifted = {}
        for down in range(2):
            for right in range(2):
                if down + right == 0:
                    shifted[0, 0] = (
                        own_ref[...].reshape(192, LANES),
                        oth_ref[...].reshape(192, LANES),
                    )
                    continue
                fits = (pixel < 81) & (line + down < 9) & (across + right < 9)
                move = jnp.where(fits & (col == row + 9 * down + right), 1.0, 0.0).astype(bf16)
                shifted[down, right] = tuple(
                    dot(move, ref[...].reshape(192, LANES)).astype(bf16)
                    for ref in (own_ref, oth_ref)
                )
        phases = [jnp.zeros((192, LANES), f32) for _ in range(4)]
        for a in range(3):
            for b in range(3):
                at = 2 * ((a + 1) % 2) + (b + 1) % 2
                left = shifted[1 if a == 0 else 0, 1 if b == 0 else 0]
                rows = slice(LANES * (3 * a + b), LANES * (3 * a + b + 1))
                phases[at] = phases[at] + dot_t(left[0], w_own_ref[rows])
                phases[at] = phases[at] + dot_t(left[1], w_oth_ref[rows])
        phases[0] = phases[0] + dot_t(own_p_ref[...].reshape(192, LANES), w_own_ref[2304:2560])
        phases[0] = phases[0] + dot_t(oth_p_ref[...].reshape(192, LANES), w_oth_ref[2304:2560])
        joined = jnp.concatenate([phase.astype(bf16) for phase in phases], axis=0)
        out_row = lax.broadcasted_iota(jnp.int32, (336, 768), 0)
        in_row = lax.broadcasted_iota(jnp.int32, (336, 768), 1)
        line = (out_row * 3641) >> 16
        across = out_row - 18 * line
        source = (2 * (line & 1) + (across & 1)) * 192 + 9 * (line >> 1) + (across >> 1)
        for image in range(2):
            spread = jnp.where(
                (in_row == source + 96 * image) & (out_row < 324), 1.0, 0.0
            ).astype(bf16)
            out[image] = dot(spread, joined).astype(bf16)

    return call(
        kernel, "image_back", (sc, own, other, w_own, w_other), "svvvv",
        [struct((2, 336, LANES)), struct((2, 96, 2 * LANES))], "vv", [], 2 * 192 * 2560 * 512 + 4 * 336 * 768 * 256, 4_000_000, 20,
    )


def add_into(out, rows, sources, vector_rows):
    for at in range(0, rows, 64):
        total = sources[0][at : at + 64].astype(f32)
        for source in sources[1:]:
            total = total + source[at : at + 64].astype(f32)
        out[at : at + 64] = total.astype(bf16)
    totals = [unpack_vectors(source[rows : rows + 16]) for source in sources]
    sums = [sum(one[1:], one[0]) for one in zip(*totals)]
    out[vector_rows : vector_rows + 16] = pack_vectors(sums)


def add_pieces(part, one, two):
    rows = one.shape[0] - 16

    def kernel(one_ref, two_ref, out):
        add_into(out, rows, (one_ref, two_ref), rows)

    return call(
        kernel, f"add_{part}", (one, two), "vv", [struct(one.shape)], "v", [], 1, 1_000_000, 20
    )[0]


def add_two(three, two, came_three, came_two):
    def kernel(three_ref, two_ref, came_three_ref, came_two_ref, out_three, out_two):
        for at in range(0, 768, 64):
            span = slice(at, at + 64)
            total = three_ref[span].astype(f32) + came_three_ref[span].astype(f32)
            out_three[span] = total.astype(bf16)
        tails = (three_ref.at[768:1168], came_two_ref.at[1168:1568])
        add_into(out_three.at[768:1168], 384, tails, 384)
        add_into(out_two, 1152, (two_ref, came_two_ref), 1152)

    return call(
        kernel, "add_two", (three, two, came_three, came_two), "vvvv", [struct((1168, LANES))] * 2, "vv",
        [], 1, 1_000_000, 20,
    )


def own_piece(sc, groups, after):
    pieces = [piece for group in groups for piece in group]

    def kernel(sc_ref, *refs):
        out, used = refs[-1], 0
        for part, group in enumerate(groups):
            sources = refs[used : used + len(group)]
            used += len(group)
            rows = group[0].shape[0] - 16

            @pl.when(sc_ref[0] == part)
            def _():
                add_into(out, rows, sources, 1152)

    return call(
        kernel, "own_piece", (sc, *pieces, *after), "s" + len(pieces) * "v" + len(after) * "a",
        [struct((1168, LANES))], "v", [], 1, 1_000_000, 20,
    )[0]


def lay_out(sc, own, other):
    def kernel(sc_ref, *refs):
        pieces, (out, vectors, wide, out_sems) = refs[:12], refs[12:]
        section, zone, core = sc_ref[0], sc_ref[1], sc_ref[2]
        at_end = (zone == 0) | (zone == 3)
        is_first = section == 0
        for tap in range(9):
            slot = tap % 3
            leaving = [
                pltpu.make_async_copy(
                    wide.at[slot, 128 * cut : 128 * cut + 128],
                    out.at[512 * tap + 128 * cut : 512 * tap + 128 * cut + 128],
                    out_sems.at[slot, cut],
                )
                for cut in range(4)
            ]
            if tap >= 3:
                for copy in leaving:
                    copy.wait()

            def place(which, row_of, rows, first):
                origin = zone ^ (0, 1, 2, 3, 2, 3)[which]
                row = pl.multiple_of(row_of(origin), rows)
                for half in range(2):
                    lane = pl.multiple_of(LANES * (core ^ half), LANES)
                    value = jnp.zeros((rows, LANES), f32)
                    if first + rows <= 1152:
                        value = pieces[which + 6 * half][first : first + rows].astype(f32)
                    wide[slot, pl.ds(row, rows), pl.ds(lane, LANES)] = value

            for kind, chosen in ((0, at_end), (1, jnp.logical_not(at_end))):
                used = (0, 1, 4, 5) if kind == 0 else (0, 1, 2, 3)

                @pl.when(chosen & jnp.logical_not(is_first))
                def _():
                    for which in used:
                        place(which, lambda origin: 128 * origin, 128, 128 * tap)

                @pl.when(chosen & is_first)
                def _():
                    for part in range(2):
                        start = 64 * (2 * tap + part)
                        for which in used:
                            place(
                                which,
                                lambda origin: 256 * part + 64 * origin,
                                64,
                                start if start < 640 else 1152,
                            )

            for copy in leaving:
                copy.start()
        for half in range(2):
            rows = unpack_vectors(pieces[6 * half][1152:1168])
            lane = pl.multiple_of(LANES * (core ^ half), LANES)
            vectors[:, pl.ds(lane, LANES)] = jnp.concatenate(rows, axis=0)
        for slot in range(3):
            for cut in range(4):
                pltpu.make_async_copy(
                    wide.at[slot, 0:128], out.at[0:128], out_sems.at[slot, cut]
                ).wait()

    return call(
        kernel, "lay_out", (sc, *own, *other), "s" + 12 * "v", [struct((4608, 512), f32), struct((4, 512), f32)], "hv",
        [pltpu.VMEM((3, 512, 512), f32), pltpu.SemaphoreType.DMA((3, 4))], 0, 15_000_000, 20,
    )


def half_of(value, half):
    return lax.dynamic_slice_in_dim(value, LANES * half, LANES, axis=value.ndim - 1)


def chip_body(images, res_ids, weights, bn_gain, bn_bias, cotangent):
    section = lax.axis_index("section")
    position = lax.axis_index("dp")
    zone, core = position // 2, position % 2
    sc = jnp.stack([section, zone, core, core]).astype(jnp.int32)

    def after(value, *tokens):
        return lax.optimization_barrier((value, *tokens))[0]

    own = split_weights(sc, weights[0], jnp.concatenate([bn_gain[0], bn_bias[0]], axis=0))
    x_1 = flip(own[0], "section", 1)
    y_1 = flip(own[1], "section", 2)

    level = lax.dynamic_index_in_dim(res_ids, section, 0, keepdims=False)
    side_own = (9 - 2 * (2 - level)).astype(f32)
    tail = jnp.broadcast_to(side_own[:, None, None], (2, 12, 256)).astype(bf16)
    image_own = jnp.concatenate([after(images, own[0])[0].reshape(2, 324, 256), tail], axis=1)
    pieces = [image_own] + [flip(image_own, "dp", 2 * at) for at in range(1, 4)]
    pieces += [flip(piece, "dp", 1) for piece in pieces]
    cot_own = after(cotangent, image_own)[0].reshape(2, 81, 512)
    cot_pair = jnp.stack([half_of(cot_own, core), flip(half_of(cot_own, 1 - core), "dp", 1)])
    cot_pair = jnp.pad(cot_pair, ((0, 0), (0, 0), (0, 15), (0, 0)))
    cot_near = jnp.stack([cot_pair, flip(cot_pair, "dp", 2)])
    cot_pieces = (cot_near, flip(cot_near, "dp", 4))
    for_x, for_y, top, bottom = relay_weights(
        "relay_2", lambda at: (at == 1) | (at == 2), (sc, *own, x_1, y_1), True
    )
    top = flip(top, "section", 1, lambda i: i == 2)
    bottom = flip(bottom, "section", 2, lambda i: i == 1)
    fields, side = prepare_images(after(sc, for_x), pieces)
    x_2 = flip(for_x, "section", 1)
    y_2 = flip(for_y, "section", 2)
    hidden_one, short_one, zhat_0, zhat_p, stats_0, w_first = stage_first(
        sc, side, after(fields, for_x), (own[0], x_1, y_1, top, bottom)
    )
    hidden_one_other = flip(hidden_one, "dp", 1)
    w_first_other = flip(w_first, "dp", 1)
    for_x, for_y = relay_weights("relay_3", lambda at: at == 3, (after(sc, stats_0), *own, x_1, y_1))
    x_3 = flip(for_x, "section", 1, lambda i: i in (1, 3))
    y_3 = flip(for_y, "section", 2, lambda i: i in (2, 3))
    messages = (*own, x_1, y_1, x_2, y_2)
    block_one, zhat_1, stats_1, keep_1, send_1 = stage_rest(
        1, sc, side, hidden_one, hidden_one_other, messages, short_one, after=cot_pieces
    )
    block_one_other = flip(block_one, "dp", 1)
    other_1 = flip(send_1, "dp", 1)
    cot = prepare_cotangent(sc, after(cot_pieces, stats_1))
    hidden_two, zhat_2, stats_2, keep_2, send_2 = stage_rest(
        2, sc, side, block_one, block_one_other, messages, None, after=(x_3, y_3, cot)
    )
    hidden_two_other = flip(hidden_two, "dp", 1)
    other_2 = flip(send_2, "dp", 1)
    messages = (*own, x_1, y_1, x_3, y_3)
    dz_3, passed, out, sums_3, keep_3, send_3 = stage_rest(
        3, sc, side, hidden_two, hidden_two_other, messages, block_one, cot
    )
    other_3 = flip(send_3, "dp", 1)
    dz_3_other = flip(dz_3, "dp", 1)

    def to_pair(part, piece):
        return flip(piece, "section", 2, lambda i: i ^ 2 in (part, part ^ 1))

    def to_owner(part, piece):
        return flip(piece, "section", 1, lambda i: i ^ 1 == part)

    piece_3 = weight_rest(3, sc, hidden_two, hidden_two_other, dz_3, sums_3)
    came_3 = to_pair(3, piece_3[0:768])
    dz_2, sums_2 = stage_back(
        2, sc, side, after(dz_3, piece_3), dz_3_other, keep_3, other_3, zhat_2, stats_2
    )
    dz_2_other = flip(dz_2, "dp", 1)
    piece_2 = weight_rest(2, sc, block_one, block_one_other, dz_2, sums_2, piece_3)
    came_2 = to_pair(2, piece_2)
    dz_1, sums_1, short_grad = stage_back(
        1, sc, side, after(dz_2, piece_2), dz_2_other, keep_2, other_2, zhat_1, stats_1, short_one,
        passed,
    )
    dz_1_other = flip(dz_1, "dp", 1)
    piece_1 = weight_rest(
        1, sc, hidden_one, hidden_one_other, after(dz_1, came_3), sums_1
    )
    came_1 = to_pair(1, piece_1)
    dz_0, sums_0, dz_p = stage_back(
        0, sc, side, after(dz_1, piece_1), dz_1_other, keep_1, other_1, zhat_0, stats_0,
        proj=(short_grad, zhat_p),
    )
    piece_0 = weight_first(sc, fields, dz_0, dz_p, sums_0)
    came_0 = to_pair(0, piece_0)
    sum_3, sum_2 = add_two(after(piece_3, piece_0), piece_2, came_3, came_2)
    last_3 = to_owner(3, sum_3)
    last_2 = to_owner(2, sum_2)
    sum_1 = add_pieces(1, after(piece_1, sum_2), came_1)
    last_1 = to_owner(1, sum_1)
    sum_0 = add_pieces(0, after(piece_0, sum_1), came_0)
    last_0 = to_owner(0, sum_0)
    keep, give = pick_images(sc, *after((dz_0, dz_p, out), sum_0))
    image_raw, block_output = image_back(sc, keep, flip(give, "dp", 1), w_first, w_first_other)
    block_output = block_output[:, 0:81]
    rows = jnp.arange(18, dtype=jnp.int32)
    inner_rows = (rows < 2 * (9 - 2 * (2 - level))[:, None]).astype(bf16)
    mask_in = inner_rows[:, :, None] * inner_rows[:, None, :]
    image_grad = image_raw[:, 0:324].reshape(2, 18, 18, 256) * mask_in[..., None]
    total = own_piece(
        sc, [(sum_0, last_0), (sum_1, last_1), (sum_2, last_2), (sum_3, last_3)],
        (image_raw,),
    )
    from_far = flip(total, "dp", 4, lambda i: i // 2 in (0, 3))
    from_near = flip(total, "dp", 2)
    from_middle = flip(total, "dp", 6, lambda i: i // 2 in (1, 2))
    from_end = flip(total, "dp", 4, lambda i: i // 2 in (1, 2))
    relayed = flip(from_far, "dp", 2, lambda i: i // 2 in (1, 2))
    gathered = [total, from_near, from_far, from_middle, from_end, relayed]
    weight_grad, vectors = lay_out(sc, gathered, [flip(piece, "dp", 1) for piece in gathered])

    return (
        block_output.reshape(1, 2, 9, 9, 512),
        image_grad[None],
        weight_grad[None],
        vectors[None, 0:2],
        vectors[None, 2:4],
    )


def solution(mesh):
    placed = (
        P("section", "dp", None, None, None),
        P(None, "dp"),
        P("section", None, None),
        P("section", None, None),
        P("section", None, None),
        P("section", "dp", None, None, None),
    )
    on_chip = mesh.shape["section"] == 4 and mesh.shape["dp"] == 8
    return jax.shard_map(
        chip_body if on_chip else pipeline_body,
        mesh=mesh,
        in_specs=placed,
        out_specs=(
            P("section", "dp", None, None, None),
            P("section", "dp", None, None, None),
            P("section", None, None),
            P("section", None, None),
            P("section", None, None),
        ),
        check_vma=False,
    )
```

```python
import jax
import jax.numpy as jnp
from jax import lax
from jax.experimental import pallas as pl
from jax.experimental.pallas import tpu as pltpu
from jax.sharding import PartitionSpec as P

epsilon = 1e-05


def passed_along(value, axis, steps):
    count = lax.axis_size(axis)
    leading, last = (max(0, -steps), min(count, count - steps))
    return lax.ppermute(value, axis, [(source, source + steps) for source in range(leading, last)])


def regions(levels, half_side):
    inner_side = half_side - 2 * (2 - levels)
    small_rows = jnp.arange(half_side, dtype=jnp.int32)
    large_rows = jnp.arange(2 * half_side, dtype=jnp.int32)
    inner_mask = (small_rows < inner_side[..., None]).astype(jnp.float32)
    outer_mask = (large_rows < 2 * inner_side[..., None]).astype(jnp.float32)
    return (
        outer_mask[..., :, None] * outer_mask[..., None, :],
        inner_mask[..., :, None] * inner_mask[..., None, :],
    )


def patches(field_in, stride, half_side):
    padded = jnp.pad(field_in, ((0, 0), (1, 1), (1, 1), (0, 0)))
    pieces = [
        padded[
            :,
            row_at : row_at + stride * half_side : stride,
            col_at : col_at + stride * half_side : stride,
            :,
        ]
        for row_at in range(3)
        for col_at in range(3)
    ]
    joined = jnp.concatenate(pieces, axis=-1)
    return joined.reshape(-1, joined.shape[-1])


def contract_rows(left_side, right_side):
    return lax.dot_general(
        left_side, right_side, (((0,), (0,)), ((), ())), preferred_element_type=jnp.float32
    )


def contract_cols(left_side, right_side):
    return lax.dot_general(
        left_side, right_side, (((1,), (1,)), ((), ())), preferred_element_type=jnp.float32
    )


def silu_slope(values):
    sigmoid = jax.nn.sigmoid(values)
    return sigmoid * (1.0 + values * (1.0 - sigmoid))


def spread_taps(tap_grads, image_count, half_side, channels):
    tap_grid = tap_grads.reshape(image_count, half_side, half_side, 9, channels)
    empty_phase = jnp.zeros((image_count, half_side + 1, half_side + 1, channels), jnp.float32)
    phases = [[empty_phase, empty_phase], [empty_phase, empty_phase]]
    for row_at in range(3):
        for col_at in range(3):
            tap_piece = tap_grid[:, :, :, 3 * row_at + col_at, :]
            top_pad = 1 if row_at == 2 else 0
            left_pad = 1 if col_at == 2 else 0
            placed = jnp.pad(
                tap_piece, ((0, 0), (top_pad, 1 - top_pad), (left_pad, 1 - left_pad), (0, 0))
            )
            phases[row_at % 2][col_at % 2] = phases[row_at % 2][col_at % 2] + placed
    row_phases = [jnp.stack([phases[parity][0], phases[parity][1]], axis=3) for parity in range(2)]
    alternated = jnp.stack(row_phases, axis=2).reshape(
        image_count, 2 * half_side + 2, 2 * half_side + 2, channels
    )
    return alternated[:, 1 : 2 * half_side + 1, 1 : 2 * half_side + 1, :]


def keep_slot(buffer_all, new_value, slot_at, keep_flag):
    current = lax.dynamic_index_in_dim(buffer_all, slot_at, 0, keepdims=False)
    return lax.dynamic_update_index_in_dim(
        buffer_all, jnp.where(keep_flag, new_value, current), slot_at, 0
    )


def pipeline_body(images, res_ids, weights, bn_gain, bn_bias, cotangent):
    sections = lax.axis_size("section")
    last_section = sections - 1
    position = lax.axis_index("section")
    micro_count = res_ids.shape[0]
    image_count = images.shape[1]
    half_side = cotangent.shape[2]
    channels = weights.shape[2]
    in_channels = images.shape[4]
    pixel_rows = image_count * half_side * half_side
    taps_in = 9 * in_channels
    matrix = weights[0]
    gain_rows = bn_gain[0]
    bias_rows = bn_bias[0]
    is_first = position == 0
    adds_short = (position == 1) | (position == 3)
    passes_short = position == 2
    makes_short = position == 1
    back_matrix = jnp.transpose(matrix.reshape(9, channels, channels)[::-1], (0, 2, 1)).reshape(
        9 * channels, channels
    )
    mask_in_all, mask_out_all = regions(res_ids, half_side)
    act_shape = (image_count, half_side, half_side, channels)
    zero_pixels = jnp.zeros((pixel_rows, channels), jnp.float32)
    zero_input = jnp.zeros((image_count, 2 * half_side, 2 * half_side, in_channels), jnp.float32)
    zero_weight = jnp.zeros((9 * channels, channels), jnp.float32)
    own_images = images[0]
    gathered = [own_images]
    for source in range(1, micro_count):
        gathered.append(passed_along(own_images, "section", -source))
    section_inputs = jnp.stack(gathered)
    own_cot = cotangent[0]
    arrived = []
    for source in range(micro_count):
        if source == last_section:
            arrived.append(own_cot)
        else:
            arrived.append(passed_along(own_cot, "section", last_section - source))
    cot_all = jnp.stack(arrived)

    def conv_first(prev_act, first_in):
        columns = patches(first_in, 2, half_side)
        main_out = jnp.dot(columns, matrix[:taps_in], preferred_element_type=jnp.float32)
        proj_out = jnp.dot(
            columns[:, 4 * in_channels : 5 * in_channels],
            matrix[taps_in : taps_in + in_channels],
            preferred_element_type=jnp.float32,
        )
        return jnp.stack([main_out, proj_out])

    def conv_rest(prev_act, first_in):
        columns = patches(prev_act, 1, half_side)
        return jnp.stack(
            [jnp.dot(columns, matrix, preferred_element_type=jnp.float32), zero_pixels]
        )

    def conv_spare(prev_act, first_in):
        return jnp.stack([zero_pixels, zero_pixels])

    def back_first(grad_conv, prev_act, first_in):
        columns = patches(first_in, 2, half_side)
        centre = columns[:, 4 * in_channels : 5 * in_channels]
        main_grad = contract_rows(columns, grad_conv[0])
        proj_grad = contract_rows(centre, grad_conv[1])
        filler = jnp.zeros((9 * channels - taps_in - in_channels, channels), jnp.float32)
        weight_now = jnp.concatenate([main_grad, proj_grad, filler], axis=0)
        tap_grads = contract_cols(grad_conv[0], matrix[:taps_in])
        centre_grad = contract_cols(grad_conv[1], matrix[taps_in : taps_in + in_channels])
        tap_grads = tap_grads + jnp.pad(centre_grad, ((0, 0), (4 * in_channels, 4 * in_channels)))
        return (
            weight_now,
            zero_pixels,
            spread_taps(tap_grads, image_count, half_side, in_channels),
        )

    def back_rest(grad_conv, prev_act, first_in):
        columns = patches(prev_act, 1, half_side)
        weight_now = contract_rows(columns, grad_conv[0])
        grad_image = grad_conv[0].reshape(act_shape)
        prev_grad = jnp.dot(
            patches(grad_image, 1, half_side), back_matrix, preferred_element_type=jnp.float32
        )
        return (weight_now, prev_grad, zero_input)

    def back_spare(grad_conv, prev_act, first_in):
        return (zero_weight, zero_pixels, zero_input)

    def finish(conv_out, mean_rows, scale_rows, flat_mask, short_in):
        normed = (conv_out - mean_rows[:, None, :]) * scale_rows[:, None, :] * gain_rows[
            :, None, :
        ] + bias_rows[:, None, :]
        pre_act = normed[0] + jnp.where(adds_short, short_in, 0.0)
        activated = jax.nn.silu(pre_act) * flat_mask[:, None]
        proj_short = normed[1] * flat_mask[:, None]
        short_out = jnp.where(is_first, proj_short, jnp.where(makes_short, activated, short_in))
        return (pre_act, activated, short_out)

    empty_act = jnp.zeros(act_shape, jnp.bfloat16)
    recv_act = empty_act
    recv_short = empty_act
    saved_act = jnp.zeros((micro_count,) + act_shape, jnp.bfloat16)
    saved_short = saved_act
    saved_final = saved_act
    saved_mean = jnp.zeros((micro_count, 2, channels), jnp.float32)
    saved_scale = saved_mean
    saved_total = jnp.zeros((micro_count,), jnp.float32)
    sweep_len = micro_count + last_section
    for tick_at in range(sweep_len):
        slot_raw = tick_at - position
        is_valid = (slot_raw >= 0) & (slot_raw < micro_count)
        slot_at = jnp.clip(slot_raw, 0, micro_count - 1)
        flat_mask = mask_out_all[slot_at].reshape(-1) * is_valid.astype(jnp.float32)
        first_in = section_inputs[slot_at] * mask_in_all[slot_at][..., None].astype(jnp.bfloat16)
        branch = jnp.where(is_valid, jnp.where(is_first, 0, 1), 2).astype(jnp.int32)
        conv_out = lax.switch(branch, [conv_first, conv_rest, conv_spare], recv_act, first_in)
        local_total = jnp.sum(flat_mask)
        weighted = conv_out * flat_mask[None, :, None]
        grand_total, sum_rows = lax.psum((local_total, jnp.sum(weighted, axis=1)), "dp")
        grand_total = jnp.maximum(grand_total, 1.0)
        statistics_mean_rows = sum_rows / grand_total
        centred = conv_out - statistics_mean_rows[:, None, :]
        variance = (
            lax.psum(jnp.sum(centred * centred * flat_mask[None, :, None], axis=1), "dp")
            / grand_total
        )
        grand_total, mean_rows, scale_rows = (
            grand_total,
            statistics_mean_rows,
            lax.rsqrt(variance + epsilon),
        )
        short_in = recv_short.reshape(pixel_rows, channels).astype(jnp.float32)
        pre_act, activated, short_out = finish(conv_out, mean_rows, scale_rows, flat_mask, short_in)
        act_low = activated.astype(jnp.bfloat16).reshape(act_shape)
        short_low = short_out.astype(jnp.bfloat16).reshape(act_shape)
        saved_act = keep_slot(saved_act, recv_act, slot_at, is_valid)
        saved_short = keep_slot(saved_short, recv_short, slot_at, is_valid)
        saved_mean = keep_slot(saved_mean, mean_rows, slot_at, is_valid)
        saved_scale = keep_slot(saved_scale, scale_rows, slot_at, is_valid)
        saved_total = keep_slot(saved_total, grand_total, slot_at, is_valid)
        saved_final = keep_slot(
            saved_final, act_low, slot_at, is_valid & (position == last_section)
        )
        if tick_at + 1 < sweep_len:
            recv_act, recv_short = passed_along((act_low, short_low), "section", 1)
    grad_act = empty_act
    grad_short = empty_act
    weight_acc = zero_weight
    gain_acc = jnp.zeros((2, channels), jnp.float32)
    bias_acc = gain_acc
    saved_dx = jnp.zeros(
        (micro_count, image_count, 2 * half_side, 2 * half_side, in_channels), jnp.bfloat16
    )
    for tick_at in range(sweep_len):
        slot_raw = tick_at - (last_section - position)
        is_valid = (slot_raw >= 0) & (slot_raw < micro_count)
        slot_at = jnp.clip(slot_raw, 0, micro_count - 1)
        flat_mask = mask_out_all[slot_at].reshape(-1) * is_valid.astype(jnp.float32)
        first_in = section_inputs[slot_at] * mask_in_all[slot_at][..., None].astype(jnp.bfloat16)
        branch = jnp.where(is_valid, jnp.where(is_first, 0, 1), 2).astype(jnp.int32)
        prev_act = saved_act[slot_at]
        conv_out = lax.switch(branch, [conv_first, conv_rest, conv_spare], prev_act, first_in)
        mean_rows = saved_mean[slot_at]
        scale_rows = saved_scale[slot_at]
        valid_total = saved_total[slot_at]
        short_in = saved_short[slot_at].reshape(pixel_rows, channels).astype(jnp.float32)
        pre_act, activated, short_out = finish(conv_out, mean_rows, scale_rows, flat_mask, short_in)
        from_act = (
            jnp.where(position == last_section, cot_all[slot_at], grad_act)
            .reshape(pixel_rows, channels)
            .astype(jnp.float32)
        )
        from_short = grad_short.reshape(pixel_rows, channels).astype(jnp.float32)
        slope = silu_slope(pre_act) * flat_mask[:, None]
        grad_pre = (from_act + jnp.where(adds_short, from_short, 0.0)) * slope
        grad_proj = jnp.where(is_first, from_short * flat_mask[:, None], 0.0)
        grad_normed = jnp.stack([grad_pre, grad_proj])
        normalized = (conv_out - mean_rows[:, None, :]) * scale_rows[:, None, :]
        bias_now, gain_now = lax.psum(
            (jnp.sum(grad_normed, axis=1), jnp.sum(grad_normed * normalized, axis=1)), "dp"
        )
        bias_acc = bias_acc + bias_now
        gain_acc = gain_acc + gain_now
        grad_conv = (
            flat_mask[None, :, None]
            * gain_rows[:, None, :]
            * scale_rows[:, None, :]
            * (
                grad_normed
                - (bias_now[:, None, :] + normalized * gain_now[:, None, :]) / valid_total
            )
        )
        grad_conv = grad_conv.astype(jnp.bfloat16)
        weight_now, prev_grad, input_grad = lax.switch(
            branch, [back_first, back_rest, back_spare], grad_conv, prev_act, first_in
        )
        weight_acc = weight_acc + weight_now
        masked_input = (input_grad * mask_in_all[slot_at][..., None]).astype(jnp.bfloat16)
        saved_dx = keep_slot(saved_dx, masked_input, slot_at, is_valid & is_first)
        send_act = (
            (prev_grad + jnp.where(passes_short, from_short, 0.0))
            .astype(jnp.bfloat16)
            .reshape(act_shape)
        )
        send_short = jnp.where(adds_short, grad_pre, 0.0).astype(jnp.bfloat16).reshape(act_shape)
        if tick_at + 1 < sweep_len:
            grad_act, grad_short = passed_along((send_act, send_short), "section", -1)
    weight_total = lax.psum(weight_acc, "dp")
    result = saved_final[last_section]
    for source in range(last_section):
        arrived_piece = passed_along(saved_final[source], "section", source - last_section)
        result = jnp.where(position == source, arrived_piece, result)
    grad_result = saved_dx[0]
    for source in range(1, micro_count):
        arrived_piece = passed_along(saved_dx[source], "section", source)
        grad_result = jnp.where(position == source, arrived_piece, grad_result)
    return (result[None], grad_result[None], weight_total[None], gain_acc[None], bias_acc[None])


f32, bf16 = jnp.float32, jnp.bfloat16
LANES = 256
GRID = (9, 9, 16, LANES)


def flip(value, axis, mask, senders=None):
    count = lax.axis_size(axis)
    pairs = [(i, i ^ mask) for i in range(count) if senders is None or senders(i)]
    return lax.ppermute(value, axis, pairs)


def struct(shape, kind=bf16):
    return jax.ShapeDtypeStruct(shape, kind)


def call(kernel, name, operands, places, outs, out_places, scratch, flops, moved, limit):
    spaces = {"s": pltpu.SMEM, "v": pltpu.VMEM, "a": pl.ANY, "h": pltpu.HBM}
    operands = [
        pltpu.with_memory_space_constraint(one, pltpu.HBM) if place == "h" else one
        for one, place in zip(operands, places)
    ]
    outs = [
        spaces[place](one.shape, one.dtype) if place in "hv" else one
        for one, place in zip(outs, out_places)
    ]
    return pl.pallas_call(
        kernel,
        out_shape=outs,
        in_specs=[pl.BlockSpec(memory_space=spaces[place]) for place in places],
        out_specs=[pl.BlockSpec(memory_space=spaces[place]) for place in out_places],
        scratch_shapes=scratch,
        name=name,
        compiler_params=pltpu.CompilerParams(vmem_limit_bytes=limit * 2**20),
        cost_estimate=pl.CostEstimate(flops=1, bytes_accessed=1, transcendentals=0),
    )(*operands)


def dot(left, right):
    return jnp.dot(left, right, preferred_element_type=f32)


def dot_t(left, right):
    return lax.dot_general(left, right, (((1,), (1,)), ((), ())), preferred_element_type=f32)


def col_sum(values):
    return jnp.sum(values, axis=0, keepdims=True)


def blank_edges(dst):
    blank = jnp.zeros((11, 16, LANES), bf16)
    dst[0] = blank
    dst[10] = blank
    dst[:, 0] = blank
    dst[:, 10] = blank


class Inside:
    def __init__(self, side):
        self.count = col_sum(side * side)
        self.masks = (None, side > 6.0, side > 8.0)

    def keep(self, ring, values):
        mask = self.masks[self.level(ring)]
        return values if mask is None else jnp.where(mask, values, 0.0)

    @staticmethod
    def level(ring):
        return 0 if ring < 5 else 1 if ring < 7 else 2

    def total(self, values_at):
        sums = [None, None, None]
        for row in range(9):
            for col in range(9):
                at = self.level(max(row, col))
                value = values_at(row, col)
                sums[at] = value if sums[at] is None else sums[at] + value
        return col_sum(sums[0] + self.keep(5, sums[1]) + self.keep(7, sums[2]))


def norm_stats(acc, inside):
    mean = inside.total(lambda row, col: acc[row, col]) / inside.count

    def squared(row, col):
        centred = acc[row, col] - mean
        return centred * centred

    return mean, lax.rsqrt(inside.total(squared) / inside.count + epsilon)


def sigmoid_of(values):
    return 0.5 * jnp.tanh(0.5 * values) + 0.5


def split_three(row):
    high = row.astype(bf16)
    rest = row - high.astype(f32)
    middle = rest.astype(bf16)
    low = (rest - middle.astype(f32)).astype(bf16)
    return [high, middle, low]


def pack_vectors(rows):
    pieces = [one.astype(f32) for row in rows for one in split_three(row)]
    pieces.append(jnp.zeros((16 - len(pieces), LANES), f32))
    return jnp.concatenate(pieces, axis=0).astype(bf16)


def unpack_vectors(block):
    wide = block.astype(f32)
    return [wide[3 * at : 3 * at + 1] + wide[3 * at + 1 : 3 * at + 2] + wide[3 * at + 2 : 3 * at + 3] for at in range(4)]


def pack_rows(ref, rows):
    ref[...] = jnp.concatenate(rows + [jnp.zeros((8 - len(rows), LANES), f32)], axis=0)


def turn_matrix(image_of_row):
    out_row = lax.broadcasted_iota(jnp.int32, (256, 256), 0)
    in_row = lax.broadcasted_iota(jnp.int32, (256, 256), 1)
    pixel_same = (out_row >> 4) == (in_row & 15)
    return jnp.where(pixel_same & ((out_row & 15) == image_of_row(in_row)), 1.0, 0.0).astype(bf16)


def split_weights(sc, matrix, vectors):
    def kernel(sc_ref, matrix_ref, vec_ref, for_x, for_y, sems):
        lane = pl.multiple_of(LANES * sc_ref[2], LANES)
        chosen = matrix_ref.at[:, pl.ds(lane, LANES)]

        def copies(target, first, at):
            return [
                pltpu.make_async_copy(
                    chosen.at[first + 640 * cut : first + 640 * cut + 640],
                    target.at[16 + 640 * cut : 656 + 640 * cut],
                    sems.at[at + cut],
                )
                for cut in range(4)
            ]

        along_x = copies(for_x, 0, 0)
        for copy in along_x:
            copy.start()
        small = pack_vectors([vec_ref[at : at + 1, pl.ds(lane, LANES)] for at in range(4)])
        for_x[0:16] = small
        for_y[0:16] = small
        for first, here in ((0, sc_ref[0] == 0), (2048, sc_ref[0] != 0)):

            @pl.when(here)
            def _():
                along_y = copies(for_y, first, 4)
                for copy in along_y:
                    copy.start()
                for copy in along_y:
                    copy.wait()

        for copy in along_x:
            copy.wait()

    return call(
        kernel, "split_weights", (sc, matrix, vectors), "shv", [struct((2576, LANES))] * 2, "vv",
        [pltpu.SemaphoreType.DMA((8,))], 0, 14_000_000, 20,
    )


def relay_weights(name, is_own, operands, first=None):
    def kernel(sc_ref, own_x, own_y, x_1, y_1, for_x, for_y, *more):
        chosen = is_own(sc_ref[0])
        for x_from, y_from, here in ((own_x, own_y, chosen), (x_1, y_1, jnp.logical_not(chosen))):

            @pl.when(here)
            def _():
                for_x[...] = y_from[272:2576]
                for_y[...] = x_from[0:2320]

        if more:
            more[0][...] = y_1[0:1296]
            more[1][...] = x_1[1296:2576]

    outs = [struct((2304, LANES)), struct((2320, LANES))]
    if first:
        outs += [struct((1296, LANES)), struct((1280, LANES))]
    return call(kernel, name, operands, "svvvv", outs, len(outs) * "v", [], 0, 14_000_000, 20)


def prepare_images(sc, pieces):
    def kernel(sc_ref, *refs):
        piece_refs, (out, side_out, held, sems) = refs[:8], refs[8:]
        core = sc_ref[2]
        copies = [
            pltpu.make_async_copy(ref, held.at[2 * at : 2 * at + 2], sems.at[at])
            for at, ref in enumerate(piece_refs)
        ]
        for copy in copies:
            copy.start()
        turn = turn_matrix(lambda r: ((r >> 4) + 8 * core) & 15)
        out[:, :, 0] = jnp.zeros((2, 2, 10, 16, LANES), bf16)
        out[:, :, :, 0] = jnp.zeros((2, 2, 10, 16, LANES), bf16)
        for copy in copies:
            copy.wait()

        def block(at):
            source = held[:, 16 * at : 16 * at + 16].reshape(256, LANES)
            return dot(turn, source).reshape(16, 16, LANES)

        last = block(20)
        side = last[4]
        side_out[...] = side
        masks = (None, 2.0 * side > 13.0, 2.0 * side > 17.0)
        for at in range(21):
            turned = last if at == 20 else block(at)
            for step in range(16 if at < 20 else 4):
                row, col = divmod(16 * at + step, 18)
                mask = masks[Inside.level(max(row, col) // 2)]
                kept = turned[step] if mask is None else jnp.where(mask, turned[step], 0.0)
                out[row % 2, col % 2, 1 + row // 2, 1 + col // 2] = kept.astype(bf16)

    outs = [struct((2, 2, 10, 10, 16, LANES)), struct((16, LANES), f32)]
    scratch = [pltpu.VMEM((16, 336, LANES), bf16), pltpu.SemaphoreType.DMA((8,))]
    return call(
        kernel, "prepare_images", (sc, *pieces), "s" + 8 * "h", outs, "vv", scratch,
        21 * 2 * 256**3, 8_000_000, 20,
    )


def prepare_cotangent(sc, pieces):
    def kernel(sc_ref, *refs):
        piece_refs, (out, held, sems) = refs[:2], refs[2:]
        core = sc_ref[2]
        copies = [
            pltpu.make_async_copy(ref, held.at[2 * at : 2 * at + 2], sems.at[at])
            for at, ref in enumerate(piece_refs)
        ]
        for copy in copies:
            copy.start()
        turn = turn_matrix(
            lambda r: (((r >> 5) & 1) ^ core) * 8 + 2 * (r >> 6) + ((r >> 4) & 1)
        )
        for copy in copies:
            copy.wait()
        for at in range(6):
            source = held[:, :, :, 16 * at : 16 * at + 16].reshape(256, LANES)
            turned = dot(turn, source).astype(bf16).reshape(16, 16, LANES)
            for step in range(16 if at < 5 else 1):
                row, col = divmod(16 * at + step, 9)
                out[row, col] = turned[step]

    scratch = [pltpu.VMEM((4, 2, 2, 96, LANES), bf16), pltpu.SemaphoreType.DMA((4,))]
    return call(
        kernel, "prepare_cotangent", (sc, *pieces), "saa", [struct(GRID)], "v", scratch,
        6 * 2 * 256**3, 2_000_000, 20,
    )[0]


def any_of(section, sections):
    chosen = section == sections[0]
    for other in sections[1:]:
        chosen = chosen | (section == other)
    return chosen


def stage_first(sc, side, fields, messages):
    def kernel(sc_ref, side_ref, field, own_x, x_1, y_1, top, bottom, hidden, short, zhat, zhat_p, stats, w, vec, acc, acc_p, short_now, out_sems):
        section = sc_ref[0]
        for at, whole in enumerate((own_x, x_1, y_1)):

            @pl.when(section == at)
            def _():
                w[...] = whole[16:2576]
                vec[...] = whole[0:16]

        @pl.when(section == 3)
        def _():
            w[0:1280] = top[16:1296]
            w[1280:2560] = bottom[...]
            vec[...] = top[0:16]

        outs = []
        for chunk in range(3):
            total = jnp.zeros((432, LANES), f32)
            for a in range(3):
                for b in range(3):
                    row_at, col_at = 3 * chunk + (0 if a == 0 else 1), 0 if b == 0 else 1
                    left = field[(a + 1) % 2, (b + 1) % 2, row_at : row_at + 3, col_at : col_at + 9]
                    at = LANES * (3 * a + b)
                    total = total + dot(left.reshape(432, LANES), w[at : at + LANES])
            span = slice(3 * chunk, 3 * chunk + 3)
            acc[span] = total.reshape(3, 9, 16, LANES)
            centre = field[0, 0, 3 * chunk + 1 : 3 * chunk + 4, 1:10].reshape(432, LANES)
            acc_p[span] = dot(centre, w[2304:2560]).reshape(3, 9, 16, LANES)
            for at, (source, target) in enumerate(((acc, zhat), (acc_p, zhat_p))):
                outs.append(
                    pltpu.make_async_copy(
                        source.at[span], target.at[span], out_sems.at[1 + 3 * at + chunk]
                    )
                )
                outs[-1].start()
        inside = Inside(side_ref[...])
        mean, scale = norm_stats(acc, inside)
        mean_p, scale_p = norm_stats(acc_p, inside)
        gain, gain_p, bias, bias_p = unpack_vectors(vec[...])
        for row in range(9):
            for col in range(9):
                ring = max(row, col)
                pre = (acc[row, col] - mean) * scale * gain + bias
                hidden[row, col] = inside.keep(ring, pre * sigmoid_of(pre)).astype(bf16)
                normed = (acc_p[row, col] - mean_p) * scale_p
                short_now[row, col] = inside.keep(ring, normed * gain_p + bias_p).astype(bf16)
            outs.append(pltpu.make_async_copy(short_now.at[row], short.at[row], out_sems.at[7 + row]))
            outs[-1].start()
        pack_rows(stats, [scale, gain, bias, mean, scale_p, gain_p, mean_p])
        for copy in outs:
            copy.wait()

    outs = [
        struct(GRID), struct(GRID), struct(GRID, f32), struct(GRID, f32), struct((8, LANES), f32),
        struct((2560, LANES)),
    ]
    scratch = [
        pltpu.VMEM((16, LANES), bf16), pltpu.VMEM(GRID, f32), pltpu.VMEM(GRID, f32),
        pltpu.VMEM(GRID, bf16), pltpu.SemaphoreType.DMA((16,)),
    ]
    return call(
        kernel, "stage_first", (sc, side, fields, *messages), "svv" + 5 * "v", outs, "vhhhvv",
        scratch, 2 * 1296 * 2560 * LANES, 8_000_000, 20,
    )


def fill_field(padded, source):
    blank_edges(padded)
    padded[1:10, 1:10] = source[...]


def fill_weights(part, section, core, messages, keep, send, vec):
    own_x, own_y, x_1, y_1, x_2, y_2 = messages
    upper = {1: {0: x_1, 1: own_x}, 2: {2: own_x, 3: x_1}, 3: {2: x_1, 3: own_x}}[part]
    lower = {1: {1: own_y, 3: y_1}, 2: {0: y_1, 2: own_y}, 3: {1: y_1, 3: own_y}}[part]
    far_upper = [section for section in range(4) if section not in upper]
    far_lower = [section for section in range(4) if section not in lower]
    entries = [((at,), ref, 16, 0) for at, ref in upper.items()] + [(far_upper, y_2, 16, 0)]
    entries += [((at,), ref, 272, 9) for at, ref in lower.items()] + [(far_lower, x_2, 0, 9)]
    for half in range(2):
        for sections, ref, first, block in entries:

            @pl.when((core == half) & any_of(section, sections))
            def _():
                for at in range(9):
                    tap, which = divmod(block + at, 2)
                    target = keep if which == half else send
                    start = first + LANES * at
                    target[LANES * tap : LANES * tap + LANES] = ref[start : start + LANES]
                if block == 0:
                    vec[...] = ref[0:16]


def stage_rest(part, sc, side, own, other, messages, short, cot=None, after=()):
    last = cot is not None
    extra = [one for one in (short, cot) if one is not None]

    def kernel(sc_ref, side_ref, own_ref, oth_ref, *refs):
        refs = list(refs)
        late_refs = [refs.pop(0) for _ in extra]
        weights = refs[0:6]
        refs = refs[6 + len(after) :]
        if last:
            dz, passed, out, sums = refs[:4]
            refs = refs[4:]
        else:
            hidden, zhat, stats = refs[:3]
            refs = refs[3:]
        w_keep, w_send, vec, padded, acc = refs[:5]
        grads, passed_now = refs[5:7] if last else (None, None)
        late, sems, out_sems = refs[-3:]
        short_ref = late.at[0] if short is not None else None
        cot_ref = late.at[1] if last else None
        section, core = sc_ref[0], sc_ref[2]
        late_loads = [
            pltpu.make_async_copy(ref, late.at[at], sems.at[at]) for at, ref in enumerate(late_refs)
        ]
        for copy in late_loads:
            copy.start()
        fill_weights(part, section, core, weights, w_keep, w_send, vec)
        fill_field(padded.at[0], own_ref)
        fill_field(padded.at[1], oth_ref)
        outs = []
        for chunk in range(3):
            total = jnp.zeros((432, LANES), f32)
            for a in range(3):
                for b in range(3):
                    for at in range(2):
                        left = padded[at, 3 * chunk + a : 3 * chunk + a + 3, b : b + 9]
                        from_row = LANES * (3 * a + b)
                        right = (w_keep, w_send)[at][from_row : from_row + LANES]
                        total = total + dot(left.reshape(432, LANES), right)
            acc[3 * chunk : 3 * chunk + 3] = total.reshape(3, 9, 16, LANES)
            if not last:
                outs.append(
                    pltpu.make_async_copy(
                        acc.at[3 * chunk : 3 * chunk + 3],
                        zhat.at[3 * chunk : 3 * chunk + 3],
                        out_sems.at[18 + chunk],
                    )
                )
                outs[-1].start()
        inside = Inside(side_ref[...])
        mean, scale = norm_stats(acc, inside)
        for copy in late_loads:
            copy.wait()
        gain, _, bias, _ = unpack_vectors(vec[...])
        if last:
            sums_now = [None, None]
        for row in range(9):
            for col in range(9):
                ring = max(row, col)
                normed = (acc[row, col] - mean) * scale
                if last:
                    acc[row, col] = normed
                pre = normed * gain + bias
                if short is not None:
                    pre = pre + short_ref[row, col].astype(f32)
                sigmoid = sigmoid_of(pre)
                target = out if last else hidden
                target[row, col] = inside.keep(ring, pre * sigmoid).astype(bf16)
                if last:
                    slope = sigmoid * (1.0 + pre * (1.0 - sigmoid))
                    grad = inside.keep(ring, cot_ref[row, col].astype(f32) * slope)
                    grads[row, col] = grad
                    passed_now[row, col] = grad.astype(bf16)
                    for at, value in enumerate((grad, grad * normed)):
                        sums_now[at] = value if sums_now[at] is None else sums_now[at] + value
            if last:
                outs.append(
                    pltpu.make_async_copy(passed_now.at[row], passed.at[row], out_sems.at[18 + row])
                )
                outs[-1].start()
        if last:
            bias_now, gain_now = col_sum(sums_now[0]), col_sum(sums_now[1])
            norm_back(dz, grads, acc, inside, gain * scale, bias_now, gain_now)
            pack_rows(sums, [gain_now, bias_now])
        else:
            pack_rows(stats, [scale, gain, bias, mean])
        for copy in outs:
            copy.wait()

    half = struct((2304, LANES))
    if last:
        outs, places = [struct(GRID), struct(GRID), struct(GRID), struct((8, LANES), f32)], "vhvv"
    else:
        outs, places = [struct(GRID), struct(GRID, f32), struct((8, LANES), f32)], "vhv"
    scratch = [
        pltpu.VMEM((16, LANES), bf16), pltpu.VMEM((2, 11, 11, 16, LANES), bf16), pltpu.VMEM(GRID, f32)
    ] + ([pltpu.VMEM(GRID, f32), pltpu.VMEM(GRID, bf16)] if last else [])
    scratch += [
        pltpu.VMEM((2, *GRID), bf16), pltpu.SemaphoreType.DMA((2,)), pltpu.SemaphoreType.DMA((27,)),
    ]
    return call(
        kernel, f"stage_{part}", (sc, side, own, other, *extra, *messages, *after),
        "svvv" + len(extra) * "a" + 6 * "v" + len(after) * "a", outs + [half, half], places + "vv", scratch,
        2 * 1296 * 4608 * LANES, 8_000_000, 20,
    )


def norm_back(dz, grads, zhat, inside, weight, bias_now, gain_now):
    constant, slope = weight * bias_now / inside.count, weight * gain_now / inside.count
    for row in range(9):
        for col in range(9):
            value = weight * grads[row, col] - (constant + slope * zhat[row, col])
            dz[row, col] = inside.keep(max(row, col), value).astype(bf16)


def stage_back(part, sc, side, dz_own, dz_other, w_own, w_other, zhat, stats, short=None, extra=None, proj=None):
    first = proj is not None
    optional = [one for one in (short, extra) if one is not None] + (list(proj) if first else [])

    def kernel(sc_ref, side_ref, stats_ref, dz_own_ref, dz_oth_ref, w_own_ref, w_oth_ref, zhat_ref, *refs):
        refs = list(refs)
        late_refs = [refs.pop(0) for one in (short, extra) if one is not None]
        if first:
            dyp_ref, zhat_p_ref = refs.pop(0), refs.pop(0)
        dz, sums = refs.pop(0), refs.pop(0)
        passed = refs.pop(0) if short is not None else None
        dz_p = refs.pop(0) if first else None
        padded, acc, held = refs[:3]
        held_p = refs[3] if first else None
        late = None if first else refs[3]
        sems = refs[-1]
        short_ref = late.at[0] if short is not None else None
        extra_ref = late.at[1] if extra is not None else None
        later = [pltpu.make_async_copy(zhat_ref, held, sems.at[4])]
        if first:
            later.append(pltpu.make_async_copy(zhat_p_ref, held_p, sems.at[5]))
        for at, ref in enumerate(late_refs):
            later.append(pltpu.make_async_copy(ref, late.at[at], sems.at[6 + at]))
        for copy in later:
            copy.start()
        fill_field(padded.at[0], dz_own_ref)
        fill_field(padded.at[1], dz_oth_ref)
        for chunk in range(3):
            total = jnp.zeros((432, LANES), f32)
            for a in range(3):
                for b in range(3):
                    for at in range(2):
                        row_at = 3 * chunk + 2 - a
                        left = padded[at, row_at : row_at + 3, 2 - b : 11 - b]
                        from_row = LANES * (3 * a + b)
                        right = (w_own_ref, w_oth_ref)[at][from_row : from_row + LANES]
                        total = total + dot_t(left.reshape(432, LANES), right)
            acc[3 * chunk : 3 * chunk + 3] = total.reshape(3, 9, 16, LANES)
        for copy in later:
            copy.wait()
        inside = Inside(side_ref[...])
        scale, gain, bias, mean, scale_p, gain_p, mean_p = [stats_ref[at : at + 1] for at in range(7)]
        sums_now = [None] * 4
        for row in range(9):
            for col in range(9):
                ring = max(row, col)
                normed = (held[row, col] - mean) * scale
                held[row, col] = normed
                pre = normed * gain + bias
                grad = acc[row, col]
                if extra is not None:
                    grad = grad + extra_ref[row, col].astype(f32)
                if short is not None:
                    pre = pre + short_ref[row, col].astype(f32)
                sigmoid = sigmoid_of(pre)
                slope = sigmoid * (1.0 + pre * (1.0 - sigmoid))
                grad = inside.keep(ring, grad.astype(bf16).astype(f32) * slope)
                acc[row, col] = grad
                if short is not None:
                    passed[row, col] = grad.astype(bf16)
                terms = [grad, grad * normed]
                if first:
                    grad_p = dyp_ref[row, col].astype(f32)
                    normed_p = (held_p[row, col] - mean_p) * scale_p
                    held_p[row, col] = normed_p
                    terms += [grad_p, grad_p * normed_p]
                for at, value in enumerate(terms):
                    sums_now[at] = value if sums_now[at] is None else sums_now[at] + value
        totals = [col_sum(value) for value in sums_now if value is not None]
        norm_back(dz, acc, held, inside, gain * scale, totals[0], totals[1])
        rows = [totals[1], totals[0]]
        if first:
            for row in range(9):
                for col in range(9):
                    acc[row, col] = dyp_ref[row, col].astype(f32)
            norm_back(dz_p, acc, held_p, inside, gain_p * scale_p, totals[2], totals[3])
            rows += [totals[3], totals[2]]
        pack_rows(sums, rows)

    outs, places = [struct(GRID), struct((8, LANES), f32)], "vv"
    if short is not None:
        outs, places = outs + [struct(GRID)], places + "v"
    if first:
        outs, places = outs + [struct(GRID)], places + "v"
    scratch = [
        pltpu.VMEM((2, 11, 11, 16, LANES), bf16), pltpu.VMEM(GRID, f32), pltpu.VMEM(GRID, f32)
    ] + [pltpu.VMEM(GRID, f32) if first else pltpu.VMEM((2, *GRID), bf16)]
    scratch += [pltpu.SemaphoreType.DMA((8,))]
    kinds = "h" * ((short is not None) + (extra is not None)) + ("vh" if first else "")
    return call(
        kernel, f"back_{part}",
        (sc, side, stats, dz_own, dz_other, w_own, w_other, zhat, *optional),
        "svvvvvvh" + kinds, outs, places, scratch, 2 * 1296 * 4608 * LANES, 10_000_000, 20,
    )


def pick_images(sc, *fields):
    def kernel(sc_ref, *refs):
        core = sc_ref[2]
        keep, give = refs[-2:]
        out_row = lax.broadcasted_iota(jnp.int32, (4, 96, 1296), 1)
        slot = lax.broadcasted_iota(jnp.int32, (4, 96, 1296), 0)
        in_row = lax.broadcasted_iota(jnp.int32, (4, 96, 1296), 2)
        image = 8 * ((slot >> 1) ^ core) + (slot & 1)
        pick = jnp.where(in_row == 16 * out_row + image, 1.0, 0.0).astype(bf16).reshape(384, 1296)
        for at, source in enumerate(refs[:-2]):
            chosen = dot(pick, source[...].reshape(1296, LANES)).astype(bf16).reshape(4, 96, LANES)
            keep[at] = chosen[0:2]
            give[at] = chosen[2:4]

    count = len(fields)
    return call(
        kernel, "pick_images", (sc, *fields), "s" + count * "v", 2 * [struct((count, 2, 96, LANES))],
        "vv", [], count * 2 * 384 * 1296 * LANES, 3_000_000, 20,
    )


def weight_rest(part, sc, own, other, dz, sums, tail=None):
    def kernel(sc_ref, own_ref, oth_ref, dz_ref, sums_ref, *refs):
        out, turned, padded = refs[-3:]
        if tail is not None:
            out[1168:1568] = refs[0][768:1168]
        zone, core = sc_ref[1], sc_ref[2]
        fill_field(padded, dz_ref)
        lane = pl.multiple_of(128 * (zone & 1), 128)
        is_own = (zone >> 1) == core

        @pl.when(is_own)
        def _():
            turned[...] = own_ref[:, :, :, pl.ds(lane, 128)].reshape(1296, 128).T

        @pl.when(jnp.logical_not(is_own))
        def _():
            turned[...] = oth_ref[:, :, :, pl.ds(lane, 128)].reshape(1296, 128).T

        left = turned[...]
        for a in range(3):
            for b in range(3):
                right = padded[2 - a : 11 - a, 2 - b : 11 - b].reshape(1296, LANES)
                at = 128 * (3 * a + b)
                out[at : at + 128] = dot(left, right).astype(bf16)
        blank = jnp.zeros((1, LANES), f32)
        out[1152:1168] = pack_vectors([sums_ref[0:1], blank, sums_ref[1:2], blank])

    scratch = [
        pltpu.VMEM((128, 1296), bf16), pltpu.VMEM((11, 11, 16, LANES), bf16)
    ]
    return call(
        kernel, f"weight_{part}", (sc, own, other, dz, sums) + (() if tail is None else (tail,)),
        "svvvv" + ("" if tail is None else "v"), [struct((1168 if tail is None else 1568, LANES))], "v",
        scratch, 2 * 1296 * 1152 * LANES, 3_000_000, 20,
    )[0]


def weight_first(sc, fields, dz, dz_p, sums):
    def kernel(sc_ref, field, dz_ref, dz_p_ref, sums_ref, out, turned, padded):
        zone = sc_ref[1]
        fill_field(padded, dz_ref)
        lane = pl.multiple_of(128 * (zone >> 1), 128)
        at = pl.multiple_of(64 * (zone & 1), 64)
        for phase in range(4):
            chosen = field[phase // 2, phase % 2, 1:10, 1:10, :, pl.ds(lane, 128)]
            turned[phase] = chosen.reshape(1296, 128).T
        for tap in range(10):
            if tap < 9:
                a, b = divmod(tap, 3)
                left = turned[2 * ((a + 1) % 2) + (b + 1) % 2, pl.ds(at, 64)]
                row_at, col_at = 2 if a == 0 else 1, 2 if b == 0 else 1
                right = padded[row_at : row_at + 9, col_at : col_at + 9].reshape(1296, LANES)
            else:
                left = turned[0, pl.ds(at, 64)]
                right = dz_p_ref[...].reshape(1296, LANES)
            out[64 * tap : 64 * tap + 64] = dot(left, right).astype(bf16)
        out[640:656] = pack_vectors([sums_ref[0:1], sums_ref[2:3], sums_ref[1:2], sums_ref[3:4]])

    scratch = [
        pltpu.VMEM((4, 128, 1296), bf16), pltpu.VMEM((11, 11, 16, LANES), bf16)
    ]
    return call(
        kernel, "weight_first", (sc, fields, dz, dz_p, sums), "svvvv", [struct((656, LANES))], "v",
        scratch, 2 * 1296 * 640 * LANES, 3_000_000, 20,
    )[0]


def image_back(sc, own, other, w_own, w_other):
    def kernel(sc_ref, own_all, oth_all, w_own_ref, w_oth_ref, out, block):
        for source, half in ((own_all, sc_ref[2]), (oth_all, 1 - sc_ref[2])):
            block[:, :, pl.ds(pl.multiple_of(LANES * half, LANES), LANES)] = source[2]
        own_ref, own_p_ref = own_all.at[0], own_all.at[1]
        oth_ref, oth_p_ref = oth_all.at[0], oth_all.at[1]
        row = lax.broadcasted_iota(jnp.int32, (192, 192), 0)
        col = lax.broadcasted_iota(jnp.int32, (192, 192), 1)
        pixel = jnp.where(row >= 96, row - 96, row)
        line = (pixel * 57) >> 9
        across = pixel - 9 * line
        shifted = {}
        for down in range(2):
            for right in range(2):
                if down + right == 0:
                    shifted[0, 0] = (
                        own_ref[...].reshape(192, LANES),
                        oth_ref[...].reshape(192, LANES),
                    )
                    continue
                fits = (pixel < 81) & (line + down < 9) & (across + right < 9)
                move = jnp.where(fits & (col == row + 9 * down + right), 1.0, 0.0).astype(bf16)
                shifted[down, right] = tuple(
                    dot(move, ref[...].reshape(192, LANES)).astype(bf16)
                    for ref in (own_ref, oth_ref)
                )
        phases = [jnp.zeros((192, LANES), f32) for _ in range(4)]
        for a in range(3):
            for b in range(3):
                at = 2 * ((a + 1) % 2) + (b + 1) % 2
                left = shifted[1 if a == 0 else 0, 1 if b == 0 else 0]
                rows = slice(LANES * (3 * a + b), LANES * (3 * a + b + 1))
                phases[at] = phases[at] + dot_t(left[0], w_own_ref[rows])
                phases[at] = phases[at] + dot_t(left[1], w_oth_ref[rows])
        phases[0] = phases[0] + dot_t(own_p_ref[...].reshape(192, LANES), w_own_ref[2304:2560])
        phases[0] = phases[0] + dot_t(oth_p_ref[...].reshape(192, LANES), w_oth_ref[2304:2560])
        joined = jnp.concatenate([phase.astype(bf16) for phase in phases], axis=0)
        out_row = lax.broadcasted_iota(jnp.int32, (336, 768), 0)
        in_row = lax.broadcasted_iota(jnp.int32, (336, 768), 1)
        line = (out_row * 3641) >> 16
        across = out_row - 18 * line
        source = (2 * (line & 1) + (across & 1)) * 192 + 9 * (line >> 1) + (across >> 1)
        for image in range(2):
            spread = jnp.where(
                (in_row == source + 96 * image) & (out_row < 324), 1.0, 0.0
            ).astype(bf16)
            out[image] = dot(spread, joined).astype(bf16)

    return call(
        kernel, "image_back", (sc, own, other, w_own, w_other), "svvvv",
        [struct((2, 336, LANES)), struct((2, 96, 2 * LANES))], "vv", [], 2 * 192 * 2560 * 512 + 4 * 336 * 768 * 256, 4_000_000, 20,
    )


def add_into(out, rows, sources, vector_rows):
    for at in range(0, rows, 64):
        total = sources[0][at : at + 64].astype(f32)
        for source in sources[1:]:
            total = total + source[at : at + 64].astype(f32)
        out[at : at + 64] = total.astype(bf16)
    totals = [unpack_vectors(source[rows : rows + 16]) for source in sources]
    sums = [sum(one[1:], one[0]) for one in zip(*totals)]
    out[vector_rows : vector_rows + 16] = pack_vectors(sums)


def add_pieces(part, one, two):
    rows = one.shape[0] - 16

    def kernel(one_ref, two_ref, out):
        add_into(out, rows, (one_ref, two_ref), rows)

    return call(
        kernel, f"add_{part}", (one, two), "vv", [struct(one.shape)], "v", [], 1, 1_000_000, 20
    )[0]


def add_two(sc, three, two, came_three, came_two):
    def kernel(sc_ref, three_ref, two_ref, came_three_ref, came_two_ref, keep, give):
        for at_three, out_three, out_two in ((True, keep, give), (False, give, keep)):

            @pl.when((sc_ref[0] == 3) if at_three else (sc_ref[0] != 3))
            def _():
                for at in range(0, 768, 64):
                    span = slice(at, at + 64)
                    total = three_ref[span].astype(f32) + came_three_ref[span].astype(f32)
                    out_three[span] = total.astype(bf16)
                tails = (three_ref.at[768:1168], came_two_ref.at[1168:1568])
                add_into(out_three.at[768:1168], 384, tails, 384)
                add_into(out_two, 1152, (two_ref, came_two_ref), 1152)

    return call(
        kernel, "add_two", (sc, three, two, came_three, came_two), "svvvv", [struct((1168, LANES))] * 2,
        "vv", [], 1, 1_000_000, 20,
    )


def own_piece(sc, groups, after):
    pieces = [piece for _, group in groups for piece in group]

    def kernel(sc_ref, *refs):
        out, used = refs[-1], 0
        for sections, group in groups:
            sources = refs[used : used + len(group)]
            used += len(group)
            rows = group[0].shape[0] - 16

            @pl.when(any_of(sc_ref[0], sections))
            def _():
                add_into(out, rows, sources, 1152)

    return call(
        kernel, "own_piece", (sc, *pieces, *after), "s" + len(pieces) * "v" + len(after) * "a",
        [struct((1168, LANES))], "v", [], 1, 1_000_000, 20,
    )[0]


def lay_out(sc, own, other):
    def kernel(sc_ref, *refs):
        pieces, (out, vectors, wide, out_sems) = refs[:12], refs[12:]
        section, zone, core = sc_ref[0], sc_ref[1], sc_ref[2]
        at_end = (zone == 0) | (zone == 3)
        is_first = section == 0
        for tap in range(9):
            slot = tap % 3
            leaving = [
                pltpu.make_async_copy(
                    wide.at[slot, 128 * cut : 128 * cut + 128],
                    out.at[512 * tap + 128 * cut : 512 * tap + 128 * cut + 128],
                    out_sems.at[slot, cut],
                )
                for cut in range(4)
            ]
            if tap >= 3:
                for copy in leaving:
                    copy.wait()

            def place(which, row_of, rows, first):
                origin = zone ^ (0, 1, 2, 3, 2, 3)[which]
                row = pl.multiple_of(row_of(origin), rows)
                for half in range(2):
                    lane = pl.multiple_of(LANES * (core ^ half), LANES)
                    value = jnp.zeros((rows, LANES), f32)
                    if first + rows <= 1152:
                        value = pieces[which + 6 * half][first : first + rows].astype(f32)
                    wide[slot, pl.ds(row, rows), pl.ds(lane, LANES)] = value

            for kind, chosen in ((0, at_end), (1, jnp.logical_not(at_end))):
                used = (0, 1, 4, 5) if kind == 0 else (0, 1, 2, 3)

                @pl.when(chosen & jnp.logical_not(is_first))
                def _():
                    for which in used:
                        place(which, lambda origin: 128 * origin, 128, 128 * tap)

                @pl.when(chosen & is_first)
                def _():
                    for part in range(2):
                        start = 64 * (2 * tap + part)
                        for which in used:
                            place(
                                which,
                                lambda origin: 256 * part + 64 * origin,
                                64,
                                start if start < 640 else 1152,
                            )

            for copy in leaving:
                copy.start()
        for half in range(2):
            rows = unpack_vectors(pieces[6 * half][1152:1168])
            lane = pl.multiple_of(LANES * (core ^ half), LANES)
            vectors[:, pl.ds(lane, LANES)] = jnp.concatenate(rows, axis=0)
        for slot in range(3):
            for cut in range(4):
                pltpu.make_async_copy(
                    wide.at[slot, 0:128], out.at[0:128], out_sems.at[slot, cut]
                ).wait()

    return call(
        kernel, "lay_out", (sc, *own, *other), "s" + 12 * "v", [struct((4608, 512), f32), struct((4, 512), f32)], "hv",
        [pltpu.VMEM((3, 512, 512), f32), pltpu.SemaphoreType.DMA((3, 4))], 0, 15_000_000, 20,
    )


def half_of(value, half):
    return lax.dynamic_slice_in_dim(value, LANES * half, LANES, axis=value.ndim - 1)


def chip_body(images, res_ids, weights, bn_gain, bn_bias, cotangent):
    section = lax.axis_index("section")
    position = lax.axis_index("dp")
    zone, core = position // 2, position % 2
    sc = jnp.stack([section, zone, core, core]).astype(jnp.int32)

    def after(value, *tokens):
        return lax.optimization_barrier((value, *tokens))[0]

    own = split_weights(sc, weights[0], jnp.concatenate([bn_gain[0], bn_bias[0]], axis=0))
    x_1 = flip(own[0], "section", 1)
    y_1 = flip(own[1], "section", 2)

    level = lax.dynamic_index_in_dim(res_ids, section, 0, keepdims=False)
    side_own = (9 - 2 * (2 - level)).astype(f32)
    tail = jnp.broadcast_to(side_own[:, None, None], (2, 12, 256)).astype(bf16)
    image_own = jnp.concatenate([after(images, own[0])[0].reshape(2, 324, 256), tail], axis=1)
    pieces = [image_own] + [flip(image_own, "dp", 2 * at) for at in range(1, 4)]
    pieces += [flip(piece, "dp", 1) for piece in pieces]
    for_x, for_y, top, bottom = relay_weights(
        "relay_2", lambda at: (at == 1) | (at == 2), (sc, *own, x_1, y_1), True
    )
    top = flip(top, "section", 1, lambda i: i == 2)
    bottom = flip(bottom, "section", 2, lambda i: i == 1)
    cot_own = after(cotangent, for_x)[0].reshape(2, 81, 512)
    cot_pair = jnp.stack([half_of(cot_own, core), flip(half_of(cot_own, 1 - core), "dp", 1)])
    cot_pair = jnp.pad(cot_pair, ((0, 0), (0, 0), (0, 15), (0, 0)))
    cot_near = jnp.stack([cot_pair, flip(cot_pair, "dp", 2)])
    fields, side = prepare_images(after(sc, for_x), pieces)
    cot_pieces = (cot_near, flip(after(cot_near, fields), "dp", 4))
    x_2 = flip(for_x, "section", 1)
    y_2 = flip(for_y, "section", 2)
    hidden_one, short_one, zhat_0, zhat_p, stats_0, w_first = stage_first(
        sc, side, after(fields, for_x), (own[0], x_1, y_1, top, bottom)
    )
    hidden_one_other = flip(hidden_one, "dp", 1)
    w_first_other = flip(w_first, "dp", 1)
    for_x, for_y = relay_weights("relay_3", lambda at: at == 3, (after(sc, stats_0), *own, x_1, y_1))
    x_3 = flip(for_x, "section", 1, lambda i: i in (1, 3))
    y_3 = flip(for_y, "section", 2, lambda i: i in (2, 3))
    messages = (*own, x_1, y_1, x_2, y_2)
    block_one, zhat_1, stats_1, keep_1, send_1 = stage_rest(
        1, sc, side, hidden_one, hidden_one_other, messages, short_one, after=cot_pieces
    )
    block_one_other = flip(block_one, "dp", 1)
    other_1 = flip(send_1, "dp", 1)
    cot = prepare_cotangent(sc, after(cot_pieces, stats_1))
    hidden_two, zhat_2, stats_2, keep_2, send_2 = stage_rest(
        2, sc, side, block_one, block_one_other, messages, None, after=(x_3, y_3, cot)
    )
    hidden_two_other = flip(hidden_two, "dp", 1)
    other_2 = flip(send_2, "dp", 1)
    messages = (*own, x_1, y_1, x_3, y_3)
    dz_3, passed, out, sums_3, keep_3, send_3 = stage_rest(
        3, sc, side, hidden_two, hidden_two_other, messages, block_one, cot
    )
    other_3 = flip(send_3, "dp", 1)
    dz_3_other = flip(dz_3, "dp", 1)

    def to_pair(part, piece):
        return flip(piece, "section", 2, lambda i: i ^ 2 in (part, part ^ 1))

    piece_3 = weight_rest(3, sc, hidden_two, hidden_two_other, dz_3, sums_3)
    came_3 = to_pair(3, piece_3[0:768])
    dz_2, sums_2 = stage_back(
        2, sc, side, after(dz_3, piece_3), dz_3_other, keep_3, other_3, zhat_2, stats_2
    )
    dz_2_other = flip(dz_2, "dp", 1)
    piece_2 = weight_rest(2, sc, block_one, block_one_other, dz_2, sums_2, piece_3)
    came_2 = to_pair(2, piece_2)
    dz_1, sums_1, short_grad = stage_back(
        1, sc, side, after(dz_2, piece_2), dz_2_other, keep_2, other_2, zhat_1, stats_1, short_one,
        passed,
    )
    dz_1_other = flip(dz_1, "dp", 1)
    piece_1 = weight_rest(
        1, sc, hidden_one, hidden_one_other, after(dz_1, came_3), sums_1
    )
    came_1 = flip(piece_1, "section", 1, lambda i: i in (0, 2))
    dz_0, sums_0, dz_p = stage_back(
        0, sc, side, after(dz_1, piece_1), dz_1_other, keep_1, other_1, zhat_0, stats_0,
        proj=(short_grad, zhat_p),
    )
    piece_0 = weight_first(sc, fields, dz_0, dz_p, sums_0)
    came_0 = flip(piece_0, "section", 2, lambda i: i in (2, 3))
    keep_late, give_late = add_two(sc, after(piece_3, piece_0), piece_2, came_3, came_2)
    last_late = flip(give_late, "section", 1, lambda i: i in (2, 3))
    sum_1 = add_pieces(1, after(piece_1, give_late), came_1)
    last_1 = flip(sum_1, "section", 2, lambda i: i == 3)
    sum_0 = add_pieces(0, after(piece_0, sum_1), came_0)
    last_0 = flip(sum_0, "section", 1, lambda i: i == 1)
    keep, give = pick_images(sc, *after((dz_0, dz_p, out), sum_0))
    image_raw, block_output = image_back(sc, keep, flip(give, "dp", 1), w_first, w_first_other)
    block_output = block_output[:, 0:81]
    rows = jnp.arange(18, dtype=jnp.int32)
    inner_rows = (rows < 2 * (9 - 2 * (2 - level))[:, None]).astype(bf16)
    mask_in = inner_rows[:, :, None] * inner_rows[:, None, :]
    image_grad = image_raw[:, 0:324].reshape(2, 18, 18, 256) * mask_in[..., None]
    total = own_piece(
        sc,
        [((0,), (sum_0, last_0)), ((1,), (sum_1, last_1)), ((2, 3), (keep_late, last_late))],
        (image_raw,),
    )
    from_far = flip(total, "dp", 4, lambda i: i // 2 in (0, 3))
    from_near = flip(total, "dp", 2)
    from_middle = flip(total, "dp", 6, lambda i: i // 2 in (1, 2))
    from_end = flip(total, "dp", 4, lambda i: i // 2 in (1, 2))
    relayed = flip(from_far, "dp", 2, lambda i: i // 2 in (1, 2))
    from_near, block_output, image_grad = lax.optimization_barrier(
        (from_near, block_output, image_grad)
    )
    gathered = [total, from_near, from_far, from_middle, from_end, relayed]
    weight_grad, vectors = lay_out(sc, gathered, [flip(piece, "dp", 1) for piece in gathered])

    return (
        block_output.reshape(1, 2, 9, 9, 512),
        image_grad[None],
        weight_grad[None],
        vectors[None, 0:2],
        vectors[None, 2:4],
    )


def solution(mesh):
    placed = (
        P("section", "dp", None, None, None),
        P(None, "dp"),
        P("section", None, None),
        P("section", None, None),
        P("section", None, None),
        P("section", "dp", None, None, None),
    )
    on_chip = mesh.shape["section"] == 4 and mesh.shape["dp"] == 8
    return jax.shard_map(
        chip_body if on_chip else pipeline_body,
        mesh=mesh,
        in_specs=placed,
        out_specs=(
            P("section", "dp", None, None, None),
            P("section", "dp", None, None, None),
            P("section", None, None),
            P("section", None, None),
            P("section", None, None),
        ),
        check_vma=False,
    )
```

```python
import jax
import jax.numpy as jnp
from jax import lax
from jax.experimental import pallas as pl
from jax.experimental.pallas import tpu as pltpu
from jax.sharding import PartitionSpec as P

epsilon = 1e-05


def passed_along(value, axis, steps):
    count = lax.axis_size(axis)
    leading, last = (max(0, -steps), min(count, count - steps))
    return lax.ppermute(value, axis, [(source, source + steps) for source in range(leading, last)])


def regions(levels, half_side):
    inner_side = half_side - 2 * (2 - levels)
    small_rows = jnp.arange(half_side, dtype=jnp.int32)
    large_rows = jnp.arange(2 * half_side, dtype=jnp.int32)
    inner_mask = (small_rows < inner_side[..., None]).astype(jnp.float32)
    outer_mask = (large_rows < 2 * inner_side[..., None]).astype(jnp.float32)
    return (
        outer_mask[..., :, None] * outer_mask[..., None, :],
        inner_mask[..., :, None] * inner_mask[..., None, :],
    )


def patches(field_in, stride, half_side):
    padded = jnp.pad(field_in, ((0, 0), (1, 1), (1, 1), (0, 0)))
    pieces = [
        padded[
            :,
            row_at : row_at + stride * half_side : stride,
            col_at : col_at + stride * half_side : stride,
            :,
        ]
        for row_at in range(3)
        for col_at in range(3)
    ]
    joined = jnp.concatenate(pieces, axis=-1)
    return joined.reshape(-1, joined.shape[-1])


def contract_rows(left_side, right_side):
    return lax.dot_general(
        left_side, right_side, (((0,), (0,)), ((), ())), preferred_element_type=jnp.float32
    )


def contract_cols(left_side, right_side):
    return lax.dot_general(
        left_side, right_side, (((1,), (1,)), ((), ())), preferred_element_type=jnp.float32
    )


def silu_slope(values):
    sigmoid = jax.nn.sigmoid(values)
    return sigmoid * (1.0 + values * (1.0 - sigmoid))


def spread_taps(tap_grads, image_count, half_side, channels):
    tap_grid = tap_grads.reshape(image_count, half_side, half_side, 9, channels)
    empty_phase = jnp.zeros((image_count, half_side + 1, half_side + 1, channels), jnp.float32)
    phases = [[empty_phase, empty_phase], [empty_phase, empty_phase]]
    for row_at in range(3):
        for col_at in range(3):
            tap_piece = tap_grid[:, :, :, 3 * row_at + col_at, :]
            top_pad = 1 if row_at == 2 else 0
            left_pad = 1 if col_at == 2 else 0
            placed = jnp.pad(
                tap_piece, ((0, 0), (top_pad, 1 - top_pad), (left_pad, 1 - left_pad), (0, 0))
            )
            phases[row_at % 2][col_at % 2] = phases[row_at % 2][col_at % 2] + placed
    row_phases = [jnp.stack([phases[parity][0], phases[parity][1]], axis=3) for parity in range(2)]
    alternated = jnp.stack(row_phases, axis=2).reshape(
        image_count, 2 * half_side + 2, 2 * half_side + 2, channels
    )
    return alternated[:, 1 : 2 * half_side + 1, 1 : 2 * half_side + 1, :]


def keep_slot(buffer_all, new_value, slot_at, keep_flag):
    current = lax.dynamic_index_in_dim(buffer_all, slot_at, 0, keepdims=False)
    return lax.dynamic_update_index_in_dim(
        buffer_all, jnp.where(keep_flag, new_value, current), slot_at, 0
    )


def pipeline_body(images, res_ids, weights, bn_gain, bn_bias, cotangent):
    sections = lax.axis_size("section")
    last_section = sections - 1
    position = lax.axis_index("section")
    micro_count = res_ids.shape[0]
    image_count = images.shape[1]
    half_side = cotangent.shape[2]
    channels = weights.shape[2]
    in_channels = images.shape[4]
    pixel_rows = image_count * half_side * half_side
    taps_in = 9 * in_channels
    matrix = weights[0]
    gain_rows = bn_gain[0]
    bias_rows = bn_bias[0]
    is_first = position == 0
    adds_short = (position == 1) | (position == 3)
    passes_short = position == 2
    makes_short = position == 1
    back_matrix = jnp.transpose(matrix.reshape(9, channels, channels)[::-1], (0, 2, 1)).reshape(
        9 * channels, channels
    )
    mask_in_all, mask_out_all = regions(res_ids, half_side)
    act_shape = (image_count, half_side, half_side, channels)
    zero_pixels = jnp.zeros((pixel_rows, channels), jnp.float32)
    zero_input = jnp.zeros((image_count, 2 * half_side, 2 * half_side, in_channels), jnp.float32)
    zero_weight = jnp.zeros((9 * channels, channels), jnp.float32)
    own_images = images[0]
    gathered = [own_images]
    for source in range(1, micro_count):
        gathered.append(passed_along(own_images, "section", -source))
    section_inputs = jnp.stack(gathered)
    own_cot = cotangent[0]
    arrived = []
    for source in range(micro_count):
        if source == last_section:
            arrived.append(own_cot)
        else:
            arrived.append(passed_along(own_cot, "section", last_section - source))
    cot_all = jnp.stack(arrived)

    def conv_first(prev_act, first_in):
        columns = patches(first_in, 2, half_side)
        main_out = jnp.dot(columns, matrix[:taps_in], preferred_element_type=jnp.float32)
        proj_out = jnp.dot(
            columns[:, 4 * in_channels : 5 * in_channels],
            matrix[taps_in : taps_in + in_channels],
            preferred_element_type=jnp.float32,
        )
        return jnp.stack([main_out, proj_out])

    def conv_rest(prev_act, first_in):
        columns = patches(prev_act, 1, half_side)
        return jnp.stack(
            [jnp.dot(columns, matrix, preferred_element_type=jnp.float32), zero_pixels]
        )

    def conv_spare(prev_act, first_in):
        return jnp.stack([zero_pixels, zero_pixels])

    def back_first(grad_conv, prev_act, first_in):
        columns = patches(first_in, 2, half_side)
        centre = columns[:, 4 * in_channels : 5 * in_channels]
        main_grad = contract_rows(columns, grad_conv[0])
        proj_grad = contract_rows(centre, grad_conv[1])
        filler = jnp.zeros((9 * channels - taps_in - in_channels, channels), jnp.float32)
        weight_now = jnp.concatenate([main_grad, proj_grad, filler], axis=0)
        tap_grads = contract_cols(grad_conv[0], matrix[:taps_in])
        centre_grad = contract_cols(grad_conv[1], matrix[taps_in : taps_in + in_channels])
        tap_grads = tap_grads + jnp.pad(centre_grad, ((0, 0), (4 * in_channels, 4 * in_channels)))
        return (
            weight_now,
            zero_pixels,
            spread_taps(tap_grads, image_count, half_side, in_channels),
        )

    def back_rest(grad_conv, prev_act, first_in):
        columns = patches(prev_act, 1, half_side)
        weight_now = contract_rows(columns, grad_conv[0])
        grad_image = grad_conv[0].reshape(act_shape)
        prev_grad = jnp.dot(
            patches(grad_image, 1, half_side), back_matrix, preferred_element_type=jnp.float32
        )
        return (weight_now, prev_grad, zero_input)

    def back_spare(grad_conv, prev_act, first_in):
        return (zero_weight, zero_pixels, zero_input)

    def finish(conv_out, mean_rows, scale_rows, flat_mask, short_in):
        normed = (conv_out - mean_rows[:, None, :]) * scale_rows[:, None, :] * gain_rows[
            :, None, :
        ] + bias_rows[:, None, :]
        pre_act = normed[0] + jnp.where(adds_short, short_in, 0.0)
        activated = jax.nn.silu(pre_act) * flat_mask[:, None]
        proj_short = normed[1] * flat_mask[:, None]
        short_out = jnp.where(is_first, proj_short, jnp.where(makes_short, activated, short_in))
        return (pre_act, activated, short_out)

    empty_act = jnp.zeros(act_shape, jnp.bfloat16)
    recv_act = empty_act
    recv_short = empty_act
    saved_act = jnp.zeros((micro_count,) + act_shape, jnp.bfloat16)
    saved_short = saved_act
    saved_final = saved_act
    saved_mean = jnp.zeros((micro_count, 2, channels), jnp.float32)
    saved_scale = saved_mean
    saved_total = jnp.zeros((micro_count,), jnp.float32)
    sweep_len = micro_count + last_section
    for tick_at in range(sweep_len):
        slot_raw = tick_at - position
        is_valid = (slot_raw >= 0) & (slot_raw < micro_count)
        slot_at = jnp.clip(slot_raw, 0, micro_count - 1)
        flat_mask = mask_out_all[slot_at].reshape(-1) * is_valid.astype(jnp.float32)
        first_in = section_inputs[slot_at] * mask_in_all[slot_at][..., None].astype(jnp.bfloat16)
        branch = jnp.where(is_valid, jnp.where(is_first, 0, 1), 2).astype(jnp.int32)
        conv_out = lax.switch(branch, [conv_first, conv_rest, conv_spare], recv_act, first_in)
        local_total = jnp.sum(flat_mask)
        weighted = conv_out * flat_mask[None, :, None]
        grand_total, sum_rows = lax.psum((local_total, jnp.sum(weighted, axis=1)), "dp")
        grand_total = jnp.maximum(grand_total, 1.0)
        statistics_mean_rows = sum_rows / grand_total
        centred = conv_out - statistics_mean_rows[:, None, :]
        variance = (
            lax.psum(jnp.sum(centred * centred * flat_mask[None, :, None], axis=1), "dp")
            / grand_total
        )
        grand_total, mean_rows, scale_rows = (
            grand_total,
            statistics_mean_rows,
            lax.rsqrt(variance + epsilon),
        )
        short_in = recv_short.reshape(pixel_rows, channels).astype(jnp.float32)
        pre_act, activated, short_out = finish(conv_out, mean_rows, scale_rows, flat_mask, short_in)
        act_low = activated.astype(jnp.bfloat16).reshape(act_shape)
        short_low = short_out.astype(jnp.bfloat16).reshape(act_shape)
        saved_act = keep_slot(saved_act, recv_act, slot_at, is_valid)
        saved_short = keep_slot(saved_short, recv_short, slot_at, is_valid)
        saved_mean = keep_slot(saved_mean, mean_rows, slot_at, is_valid)
        saved_scale = keep_slot(saved_scale, scale_rows, slot_at, is_valid)
        saved_total = keep_slot(saved_total, grand_total, slot_at, is_valid)
        saved_final = keep_slot(
            saved_final, act_low, slot_at, is_valid & (position == last_section)
        )
        if tick_at + 1 < sweep_len:
            recv_act, recv_short = passed_along((act_low, short_low), "section", 1)
    grad_act = empty_act
    grad_short = empty_act
    weight_acc = zero_weight
    gain_acc = jnp.zeros((2, channels), jnp.float32)
    bias_acc = gain_acc
    saved_dx = jnp.zeros(
        (micro_count, image_count, 2 * half_side, 2 * half_side, in_channels), jnp.bfloat16
    )
    for tick_at in range(sweep_len):
        slot_raw = tick_at - (last_section - position)
        is_valid = (slot_raw >= 0) & (slot_raw < micro_count)
        slot_at = jnp.clip(slot_raw, 0, micro_count - 1)
        flat_mask = mask_out_all[slot_at].reshape(-1) * is_valid.astype(jnp.float32)
        first_in = section_inputs[slot_at] * mask_in_all[slot_at][..., None].astype(jnp.bfloat16)
        branch = jnp.where(is_valid, jnp.where(is_first, 0, 1), 2).astype(jnp.int32)
        prev_act = saved_act[slot_at]
        conv_out = lax.switch(branch, [conv_first, conv_rest, conv_spare], prev_act, first_in)
        mean_rows = saved_mean[slot_at]
        scale_rows = saved_scale[slot_at]
        valid_total = saved_total[slot_at]
        short_in = saved_short[slot_at].reshape(pixel_rows, channels).astype(jnp.float32)
        pre_act, activated, short_out = finish(conv_out, mean_rows, scale_rows, flat_mask, short_in)
        from_act = (
            jnp.where(position == last_section, cot_all[slot_at], grad_act)
            .reshape(pixel_rows, channels)
            .astype(jnp.float32)
        )
        from_short = grad_short.reshape(pixel_rows, channels).astype(jnp.float32)
        slope = silu_slope(pre_act) * flat_mask[:, None]
        grad_pre = (from_act + jnp.where(adds_short, from_short, 0.0)) * slope
        grad_proj = jnp.where(is_first, from_short * flat_mask[:, None], 0.0)
        grad_normed = jnp.stack([grad_pre, grad_proj])
        normalized = (conv_out - mean_rows[:, None, :]) * scale_rows[:, None, :]
        bias_now, gain_now = lax.psum(
            (jnp.sum(grad_normed, axis=1), jnp.sum(grad_normed * normalized, axis=1)), "dp"
        )
        bias_acc = bias_acc + bias_now
        gain_acc = gain_acc + gain_now
        grad_conv = (
            flat_mask[None, :, None]
            * gain_rows[:, None, :]
            * scale_rows[:, None, :]
            * (
                grad_normed
                - (bias_now[:, None, :] + normalized * gain_now[:, None, :]) / valid_total
            )
        )
        grad_conv = grad_conv.astype(jnp.bfloat16)
        weight_now, prev_grad, input_grad = lax.switch(
            branch, [back_first, back_rest, back_spare], grad_conv, prev_act, first_in
        )
        weight_acc = weight_acc + weight_now
        masked_input = (input_grad * mask_in_all[slot_at][..., None]).astype(jnp.bfloat16)
        saved_dx = keep_slot(saved_dx, masked_input, slot_at, is_valid & is_first)
        send_act = (
            (prev_grad + jnp.where(passes_short, from_short, 0.0))
            .astype(jnp.bfloat16)
            .reshape(act_shape)
        )
        send_short = jnp.where(adds_short, grad_pre, 0.0).astype(jnp.bfloat16).reshape(act_shape)
        if tick_at + 1 < sweep_len:
            grad_act, grad_short = passed_along((send_act, send_short), "section", -1)
    weight_total = lax.psum(weight_acc, "dp")
    result = saved_final[last_section]
    for source in range(last_section):
        arrived_piece = passed_along(saved_final[source], "section", source - last_section)
        result = jnp.where(position == source, arrived_piece, result)
    grad_result = saved_dx[0]
    for source in range(1, micro_count):
        arrived_piece = passed_along(saved_dx[source], "section", source)
        grad_result = jnp.where(position == source, arrived_piece, grad_result)
    return (result[None], grad_result[None], weight_total[None], gain_acc[None], bias_acc[None])


f32, bf16 = jnp.float32, jnp.bfloat16
LANES = 256
GRID = (9, 9, 16, LANES)


def flip(value, axis, mask, senders=None):
    count = lax.axis_size(axis)
    pairs = [(i, i ^ mask) for i in range(count) if senders is None or senders(i)]
    return lax.ppermute(value, axis, pairs)


def struct(shape, kind=bf16):
    return jax.ShapeDtypeStruct(shape, kind)


def call(kernel, name, operands, places, outs, out_places, scratch, flops, moved, limit):
    spaces = {"s": pltpu.SMEM, "v": pltpu.VMEM, "a": pl.ANY, "h": pltpu.HBM}
    operands = [
        pltpu.with_memory_space_constraint(one, pltpu.HBM) if place == "h" else one
        for one, place in zip(operands, places)
    ]
    outs = [
        spaces[place](one.shape, one.dtype) if place in "hv" else one
        for one, place in zip(outs, out_places)
    ]
    return pl.pallas_call(
        kernel,
        out_shape=outs,
        in_specs=[pl.BlockSpec(memory_space=spaces[place]) for place in places],
        out_specs=[pl.BlockSpec(memory_space=spaces[place]) for place in out_places],
        scratch_shapes=scratch,
        name=name,
        compiler_params=pltpu.CompilerParams(vmem_limit_bytes=limit * 2**20),
        cost_estimate=pl.CostEstimate(flops=1, bytes_accessed=1, transcendentals=0),
    )(*operands)


def dot(left, right):
    return jnp.dot(left, right, preferred_element_type=f32)


def dot_t(left, right):
    return lax.dot_general(left, right, (((1,), (1,)), ((), ())), preferred_element_type=f32)


def col_sum(values):
    return jnp.sum(values, axis=0, keepdims=True)


def blank_edges(dst):
    blank = jnp.zeros((11, 16, LANES), bf16)
    dst[0] = blank
    dst[10] = blank
    dst[:, 0] = blank
    dst[:, 10] = blank


class Inside:
    def __init__(self, side):
        self.count = col_sum(side * side)
        self.masks = (None, side > 6.0, side > 8.0)

    def keep(self, ring, values):
        mask = self.masks[self.level(ring)]
        return values if mask is None else jnp.where(mask, values, 0.0)

    @staticmethod
    def level(ring):
        return 0 if ring < 5 else 1 if ring < 7 else 2

    def total(self, values_at):
        sums = [None, None, None]
        for row in range(9):
            for col in range(9):
                at = self.level(max(row, col))
                value = values_at(row, col)
                sums[at] = value if sums[at] is None else sums[at] + value
        return col_sum(sums[0] + self.keep(5, sums[1]) + self.keep(7, sums[2]))


def norm_stats(acc, inside):
    mean = inside.total(lambda row, col: acc[row, col]) / inside.count

    def squared(row, col):
        centred = acc[row, col] - mean
        return centred * centred

    return mean, lax.rsqrt(inside.total(squared) / inside.count + epsilon)


def sigmoid_of(values):
    return 0.5 * jnp.tanh(0.5 * values) + 0.5


def split_three(row):
    high = row.astype(bf16)
    rest = row - high.astype(f32)
    middle = rest.astype(bf16)
    low = (rest - middle.astype(f32)).astype(bf16)
    return [high, middle, low]


def pack_vectors(rows):
    pieces = [one.astype(f32) for row in rows for one in split_three(row)]
    pieces.append(jnp.zeros((16 - len(pieces), LANES), f32))
    return jnp.concatenate(pieces, axis=0).astype(bf16)


def unpack_vectors(block):
    wide = block.astype(f32)
    return [wide[3 * at : 3 * at + 1] + wide[3 * at + 1 : 3 * at + 2] + wide[3 * at + 2 : 3 * at + 3] for at in range(4)]


def pack_rows(ref, rows):
    ref[...] = jnp.concatenate(rows + [jnp.zeros((8 - len(rows), LANES), f32)], axis=0)


def turn_matrix(image_of_row):
    out_row = lax.broadcasted_iota(jnp.int32, (256, 256), 0)
    in_row = lax.broadcasted_iota(jnp.int32, (256, 256), 1)
    pixel_same = (out_row >> 4) == (in_row & 15)
    return jnp.where(pixel_same & ((out_row & 15) == image_of_row(in_row)), 1.0, 0.0).astype(bf16)


def split_weights(sc, matrix, vectors):
    def kernel(sc_ref, matrix_ref, vec_ref, for_x, for_y, sems):
        lane = pl.multiple_of(LANES * sc_ref[2], LANES)
        chosen = matrix_ref.at[:, pl.ds(lane, LANES)]

        def copies(target, first, at):
            return [
                pltpu.make_async_copy(
                    chosen.at[first + 640 * cut : first + 640 * cut + 640],
                    target.at[16 + 640 * cut : 656 + 640 * cut],
                    sems.at[at + cut],
                )
                for cut in range(4)
            ]

        along_x = copies(for_x, 0, 0)
        for copy in along_x:
            copy.start()
        small = pack_vectors([vec_ref[at : at + 1, pl.ds(lane, LANES)] for at in range(4)])
        for_x[0:16] = small
        for_y[0:16] = small
        for first, here in ((0, sc_ref[0] == 0), (2048, sc_ref[0] != 0)):

            @pl.when(here)
            def _():
                along_y = copies(for_y, first, 4)
                for copy in along_y:
                    copy.start()
                for copy in along_y:
                    copy.wait()

        for copy in along_x:
            copy.wait()

    return call(
        kernel, "split_weights", (sc, matrix, vectors), "shv", [struct((2576, LANES))] * 2, "vv",
        [pltpu.SemaphoreType.DMA((8,))], 0, 14_000_000, 20,
    )


def relay_weights(name, is_own, operands, first=None):
    def kernel(sc_ref, own_x, own_y, x_1, y_1, for_x, for_y, *more):
        chosen = is_own(sc_ref[0])
        for x_from, y_from, here in ((own_x, own_y, chosen), (x_1, y_1, jnp.logical_not(chosen))):

            @pl.when(here)
            def _():
                for_x[...] = y_from[272:2576]
                for_y[...] = x_from[0:2320]

        if more:
            more[0][...] = y_1[0:1296]
            more[1][...] = x_1[1296:2576]

    outs = [struct((2304, LANES)), struct((2320, LANES))]
    if first:
        outs += [struct((1296, LANES)), struct((1280, LANES))]
    return call(kernel, name, operands, "svvvv", outs, len(outs) * "v", [], 0, 14_000_000, 20)


def prepare_images(sc, pieces):
    def kernel(sc_ref, *refs):
        piece_refs, (out, side_out, held, sems) = refs[:8], refs[8:]
        core = sc_ref[2]
        copies = [
            pltpu.make_async_copy(ref, held.at[2 * at : 2 * at + 2], sems.at[at])
            for at, ref in enumerate(piece_refs)
        ]
        for copy in copies:
            copy.start()
        turn = turn_matrix(lambda r: ((r >> 4) + 8 * core) & 15)
        out[:, :, 0] = jnp.zeros((2, 2, 10, 16, LANES), bf16)
        out[:, :, :, 0] = jnp.zeros((2, 2, 10, 16, LANES), bf16)
        for copy in copies:
            copy.wait()

        def block(at):
            source = held[:, 16 * at : 16 * at + 16].reshape(256, LANES)
            return dot(turn, source).reshape(16, 16, LANES)

        last = block(20)
        side = last[4]
        side_out[...] = side
        masks = (None, 2.0 * side > 13.0, 2.0 * side > 17.0)
        for at in range(21):
            turned = last if at == 20 else block(at)
            for step in range(16 if at < 20 else 4):
                row, col = divmod(16 * at + step, 18)
                mask = masks[Inside.level(max(row, col) // 2)]
                kept = turned[step] if mask is None else jnp.where(mask, turned[step], 0.0)
                out[row % 2, col % 2, 1 + row // 2, 1 + col // 2] = kept.astype(bf16)

    outs = [struct((2, 2, 10, 10, 16, LANES)), struct((16, LANES), f32)]
    scratch = [pltpu.VMEM((16, 336, LANES), bf16), pltpu.SemaphoreType.DMA((8,))]
    return call(
        kernel, "prepare_images", (sc, *pieces), "s" + 8 * "h", outs, "vv", scratch,
        21 * 2 * 256**3, 8_000_000, 20,
    )


def prepare_cotangent(sc, pieces):
    def kernel(sc_ref, *refs):
        piece_refs, (out, held, sems) = refs[:2], refs[2:]
        core = sc_ref[2]
        copies = [
            pltpu.make_async_copy(ref, held.at[2 * at : 2 * at + 2], sems.at[at])
            for at, ref in enumerate(piece_refs)
        ]
        for copy in copies:
            copy.start()
        turn = turn_matrix(
            lambda r: (((r >> 5) & 1) ^ core) * 8 + 2 * (r >> 6) + ((r >> 4) & 1)
        )
        for copy in copies:
            copy.wait()
        for at in range(6):
            source = held[:, :, :, 16 * at : 16 * at + 16].reshape(256, LANES)
            turned = dot(turn, source).astype(bf16).reshape(16, 16, LANES)
            for step in range(16 if at < 5 else 1):
                row, col = divmod(16 * at + step, 9)
                out[row, col] = turned[step]

    scratch = [pltpu.VMEM((4, 2, 2, 96, LANES), bf16), pltpu.SemaphoreType.DMA((4,))]
    return call(
        kernel, "prepare_cotangent", (sc, *pieces), "saa", [struct(GRID)], "v", scratch,
        6 * 2 * 256**3, 2_000_000, 20,
    )[0]


def any_of(section, sections):
    chosen = section == sections[0]
    for other in sections[1:]:
        chosen = chosen | (section == other)
    return chosen


def stage_first(sc, side, fields, messages):
    def kernel(sc_ref, side_ref, field, own_x, x_1, y_1, top, bottom, hidden, short, zhat, zhat_p, stats, w, vec, acc, acc_p, short_now, out_sems):
        section = sc_ref[0]
        for at, whole in enumerate((own_x, x_1, y_1)):

            @pl.when(section == at)
            def _():
                w[...] = whole[16:2576]
                vec[...] = whole[0:16]

        @pl.when(section == 3)
        def _():
            w[0:1280] = top[16:1296]
            w[1280:2560] = bottom[...]
            vec[...] = top[0:16]

        outs = []
        for chunk in range(3):
            total = jnp.zeros((432, LANES), f32)
            for a in range(3):
                for b in range(3):
                    row_at, col_at = 3 * chunk + (0 if a == 0 else 1), 0 if b == 0 else 1
                    left = field[(a + 1) % 2, (b + 1) % 2, row_at : row_at + 3, col_at : col_at + 9]
                    at = LANES * (3 * a + b)
                    total = total + dot(left.reshape(432, LANES), w[at : at + LANES])
            span = slice(3 * chunk, 3 * chunk + 3)
            acc[span] = total.reshape(3, 9, 16, LANES)
            centre = field[0, 0, 3 * chunk + 1 : 3 * chunk + 4, 1:10].reshape(432, LANES)
            acc_p[span] = dot(centre, w[2304:2560]).reshape(3, 9, 16, LANES)
            for at, (source, target) in enumerate(((acc, zhat), (acc_p, zhat_p))):
                outs.append(
                    pltpu.make_async_copy(
                        source.at[span], target.at[span], out_sems.at[1 + 3 * at + chunk]
                    )
                )
                outs[-1].start()
        inside = Inside(side_ref[...])
        mean, scale = norm_stats(acc, inside)
        mean_p, scale_p = norm_stats(acc_p, inside)
        gain, gain_p, bias, bias_p = unpack_vectors(vec[...])
        for row in range(9):
            for col in range(9):
                ring = max(row, col)
                pre = (acc[row, col] - mean) * scale * gain + bias
                hidden[row, col] = inside.keep(ring, pre * sigmoid_of(pre)).astype(bf16)
                normed = (acc_p[row, col] - mean_p) * scale_p
                short_now[row, col] = inside.keep(ring, normed * gain_p + bias_p).astype(bf16)
            outs.append(pltpu.make_async_copy(short_now.at[row], short.at[row], out_sems.at[7 + row]))
            outs[-1].start()
        pack_rows(stats, [scale, gain, bias, mean, scale_p, gain_p, mean_p])
        for copy in outs:
            copy.wait()

    outs = [
        struct(GRID), struct(GRID), struct(GRID, f32), struct(GRID, f32), struct((8, LANES), f32),
        struct((2560, LANES)),
    ]
    scratch = [
        pltpu.VMEM((16, LANES), bf16), pltpu.VMEM(GRID, f32), pltpu.VMEM(GRID, f32),
        pltpu.VMEM(GRID, bf16), pltpu.SemaphoreType.DMA((16,)),
    ]
    return call(
        kernel, "stage_first", (sc, side, fields, *messages), "svv" + 5 * "v", outs, "vhhhvv",
        scratch, 2 * 1296 * 2560 * LANES, 8_000_000, 20,
    )


def fill_field(padded, source):
    blank_edges(padded)
    padded[1:10, 1:10] = source[...]


def fill_weights(part, section, core, messages, keep, send, vec):
    own_x, own_y, x_1, y_1, x_2, y_2 = messages
    upper = {1: {0: x_1, 1: own_x}, 2: {2: own_x, 3: x_1}, 3: {2: x_1, 3: own_x}}[part]
    lower = {1: {1: own_y, 3: y_1}, 2: {0: y_1, 2: own_y}, 3: {1: y_1, 3: own_y}}[part]
    far_upper = [section for section in range(4) if section not in upper]
    far_lower = [section for section in range(4) if section not in lower]
    entries = [((at,), ref, 16, 0) for at, ref in upper.items()] + [(far_upper, y_2, 16, 0)]
    entries += [((at,), ref, 272, 9) for at, ref in lower.items()] + [(far_lower, x_2, 0, 9)]
    for half in range(2):
        for sections, ref, first, block in entries:

            @pl.when((core == half) & any_of(section, sections))
            def _():
                for at in range(9):
                    tap, which = divmod(block + at, 2)
                    target = keep if which == half else send
                    start = first + LANES * at
                    target[LANES * tap : LANES * tap + LANES] = ref[start : start + LANES]
                if block == 0:
                    vec[...] = ref[0:16]


def stage_rest(part, sc, side, own, other, messages, short, cot=None, after=()):
    last = cot is not None
    extra = [one for one in (short, cot) if one is not None]

    def kernel(sc_ref, side_ref, own_ref, oth_ref, *refs):
        refs = list(refs)
        late_refs = [refs.pop(0) for _ in extra]
        weights = refs[0:6]
        refs = refs[6 + len(after) :]
        if last:
            dz, passed, out, sums = refs[:4]
            refs = refs[4:]
        else:
            hidden, zhat, stats = refs[:3]
            refs = refs[3:]
        w_keep, w_send, vec, padded, acc = refs[:5]
        grads, passed_now = refs[5:7] if last else (None, None)
        late, sems, out_sems = refs[-3:]
        short_ref = late.at[0] if short is not None else None
        cot_ref = late.at[1] if last else None
        section, core = sc_ref[0], sc_ref[2]
        late_loads = [
            pltpu.make_async_copy(ref, late.at[at], sems.at[at]) for at, ref in enumerate(late_refs)
        ]
        for copy in late_loads:
            copy.start()
        fill_weights(part, section, core, weights, w_keep, w_send, vec)
        fill_field(padded.at[0], own_ref)
        fill_field(padded.at[1], oth_ref)
        outs = []
        for chunk in range(3):
            total = jnp.zeros((432, LANES), f32)
            for a in range(3):
                for b in range(3):
                    for at in range(2):
                        left = padded[at, 3 * chunk + a : 3 * chunk + a + 3, b : b + 9]
                        from_row = LANES * (3 * a + b)
                        right = (w_keep, w_send)[at][from_row : from_row + LANES]
                        total = total + dot(left.reshape(432, LANES), right)
            acc[3 * chunk : 3 * chunk + 3] = total.reshape(3, 9, 16, LANES)
            if not last:
                outs.append(
                    pltpu.make_async_copy(
                        acc.at[3 * chunk : 3 * chunk + 3],
                        zhat.at[3 * chunk : 3 * chunk + 3],
                        out_sems.at[18 + chunk],
                    )
                )
                outs[-1].start()
        inside = Inside(side_ref[...])
        mean, scale = norm_stats(acc, inside)
        for copy in late_loads:
            copy.wait()
        gain, _, bias, _ = unpack_vectors(vec[...])
        if last:
            sums_now = [None, None]
        for row in range(9):
            for col in range(9):
                ring = max(row, col)
                normed = (acc[row, col] - mean) * scale
                if last:
                    acc[row, col] = normed
                pre = normed * gain + bias
                if short is not None:
                    pre = pre + short_ref[row, col].astype(f32)
                sigmoid = sigmoid_of(pre)
                target = out if last else hidden
                target[row, col] = inside.keep(ring, pre * sigmoid).astype(bf16)
                if last:
                    slope = sigmoid * (1.0 + pre * (1.0 - sigmoid))
                    grad = inside.keep(ring, cot_ref[row, col].astype(f32) * slope)
                    grads[row, col] = grad
                    passed_now[row, col] = grad.astype(bf16)
                    for at, value in enumerate((grad, grad * normed)):
                        sums_now[at] = value if sums_now[at] is None else sums_now[at] + value
            if last:
                outs.append(
                    pltpu.make_async_copy(passed_now.at[row], passed.at[row], out_sems.at[18 + row])
                )
                outs[-1].start()
        if last:
            bias_now, gain_now = col_sum(sums_now[0]), col_sum(sums_now[1])
            norm_back(dz, grads, acc, inside, gain * scale, bias_now, gain_now)
            pack_rows(sums, [gain_now, bias_now])
        else:
            pack_rows(stats, [scale, gain, bias, mean])
        for copy in outs:
            copy.wait()

    half = struct((2304, LANES))
    if last:
        outs, places = [struct(GRID), struct(GRID), struct(GRID), struct((8, LANES), f32)], "vhvv"
    else:
        outs, places = [struct(GRID), struct(GRID, f32), struct((8, LANES), f32)], "vhv"
    scratch = [
        pltpu.VMEM((16, LANES), bf16), pltpu.VMEM((2, 11, 11, 16, LANES), bf16), pltpu.VMEM(GRID, f32)
    ] + ([pltpu.VMEM(GRID, f32), pltpu.VMEM(GRID, bf16)] if last else [])
    scratch += [
        pltpu.VMEM((2, *GRID), bf16), pltpu.SemaphoreType.DMA((2,)), pltpu.SemaphoreType.DMA((27,)),
    ]
    return call(
        kernel, f"stage_{part}", (sc, side, own, other, *extra, *messages, *after),
        "svvv" + len(extra) * "a" + 6 * "v" + len(after) * "a", outs + [half, half], places + "vv", scratch,
        2 * 1296 * 4608 * LANES, 8_000_000, 20,
    )


def norm_back(dz, grads, zhat, inside, weight, bias_now, gain_now):
    constant, slope = weight * bias_now / inside.count, weight * gain_now / inside.count
    for row in range(9):
        for col in range(9):
            value = weight * grads[row, col] - (constant + slope * zhat[row, col])
            dz[row, col] = inside.keep(max(row, col), value).astype(bf16)


def stage_back(part, sc, side, dz_own, dz_other, w_own, w_other, zhat, stats, short=None, extra=None, proj=None):
    first = proj is not None
    optional = [one for one in (short, extra) if one is not None] + (list(proj) if first else [])

    def kernel(sc_ref, side_ref, stats_ref, dz_own_ref, dz_oth_ref, w_own_ref, w_oth_ref, zhat_ref, *refs):
        refs = list(refs)
        late_refs = [refs.pop(0) for one in (short, extra) if one is not None]
        if first:
            dyp_ref, zhat_p_ref = refs.pop(0), refs.pop(0)
        dz, sums = refs.pop(0), refs.pop(0)
        passed = refs.pop(0) if short is not None else None
        dz_p = refs.pop(0) if first else None
        padded, acc, held = refs[:3]
        held_p = refs[3] if first else None
        late = None if first else refs[3]
        sems = refs[-1]
        short_ref = late.at[0] if short is not None else None
        extra_ref = late.at[1] if extra is not None else None
        later = [pltpu.make_async_copy(zhat_ref, held, sems.at[4])]
        if first:
            later.append(pltpu.make_async_copy(zhat_p_ref, held_p, sems.at[5]))
        for at, ref in enumerate(late_refs):
            later.append(pltpu.make_async_copy(ref, late.at[at], sems.at[6 + at]))
        for copy in later:
            copy.start()
        fill_field(padded.at[0], dz_own_ref)
        fill_field(padded.at[1], dz_oth_ref)
        for chunk in range(3):
            total = jnp.zeros((432, LANES), f32)
            for a in range(3):
                for b in range(3):
                    for at in range(2):
                        row_at = 3 * chunk + 2 - a
                        left = padded[at, row_at : row_at + 3, 2 - b : 11 - b]
                        from_row = LANES * (3 * a + b)
                        right = (w_own_ref, w_oth_ref)[at][from_row : from_row + LANES]
                        total = total + dot_t(left.reshape(432, LANES), right)
            acc[3 * chunk : 3 * chunk + 3] = total.reshape(3, 9, 16, LANES)
        for copy in later:
            copy.wait()
        inside = Inside(side_ref[...])
        scale, gain, bias, mean, scale_p, gain_p, mean_p = [stats_ref[at : at + 1] for at in range(7)]
        sums_now = [None] * 4
        for row in range(9):
            for col in range(9):
                ring = max(row, col)
                normed = (held[row, col] - mean) * scale
                held[row, col] = normed
                pre = normed * gain + bias
                grad = acc[row, col]
                if extra is not None:
                    grad = grad + extra_ref[row, col].astype(f32)
                if short is not None:
                    pre = pre + short_ref[row, col].astype(f32)
                sigmoid = sigmoid_of(pre)
                slope = sigmoid * (1.0 + pre * (1.0 - sigmoid))
                grad = inside.keep(ring, grad.astype(bf16).astype(f32) * slope)
                acc[row, col] = grad
                if short is not None:
                    passed[row, col] = grad.astype(bf16)
                terms = [grad, grad * normed]
                if first:
                    grad_p = dyp_ref[row, col].astype(f32)
                    normed_p = (held_p[row, col] - mean_p) * scale_p
                    held_p[row, col] = normed_p
                    terms += [grad_p, grad_p * normed_p]
                for at, value in enumerate(terms):
                    sums_now[at] = value if sums_now[at] is None else sums_now[at] + value
        totals = [col_sum(value) for value in sums_now if value is not None]
        norm_back(dz, acc, held, inside, gain * scale, totals[0], totals[1])
        rows = [totals[1], totals[0]]
        if first:
            for row in range(9):
                for col in range(9):
                    acc[row, col] = dyp_ref[row, col].astype(f32)
            norm_back(dz_p, acc, held_p, inside, gain_p * scale_p, totals[2], totals[3])
            rows += [totals[3], totals[2]]
        pack_rows(sums, rows)

    outs, places = [struct(GRID), struct((8, LANES), f32)], "vv"
    if short is not None:
        outs, places = outs + [struct(GRID)], places + "v"
    if first:
        outs, places = outs + [struct(GRID)], places + "v"
    scratch = [
        pltpu.VMEM((2, 11, 11, 16, LANES), bf16), pltpu.VMEM(GRID, f32), pltpu.VMEM(GRID, f32)
    ] + [pltpu.VMEM(GRID, f32) if first else pltpu.VMEM((2, *GRID), bf16)]
    scratch += [pltpu.SemaphoreType.DMA((8,))]
    kinds = "h" * ((short is not None) + (extra is not None)) + ("vh" if first else "")
    return call(
        kernel, f"back_{part}",
        (sc, side, stats, dz_own, dz_other, w_own, w_other, zhat, *optional),
        "svvvvvvh" + kinds, outs, places, scratch, 2 * 1296 * 4608 * LANES, 10_000_000, 20,
    )


def pick_images(sc, *fields):
    def kernel(sc_ref, *refs):
        core = sc_ref[2]
        keep, give = refs[-2:]
        out_row = lax.broadcasted_iota(jnp.int32, (4, 96, 1296), 1)
        slot = lax.broadcasted_iota(jnp.int32, (4, 96, 1296), 0)
        in_row = lax.broadcasted_iota(jnp.int32, (4, 96, 1296), 2)
        image = 8 * ((slot >> 1) ^ core) + (slot & 1)
        pick = jnp.where(in_row == 16 * out_row + image, 1.0, 0.0).astype(bf16).reshape(384, 1296)
        for at, source in enumerate(refs[:-2]):
            chosen = dot(pick, source[...].reshape(1296, LANES)).astype(bf16).reshape(4, 96, LANES)
            keep[at] = chosen[0:2]
            give[at] = chosen[2:4]

    count = len(fields)
    return call(
        kernel, "pick_images", (sc, *fields), "s" + count * "v", 2 * [struct((count, 2, 96, LANES))],
        "vv", [], count * 2 * 384 * 1296 * LANES, 3_000_000, 20,
    )


def weight_rest(part, sc, own, other, dz, sums, tail=None):
    def kernel(sc_ref, own_ref, oth_ref, dz_ref, sums_ref, *refs):
        out, turned, padded = refs[-3:]
        if tail is not None:
            out[1168:1568] = refs[0][768:1168]
        zone, core = sc_ref[1], sc_ref[2]
        fill_field(padded, dz_ref)
        lane = pl.multiple_of(128 * (zone & 1), 128)
        is_own = (zone >> 1) == core

        @pl.when(is_own)
        def _():
            turned[...] = own_ref[:, :, :, pl.ds(lane, 128)].reshape(1296, 128).T

        @pl.when(jnp.logical_not(is_own))
        def _():
            turned[...] = oth_ref[:, :, :, pl.ds(lane, 128)].reshape(1296, 128).T

        left = turned[...]
        for a in range(3):
            for b in range(3):
                right = padded[2 - a : 11 - a, 2 - b : 11 - b].reshape(1296, LANES)
                at = 128 * (3 * a + b)
                out[at : at + 128] = dot(left, right).astype(bf16)
        blank = jnp.zeros((1, LANES), f32)
        out[1152:1168] = pack_vectors([sums_ref[0:1], blank, sums_ref[1:2], blank])

    scratch = [
        pltpu.VMEM((128, 1296), bf16), pltpu.VMEM((11, 11, 16, LANES), bf16)
    ]
    return call(
        kernel, f"weight_{part}", (sc, own, other, dz, sums) + (() if tail is None else (tail,)),
        "svvvv" + ("" if tail is None else "v"), [struct((1168 if tail is None else 1568, LANES))], "v",
        scratch, 2 * 1296 * 1152 * LANES, 3_000_000, 20,
    )[0]


def weight_first(sc, fields, dz, dz_p, sums):
    def kernel(sc_ref, field, dz_ref, dz_p_ref, sums_ref, out, turned, padded):
        zone = sc_ref[1]
        fill_field(padded, dz_ref)
        lane = pl.multiple_of(128 * (zone >> 1), 128)
        at = pl.multiple_of(64 * (zone & 1), 64)
        for phase in range(4):
            chosen = field[phase // 2, phase % 2, 1:10, 1:10, :, pl.ds(lane, 128)]
            turned[phase] = chosen.reshape(1296, 128).T
        for tap in range(10):
            if tap < 9:
                a, b = divmod(tap, 3)
                left = turned[2 * ((a + 1) % 2) + (b + 1) % 2, pl.ds(at, 64)]
                row_at, col_at = 2 if a == 0 else 1, 2 if b == 0 else 1
                right = padded[row_at : row_at + 9, col_at : col_at + 9].reshape(1296, LANES)
            else:
                left = turned[0, pl.ds(at, 64)]
                right = dz_p_ref[...].reshape(1296, LANES)
            out[64 * tap : 64 * tap + 64] = dot(left, right).astype(bf16)
        out[640:656] = pack_vectors([sums_ref[0:1], sums_ref[2:3], sums_ref[1:2], sums_ref[3:4]])

    scratch = [
        pltpu.VMEM((4, 128, 1296), bf16), pltpu.VMEM((11, 11, 16, LANES), bf16)
    ]
    return call(
        kernel, "weight_first", (sc, fields, dz, dz_p, sums), "svvvv", [struct((656, LANES))], "v",
        scratch, 2 * 1296 * 640 * LANES, 3_000_000, 20,
    )[0]


def image_back(sc, own, other, w_own, w_other):
    def kernel(sc_ref, own_all, oth_all, w_own_ref, w_oth_ref, out, block):
        for source, half in ((own_all, sc_ref[2]), (oth_all, 1 - sc_ref[2])):
            block[:, :, pl.ds(pl.multiple_of(LANES * half, LANES), LANES)] = source[2]
        own_ref, own_p_ref = own_all.at[0], own_all.at[1]
        oth_ref, oth_p_ref = oth_all.at[0], oth_all.at[1]
        row = lax.broadcasted_iota(jnp.int32, (192, 192), 0)
        col = lax.broadcasted_iota(jnp.int32, (192, 192), 1)
        pixel = jnp.where(row >= 96, row - 96, row)
        line = (pixel * 57) >> 9
        across = pixel - 9 * line
        shifted = {}
        for down in range(2):
            for right in range(2):
                if down + right == 0:
                    shifted[0, 0] = (
                        own_ref[...].reshape(192, LANES),
                        oth_ref[...].reshape(192, LANES),
                    )
                    continue
                fits = (pixel < 81) & (line + down < 9) & (across + right < 9)
                move = jnp.where(fits & (col == row + 9 * down + right), 1.0, 0.0).astype(bf16)
                shifted[down, right] = tuple(
                    dot(move, ref[...].reshape(192, LANES)).astype(bf16)
                    for ref in (own_ref, oth_ref)
                )
        phases = [jnp.zeros((192, LANES), f32) for _ in range(4)]
        for a in range(3):
            for b in range(3):
                at = 2 * ((a + 1) % 2) + (b + 1) % 2
                left = shifted[1 if a == 0 else 0, 1 if b == 0 else 0]
                rows = slice(LANES * (3 * a + b), LANES * (3 * a + b + 1))
                phases[at] = phases[at] + dot_t(left[0], w_own_ref[rows])
                phases[at] = phases[at] + dot_t(left[1], w_oth_ref[rows])
        phases[0] = phases[0] + dot_t(own_p_ref[...].reshape(192, LANES), w_own_ref[2304:2560])
        phases[0] = phases[0] + dot_t(oth_p_ref[...].reshape(192, LANES), w_oth_ref[2304:2560])
        joined = jnp.concatenate([phase.astype(bf16) for phase in phases], axis=0)
        out_row = lax.broadcasted_iota(jnp.int32, (336, 768), 0)
        in_row = lax.broadcasted_iota(jnp.int32, (336, 768), 1)
        line = (out_row * 3641) >> 16
        across = out_row - 18 * line
        source = (2 * (line & 1) + (across & 1)) * 192 + 9 * (line >> 1) + (across >> 1)
        for image in range(2):
            spread = jnp.where(
                (in_row == source + 96 * image) & (out_row < 324), 1.0, 0.0
            ).astype(bf16)
            out[image] = dot(spread, joined).astype(bf16)

    return call(
        kernel, "image_back", (sc, own, other, w_own, w_other), "svvvv",
        [struct((2, 336, LANES)), struct((2, 96, 2 * LANES))], "vv", [], 2 * 192 * 2560 * 512 + 4 * 336 * 768 * 256, 4_000_000, 20,
    )


def add_into(out, rows, sources, vector_rows):
    for at in range(0, rows, 64):
        total = sources[0][at : at + 64].astype(f32)
        for source in sources[1:]:
            total = total + source[at : at + 64].astype(f32)
        out[at : at + 64] = total.astype(bf16)
    totals = [unpack_vectors(source[rows : rows + 16]) for source in sources]
    sums = [sum(one[1:], one[0]) for one in zip(*totals)]
    out[vector_rows : vector_rows + 16] = pack_vectors(sums)


def add_pieces(part, one, two):
    rows = one.shape[0] - 16

    def kernel(one_ref, two_ref, out):
        add_into(out, rows, (one_ref, two_ref), rows)

    return call(
        kernel, f"add_{part}", (one, two), "vv", [struct(one.shape)], "v", [], 1, 1_000_000, 20
    )[0]


def add_two(sc, three, two, came_three, came_two):
    def kernel(sc_ref, three_ref, two_ref, came_three_ref, came_two_ref, keep, give):
        for at_three, out_three, out_two in ((True, keep, give), (False, give, keep)):

            @pl.when((sc_ref[0] == 3) if at_three else (sc_ref[0] != 3))
            def _():
                for at in range(0, 768, 64):
                    span = slice(at, at + 64)
                    total = three_ref[span].astype(f32) + came_three_ref[span].astype(f32)
                    out_three[span] = total.astype(bf16)
                tails = (three_ref.at[768:1168], came_two_ref.at[1168:1568])
                add_into(out_three.at[768:1168], 384, tails, 384)
                add_into(out_two, 1152, (two_ref, came_two_ref), 1152)

    return call(
        kernel, "add_two", (sc, three, two, came_three, came_two), "svvvv", [struct((1168, LANES))] * 2,
        "vv", [], 1, 1_000_000, 20,
    )


def own_piece(sc, groups, after):
    pieces = [piece for _, group in groups for piece in group]

    def kernel(sc_ref, *refs):
        out, used = refs[-1], 0
        for sections, group in groups:
            sources = refs[used : used + len(group)]
            used += len(group)
            rows = group[0].shape[0] - 16

            @pl.when(any_of(sc_ref[0], sections))
            def _():
                add_into(out, rows, sources, 1152)

    return call(
        kernel, "own_piece", (sc, *pieces, *after), "s" + len(pieces) * "v" + len(after) * "a",
        [struct((1168, LANES))], "v", [], 1, 1_000_000, 20,
    )[0]


def lay_out(sc, own, other):
    def kernel(sc_ref, *refs):
        pieces, (out, vectors, wide, out_sems) = refs[:12], refs[12:]
        section, zone, core = sc_ref[0], sc_ref[1], sc_ref[2]
        at_end = (zone == 0) | (zone == 3)
        is_first = section == 0
        for tap in range(9):
            slot = tap % 3
            leaving = [
                pltpu.make_async_copy(
                    wide.at[slot, 128 * cut : 128 * cut + 128],
                    out.at[512 * tap + 128 * cut : 512 * tap + 128 * cut + 128],
                    out_sems.at[slot, cut],
                )
                for cut in range(4)
            ]
            if tap >= 3:
                for copy in leaving:
                    copy.wait()

            def place(which, row_of, rows, first):
                origin = zone ^ (0, 1, 2, 3, 2, 3)[which]
                row = pl.multiple_of(row_of(origin), rows)
                for half in range(2):
                    lane = pl.multiple_of(LANES * (core ^ half), LANES)
                    value = jnp.zeros((rows, LANES), f32)
                    if first + rows <= 1152:
                        value = pieces[which + 6 * half][first : first + rows].astype(f32)
                    wide[slot, pl.ds(row, rows), pl.ds(lane, LANES)] = value

            for kind, chosen in ((0, at_end), (1, jnp.logical_not(at_end))):
                used = (0, 1, 4, 5) if kind == 0 else (0, 1, 2, 3)

                @pl.when(chosen & jnp.logical_not(is_first))
                def _():
                    for which in used:
                        place(which, lambda origin: 128 * origin, 128, 128 * tap)

                @pl.when(chosen & is_first)
                def _():
                    for part in range(2):
                        start = 64 * (2 * tap + part)
                        for which in used:
                            place(
                                which,
                                lambda origin: 256 * part + 64 * origin,
                                64,
                                start if start < 640 else 1152,
                            )

            for copy in leaving:
                copy.start()
        for half in range(2):
            rows = unpack_vectors(pieces[6 * half][1152:1168])
            lane = pl.multiple_of(LANES * (core ^ half), LANES)
            vectors[:, pl.ds(lane, LANES)] = jnp.concatenate(rows, axis=0)
        for slot in range(3):
            for cut in range(4):
                pltpu.make_async_copy(
                    wide.at[slot, 0:128], out.at[0:128], out_sems.at[slot, cut]
                ).wait()

    return call(
        kernel, "lay_out", (sc, *own, *other), "s" + 12 * "v", [struct((4608, 512), f32), struct((4, 512), f32)], "hv",
        [pltpu.VMEM((3, 512, 512), f32), pltpu.SemaphoreType.DMA((3, 4))], 0, 15_000_000, 20,
    )


def half_of(value, half):
    return lax.dynamic_slice_in_dim(value, LANES * half, LANES, axis=value.ndim - 1)


def chip_body(images, res_ids, weights, bn_gain, bn_bias, cotangent):
    section = lax.axis_index("section")
    position = lax.axis_index("dp")
    zone, core = position // 2, position % 2
    sc = jnp.stack([section, zone, core, core]).astype(jnp.int32)

    def after(value, *tokens):
        return lax.optimization_barrier((value, *tokens))[0]

    own = split_weights(sc, weights[0], jnp.concatenate([bn_gain[0], bn_bias[0]], axis=0))
    x_1 = flip(own[0], "section", 1)
    y_1 = flip(own[1], "section", 2)

    level = lax.dynamic_index_in_dim(res_ids, section, 0, keepdims=False)
    side_own = (9 - 2 * (2 - level)).astype(f32)
    tail = jnp.broadcast_to(side_own[:, None, None], (2, 12, 256)).astype(bf16)
    image_own = jnp.concatenate([after(images, own[0])[0].reshape(2, 324, 256), tail], axis=1)
    pieces = [image_own] + [flip(image_own, "dp", 2 * at) for at in range(1, 4)]
    pieces += [flip(piece, "dp", 1) for piece in pieces]
    cot_own = after(cotangent, pieces[1])[0].reshape(2, 81, 512)
    cot_pair = jnp.stack([half_of(cot_own, core), flip(half_of(cot_own, 1 - core), "dp", 1)])
    cot_pair = jnp.pad(cot_pair, ((0, 0), (0, 0), (0, 15), (0, 0)))
    cot_near = jnp.stack([cot_pair, flip(cot_pair, "dp", 2)])
    for_x, for_y, top, bottom = relay_weights(
        "relay_2", lambda at: (at == 1) | (at == 2), (after(sc, cot_near), *own, x_1, y_1), True
    )
    top = flip(top, "section", 1, lambda i: i == 2)
    bottom = flip(bottom, "section", 2, lambda i: i == 1)
    fields, side = prepare_images(after(sc, for_x), pieces)
    cot_pieces = (cot_near, flip(after(cot_near, fields), "dp", 4))
    x_2 = flip(for_x, "section", 1)
    y_2 = flip(for_y, "section", 2)
    hidden_one, short_one, zhat_0, zhat_p, stats_0, w_first = stage_first(
        sc, side, after(fields, for_x), (own[0], x_1, y_1, top, bottom)
    )
    hidden_one_other = flip(hidden_one, "dp", 1)
    w_first_other = flip(w_first, "dp", 1)
    for_x, for_y = relay_weights("relay_3", lambda at: at == 3, (after(sc, stats_0), *own, x_1, y_1))
    x_3 = flip(for_x, "section", 1, lambda i: i in (1, 3))
    y_3 = flip(for_y, "section", 2, lambda i: i in (2, 3))
    messages = (*own, x_1, y_1, x_2, y_2)
    block_one, zhat_1, stats_1, keep_1, send_1 = stage_rest(
        1, sc, side, hidden_one, hidden_one_other, messages, short_one, after=cot_pieces
    )
    block_one_other = flip(block_one, "dp", 1)
    other_1 = flip(send_1, "dp", 1)
    cot = prepare_cotangent(sc, after(cot_pieces, stats_1))
    hidden_two, zhat_2, stats_2, keep_2, send_2 = stage_rest(
        2, sc, side, block_one, block_one_other, messages, None, after=(x_3, y_3, cot)
    )
    hidden_two_other = flip(hidden_two, "dp", 1)
    other_2 = flip(send_2, "dp", 1)
    messages = (*own, x_1, y_1, x_3, y_3)
    dz_3, passed, out, sums_3, keep_3, send_3 = stage_rest(
        3, sc, side, hidden_two, hidden_two_other, messages, block_one, cot
    )
    other_3 = flip(send_3, "dp", 1)
    dz_3_other = flip(dz_3, "dp", 1)

    def to_pair(part, piece):
        return flip(piece, "section", 2, lambda i: i ^ 2 in (part, part ^ 1))

    piece_3 = weight_rest(3, sc, hidden_two, hidden_two_other, dz_3, sums_3)
    came_3 = to_pair(3, piece_3[0:768])
    dz_2, sums_2 = stage_back(
        2, sc, side, after(dz_3, piece_3), dz_3_other, keep_3, other_3, zhat_2, stats_2
    )
    dz_2_other = flip(dz_2, "dp", 1)
    piece_2 = weight_rest(2, sc, block_one, block_one_other, dz_2, sums_2, piece_3)
    came_2 = to_pair(2, piece_2)
    dz_1, sums_1, short_grad = stage_back(
        1, sc, side, after(dz_2, piece_2), dz_2_other, keep_2, other_2, zhat_1, stats_1, short_one,
        passed,
    )
    dz_1_other = flip(dz_1, "dp", 1)
    piece_1 = weight_rest(
        1, sc, hidden_one, hidden_one_other, after(dz_1, came_3), sums_1
    )
    came_1 = flip(piece_1, "section", 1, lambda i: i in (0, 2))
    dz_0, sums_0, dz_p = stage_back(
        0, sc, side, after(dz_1, piece_1), dz_1_other, keep_1, other_1, zhat_0, stats_0,
        proj=(short_grad, zhat_p),
    )
    piece_0 = weight_first(sc, fields, dz_0, dz_p, sums_0)
    came_0 = flip(piece_0, "section", 2, lambda i: i in (2, 3))
    keep_late, give_late = add_two(sc, after(piece_3, piece_0), piece_2, came_3, came_2)
    last_late = flip(give_late, "section", 1, lambda i: i in (2, 3))
    sum_1 = add_pieces(1, after(piece_1, give_late), came_1)
    last_1 = flip(sum_1, "section", 2, lambda i: i == 3)
    sum_0 = add_pieces(0, after(piece_0, sum_1), came_0)
    last_0 = flip(sum_0, "section", 1, lambda i: i == 1)
    keep, give = pick_images(sc, *after((dz_0, dz_p, out), sum_0))
    image_raw, block_output = image_back(sc, keep, flip(give, "dp", 1), w_first, w_first_other)
    block_output = block_output[:, 0:81]
    rows = jnp.arange(18, dtype=jnp.int32)
    inner_rows = (rows < 2 * (9 - 2 * (2 - level))[:, None]).astype(bf16)
    mask_in = inner_rows[:, :, None] * inner_rows[:, None, :]
    image_grad = image_raw[:, 0:324].reshape(2, 18, 18, 256) * mask_in[..., None]
    total = own_piece(
        sc,
        [((0,), (sum_0, last_0)), ((1,), (sum_1, last_1)), ((2, 3), (keep_late, last_late))],
        (image_raw,),
    )
    from_far = flip(total, "dp", 4, lambda i: i // 2 in (0, 3))
    from_near = flip(total, "dp", 2)
    from_middle = flip(total, "dp", 6, lambda i: i // 2 in (1, 2))
    from_end = flip(total, "dp", 4, lambda i: i // 2 in (1, 2))
    relayed = flip(from_far, "dp", 2, lambda i: i // 2 in (1, 2))
    from_near, block_output, image_grad = lax.optimization_barrier(
        (from_near, block_output, image_grad)
    )
    gathered = [total, from_near, from_far, from_middle, from_end, relayed]
    weight_grad, vectors = lay_out(sc, gathered, [flip(piece, "dp", 1) for piece in gathered])

    return (
        block_output.reshape(1, 2, 9, 9, 512),
        image_grad[None],
        weight_grad[None],
        vectors[None, 0:2],
        vectors[None, 2:4],
    )


def solution(mesh):
    placed = (
        P("section", "dp", None, None, None),
        P(None, "dp"),
        P("section", None, None),
        P("section", None, None),
        P("section", None, None),
        P("section", "dp", None, None, None),
    )
    on_chip = mesh.shape["section"] == 4 and mesh.shape["dp"] == 8
    return jax.shard_map(
        chip_body if on_chip else pipeline_body,
        mesh=mesh,
        in_specs=placed,
        out_specs=(
            P("section", "dp", None, None, None),
            P("section", "dp", None, None, None),
            P("section", None, None),
            P("section", None, None),
            P("section", None, None),
        ),
        check_vma=False,
    )
```

```python
import jax
import jax.numpy as jnp
from jax import lax
from jax.experimental import pallas as pl
from jax.experimental.pallas import tpu as pltpu
from jax.sharding import PartitionSpec as P

epsilon = 1e-05


def passed_along(value, axis, steps):
    count = lax.axis_size(axis)
    leading, last = (max(0, -steps), min(count, count - steps))
    return lax.ppermute(value, axis, [(source, source + steps) for source in range(leading, last)])


def regions(levels, half_side):
    inner_side = half_side - 2 * (2 - levels)
    small_rows = jnp.arange(half_side, dtype=jnp.int32)
    large_rows = jnp.arange(2 * half_side, dtype=jnp.int32)
    inner_mask = (small_rows < inner_side[..., None]).astype(jnp.float32)
    outer_mask = (large_rows < 2 * inner_side[..., None]).astype(jnp.float32)
    return (
        outer_mask[..., :, None] * outer_mask[..., None, :],
        inner_mask[..., :, None] * inner_mask[..., None, :],
    )


def patches(field_in, stride, half_side):
    padded = jnp.pad(field_in, ((0, 0), (1, 1), (1, 1), (0, 0)))
    pieces = [
        padded[
            :,
            row_at : row_at + stride * half_side : stride,
            col_at : col_at + stride * half_side : stride,
            :,
        ]
        for row_at in range(3)
        for col_at in range(3)
    ]
    joined = jnp.concatenate(pieces, axis=-1)
    return joined.reshape(-1, joined.shape[-1])


def contract_rows(left_side, right_side):
    return lax.dot_general(
        left_side, right_side, (((0,), (0,)), ((), ())), preferred_element_type=jnp.float32
    )


def contract_cols(left_side, right_side):
    return lax.dot_general(
        left_side, right_side, (((1,), (1,)), ((), ())), preferred_element_type=jnp.float32
    )


def silu_slope(values):
    sigmoid = jax.nn.sigmoid(values)
    return sigmoid * (1.0 + values * (1.0 - sigmoid))


def spread_taps(tap_grads, image_count, half_side, channels):
    tap_grid = tap_grads.reshape(image_count, half_side, half_side, 9, channels)
    empty_phase = jnp.zeros((image_count, half_side + 1, half_side + 1, channels), jnp.float32)
    phases = [[empty_phase, empty_phase], [empty_phase, empty_phase]]
    for row_at in range(3):
        for col_at in range(3):
            tap_piece = tap_grid[:, :, :, 3 * row_at + col_at, :]
            top_pad = 1 if row_at == 2 else 0
            left_pad = 1 if col_at == 2 else 0
            placed = jnp.pad(
                tap_piece, ((0, 0), (top_pad, 1 - top_pad), (left_pad, 1 - left_pad), (0, 0))
            )
            phases[row_at % 2][col_at % 2] = phases[row_at % 2][col_at % 2] + placed
    row_phases = [jnp.stack([phases[parity][0], phases[parity][1]], axis=3) for parity in range(2)]
    alternated = jnp.stack(row_phases, axis=2).reshape(
        image_count, 2 * half_side + 2, 2 * half_side + 2, channels
    )
    return alternated[:, 1 : 2 * half_side + 1, 1 : 2 * half_side + 1, :]


def keep_slot(buffer_all, new_value, slot_at, keep_flag):
    current = lax.dynamic_index_in_dim(buffer_all, slot_at, 0, keepdims=False)
    return lax.dynamic_update_index_in_dim(
        buffer_all, jnp.where(keep_flag, new_value, current), slot_at, 0
    )


def pipeline_body(images, res_ids, weights, bn_gain, bn_bias, cotangent):
    sections = lax.axis_size("section")
    last_section = sections - 1
    position = lax.axis_index("section")
    micro_count = res_ids.shape[0]
    image_count = images.shape[1]
    half_side = cotangent.shape[2]
    channels = weights.shape[2]
    in_channels = images.shape[4]
    pixel_rows = image_count * half_side * half_side
    taps_in = 9 * in_channels
    matrix = weights[0]
    gain_rows = bn_gain[0]
    bias_rows = bn_bias[0]
    is_first = position == 0
    adds_short = (position == 1) | (position == 3)
    passes_short = position == 2
    makes_short = position == 1
    back_matrix = jnp.transpose(matrix.reshape(9, channels, channels)[::-1], (0, 2, 1)).reshape(
        9 * channels, channels
    )
    mask_in_all, mask_out_all = regions(res_ids, half_side)
    act_shape = (image_count, half_side, half_side, channels)
    zero_pixels = jnp.zeros((pixel_rows, channels), jnp.float32)
    zero_input = jnp.zeros((image_count, 2 * half_side, 2 * half_side, in_channels), jnp.float32)
    zero_weight = jnp.zeros((9 * channels, channels), jnp.float32)
    own_images = images[0]
    gathered = [own_images]
    for source in range(1, micro_count):
        gathered.append(passed_along(own_images, "section", -source))
    section_inputs = jnp.stack(gathered)
    own_cot = cotangent[0]
    arrived = []
    for source in range(micro_count):
        if source == last_section:
            arrived.append(own_cot)
        else:
            arrived.append(passed_along(own_cot, "section", last_section - source))
    cot_all = jnp.stack(arrived)

    def conv_first(prev_act, first_in):
        columns = patches(first_in, 2, half_side)
        main_out = jnp.dot(columns, matrix[:taps_in], preferred_element_type=jnp.float32)
        proj_out = jnp.dot(
            columns[:, 4 * in_channels : 5 * in_channels],
            matrix[taps_in : taps_in + in_channels],
            preferred_element_type=jnp.float32,
        )
        return jnp.stack([main_out, proj_out])

    def conv_rest(prev_act, first_in):
        columns = patches(prev_act, 1, half_side)
        return jnp.stack(
            [jnp.dot(columns, matrix, preferred_element_type=jnp.float32), zero_pixels]
        )

    def conv_spare(prev_act, first_in):
        return jnp.stack([zero_pixels, zero_pixels])

    def back_first(grad_conv, prev_act, first_in):
        columns = patches(first_in, 2, half_side)
        centre = columns[:, 4 * in_channels : 5 * in_channels]
        main_grad = contract_rows(columns, grad_conv[0])
        proj_grad = contract_rows(centre, grad_conv[1])
        filler = jnp.zeros((9 * channels - taps_in - in_channels, channels), jnp.float32)
        weight_now = jnp.concatenate([main_grad, proj_grad, filler], axis=0)
        tap_grads = contract_cols(grad_conv[0], matrix[:taps_in])
        centre_grad = contract_cols(grad_conv[1], matrix[taps_in : taps_in + in_channels])
        tap_grads = tap_grads + jnp.pad(centre_grad, ((0, 0), (4 * in_channels, 4 * in_channels)))
        return (
            weight_now,
            zero_pixels,
            spread_taps(tap_grads, image_count, half_side, in_channels),
        )

    def back_rest(grad_conv, prev_act, first_in):
        columns = patches(prev_act, 1, half_side)
        weight_now = contract_rows(columns, grad_conv[0])
        grad_image = grad_conv[0].reshape(act_shape)
        prev_grad = jnp.dot(
            patches(grad_image, 1, half_side), back_matrix, preferred_element_type=jnp.float32
        )
        return (weight_now, prev_grad, zero_input)

    def back_spare(grad_conv, prev_act, first_in):
        return (zero_weight, zero_pixels, zero_input)

    def finish(conv_out, mean_rows, scale_rows, flat_mask, short_in):
        normed = (conv_out - mean_rows[:, None, :]) * scale_rows[:, None, :] * gain_rows[
            :, None, :
        ] + bias_rows[:, None, :]
        pre_act = normed[0] + jnp.where(adds_short, short_in, 0.0)
        activated = jax.nn.silu(pre_act) * flat_mask[:, None]
        proj_short = normed[1] * flat_mask[:, None]
        short_out = jnp.where(is_first, proj_short, jnp.where(makes_short, activated, short_in))
        return (pre_act, activated, short_out)

    empty_act = jnp.zeros(act_shape, jnp.bfloat16)
    recv_act = empty_act
    recv_short = empty_act
    saved_act = jnp.zeros((micro_count,) + act_shape, jnp.bfloat16)
    saved_short = saved_act
    saved_final = saved_act
    saved_mean = jnp.zeros((micro_count, 2, channels), jnp.float32)
    saved_scale = saved_mean
    saved_total = jnp.zeros((micro_count,), jnp.float32)
    sweep_len = micro_count + last_section
    for tick_at in range(sweep_len):
        slot_raw = tick_at - position
        is_valid = (slot_raw >= 0) & (slot_raw < micro_count)
        slot_at = jnp.clip(slot_raw, 0, micro_count - 1)
        flat_mask = mask_out_all[slot_at].reshape(-1) * is_valid.astype(jnp.float32)
        first_in = section_inputs[slot_at] * mask_in_all[slot_at][..., None].astype(jnp.bfloat16)
        branch = jnp.where(is_valid, jnp.where(is_first, 0, 1), 2).astype(jnp.int32)
        conv_out = lax.switch(branch, [conv_first, conv_rest, conv_spare], recv_act, first_in)
        local_total = jnp.sum(flat_mask)
        weighted = conv_out * flat_mask[None, :, None]
        grand_total, sum_rows = lax.psum((local_total, jnp.sum(weighted, axis=1)), "dp")
        grand_total = jnp.maximum(grand_total, 1.0)
        statistics_mean_rows = sum_rows / grand_total
        centred = conv_out - statistics_mean_rows[:, None, :]
        variance = (
            lax.psum(jnp.sum(centred * centred * flat_mask[None, :, None], axis=1), "dp")
            / grand_total
        )
        grand_total, mean_rows, scale_rows = (
            grand_total,
            statistics_mean_rows,
            lax.rsqrt(variance + epsilon),
        )
        short_in = recv_short.reshape(pixel_rows, channels).astype(jnp.float32)
        pre_act, activated, short_out = finish(conv_out, mean_rows, scale_rows, flat_mask, short_in)
        act_low = activated.astype(jnp.bfloat16).reshape(act_shape)
        short_low = short_out.astype(jnp.bfloat16).reshape(act_shape)
        saved_act = keep_slot(saved_act, recv_act, slot_at, is_valid)
        saved_short = keep_slot(saved_short, recv_short, slot_at, is_valid)
        saved_mean = keep_slot(saved_mean, mean_rows, slot_at, is_valid)
        saved_scale = keep_slot(saved_scale, scale_rows, slot_at, is_valid)
        saved_total = keep_slot(saved_total, grand_total, slot_at, is_valid)
        saved_final = keep_slot(
            saved_final, act_low, slot_at, is_valid & (position == last_section)
        )
        if tick_at + 1 < sweep_len:
            recv_act, recv_short = passed_along((act_low, short_low), "section", 1)
    grad_act = empty_act
    grad_short = empty_act
    weight_acc = zero_weight
    gain_acc = jnp.zeros((2, channels), jnp.float32)
    bias_acc = gain_acc
    saved_dx = jnp.zeros(
        (micro_count, image_count, 2 * half_side, 2 * half_side, in_channels), jnp.bfloat16
    )
    for tick_at in range(sweep_len):
        slot_raw = tick_at - (last_section - position)
        is_valid = (slot_raw >= 0) & (slot_raw < micro_count)
        slot_at = jnp.clip(slot_raw, 0, micro_count - 1)
        flat_mask = mask_out_all[slot_at].reshape(-1) * is_valid.astype(jnp.float32)
        first_in = section_inputs[slot_at] * mask_in_all[slot_at][..., None].astype(jnp.bfloat16)
        branch = jnp.where(is_valid, jnp.where(is_first, 0, 1), 2).astype(jnp.int32)
        prev_act = saved_act[slot_at]
        conv_out = lax.switch(branch, [conv_first, conv_rest, conv_spare], prev_act, first_in)
        mean_rows = saved_mean[slot_at]
        scale_rows = saved_scale[slot_at]
        valid_total = saved_total[slot_at]
        short_in = saved_short[slot_at].reshape(pixel_rows, channels).astype(jnp.float32)
        pre_act, activated, short_out = finish(conv_out, mean_rows, scale_rows, flat_mask, short_in)
        from_act = (
            jnp.where(position == last_section, cot_all[slot_at], grad_act)
            .reshape(pixel_rows, channels)
            .astype(jnp.float32)
        )
        from_short = grad_short.reshape(pixel_rows, channels).astype(jnp.float32)
        slope = silu_slope(pre_act) * flat_mask[:, None]
        grad_pre = (from_act + jnp.where(adds_short, from_short, 0.0)) * slope
        grad_proj = jnp.where(is_first, from_short * flat_mask[:, None], 0.0)
        grad_normed = jnp.stack([grad_pre, grad_proj])
        normalized = (conv_out - mean_rows[:, None, :]) * scale_rows[:, None, :]
        bias_now, gain_now = lax.psum(
            (jnp.sum(grad_normed, axis=1), jnp.sum(grad_normed * normalized, axis=1)), "dp"
        )
        bias_acc = bias_acc + bias_now
        gain_acc = gain_acc + gain_now
        grad_conv = (
            flat_mask[None, :, None]
            * gain_rows[:, None, :]
            * scale_rows[:, None, :]
            * (
                grad_normed
                - (bias_now[:, None, :] + normalized * gain_now[:, None, :]) / valid_total
            )
        )
        grad_conv = grad_conv.astype(jnp.bfloat16)
        weight_now, prev_grad, input_grad = lax.switch(
            branch, [back_first, back_rest, back_spare], grad_conv, prev_act, first_in
        )
        weight_acc = weight_acc + weight_now
        masked_input = (input_grad * mask_in_all[slot_at][..., None]).astype(jnp.bfloat16)
        saved_dx = keep_slot(saved_dx, masked_input, slot_at, is_valid & is_first)
        send_act = (
            (prev_grad + jnp.where(passes_short, from_short, 0.0))
            .astype(jnp.bfloat16)
            .reshape(act_shape)
        )
        send_short = jnp.where(adds_short, grad_pre, 0.0).astype(jnp.bfloat16).reshape(act_shape)
        if tick_at + 1 < sweep_len:
            grad_act, grad_short = passed_along((send_act, send_short), "section", -1)
    weight_total = lax.psum(weight_acc, "dp")
    result = saved_final[last_section]
    for source in range(last_section):
        arrived_piece = passed_along(saved_final[source], "section", source - last_section)
        result = jnp.where(position == source, arrived_piece, result)
    grad_result = saved_dx[0]
    for source in range(1, micro_count):
        arrived_piece = passed_along(saved_dx[source], "section", source)
        grad_result = jnp.where(position == source, arrived_piece, grad_result)
    return (result[None], grad_result[None], weight_total[None], gain_acc[None], bias_acc[None])


f32, bf16 = jnp.float32, jnp.bfloat16
LANES = 256
GRID = (9, 9, 16, LANES)


def flip(value, axis, mask, senders=None):
    count = lax.axis_size(axis)
    pairs = [(i, i ^ mask) for i in range(count) if senders is None or senders(i)]
    return lax.ppermute(value, axis, pairs)


def struct(shape, kind=bf16):
    return jax.ShapeDtypeStruct(shape, kind)


def call(kernel, name, operands, places, outs, out_places, scratch, flops, moved, limit):
    spaces = {"s": pltpu.SMEM, "v": pltpu.VMEM, "a": pl.ANY, "h": pltpu.HBM}
    operands = [
        pltpu.with_memory_space_constraint(one, pltpu.HBM) if place == "h" else one
        for one, place in zip(operands, places)
    ]
    outs = [
        spaces[place](one.shape, one.dtype) if place in "hv" else one
        for one, place in zip(outs, out_places)
    ]
    return pl.pallas_call(
        kernel,
        out_shape=outs,
        in_specs=[pl.BlockSpec(memory_space=spaces[place]) for place in places],
        out_specs=[pl.BlockSpec(memory_space=spaces[place]) for place in out_places],
        scratch_shapes=scratch,
        name=name,
        compiler_params=pltpu.CompilerParams(vmem_limit_bytes=limit * 2**20),
        cost_estimate=pl.CostEstimate(flops=1, bytes_accessed=1, transcendentals=0),
    )(*operands)


def dot(left, right):
    return jnp.dot(left, right, preferred_element_type=f32)


def dot_t(left, right):
    return lax.dot_general(left, right, (((1,), (1,)), ((), ())), preferred_element_type=f32)


def col_sum(values):
    return jnp.sum(values, axis=0, keepdims=True)


def blank_edges(dst):
    blank = jnp.zeros((11, 16, LANES), bf16)
    dst[0] = blank
    dst[10] = blank
    dst[:, 0] = blank
    dst[:, 10] = blank


class Inside:
    def __init__(self, side):
        self.count = col_sum(side * side)
        self.masks = (None, side > 6.0, side > 8.0)

    def keep(self, ring, values):
        mask = self.masks[self.level(ring)]
        return values if mask is None else jnp.where(mask, values, 0.0)

    @staticmethod
    def level(ring):
        return 0 if ring < 5 else 1 if ring < 7 else 2

    def total(self, values_at):
        sums = [None, None, None]
        for row in range(9):
            for col in range(9):
                at = self.level(max(row, col))
                value = values_at(row, col)
                sums[at] = value if sums[at] is None else sums[at] + value
        return col_sum(sums[0] + self.keep(5, sums[1]) + self.keep(7, sums[2]))


def norm_stats(acc, inside):
    mean = inside.total(lambda row, col: acc[row, col]) / inside.count

    def squared(row, col):
        centred = acc[row, col] - mean
        return centred * centred

    return mean, lax.rsqrt(inside.total(squared) / inside.count + epsilon)


def sigmoid_of(values):
    return 0.5 * jnp.tanh(0.5 * values) + 0.5


def split_three(row):
    high = row.astype(bf16)
    rest = row - high.astype(f32)
    middle = rest.astype(bf16)
    low = (rest - middle.astype(f32)).astype(bf16)
    return [high, middle, low]


def pack_vectors(rows):
    pieces = [one.astype(f32) for row in rows for one in split_three(row)]
    pieces.append(jnp.zeros((16 - len(pieces), LANES), f32))
    return jnp.concatenate(pieces, axis=0).astype(bf16)


def unpack_vectors(block):
    wide = block.astype(f32)
    return [wide[3 * at : 3 * at + 1] + wide[3 * at + 1 : 3 * at + 2] + wide[3 * at + 2 : 3 * at + 3] for at in range(4)]


def pack_rows(ref, rows):
    ref[...] = jnp.concatenate(rows + [jnp.zeros((8 - len(rows), LANES), f32)], axis=0)


def turn_matrix(image_of_row):
    out_row = lax.broadcasted_iota(jnp.int32, (256, 256), 0)
    in_row = lax.broadcasted_iota(jnp.int32, (256, 256), 1)
    pixel_same = (out_row >> 4) == (in_row & 15)
    return jnp.where(pixel_same & ((out_row & 15) == image_of_row(in_row)), 1.0, 0.0).astype(bf16)


def split_weights(sc, matrix, vectors):
    def kernel(sc_ref, matrix_ref, vec_ref, for_x, for_y, sems):
        lane = pl.multiple_of(LANES * sc_ref[2], LANES)
        chosen = matrix_ref.at[:, pl.ds(lane, LANES)]

        def copies(target, first, at):
            return [
                pltpu.make_async_copy(
                    chosen.at[first + 640 * cut : first + 640 * cut + 640],
                    target.at[16 + 640 * cut : 656 + 640 * cut],
                    sems.at[at + cut],
                )
                for cut in range(4)
            ]

        along_x = copies(for_x, 0, 0)
        for copy in along_x:
            copy.start()
        small = pack_vectors([vec_ref[at : at + 1, pl.ds(lane, LANES)] for at in range(4)])
        for_x[0:16] = small
        for_y[0:16] = small
        for first, here in ((0, sc_ref[0] == 0), (2048, sc_ref[0] != 0)):

            @pl.when(here)
            def _():
                along_y = copies(for_y, first, 4)
                for copy in along_y:
                    copy.start()
                for copy in along_y:
                    copy.wait()

        for copy in along_x:
            copy.wait()

    return call(
        kernel, "split_weights", (sc, matrix, vectors), "shv", [struct((2576, LANES))] * 2, "vv",
        [pltpu.SemaphoreType.DMA((8,))], 0, 14_000_000, 20,
    )


def relay_weights(name, is_own, operands, first=None):
    def kernel(sc_ref, own_x, own_y, x_1, y_1, for_x, for_y, *more):
        chosen = is_own(sc_ref[0])
        for x_from, y_from, here in ((own_x, own_y, chosen), (x_1, y_1, jnp.logical_not(chosen))):

            @pl.when(here)
            def _():
                for_x[...] = y_from[272:2576]
                for_y[...] = x_from[0:2320]

        if more:
            more[0][...] = y_1[0:1296]
            more[1][...] = x_1[1296:2576]

    outs = [struct((2304, LANES)), struct((2320, LANES))]
    if first:
        outs += [struct((1296, LANES)), struct((1280, LANES))]
    return call(kernel, name, operands, "svvvv", outs, len(outs) * "v", [], 0, 14_000_000, 20)


def prepare_images(sc, pieces):
    def kernel(sc_ref, *refs):
        piece_refs, (out, side_out, held, sems) = refs[:8], refs[8:]
        core = sc_ref[2]
        copies = [
            pltpu.make_async_copy(ref, held.at[2 * at : 2 * at + 2], sems.at[at])
            for at, ref in enumerate(piece_refs)
        ]
        for copy in copies:
            copy.start()
        turn = turn_matrix(lambda r: ((r >> 4) + 8 * core) & 15)
        out[:, :, 0] = jnp.zeros((2, 2, 10, 16, LANES), bf16)
        out[:, :, :, 0] = jnp.zeros((2, 2, 10, 16, LANES), bf16)
        for copy in copies:
            copy.wait()

        def block(at):
            source = held[:, 16 * at : 16 * at + 16].reshape(256, LANES)
            return dot(turn, source).reshape(16, 16, LANES)

        last = block(20)
        side = last[4]
        side_out[...] = side
        masks = (None, 2.0 * side > 13.0, 2.0 * side > 17.0)
        for at in range(21):
            turned = last if at == 20 else block(at)
            for step in range(16 if at < 20 else 4):
                row, col = divmod(16 * at + step, 18)
                mask = masks[Inside.level(max(row, col) // 2)]
                kept = turned[step] if mask is None else jnp.where(mask, turned[step], 0.0)
                out[row % 2, col % 2, 1 + row // 2, 1 + col // 2] = kept.astype(bf16)

    outs = [struct((2, 2, 10, 10, 16, LANES)), struct((16, LANES), f32)]
    scratch = [pltpu.VMEM((16, 336, LANES), bf16), pltpu.SemaphoreType.DMA((8,))]
    return call(
        kernel, "prepare_images", (sc, *pieces), "s" + 8 * "h", outs, "vv", scratch,
        21 * 2 * 256**3, 8_000_000, 20,
    )


def prepare_cotangent(sc, pieces):
    def kernel(sc_ref, *refs):
        piece_refs, (out, held, sems) = refs[:2], refs[2:]
        core = sc_ref[2]
        copies = [
            pltpu.make_async_copy(ref, held.at[2 * at : 2 * at + 2], sems.at[at])
            for at, ref in enumerate(piece_refs)
        ]
        for copy in copies:
            copy.start()
        turn = turn_matrix(
            lambda r: (((r >> 5) & 1) ^ core) * 8 + 2 * (r >> 6) + ((r >> 4) & 1)
        )
        for copy in copies:
            copy.wait()
        for at in range(6):
            source = held[:, :, :, 16 * at : 16 * at + 16].reshape(256, LANES)
            turned = dot(turn, source).astype(bf16).reshape(16, 16, LANES)
            for step in range(16 if at < 5 else 1):
                row, col = divmod(16 * at + step, 9)
                out[row, col] = turned[step]

    scratch = [pltpu.VMEM((4, 2, 2, 96, LANES), bf16), pltpu.SemaphoreType.DMA((4,))]
    return call(
        kernel, "prepare_cotangent", (sc, *pieces), "saa", [struct(GRID)], "v", scratch,
        6 * 2 * 256**3, 2_000_000, 20,
    )[0]


def any_of(section, sections):
    chosen = section == sections[0]
    for other in sections[1:]:
        chosen = chosen | (section == other)
    return chosen


def stage_first(sc, side, fields, messages):
    def kernel(sc_ref, side_ref, field, own_x, x_1, y_1, top, bottom, hidden, short, zhat, zhat_p, stats, w, vec, acc, acc_p, short_now, out_sems):
        section = sc_ref[0]
        for at, whole in enumerate((own_x, x_1, y_1)):

            @pl.when(section == at)
            def _():
                w[...] = whole[16:2576]
                vec[...] = whole[0:16]

        @pl.when(section == 3)
        def _():
            w[0:1280] = top[16:1296]
            w[1280:2560] = bottom[...]
            vec[...] = top[0:16]

        outs = []
        for chunk in range(3):
            total = jnp.zeros((432, LANES), f32)
            for a in range(3):
                for b in range(3):
                    row_at, col_at = 3 * chunk + (0 if a == 0 else 1), 0 if b == 0 else 1
                    left = field[(a + 1) % 2, (b + 1) % 2, row_at : row_at + 3, col_at : col_at + 9]
                    at = LANES * (3 * a + b)
                    total = total + dot(left.reshape(432, LANES), w[at : at + LANES])
            span = slice(3 * chunk, 3 * chunk + 3)
            acc[span] = total.reshape(3, 9, 16, LANES)
            centre = field[0, 0, 3 * chunk + 1 : 3 * chunk + 4, 1:10].reshape(432, LANES)
            acc_p[span] = dot(centre, w[2304:2560]).reshape(3, 9, 16, LANES)
            for at, (source, target) in enumerate(((acc, zhat), (acc_p, zhat_p))):
                outs.append(
                    pltpu.make_async_copy(
                        source.at[span], target.at[span], out_sems.at[1 + 3 * at + chunk]
                    )
                )
                outs[-1].start()
        inside = Inside(side_ref[...])
        mean, scale = norm_stats(acc, inside)
        mean_p, scale_p = norm_stats(acc_p, inside)
        gain, gain_p, bias, bias_p = unpack_vectors(vec[...])
        for row in range(9):
            for col in range(9):
                ring = max(row, col)
                pre = (acc[row, col] - mean) * scale * gain + bias
                hidden[row, col] = inside.keep(ring, pre * sigmoid_of(pre)).astype(bf16)
                normed = (acc_p[row, col] - mean_p) * scale_p
                short_now[row, col] = inside.keep(ring, normed * gain_p + bias_p).astype(bf16)
            outs.append(pltpu.make_async_copy(short_now.at[row], short.at[row], out_sems.at[7 + row]))
            outs[-1].start()
        pack_rows(stats, [scale, gain, bias, mean, scale_p, gain_p, mean_p])
        for copy in outs:
            copy.wait()

    outs = [
        struct(GRID), struct(GRID), struct(GRID, f32), struct(GRID, f32), struct((8, LANES), f32),
        struct((2560, LANES)),
    ]
    scratch = [
        pltpu.VMEM((16, LANES), bf16), pltpu.VMEM(GRID, f32), pltpu.VMEM(GRID, f32),
        pltpu.VMEM(GRID, bf16), pltpu.SemaphoreType.DMA((16,)),
    ]
    return call(
        kernel, "stage_first", (sc, side, fields, *messages), "svv" + 5 * "v", outs, "vhhhvv",
        scratch, 2 * 1296 * 2560 * LANES, 8_000_000, 20,
    )


def fill_field(padded, source):
    blank_edges(padded)
    padded[1:10, 1:10] = source[...]


def fill_weights(part, section, core, messages, keep, send, vec):
    own_x, own_y, x_1, y_1, x_2, y_2 = messages
    upper = {1: {0: x_1, 1: own_x}, 2: {2: own_x, 3: x_1}, 3: {2: x_1, 3: own_x}}[part]
    lower = {1: {1: own_y, 3: y_1}, 2: {0: y_1, 2: own_y}, 3: {1: y_1, 3: own_y}}[part]
    far_upper = [section for section in range(4) if section not in upper]
    far_lower = [section for section in range(4) if section not in lower]
    entries = [((at,), ref, 16, 0) for at, ref in upper.items()] + [(far_upper, y_2, 16, 0)]
    entries += [((at,), ref, 272, 9) for at, ref in lower.items()] + [(far_lower, x_2, 0, 9)]
    for half in range(2):
        for sections, ref, first, block in entries:

            @pl.when((core == half) & any_of(section, sections))
            def _():
                for at in range(9):
                    tap, which = divmod(block + at, 2)
                    target = keep if which == half else send
                    start = first + LANES * at
                    target[LANES * tap : LANES * tap + LANES] = ref[start : start + LANES]
                if block == 0:
                    vec[...] = ref[0:16]


def stage_rest(part, sc, side, own, other, messages, short, cot=None, after=()):
    last = cot is not None
    extra = [one for one in (short, cot) if one is not None]

    def kernel(sc_ref, side_ref, own_ref, oth_ref, *refs):
        refs = list(refs)
        late_refs = [refs.pop(0) for _ in extra]
        weights = refs[0:6]
        refs = refs[6 + len(after) :]
        if last:
            dz, passed, out, sums = refs[:4]
            refs = refs[4:]
        else:
            hidden, zhat, stats = refs[:3]
            refs = refs[3:]
        w_keep, w_send, vec, padded, acc = refs[:5]
        grads, passed_now = refs[5:7] if last else (None, None)
        late, sems, out_sems = refs[-3:]
        short_ref = late.at[0] if short is not None else None
        cot_ref = late.at[1] if last else None
        section, core = sc_ref[0], sc_ref[2]
        late_loads = [
            pltpu.make_async_copy(ref, late.at[at], sems.at[at]) for at, ref in enumerate(late_refs)
        ]
        for copy in late_loads:
            copy.start()
        fill_weights(part, section, core, weights, w_keep, w_send, vec)
        fill_field(padded.at[0], own_ref)
        fill_field(padded.at[1], oth_ref)
        outs = []
        for chunk in range(3):
            total = jnp.zeros((432, LANES), f32)
            for a in range(3):
                for b in range(3):
                    for at in range(2):
                        left = padded[at, 3 * chunk + a : 3 * chunk + a + 3, b : b + 9]
                        from_row = LANES * (3 * a + b)
                        right = (w_keep, w_send)[at][from_row : from_row + LANES]
                        total = total + dot(left.reshape(432, LANES), right)
            acc[3 * chunk : 3 * chunk + 3] = total.reshape(3, 9, 16, LANES)
            if not last:
                outs.append(
                    pltpu.make_async_copy(
                        acc.at[3 * chunk : 3 * chunk + 3],
                        zhat.at[3 * chunk : 3 * chunk + 3],
                        out_sems.at[18 + chunk],
                    )
                )
                outs[-1].start()
        inside = Inside(side_ref[...])
        mean, scale = norm_stats(acc, inside)
        for copy in late_loads:
            copy.wait()
        gain, _, bias, _ = unpack_vectors(vec[...])
        if last:
            sums_now = [None, None]
        for row in range(9):
            for col in range(9):
                ring = max(row, col)
                normed = (acc[row, col] - mean) * scale
                if last:
                    acc[row, col] = normed
                pre = normed * gain + bias
                if short is not None:
                    pre = pre + short_ref[row, col].astype(f32)
                sigmoid = sigmoid_of(pre)
                target = out if last else hidden
                target[row, col] = inside.keep(ring, pre * sigmoid).astype(bf16)
                if last:
                    slope = sigmoid * (1.0 + pre * (1.0 - sigmoid))
                    grad = inside.keep(ring, cot_ref[row, col].astype(f32) * slope)
                    grads[row, col] = grad
                    passed_now[row, col] = grad.astype(bf16)
                    for at, value in enumerate((grad, grad * normed)):
                        sums_now[at] = value if sums_now[at] is None else sums_now[at] + value
            if last:
                outs.append(
                    pltpu.make_async_copy(passed_now.at[row], passed.at[row], out_sems.at[18 + row])
                )
                outs[-1].start()
        if last:
            bias_now, gain_now = col_sum(sums_now[0]), col_sum(sums_now[1])
            norm_back(dz, grads, acc, inside, gain * scale, bias_now, gain_now)
            pack_rows(sums, [gain_now, bias_now])
        else:
            pack_rows(stats, [scale, gain, bias, mean])
        for copy in outs:
            copy.wait()

    half = struct((2304, LANES))
    if last:
        outs, places = [struct(GRID), struct(GRID), struct(GRID), struct((8, LANES), f32)], "vhvv"
    else:
        outs, places = [struct(GRID), struct(GRID, f32), struct((8, LANES), f32)], "vhv"
    scratch = [
        pltpu.VMEM((16, LANES), bf16), pltpu.VMEM((2, 11, 11, 16, LANES), bf16), pltpu.VMEM(GRID, f32)
    ] + ([pltpu.VMEM(GRID, f32), pltpu.VMEM(GRID, bf16)] if last else [])
    scratch += [
        pltpu.VMEM((2, *GRID), bf16), pltpu.SemaphoreType.DMA((2,)), pltpu.SemaphoreType.DMA((27,)),
    ]
    return call(
        kernel, f"stage_{part}", (sc, side, own, other, *extra, *messages, *after),
        "svvv" + len(extra) * "a" + 6 * "v" + len(after) * "a", outs + [half, half], places + "vv", scratch,
        2 * 1296 * 4608 * LANES, 8_000_000, 20,
    )


def norm_back(dz, grads, zhat, inside, weight, bias_now, gain_now):
    constant, slope = weight * bias_now / inside.count, weight * gain_now / inside.count
    for row in range(9):
        for col in range(9):
            value = weight * grads[row, col] - (constant + slope * zhat[row, col])
            dz[row, col] = inside.keep(max(row, col), value).astype(bf16)


def stage_back(part, sc, side, dz_own, dz_other, w_own, w_other, zhat, stats, short=None, extra=None, proj=None):
    first = proj is not None
    optional = [one for one in (short, extra) if one is not None] + (list(proj) if first else [])

    def kernel(sc_ref, side_ref, stats_ref, dz_own_ref, dz_oth_ref, w_own_ref, w_oth_ref, zhat_ref, *refs):
        refs = list(refs)
        late_refs = [refs.pop(0) for one in (short, extra) if one is not None]
        if first:
            dyp_ref, zhat_p_ref = refs.pop(0), refs.pop(0)
        dz, sums = refs.pop(0), refs.pop(0)
        passed = refs.pop(0) if short is not None else None
        dz_p = refs.pop(0) if first else None
        padded, acc, held = refs[:3]
        held_p = refs[3] if first else None
        late = None if first else refs[3]
        sems = refs[-1]
        short_ref = late.at[0] if short is not None else None
        extra_ref = late.at[1] if extra is not None else None
        later = [pltpu.make_async_copy(zhat_ref, held, sems.at[4])]
        if first:
            later.append(pltpu.make_async_copy(zhat_p_ref, held_p, sems.at[5]))
        for at, ref in enumerate(late_refs):
            later.append(pltpu.make_async_copy(ref, late.at[at], sems.at[6 + at]))
        for copy in later:
            copy.start()
        fill_field(padded.at[0], dz_own_ref)
        fill_field(padded.at[1], dz_oth_ref)
        for chunk in range(3):
            total = jnp.zeros((432, LANES), f32)
            for a in range(3):
                for b in range(3):
                    for at in range(2):
                        row_at = 3 * chunk + 2 - a
                        left = padded[at, row_at : row_at + 3, 2 - b : 11 - b]
                        from_row = LANES * (3 * a + b)
                        right = (w_own_ref, w_oth_ref)[at][from_row : from_row + LANES]
                        total = total + dot_t(left.reshape(432, LANES), right)
            acc[3 * chunk : 3 * chunk + 3] = total.reshape(3, 9, 16, LANES)
        for copy in later:
            copy.wait()
        inside = Inside(side_ref[...])
        scale, gain, bias, mean, scale_p, gain_p, mean_p = [stats_ref[at : at + 1] for at in range(7)]
        sums_now = [None] * 4
        for row in range(9):
            for col in range(9):
                ring = max(row, col)
                normed = (held[row, col] - mean) * scale
                held[row, col] = normed
                pre = normed * gain + bias
                grad = acc[row, col]
                if extra is not None:
                    grad = grad + extra_ref[row, col].astype(f32)
                if short is not None:
                    pre = pre + short_ref[row, col].astype(f32)
                sigmoid = sigmoid_of(pre)
                slope = sigmoid * (1.0 + pre * (1.0 - sigmoid))
                grad = inside.keep(ring, grad.astype(bf16).astype(f32) * slope)
                acc[row, col] = grad
                if short is not None:
                    passed[row, col] = grad.astype(bf16)
                terms = [grad, grad * normed]
                if first:
                    grad_p = dyp_ref[row, col].astype(f32)
                    normed_p = (held_p[row, col] - mean_p) * scale_p
                    held_p[row, col] = normed_p
                    terms += [grad_p, grad_p * normed_p]
                for at, value in enumerate(terms):
                    sums_now[at] = value if sums_now[at] is None else sums_now[at] + value
        totals = [col_sum(value) for value in sums_now if value is not None]
        norm_back(dz, acc, held, inside, gain * scale, totals[0], totals[1])
        rows = [totals[1], totals[0]]
        if first:
            for row in range(9):
                for col in range(9):
                    acc[row, col] = dyp_ref[row, col].astype(f32)
            norm_back(dz_p, acc, held_p, inside, gain_p * scale_p, totals[2], totals[3])
            rows += [totals[3], totals[2]]
        pack_rows(sums, rows)

    outs, places = [struct(GRID), struct((8, LANES), f32)], "vv"
    if short is not None:
        outs, places = outs + [struct(GRID)], places + "v"
    if first:
        outs, places = outs + [struct(GRID)], places + "v"
    scratch = [
        pltpu.VMEM((2, 11, 11, 16, LANES), bf16), pltpu.VMEM(GRID, f32), pltpu.VMEM(GRID, f32)
    ] + [pltpu.VMEM(GRID, f32) if first else pltpu.VMEM((2, *GRID), bf16)]
    scratch += [pltpu.SemaphoreType.DMA((8,))]
    kinds = "h" * ((short is not None) + (extra is not None)) + ("vh" if first else "")
    return call(
        kernel, f"back_{part}",
        (sc, side, stats, dz_own, dz_other, w_own, w_other, zhat, *optional),
        "svvvvvvh" + kinds, outs, places, scratch, 2 * 1296 * 4608 * LANES, 10_000_000, 20,
    )


def pick_images(sc, *fields):
    def kernel(sc_ref, *refs):
        core = sc_ref[2]
        keep, give = refs[-2:]
        out_row = lax.broadcasted_iota(jnp.int32, (4, 96, 1296), 1)
        slot = lax.broadcasted_iota(jnp.int32, (4, 96, 1296), 0)
        in_row = lax.broadcasted_iota(jnp.int32, (4, 96, 1296), 2)
        image = 8 * ((slot >> 1) ^ core) + (slot & 1)
        pick = jnp.where(in_row == 16 * out_row + image, 1.0, 0.0).astype(bf16).reshape(384, 1296)
        for at, source in enumerate(refs[:-2]):
            chosen = dot(pick, source[...].reshape(1296, LANES)).astype(bf16).reshape(4, 96, LANES)
            keep[at] = chosen[0:2]
            give[at] = chosen[2:4]

    count = len(fields)
    return call(
        kernel, "pick_images", (sc, *fields), "s" + count * "v", 2 * [struct((count, 2, 96, LANES))],
        "vv", [], count * 2 * 384 * 1296 * LANES, 3_000_000, 20,
    )


def weight_rest(part, sc, own, other, dz, sums, tail=None):
    def kernel(sc_ref, own_ref, oth_ref, dz_ref, sums_ref, *refs):
        out, turned, padded = refs[-3:]
        if tail is not None:
            out[1168:1568] = refs[0][768:1168]
        zone, core = sc_ref[1], sc_ref[2]
        fill_field(padded, dz_ref)
        lane = pl.multiple_of(128 * (zone & 1), 128)
        is_own = (zone >> 1) == core

        @pl.when(is_own)
        def _():
            turned[...] = own_ref[:, :, :, pl.ds(lane, 128)].reshape(1296, 128).T

        @pl.when(jnp.logical_not(is_own))
        def _():
            turned[...] = oth_ref[:, :, :, pl.ds(lane, 128)].reshape(1296, 128).T

        left = turned[...]
        for a in range(3):
            for b in range(3):
                right = padded[2 - a : 11 - a, 2 - b : 11 - b].reshape(1296, LANES)
                at = 128 * (3 * a + b)
                out[at : at + 128] = dot(left, right).astype(bf16)
        blank = jnp.zeros((1, LANES), f32)
        out[1152:1168] = pack_vectors([sums_ref[0:1], blank, sums_ref[1:2], blank])

    scratch = [
        pltpu.VMEM((128, 1296), bf16), pltpu.VMEM((11, 11, 16, LANES), bf16)
    ]
    return call(
        kernel, f"weight_{part}", (sc, own, other, dz, sums) + (() if tail is None else (tail,)),
        "svvvv" + ("" if tail is None else "v"), [struct((1168 if tail is None else 1568, LANES))], "v",
        scratch, 2 * 1296 * 1152 * LANES, 3_000_000, 20,
    )[0]


def weight_first(sc, fields, dz, dz_p, sums):
    def kernel(sc_ref, field, dz_ref, dz_p_ref, sums_ref, out, turned, padded):
        zone = sc_ref[1]
        fill_field(padded, dz_ref)
        lane = pl.multiple_of(128 * (zone >> 1), 128)
        at = pl.multiple_of(64 * (zone & 1), 64)
        for phase in range(4):
            chosen = field[phase // 2, phase % 2, 1:10, 1:10, :, pl.ds(lane, 128)]
            turned[phase] = chosen.reshape(1296, 128).T
        for tap in range(10):
            if tap < 9:
                a, b = divmod(tap, 3)
                left = turned[2 * ((a + 1) % 2) + (b + 1) % 2, pl.ds(at, 64)]
                row_at, col_at = 2 if a == 0 else 1, 2 if b == 0 else 1
                right = padded[row_at : row_at + 9, col_at : col_at + 9].reshape(1296, LANES)
            else:
                left = turned[0, pl.ds(at, 64)]
                right = dz_p_ref[...].reshape(1296, LANES)
            out[64 * tap : 64 * tap + 64] = dot(left, right).astype(bf16)
        out[640:656] = pack_vectors([sums_ref[0:1], sums_ref[2:3], sums_ref[1:2], sums_ref[3:4]])

    scratch = [
        pltpu.VMEM((4, 128, 1296), bf16), pltpu.VMEM((11, 11, 16, LANES), bf16)
    ]
    return call(
        kernel, "weight_first", (sc, fields, dz, dz_p, sums), "svvvv", [struct((656, LANES))], "v",
        scratch, 2 * 1296 * 640 * LANES, 3_000_000, 20,
    )[0]


def image_back(sc, own, other, w_own, w_other):
    def kernel(sc_ref, own_all, oth_all, w_own_ref, w_oth_ref, out, block):
        for source, half in ((own_all, sc_ref[2]), (oth_all, 1 - sc_ref[2])):
            block[:, :, pl.ds(pl.multiple_of(LANES * half, LANES), LANES)] = source[2]
        own_ref, own_p_ref = own_all.at[0], own_all.at[1]
        oth_ref, oth_p_ref = oth_all.at[0], oth_all.at[1]
        row = lax.broadcasted_iota(jnp.int32, (192, 192), 0)
        col = lax.broadcasted_iota(jnp.int32, (192, 192), 1)
        pixel = jnp.where(row >= 96, row - 96, row)
        line = (pixel * 57) >> 9
        across = pixel - 9 * line
        shifted = {}
        for down in range(2):
            for right in range(2):
                if down + right == 0:
                    shifted[0, 0] = (
                        own_ref[...].reshape(192, LANES),
                        oth_ref[...].reshape(192, LANES),
                    )
                    continue
                fits = (pixel < 81) & (line + down < 9) & (across + right < 9)
                move = jnp.where(fits & (col == row + 9 * down + right), 1.0, 0.0).astype(bf16)
                shifted[down, right] = tuple(
                    dot(move, ref[...].reshape(192, LANES)).astype(bf16)
                    for ref in (own_ref, oth_ref)
                )
        phases = [jnp.zeros((192, LANES), f32) for _ in range(4)]
        for a in range(3):
            for b in range(3):
                at = 2 * ((a + 1) % 2) + (b + 1) % 2
                left = shifted[1 if a == 0 else 0, 1 if b == 0 else 0]
                rows = slice(LANES * (3 * a + b), LANES * (3 * a + b + 1))
                phases[at] = phases[at] + dot_t(left[0], w_own_ref[rows])
                phases[at] = phases[at] + dot_t(left[1], w_oth_ref[rows])
        phases[0] = phases[0] + dot_t(own_p_ref[...].reshape(192, LANES), w_own_ref[2304:2560])
        phases[0] = phases[0] + dot_t(oth_p_ref[...].reshape(192, LANES), w_oth_ref[2304:2560])
        joined = jnp.concatenate([phase.astype(bf16) for phase in phases], axis=0)
        out_row = lax.broadcasted_iota(jnp.int32, (336, 768), 0)
        in_row = lax.broadcasted_iota(jnp.int32, (336, 768), 1)
        line = (out_row * 3641) >> 16
        across = out_row - 18 * line
        source = (2 * (line & 1) + (across & 1)) * 192 + 9 * (line >> 1) + (across >> 1)
        for image in range(2):
            spread = jnp.where(
                (in_row == source + 96 * image) & (out_row < 324), 1.0, 0.0
            ).astype(bf16)
            out[image] = dot(spread, joined).astype(bf16)

    return call(
        kernel, "image_back", (sc, own, other, w_own, w_other), "svvvv",
        [struct((2, 336, LANES)), struct((2, 96, 2 * LANES))], "vv", [], 2 * 192 * 2560 * 512 + 4 * 336 * 768 * 256, 4_000_000, 20,
    )


def add_into(out, rows, sources, vector_rows):
    for at in range(0, rows, 64):
        total = sources[0][at : at + 64].astype(f32)
        for source in sources[1:]:
            total = total + source[at : at + 64].astype(f32)
        out[at : at + 64] = total.astype(bf16)
    totals = [unpack_vectors(source[rows : rows + 16]) for source in sources]
    sums = [sum(one[1:], one[0]) for one in zip(*totals)]
    out[vector_rows : vector_rows + 16] = pack_vectors(sums)


def add_pieces(part, one, two):
    rows = one.shape[0] - 16

    def kernel(one_ref, two_ref, out):
        add_into(out, rows, (one_ref, two_ref), rows)

    return call(
        kernel, f"add_{part}", (one, two), "vv", [struct(one.shape)], "v", [], 1, 1_000_000, 20
    )[0]


def add_two(sc, three, two, came_three, came_two):
    def kernel(sc_ref, three_ref, two_ref, came_three_ref, came_two_ref, keep, give):
        for at_three, out_three, out_two in ((True, keep, give), (False, give, keep)):

            @pl.when((sc_ref[0] == 3) if at_three else (sc_ref[0] != 3))
            def _():
                for at in range(0, 768, 64):
                    span = slice(at, at + 64)
                    total = three_ref[span].astype(f32) + came_three_ref[span].astype(f32)
                    out_three[span] = total.astype(bf16)
                tails = (three_ref.at[768:1168], came_two_ref.at[1168:1568])
                add_into(out_three.at[768:1168], 384, tails, 384)
                add_into(out_two, 1152, (two_ref, came_two_ref), 1152)

    return call(
        kernel, "add_two", (sc, three, two, came_three, came_two), "svvvv", [struct((1168, LANES))] * 2,
        "vv", [], 1, 1_000_000, 20,
    )


def own_piece(sc, groups, after):
    pieces = [piece for _, group in groups for piece in group]

    def kernel(sc_ref, *refs):
        out, used = refs[-1], 0
        for sections, group in groups:
            sources = refs[used : used + len(group)]
            used += len(group)
            rows = group[0].shape[0] - 16

            @pl.when(any_of(sc_ref[0], sections))
            def _():
                add_into(out, rows, sources, 1152)

    return call(
        kernel, "own_piece", (sc, *pieces, *after), "s" + len(pieces) * "v" + len(after) * "a",
        [struct((1168, LANES))], "v", [], 1, 1_000_000, 20,
    )[0]


def lay_out(sc, own, other):
    def kernel(sc_ref, *refs):
        pieces, (out, vectors, wide, out_sems) = refs[:12], refs[12:]
        section, zone, core = sc_ref[0], sc_ref[1], sc_ref[2]
        at_end = (zone == 0) | (zone == 3)
        is_first = section == 0
        for tap in range(9):
            slot = tap % 3
            leaving = [
                pltpu.make_async_copy(
                    wide.at[slot, 128 * cut : 128 * cut + 128],
                    out.at[512 * tap + 128 * cut : 512 * tap + 128 * cut + 128],
                    out_sems.at[slot, cut],
                )
                for cut in range(4)
            ]
            if tap >= 3:
                for copy in leaving:
                    copy.wait()

            def place(which, row_of, rows, first):
                origin = zone ^ (0, 1, 2, 3, 2, 3)[which]
                row = pl.multiple_of(row_of(origin), rows)
                for half in range(2):
                    lane = pl.multiple_of(LANES * (core ^ half), LANES)
                    value = jnp.zeros((rows, LANES), f32)
                    if first + rows <= 1152:
                        value = pieces[which + 6 * half][first : first + rows].astype(f32)
                    wide[slot, pl.ds(row, rows), pl.ds(lane, LANES)] = value

            for kind, chosen in ((0, at_end), (1, jnp.logical_not(at_end))):
                used = (0, 1, 4, 5) if kind == 0 else (0, 1, 2, 3)

                @pl.when(chosen & jnp.logical_not(is_first))
                def _():
                    for which in used:
                        place(which, lambda origin: 128 * origin, 128, 128 * tap)

                @pl.when(chosen & is_first)
                def _():
                    for part in range(2):
                        start = 64 * (2 * tap + part)
                        for which in used:
                            place(
                                which,
                                lambda origin: 256 * part + 64 * origin,
                                64,
                                start if start < 640 else 1152,
                            )

            for copy in leaving:
                copy.start()
        for half in range(2):
            rows = unpack_vectors(pieces[6 * half][1152:1168])
            lane = pl.multiple_of(LANES * (core ^ half), LANES)
            vectors[:, pl.ds(lane, LANES)] = jnp.concatenate(rows, axis=0)
        for slot in range(3):
            for cut in range(4):
                pltpu.make_async_copy(
                    wide.at[slot, 0:128], out.at[0:128], out_sems.at[slot, cut]
                ).wait()

    return call(
        kernel, "lay_out", (sc, *own, *other), "s" + 12 * "v", [struct((4608, 512), f32), struct((4, 512), f32)], "hv",
        [pltpu.VMEM((3, 512, 512), f32), pltpu.SemaphoreType.DMA((3, 4))], 0, 15_000_000, 20,
    )


def half_of(value, half):
    return lax.dynamic_slice_in_dim(value, LANES * half, LANES, axis=value.ndim - 1)


def chip_body(images, res_ids, weights, bn_gain, bn_bias, cotangent):
    section = lax.axis_index("section")
    position = lax.axis_index("dp")
    zone, core = position // 2, position % 2
    sc = jnp.stack([section, zone, core, core]).astype(jnp.int32)

    def after(value, *tokens):
        return lax.optimization_barrier((value, *tokens))[0]

    own = split_weights(sc, weights[0], jnp.concatenate([bn_gain[0], bn_bias[0]], axis=0))
    x_1 = flip(own[0], "section", 1)
    y_1 = flip(own[1], "section", 2)

    level = lax.dynamic_index_in_dim(res_ids, section, 0, keepdims=False)
    side_own = (9 - 2 * (2 - level)).astype(f32)
    tail = jnp.broadcast_to(side_own[:, None, None], (2, 12, 256)).astype(bf16)
    image_own = jnp.concatenate([after(images, own[0])[0].reshape(2, 324, 256), tail], axis=1)
    pieces = [image_own] + [flip(image_own, "dp", 2 * at) for at in range(1, 4)]
    pieces += [flip(piece, "dp", 1) for piece in pieces]
    cot_own = after(cotangent, pieces[1])[0].reshape(2, 81, 512)
    cot_pair = jnp.stack([half_of(cot_own, core), flip(half_of(cot_own, 1 - core), "dp", 1)])
    cot_pair = jnp.pad(cot_pair, ((0, 0), (0, 0), (0, 15), (0, 0)))
    cot_near = jnp.stack([cot_pair, flip(cot_pair, "dp", 2)])
    for_x, for_y, top, bottom = relay_weights(
        "relay_2", lambda at: (at == 1) | (at == 2), (after(sc, cot_near, *pieces[3:6]), *own, x_1, y_1), True
    )
    top = flip(top, "section", 1, lambda i: i == 2)
    bottom = flip(bottom, "section", 2, lambda i: i == 1)
    fields, side = prepare_images(after(sc, for_x), pieces)
    cot_pieces = (cot_near, flip(after(cot_near, fields), "dp", 4))
    x_2 = flip(for_x, "section", 1)
    y_2 = flip(for_y, "section", 2)
    hidden_one, short_one, zhat_0, zhat_p, stats_0, w_first = stage_first(
        sc, side, after(fields, for_x), (own[0], x_1, y_1, top, bottom)
    )
    hidden_one_other = flip(hidden_one, "dp", 1)
    w_first_other = flip(w_first, "dp", 1)
    for_x, for_y = relay_weights("relay_3", lambda at: at == 3, (after(sc, stats_0), *own, x_1, y_1))
    x_3 = flip(for_x, "section", 1, lambda i: i in (1, 3))
    y_3 = flip(for_y, "section", 2, lambda i: i in (2, 3))
    messages = (*own, x_1, y_1, x_2, y_2)
    block_one, zhat_1, stats_1, keep_1, send_1 = stage_rest(
        1, sc, side, hidden_one, hidden_one_other, messages, short_one, after=cot_pieces
    )
    block_one_other = flip(block_one, "dp", 1)
    other_1 = flip(send_1, "dp", 1)
    cot = prepare_cotangent(sc, after(cot_pieces, stats_1))
    hidden_two, zhat_2, stats_2, keep_2, send_2 = stage_rest(
        2, sc, side, block_one, block_one_other, messages, None, after=(x_3, y_3, cot)
    )
    hidden_two_other = flip(hidden_two, "dp", 1)
    other_2 = flip(send_2, "dp", 1)
    messages = (*own, x_1, y_1, x_3, y_3)
    dz_3, passed, out, sums_3, keep_3, send_3 = stage_rest(
        3, sc, side, hidden_two, hidden_two_other, messages, block_one, cot
    )
    other_3 = flip(send_3, "dp", 1)
    dz_3_other = flip(dz_3, "dp", 1)

    def to_pair(part, piece):
        return flip(piece, "section", 2, lambda i: i ^ 2 in (part, part ^ 1))

    piece_3 = weight_rest(3, sc, hidden_two, hidden_two_other, dz_3, sums_3)
    came_3 = to_pair(3, piece_3[0:768])
    dz_2, sums_2 = stage_back(
        2, sc, side, after(dz_3, piece_3), dz_3_other, keep_3, other_3, zhat_2, stats_2
    )
    dz_2_other = flip(dz_2, "dp", 1)
    piece_2 = weight_rest(2, sc, block_one, block_one_other, dz_2, sums_2, piece_3)
    came_2 = to_pair(2, piece_2)
    dz_1, sums_1, short_grad = stage_back(
        1, sc, side, after(dz_2, piece_2), dz_2_other, keep_2, other_2, zhat_1, stats_1, short_one,
        passed,
    )
    dz_1_other = flip(dz_1, "dp", 1)
    piece_1 = weight_rest(
        1, sc, hidden_one, hidden_one_other, after(dz_1, came_3), sums_1
    )
    came_1 = flip(piece_1, "section", 1, lambda i: i in (0, 2))
    dz_0, sums_0, dz_p = stage_back(
        0, sc, side, after(dz_1, piece_1), dz_1_other, keep_1, other_1, zhat_0, stats_0,
        proj=(short_grad, zhat_p),
    )
    piece_0 = weight_first(sc, fields, dz_0, dz_p, sums_0)
    came_0 = flip(piece_0, "section", 2, lambda i: i in (2, 3))
    keep_late, give_late = add_two(sc, after(piece_3, piece_0), piece_2, came_3, came_2)
    last_late = flip(give_late, "section", 1, lambda i: i in (2, 3))
    sum_1 = add_pieces(1, after(piece_1, give_late), came_1)
    last_1 = flip(sum_1, "section", 2, lambda i: i == 3)
    sum_0 = add_pieces(0, after(piece_0, sum_1), came_0)
    last_0 = flip(sum_0, "section", 1, lambda i: i == 1)
    keep, give = pick_images(sc, *after((dz_0, dz_p, out), sum_0))
    image_raw, block_output = image_back(sc, keep, flip(give, "dp", 1), w_first, w_first_other)
    block_output = block_output[:, 0:81]
    rows = jnp.arange(18, dtype=jnp.int32)
    inner_rows = (rows < 2 * (9 - 2 * (2 - level))[:, None]).astype(bf16)
    mask_in = inner_rows[:, :, None] * inner_rows[:, None, :]
    image_grad = image_raw[:, 0:324].reshape(2, 18, 18, 256) * mask_in[..., None]
    total = own_piece(
        sc,
        [((0,), (sum_0, last_0)), ((1,), (sum_1, last_1)), ((2, 3), (keep_late, last_late))],
        (image_raw,),
    )
    from_far = flip(total, "dp", 4, lambda i: i // 2 in (0, 3))
    from_near = flip(total, "dp", 2)
    from_middle = flip(total, "dp", 6, lambda i: i // 2 in (1, 2))
    from_end = flip(total, "dp", 4, lambda i: i // 2 in (1, 2))
    relayed = flip(from_far, "dp", 2, lambda i: i // 2 in (1, 2))
    from_near, block_output, image_grad = lax.optimization_barrier(
        (from_near, block_output, image_grad)
    )
    gathered = [total, from_near, from_far, from_middle, from_end, relayed]
    weight_grad, vectors = lay_out(sc, gathered, [flip(piece, "dp", 1) for piece in gathered])

    return (
        block_output.reshape(1, 2, 9, 9, 512),
        image_grad[None],
        weight_grad[None],
        vectors[None, 0:2],
        vectors[None, 2:4],
    )


def solution(mesh):
    placed = (
        P("section", "dp", None, None, None),
        P(None, "dp"),
        P("section", None, None),
        P("section", None, None),
        P("section", None, None),
        P("section", "dp", None, None, None),
    )
    on_chip = mesh.shape["section"] == 4 and mesh.shape["dp"] == 8
    return jax.shard_map(
        chip_body if on_chip else pipeline_body,
        mesh=mesh,
        in_specs=placed,
        out_specs=(
            P("section", "dp", None, None, None),
            P("section", "dp", None, None, None),
            P("section", None, None),
            P("section", None, None),
            P("section", None, None),
        ),
        check_vma=False,
    )
```
